32 devices in a mesh: rows: 16 (over z, y, core), blk: 2 (over x).
Axes of the slice: x: 2, y: 2, z: 4, core: 2. Of those that a mesh axis runs over, the one named last changes fastest.
Arguments:
- hidden: bfloat16 [16, 768, 1280], P('rows', 'blk'), may hold values from -6 to 6
- starts: int32 [16, 4], P('rows'), may hold values from 0 to 767, as said below
- first_gain: float32 [1280], replicated, may hold values from 0.5 to 2
- first_shift: float32 [1280], replicated, may hold values from -3 to 3
- qkv_weight: bfloat16 [1280, 3840], P('rows'), may hold values from -0.15625 to 0.15625
- out_weight: bfloat16 [1280, 1280], P('rows'), may hold values from -0.625 to 0.625
- second_gain: float32 [1280], replicated, may hold values from 0.5 to 2
- second_shift: float32 [1280], replicated, may hold values from -3 to 3
- up_weight: bfloat16 [1280, 5120], P('rows'), may hold values from -0.15625 to 0.15625
- hidden_bias: float32 [5120], replicated, may hold values from -3 to 3
- down_weight: bfloat16 [5120, 1280], P('rows'), may hold values from -0.078125 to 0.078125
- cotangent: bfloat16 [16, 768, 1280], P('rows', 'blk'), may hold values from -6 to 6
Outputs:
- output: float32 [16, 768, 1280], P('rows', 'blk')
- grad_hidden: float32 [16, 768, 1280], P('rows', 'blk')
- grad_qkv: float32 [1280, 3840], P('rows')
- grad_out: float32 [1280, 1280], P('rows')
- grad_up: float32 [1280, 5120], P('rows')
- grad_down: float32 [5120, 1280], P('rows')
- grad_first_gain: float32 [1280], replicated
- grad_first_shift: float32 [1280], replicated
- grad_second_gain: float32 [1280], replicated
- grad_second_shift: float32 [1280], replicated
- grad_hidden_bias: float32 [5120], replicated
The draws below stay inside these ranges and needn't reach their ends.
Inputs may be any that keep to these rules, and one draw needn't show every extreme that they name: Each row of starts lists the first positions (CLS tokens) of its 4 cells in increasing order, beginning with 0; every cell holds one position or more, and a cell runs up to the next start (the last up to 768). In every row one cell begins among the first 384 positions and ends among the last 384.
All inputs are finite; a program needn't handle non-finite values.
Results may differ from the reference program's by a relative error of at most 0.02.
Values may be sent and summed in bfloat16 or wider, within the bound.
A program may use at most 256 MiB of HBM per device.

```python
import math
import jax
import jax.numpy as jnp
from jax import lax

D = 1280
HEADS = 20
HEAD_DIM = 64
FF = 5120
ROW_DEV = 384
CELLS = 4
ROW_LEN = 768
PACKS = 16


def draw_starts(key, part):
    key = jax.random.fold_in(key, 7)
    length_key, pick_key = jax.random.split(key)
    longest = (ROW_DEV - 1) // (CELLS - 1)
    shortest = longest // 2 + 1
    lengths = jax.random.randint(length_key, (PACKS, CELLS), shortest, longest + 1)
    chosen = jax.random.randint(pick_key, (PACKS, 1), 0, CELLS)
    picked = jnp.arange(CELLS)[None, :] == chosen
    others = jnp.sum(jnp.where(picked, 0, lengths), axis=1, keepdims=True)
    lengths = jnp.where(picked, ROW_LEN - others, lengths)
    return (jnp.cumsum(lengths, axis=1) - lengths).astype(jnp.int32)


def block_scale(stream_key, extent, shards, least, largest):
    factor_of = 1.0
    for dim, parts in shards:
        heights = jax.random.uniform(jax.random.fold_in(jax.random.fold_in(stream_key, 6), dim), (parts,), jnp.float32, least / len(shards), largest / len(shards))
        factor_of = factor_of * jnp.repeat(jnp.exp(heights), extent[dim] // parts).reshape((-1,) + (1,) * (len(extent) - 1 - dim))
    return factor_of


def normal_values(stream_key, extent, scale, limit, shards=(), kind=jnp.bfloat16):
    result = scale * jax.random.normal(stream_key, extent, jnp.float32)
    if shards:
        result = result * block_scale(stream_key, extent, shards, -0.22, 0.18)
    return jnp.clip(result, -limit, limit).astype(kind)


def setup_inputs(seed: int = 0) -> dict:
    seeds = jax.random.split(jax.random.key(seed), 13)
    return {
        "hidden": normal_values(seeds[0], (PACKS, ROW_LEN, D), 1.0, 6.0, ((0, 16), (1, 2))),
        "starts": draw_starts(jax.random.fold_in(seeds[12], 71), 0),
        "first_gain": jnp.clip(jnp.exp(jax.random.uniform(seeds[2], (D,), jnp.float32, math.log(0.5), math.log(2.0))), 0.5, 2.0),
        "first_shift": normal_values(seeds[3], (D,), 0.5, 3.0, (), jnp.float32),
        "qkv_weight": normal_values(seeds[4], (D, 3 * D), D ** -0.5, 0.15625, ((0, 16),)),
        "out_weight": normal_values(seeds[5], (D, D), (max(1, D * 64 // ROW_LEN)) ** -0.5, 0.625, ((0, 16),)),
        "second_gain": jnp.clip(jnp.exp(jax.random.uniform(seeds[6], (D,), jnp.float32, math.log(0.5), math.log(2.0))), 0.5, 2.0),
        "second_shift": normal_values(seeds[7], (D,), 0.5, 3.0, (), jnp.float32),
        "up_weight": normal_values(seeds[8], (D, FF), D ** -0.5, 0.15625, ((0, 16),)),
        "hidden_bias": normal_values(seeds[9], (FF,), 0.5, 3.0, (), jnp.float32),
        "down_weight": normal_values(seeds[10], (FF, D), FF ** -0.5, 0.078125, ((0, 16),)),
        "cotangent": normal_values(seeds[11], (PACKS, ROW_LEN, D), 1.0, 6.0, ((0, 16), (1, 2))),
    }


@jax.custom_vjp
def low(v):
    return lax.optimization_barrier(v.astype(jnp.bfloat16)).astype(jnp.float32)

@jax.custom_vjp
def low_back(v):
    return v

def low_keep(v):
    return (low(v), None)

def low_pass(kept, grad):
    return (grad,)

def back_keep(v):
    return (v, None)

def back_low(kept, grad):
    return (low(grad),)
low.defvjp(low_keep, low_pass)
low_back.defvjp(back_keep, back_low)
highest = lax.Precision.HIGHEST
masked_score = -1e+30

def matmul(left, right):
    return jnp.dot(left, right, precision=highest)

def layer_norm(values, gain, shift):
    mean_value = lax.optimization_barrier(jnp.mean(values, axis=-1, keepdims=True))
    centred = values - mean_value
    variance = lax.optimization_barrier(jnp.mean(centred * centred, axis=-1, keepdims=True))
    return centred * lax.rsqrt(variance + 1e-05) * gain + shift

def segment_of(starts_row, positions):
    reached = starts_row[None, :] <= positions[:, None]
    return lax.optimization_barrier(jnp.sum(reached.astype(jnp.int32), axis=1)) - 1

def row_layer(hidden_row, segment, params):
    first_gain, first_shift, qkv_weight, out_weight, second_gain, second_shift, up_weight, hidden_bias, down_weight = params
    length = hidden_row.shape[0]
    model_width = hidden_row.shape[1]
    normed = low(layer_norm(hidden_row, first_gain, first_shift))
    packed = low(low_back(matmul(normed, qkv_weight)))
    split_heads = packed.reshape(length, 3, HEADS, HEAD_DIM).transpose(1, 2, 0, 3)
    same_cell = segment[:, None] == segment[None, :]

    def one_head(triple):
        query_rows, key_rows, value_rows = triple
        scores = low_back(matmul(query_rows, key_rows.T) * HEAD_DIM ** (-0.5))
        scores = jnp.where(same_cell, scores, masked_score)
        row_top = lax.optimization_barrier(jnp.max(scores, axis=-1, keepdims=True))
        weights = jnp.exp(scores - row_top)
        probability = low(weights / lax.optimization_barrier(jnp.sum(weights, axis=-1, keepdims=True)))
        return matmul(probability, value_rows)
    per_head = lax.map(jax.checkpoint(one_head), (split_heads[0], split_heads[1], split_heads[2]))
    attended = low(low_back(per_head.transpose(1, 0, 2).reshape(length, model_width)))
    residual = hidden_row + low_back(matmul(attended, out_weight))
    second = low(layer_norm(residual, second_gain, second_shift))
    up_values = low_back(matmul(second, up_weight) + hidden_bias)
    activated = low(jax.nn.gelu(up_values, approximate=False))
    return residual + matmul(activated, down_weight)

def reference(hidden, starts, first_gain, first_shift, qkv_weight, out_weight, second_gain, second_shift, up_weight, hidden_bias, down_weight, cotangent):
    params = tuple((argument.astype(jnp.float32) for argument in (first_gain, first_shift, qkv_weight, out_weight, second_gain, second_shift, up_weight, hidden_bias, down_weight)))
    positions = jnp.arange(ROW_LEN, dtype=jnp.int32)

    def one_row(totals, row_data):
        hidden_row, starts_row, cot_row = row_data
        segment = segment_of(starts_row, positions)
        output_row, pullback = jax.vjp(lambda values, weights: row_layer(values, segment, weights), hidden_row, params)
        grad_row, grad_params = pullback(cot_row)
        return (jax.tree.map(jnp.add, totals, grad_params), (output_row, grad_row))
    initial_grads = jax.tree.map(jnp.zeros_like, params)
    totals, (output, grad_hidden) = lax.scan(one_row, initial_grads, (hidden.astype(jnp.float32), starts, cotangent.astype(jnp.float32)))
    grad_first_gain, grad_first_shift, grad_qkv, grad_out, grad_second_gain, grad_second_shift, grad_up, grad_hidden_bias, grad_down = totals
    return (output, grad_hidden, grad_qkv, grad_out, grad_up, grad_down, grad_first_gain, grad_first_shift, grad_second_gain, grad_second_shift, grad_hidden_bias)
```

```python
import math

import jax
import jax.numpy as jnp
from jax import lax
from jax.sharding import PartitionSpec as P

HEADS = 20
HEAD_DIM = 64


masked_score = -1e30
block_limit = 512


def layer_norm(values, gain, shift):
    mean_value = jnp.mean(values, axis=-1, keepdims=True)
    centred = values - mean_value
    variance = jnp.mean(centred * centred, axis=-1, keepdims=True)
    return centred * lax.rsqrt(variance + 1e-05) * gain + shift


def segment_of(starts_row, positions):
    reached = starts_row[None, :] <= positions[:, None]
    return jnp.sum(reached.astype(jnp.int32), axis=1) - 1


def scores_with_mask(queries, key_block, query_seg, key_seg):
    products = jnp.einsum("qhe,khe->hqk", queries, key_block, preferred_element_type=jnp.float32)
    products = products * queries.shape[2] ** (-0.5)
    allowed = (query_seg[:, None] == key_seg[None, :])[None, :, :]
    return (jnp.where(allowed, products, masked_score), allowed)


def attend_rows(running, key_rows, value_rows, queries, query_seg, starts_row):
    piece_rows = key_rows.shape[0]
    step_rows = math.gcd(piece_rows, block_limit)
    head_count = queries.shape[1]
    head_width = queries.shape[2]

    def one_block(block_index, state):
        row_top, denominator, weighted = state
        block_start = block_index * step_rows
        key_block = lax.dynamic_slice_in_dim(key_rows, block_start, step_rows, 0).reshape(
            step_rows, head_count, head_width
        )
        value_block = lax.dynamic_slice_in_dim(value_rows, block_start, step_rows, 0).reshape(
            step_rows, head_count, head_width
        )
        key_seg = segment_of(starts_row, block_start + jnp.arange(step_rows, dtype=jnp.int32))
        scores, allowed = scores_with_mask(queries, key_block, query_seg, key_seg)
        new_top = jnp.maximum(row_top, jnp.max(scores, axis=-1))
        factor = jnp.exp(row_top - new_top)
        weights = jnp.where(allowed, jnp.exp(scores - new_top[:, :, None]), 0.0)
        denominator = denominator * factor + jnp.sum(weights, axis=-1)
        weighted = weighted * factor[:, :, None] + jnp.einsum(
            "hqk,khe->hqe",
            weights.astype(jnp.bfloat16),
            value_block,
            preferred_element_type=jnp.float32,
        )
        return (new_top, denominator, weighted)

    return lax.fori_loop(0, piece_rows // step_rows, one_block, running)


def on_device(
    hidden,
    starts,
    first_gain,
    first_shift,
    qkv_weight,
    out_weight,
    second_gain,
    second_shift,
    up_weight,
    hidden_bias,
    down_weight,
    cotangent,
):
    rows_here = hidden.shape[1]
    model_width = hidden.shape[2]
    head_count = HEADS
    head_width = HEAD_DIM
    score_scale = head_width ** (-0.5)
    inputs = hidden[0].astype(jnp.float32)
    starts_row = starts[0]
    offset = lax.axis_index("blk") * rows_here
    query_seg = segment_of(starts_row, offset + jnp.arange(rows_here, dtype=jnp.int32))
    qkv_full, out_full, up_full, down_full = (
        lax.all_gather(qkv_weight, "rows", axis=0, tiled=True),
        lax.all_gather(out_weight, "rows", axis=0, tiled=True),
        lax.all_gather(up_weight, "rows", axis=0, tiled=True),
        lax.all_gather(down_weight, "rows", axis=0, tiled=True),
    )
    normed_low = layer_norm(inputs, first_gain, first_shift).astype(jnp.bfloat16)
    packed = jnp.dot(normed_low, qkv_full, preferred_element_type=jnp.float32).astype(jnp.bfloat16)
    queries = packed[:, :model_width].reshape(rows_here, head_count, head_width)
    key_rows = packed[:, model_width : 2 * model_width]
    value_rows = packed[:, 2 * model_width :]
    initial = (
        jnp.full((head_count, rows_here), masked_score, jnp.float32),
        jnp.zeros((head_count, rows_here), jnp.float32),
        jnp.zeros((head_count, rows_here, head_width), jnp.float32),
    )
    row_top, denominator, weighted = attend_rows(
        initial,
        lax.all_gather(key_rows, "blk", axis=0, tiled=True),
        lax.all_gather(value_rows, "blk", axis=0, tiled=True),
        queries,
        query_seg,
        starts_row,
    )
    log_total = row_top + jnp.log(denominator)
    attended = jnp.transpose(weighted / denominator[:, :, None], (1, 0, 2))
    attended_low = attended.reshape(rows_here, model_width).astype(jnp.bfloat16)
    residual = inputs + jnp.dot(attended_low, out_full, preferred_element_type=jnp.float32)
    second_low = layer_norm(residual, second_gain, second_shift).astype(jnp.bfloat16)
    up_values = jnp.dot(second_low, up_full, preferred_element_type=jnp.float32) + hidden_bias
    activated_low = jax.nn.gelu(up_values, approximate=False).astype(jnp.bfloat16)
    output = residual + jnp.dot(activated_low, down_full, preferred_element_type=jnp.float32)
    cot_low = cotangent[0]
    d_activated = jnp.einsum("tc,fc->tf", cot_low, down_full, preferred_element_type=jnp.float32)
    unused_gelu, gelu_pull = jax.vjp(
        lambda values: jax.nn.gelu(values, approximate=False), up_values
    )
    d_up_low = gelu_pull(d_activated)[0].astype(jnp.bfloat16)
    d_second = jnp.einsum("tf,cf->tc", d_up_low, up_full, preferred_element_type=jnp.float32)
    unused_second, second_pull = jax.vjp(layer_norm, residual, second_gain, second_shift)
    d_norm_two, d_second_gain, d_second_shift = second_pull(d_second)
    d_residual = cot_low.astype(jnp.float32) + d_norm_two
    d_branch_low = d_residual.astype(jnp.bfloat16)
    d_attended_low = jnp.einsum(
        "tc,kc->tk", d_branch_low, out_full, preferred_element_type=jnp.float32
    ).astype(jnp.bfloat16)
    d_attended3 = d_attended_low.reshape(rows_here, head_count, head_width)
    row_dots = jnp.einsum("qhe,qhe->hq", d_attended3.astype(jnp.float32), attended)
    keys_all, values_all = (
        lax.all_gather(key_rows, "blk", axis=0, tiled=True),
        lax.all_gather(value_rows, "blk", axis=0, tiled=True),
    )
    length = keys_all.shape[0]
    step_rows = math.gcd(length, block_limit)

    def block_terms(block_index):
        block_start = block_index * step_rows
        key_block = lax.dynamic_slice_in_dim(keys_all, block_start, step_rows, 0).reshape(
            step_rows, head_count, head_width
        )
        value_block = lax.dynamic_slice_in_dim(values_all, block_start, step_rows, 0).reshape(
            step_rows, head_count, head_width
        )
        key_seg = segment_of(starts_row, block_start + jnp.arange(step_rows, dtype=jnp.int32))
        scores, allowed = scores_with_mask(queries, key_block, query_seg, key_seg)
        probability = jnp.where(allowed, jnp.exp(scores - log_total[:, :, None]), 0.0)
        d_probs = jnp.einsum(
            "qhe,khe->hqk", d_attended3, value_block, preferred_element_type=jnp.float32
        )
        d_scores = (probability * (d_probs - row_dots[:, :, None])).astype(jnp.bfloat16)
        return (key_block, probability, d_scores)

    dq_start = jnp.zeros((rows_here, head_count, head_width), jnp.float32)

    def back_block(dq_sum, block_index):
        key_block, probability, d_scores = block_terms(block_index)
        dq_sum = dq_sum + jnp.einsum(
            "hqk,khe->qhe", d_scores, key_block, preferred_element_type=jnp.float32
        )
        dk_block = (
            jnp.einsum("hqk,qhe->khe", d_scores, queries, preferred_element_type=jnp.float32)
            * score_scale
        )
        dv_block = jnp.einsum(
            "hqk,qhe->khe",
            probability.astype(jnp.bfloat16),
            d_attended3,
            preferred_element_type=jnp.float32,
        )
        return (
            dq_sum,
            (dk_block.reshape(step_rows, model_width), dv_block.reshape(step_rows, model_width)),
        )

    dq_sum, (dk_terms, dv_terms) = lax.scan(back_block, dq_start, jnp.arange(length // step_rows))
    dk_rows, dv_rows = (
        lax.psum_scatter(
            dk_terms.reshape(length, model_width).astype(jnp.bfloat16),
            "blk",
            scatter_dimension=0,
            tiled=True,
        ).astype(jnp.float32),
        lax.psum_scatter(
            dv_terms.reshape(length, model_width).astype(jnp.bfloat16),
            "blk",
            scatter_dimension=0,
            tiled=True,
        ).astype(jnp.float32),
    )
    d_packed = jnp.concatenate(
        [(dq_sum * score_scale).reshape(rows_here, model_width), dk_rows, dv_rows], axis=1
    ).astype(jnp.bfloat16)
    d_normed = jnp.einsum("tn,cn->tc", d_packed, qkv_full, preferred_element_type=jnp.float32)
    unused_first, first_pull = jax.vjp(layer_norm, inputs, first_gain, first_shift)
    d_norm_one, d_first_gain, d_first_shift = first_pull(d_normed)
    grad_hidden = d_residual + d_norm_one
    d_bias = jnp.sum(d_up_low, axis=0, dtype=jnp.float32)
    wide_share = lax.psum_scatter(
        jnp.concatenate(
            [
                jnp.einsum("tc,tn->cn", normed_low, d_packed, preferred_element_type=jnp.float32),
                jnp.einsum(
                    "tc,tn->cn", attended_low, d_branch_low, preferred_element_type=jnp.float32
                ),
                jnp.einsum("tc,tn->cn", second_low, d_up_low, preferred_element_type=jnp.float32),
            ],
            axis=1,
        ).astype(jnp.bfloat16),
        "rows",
        scatter_dimension=0,
        tiled=True,
    )
    down_share = lax.psum_scatter(
        jnp.einsum("tf,tn->fn", activated_low, cot_low, preferred_element_type=jnp.float32).astype(
            jnp.bfloat16
        ),
        "rows",
        scatter_dimension=0,
        tiled=True,
    )
    wide_grads, down_grads = (
        lax.psum(wide_share, "blk").astype(jnp.float32),
        lax.psum(down_share, "blk").astype(jnp.float32),
    )
    grad_qkv = wide_grads[:, : 3 * model_width]
    grad_out = wide_grads[:, 3 * model_width : 4 * model_width]
    grad_up = wide_grads[:, 4 * model_width :]
    small_grads = lax.psum(
        (d_first_gain, d_first_shift, d_second_gain, d_second_shift, d_bias), ("rows", "blk")
    )
    return (
        output[None],
        grad_hidden[None],
        grad_qkv,
        grad_out,
        grad_up,
        down_grads,
        small_grads[0],
        small_grads[1],
        small_grads[2],
        small_grads[3],
        small_grads[4],
    )


def split_layer(
    hidden, starts, first_gain, first_shift, qkv_weight, out_weight, second_gain, second_shift,
    up_weight, hidden_bias, down_weight, cotangent,
):
    own_rows, width = hidden.shape[1], hidden.shape[2]
    pieces = lax.axis_size("blk")
    piece = lax.axis_index("blk")
    shards = lax.axis_size("rows")
    heads = HEADS // pieces
    cols = heads * HEAD_DIM
    length = own_rows * pieces
    units = down_weight.shape[0] // pieces
    scale = HEAD_DIM ** (-0.5)
    starts_row = starts[0]

    qkv_own = lax.dynamic_index_in_dim(
        qkv_weight.reshape(-1, 3, pieces, cols), piece, 2, keepdims=False
    ).reshape(-1, 3 * cols)
    up_own = lax.dynamic_index_in_dim(
        up_weight.reshape(-1, shards, pieces, units), piece, 2, keepdims=False
    ).reshape(-1, shards * units)
    bias_own = lax.dynamic_index_in_dim(
        hidden_bias.reshape(shards, pieces, units), piece, 1, keepdims=False
    ).reshape(-1)
    down_own = lax.dynamic_slice_in_dim(down_weight, piece * units, units, 0)
    hidden_all = lax.all_gather(hidden[0], "blk", axis=0, tiled=True)
    dy_all = lax.all_gather(cotangent[0], "blk", axis=0, tiled=True)
    qkv_all = lax.all_gather(qkv_own, "rows", axis=0, tiled=True)
    out_all = lax.all_gather(out_weight, "rows", axis=0, tiled=True)
    up_all = lax.all_gather(up_own, "rows", axis=0, tiled=True)
    down_all = lax.all_gather(down_own, "rows", axis=0, tiled=True)

    f32 = jnp.float32
    bf16 = jnp.bfloat16
    normed = layer_norm(hidden_all.astype(f32), first_gain, first_shift).astype(bf16)
    packed = jnp.dot(normed, qkv_all, preferred_element_type=f32).astype(bf16)
    q, k, v = (
        packed[:, i * cols : (i + 1) * cols].reshape(length, heads, HEAD_DIM).transpose(1, 0, 2)
        for i in range(3)
    )
    seg = segment_of(starts_row, jnp.arange(length, dtype=jnp.int32))
    allowed = (seg[:, None] == seg[None, :])[None]
    scores = jnp.einsum("hqe,hke->hqk", q, k, preferred_element_type=f32) * scale
    scores = jnp.where(allowed, scores, masked_score)
    top = jnp.max(scores, axis=-1, keepdims=True)
    weights = jnp.exp(scores - top)
    total = jnp.sum(weights, axis=-1, keepdims=True)
    log_total = top + jnp.log(total)
    attended = jnp.einsum(
        "hqk,hke->hqe", (weights / total).astype(bf16), v, preferred_element_type=f32
    )
    attended_part = attended.transpose(1, 0, 2).reshape(length, cols).astype(bf16)
    attended_low = lax.all_to_all(attended_part, "blk", 0, 1, tiled=True)
    inputs = hidden[0].astype(f32)
    residual = inputs + jnp.dot(attended_low, out_all, preferred_element_type=f32)
    second_own = layer_norm(residual, second_gain, second_shift).astype(bf16)
    second = lax.all_gather(second_own, "blk", axis=0, tiled=True)
    up_values = jnp.dot(second, up_all, preferred_element_type=f32) + bias_own
    activated = jax.nn.gelu(up_values, approximate=False).astype(bf16)
    down_part = jnp.dot(activated, down_all, preferred_element_type=f32).astype(bf16)
    output = residual + lax.psum_scatter(
        down_part, "blk", scatter_dimension=0, tiled=True
    ).astype(f32)

    grad_down = jnp.einsum("tf,tn->fn", activated, dy_all, preferred_element_type=f32)
    d_act = jnp.einsum("tc,fc->tf", dy_all, down_all, preferred_element_type=f32)
    _, gelu_pull = jax.vjp(lambda u: jax.nn.gelu(u, approximate=False), up_values)
    d_up = gelu_pull(d_act)[0].astype(bf16)
    grad_up = jnp.einsum("tc,tn->cn", second, d_up, preferred_element_type=f32)
    d_second_part = jnp.einsum("tf,cf->tc", d_up, up_all, preferred_element_type=f32)
    d_second = lax.psum_scatter(
        d_second_part.astype(bf16), "blk", scatter_dimension=0, tiled=True
    ).astype(f32)
    _, second_pull = jax.vjp(layer_norm, residual, second_gain, second_shift)
    d_norm_two, d_second_gain, d_second_shift = second_pull(d_second)
    d_residual = cotangent[0].astype(f32) + d_norm_two
    d_branch = d_residual.astype(bf16)
    grad_out = jnp.einsum("tc,tn->cn", attended_low, d_branch, preferred_element_type=f32)
    d_att_own = jnp.einsum("tc,kc->tk", d_branch, out_all, preferred_element_type=f32)
    d_att = lax.all_to_all(d_att_own.astype(bf16), "blk", 1, 0, tiled=True)
    d_att3 = d_att.reshape(length, heads, HEAD_DIM).transpose(1, 0, 2)
    row_dots = jnp.sum(d_att3.astype(f32) * attended, axis=-1, keepdims=True)
    probs = jnp.where(allowed, jnp.exp(scores - log_total), 0.0)
    d_probs = jnp.einsum("hqe,hke->hqk", d_att3, v, preferred_element_type=f32)
    d_scores = (probs * (d_probs - row_dots)).astype(bf16)
    dq = jnp.einsum("hqk,hke->qhe", d_scores, k, preferred_element_type=f32) * scale
    dk = jnp.einsum("hqk,hqe->khe", d_scores, q, preferred_element_type=f32) * scale
    dv = jnp.einsum("hqk,hqe->khe", probs.astype(bf16), d_att3, preferred_element_type=f32)
    d_packed = jnp.concatenate([t.reshape(length, cols) for t in (dq, dk, dv)], axis=1).astype(bf16)
    grad_qkv = jnp.einsum("tc,tn->cn", normed, d_packed, preferred_element_type=f32)
    d_normed_part = jnp.einsum("tn,cn->tc", d_packed, qkv_all, preferred_element_type=f32)
    d_normed = lax.psum_scatter(
        d_normed_part.astype(bf16), "blk", scatter_dimension=0, tiled=True
    ).astype(f32)
    _, first_pull = jax.vjp(layer_norm, inputs, first_gain, first_shift)
    d_norm_one, d_first_gain, d_first_shift = first_pull(d_normed)
    grad_hidden = d_residual + d_norm_one

    def scattered(grad):
        return lax.psum_scatter(grad.astype(bf16), "rows", scatter_dimension=0, tiled=True)

    def both(part):
        return lax.all_gather(part, "blk", axis=0).astype(f32)

    down_share = both(scattered(grad_down)).reshape(pieces * units, width)
    up_share = both(scattered(grad_up)).reshape(pieces, -1, shards, units)
    up_share = up_share.transpose(1, 2, 0, 3).reshape(-1, pieces * shards * units)
    qkv_share = both(scattered(grad_qkv)).reshape(pieces, -1, 3, cols)
    qkv_share = qkv_share.transpose(1, 2, 0, 3).reshape(-1, 3 * pieces * cols)
    out_share = lax.psum(scattered(grad_out), "blk").astype(f32)
    d_bias_own = jnp.sum(d_up.astype(f32), axis=0)
    slots = jnp.zeros((shards, pieces, units), f32)
    d_bias = lax.dynamic_update_index_in_dim(slots, d_bias_own.reshape(shards, units), piece, 1)
    small = lax.psum(
        (d_first_gain, d_first_shift, d_second_gain, d_second_shift, d_bias.reshape(-1)),
        ("rows", "blk"),
    )
    return (output[None], grad_hidden[None], qkv_share, out_share, up_share, down_share) + small


def splits_evenly(mesh):
    pieces = mesh.shape["blk"]
    return HEADS % pieces == 0 and HEADS // pieces * HEAD_DIM % 128 == 0


def solution(mesh):
    in_specs = (
        P("rows", "blk", None),
        P("rows", None),
        P(),
        P(),
        P("rows", None),
        P("rows", None),
        P(),
        P(),
        P("rows", None),
        P(),
        P("rows", None),
        P("rows", "blk", None),
    )
    out_specs = (
        P("rows", "blk", None),
        P("rows", "blk", None),
        P("rows", None),
        P("rows", None),
        P("rows", None),
        P("rows", None),
        P(),
        P(),
        P(),
        P(),
        P(),
    )
    layer = split_layer if splits_evenly(mesh) else on_device
    return jax.shard_map(
        layer, mesh=mesh, in_specs=in_specs, out_specs=out_specs, check_vma=False
    )
```

```python
import math

import jax
import jax.numpy as jnp
from jax import lax
from jax.experimental import pallas as pl
from jax.experimental.pallas import tpu as pltpu
from jax.sharding import PartitionSpec as P

HEADS = 20
HEAD_DIM = 64


masked_score = -1e30
block_limit = 512


def layer_norm(values, gain, shift):
    mean_value = jnp.mean(values, axis=-1, keepdims=True)
    centred = values - mean_value
    variance = jnp.mean(centred * centred, axis=-1, keepdims=True)
    return centred * lax.rsqrt(variance + 1e-05) * gain + shift


def segment_of(starts_row, positions):
    reached = starts_row[None, :] <= positions[:, None]
    return jnp.sum(reached.astype(jnp.int32), axis=1) - 1


def scores_with_mask(queries, key_block, query_seg, key_seg):
    products = jnp.einsum("qhe,khe->hqk", queries, key_block, preferred_element_type=jnp.float32)
    products = products * queries.shape[2] ** (-0.5)
    allowed = (query_seg[:, None] == key_seg[None, :])[None, :, :]
    return (jnp.where(allowed, products, masked_score), allowed)


def attend_rows(running, key_rows, value_rows, queries, query_seg, starts_row):
    piece_rows = key_rows.shape[0]
    step_rows = math.gcd(piece_rows, block_limit)
    head_count = queries.shape[1]
    head_width = queries.shape[2]

    def one_block(block_index, state):
        row_top, denominator, weighted = state
        block_start = block_index * step_rows
        key_block = lax.dynamic_slice_in_dim(key_rows, block_start, step_rows, 0).reshape(
            step_rows, head_count, head_width
        )
        value_block = lax.dynamic_slice_in_dim(value_rows, block_start, step_rows, 0).reshape(
            step_rows, head_count, head_width
        )
        key_seg = segment_of(starts_row, block_start + jnp.arange(step_rows, dtype=jnp.int32))
        scores, allowed = scores_with_mask(queries, key_block, query_seg, key_seg)
        new_top = jnp.maximum(row_top, jnp.max(scores, axis=-1))
        factor = jnp.exp(row_top - new_top)
        weights = jnp.where(allowed, jnp.exp(scores - new_top[:, :, None]), 0.0)
        denominator = denominator * factor + jnp.sum(weights, axis=-1)
        weighted = weighted * factor[:, :, None] + jnp.einsum(
            "hqk,khe->hqe",
            weights.astype(jnp.bfloat16),
            value_block,
            preferred_element_type=jnp.float32,
        )
        return (new_top, denominator, weighted)

    return lax.fori_loop(0, piece_rows // step_rows, one_block, running)


def on_device(
    hidden,
    starts,
    first_gain,
    first_shift,
    qkv_weight,
    out_weight,
    second_gain,
    second_shift,
    up_weight,
    hidden_bias,
    down_weight,
    cotangent,
):
    rows_here = hidden.shape[1]
    model_width = hidden.shape[2]
    head_count = HEADS
    head_width = HEAD_DIM
    score_scale = head_width ** (-0.5)
    inputs = hidden[0].astype(jnp.float32)
    starts_row = starts[0]
    offset = lax.axis_index("blk") * rows_here
    query_seg = segment_of(starts_row, offset + jnp.arange(rows_here, dtype=jnp.int32))
    qkv_full, out_full, up_full, down_full = (
        lax.all_gather(qkv_weight, "rows", axis=0, tiled=True),
        lax.all_gather(out_weight, "rows", axis=0, tiled=True),
        lax.all_gather(up_weight, "rows", axis=0, tiled=True),
        lax.all_gather(down_weight, "rows", axis=0, tiled=True),
    )
    normed_low = layer_norm(inputs, first_gain, first_shift).astype(jnp.bfloat16)
    packed = jnp.dot(normed_low, qkv_full, preferred_element_type=jnp.float32).astype(jnp.bfloat16)
    queries = packed[:, :model_width].reshape(rows_here, head_count, head_width)
    key_rows = packed[:, model_width : 2 * model_width]
    value_rows = packed[:, 2 * model_width :]
    initial = (
        jnp.full((head_count, rows_here), masked_score, jnp.float32),
        jnp.zeros((head_count, rows_here), jnp.float32),
        jnp.zeros((head_count, rows_here, head_width), jnp.float32),
    )
    row_top, denominator, weighted = attend_rows(
        initial,
        lax.all_gather(key_rows, "blk", axis=0, tiled=True),
        lax.all_gather(value_rows, "blk", axis=0, tiled=True),
        queries,
        query_seg,
        starts_row,
    )
    log_total = row_top + jnp.log(denominator)
    attended = jnp.transpose(weighted / denominator[:, :, None], (1, 0, 2))
    attended_low = attended.reshape(rows_here, model_width).astype(jnp.bfloat16)
    residual = inputs + jnp.dot(attended_low, out_full, preferred_element_type=jnp.float32)
    second_low = layer_norm(residual, second_gain, second_shift).astype(jnp.bfloat16)
    up_values = jnp.dot(second_low, up_full, preferred_element_type=jnp.float32) + hidden_bias
    activated_low = jax.nn.gelu(up_values, approximate=False).astype(jnp.bfloat16)
    output = residual + jnp.dot(activated_low, down_full, preferred_element_type=jnp.float32)
    cot_low = cotangent[0]
    d_activated = jnp.einsum("tc,fc->tf", cot_low, down_full, preferred_element_type=jnp.float32)
    unused_gelu, gelu_pull = jax.vjp(
        lambda values: jax.nn.gelu(values, approximate=False), up_values
    )
    d_up_low = gelu_pull(d_activated)[0].astype(jnp.bfloat16)
    d_second = jnp.einsum("tf,cf->tc", d_up_low, up_full, preferred_element_type=jnp.float32)
    unused_second, second_pull = jax.vjp(layer_norm, residual, second_gain, second_shift)
    d_norm_two, d_second_gain, d_second_shift = second_pull(d_second)
    d_residual = cot_low.astype(jnp.float32) + d_norm_two
    d_branch_low = d_residual.astype(jnp.bfloat16)
    d_attended_low = jnp.einsum(
        "tc,kc->tk", d_branch_low, out_full, preferred_element_type=jnp.float32
    ).astype(jnp.bfloat16)
    d_attended3 = d_attended_low.reshape(rows_here, head_count, head_width)
    row_dots = jnp.einsum("qhe,qhe->hq", d_attended3.astype(jnp.float32), attended)
    keys_all, values_all = (
        lax.all_gather(key_rows, "blk", axis=0, tiled=True),
        lax.all_gather(value_rows, "blk", axis=0, tiled=True),
    )
    length = keys_all.shape[0]
    step_rows = math.gcd(length, block_limit)

    def block_terms(block_index):
        block_start = block_index * step_rows
        key_block = lax.dynamic_slice_in_dim(keys_all, block_start, step_rows, 0).reshape(
            step_rows, head_count, head_width
        )
        value_block = lax.dynamic_slice_in_dim(values_all, block_start, step_rows, 0).reshape(
            step_rows, head_count, head_width
        )
        key_seg = segment_of(starts_row, block_start + jnp.arange(step_rows, dtype=jnp.int32))
        scores, allowed = scores_with_mask(queries, key_block, query_seg, key_seg)
        probability = jnp.where(allowed, jnp.exp(scores - log_total[:, :, None]), 0.0)
        d_probs = jnp.einsum(
            "qhe,khe->hqk", d_attended3, value_block, preferred_element_type=jnp.float32
        )
        d_scores = (probability * (d_probs - row_dots[:, :, None])).astype(jnp.bfloat16)
        return (key_block, probability, d_scores)

    dq_start = jnp.zeros((rows_here, head_count, head_width), jnp.float32)

    def back_block(dq_sum, block_index):
        key_block, probability, d_scores = block_terms(block_index)
        dq_sum = dq_sum + jnp.einsum(
            "hqk,khe->qhe", d_scores, key_block, preferred_element_type=jnp.float32
        )
        dk_block = (
            jnp.einsum("hqk,qhe->khe", d_scores, queries, preferred_element_type=jnp.float32)
            * score_scale
        )
        dv_block = jnp.einsum(
            "hqk,qhe->khe",
            probability.astype(jnp.bfloat16),
            d_attended3,
            preferred_element_type=jnp.float32,
        )
        return (
            dq_sum,
            (dk_block.reshape(step_rows, model_width), dv_block.reshape(step_rows, model_width)),
        )

    dq_sum, (dk_terms, dv_terms) = lax.scan(back_block, dq_start, jnp.arange(length // step_rows))
    dk_rows, dv_rows = (
        lax.psum_scatter(
            dk_terms.reshape(length, model_width).astype(jnp.bfloat16),
            "blk",
            scatter_dimension=0,
            tiled=True,
        ).astype(jnp.float32),
        lax.psum_scatter(
            dv_terms.reshape(length, model_width).astype(jnp.bfloat16),
            "blk",
            scatter_dimension=0,
            tiled=True,
        ).astype(jnp.float32),
    )
    d_packed = jnp.concatenate(
        [(dq_sum * score_scale).reshape(rows_here, model_width), dk_rows, dv_rows], axis=1
    ).astype(jnp.bfloat16)
    d_normed = jnp.einsum("tn,cn->tc", d_packed, qkv_full, preferred_element_type=jnp.float32)
    unused_first, first_pull = jax.vjp(layer_norm, inputs, first_gain, first_shift)
    d_norm_one, d_first_gain, d_first_shift = first_pull(d_normed)
    grad_hidden = d_residual + d_norm_one
    d_bias = jnp.sum(d_up_low, axis=0, dtype=jnp.float32)
    wide_share = lax.psum_scatter(
        jnp.concatenate(
            [
                jnp.einsum("tc,tn->cn", normed_low, d_packed, preferred_element_type=jnp.float32),
                jnp.einsum(
                    "tc,tn->cn", attended_low, d_branch_low, preferred_element_type=jnp.float32
                ),
                jnp.einsum("tc,tn->cn", second_low, d_up_low, preferred_element_type=jnp.float32),
            ],
            axis=1,
        ).astype(jnp.bfloat16),
        "rows",
        scatter_dimension=0,
        tiled=True,
    )
    down_share = lax.psum_scatter(
        jnp.einsum("tf,tn->fn", activated_low, cot_low, preferred_element_type=jnp.float32).astype(
            jnp.bfloat16
        ),
        "rows",
        scatter_dimension=0,
        tiled=True,
    )
    wide_grads, down_grads = (
        lax.psum(wide_share, "blk").astype(jnp.float32),
        lax.psum(down_share, "blk").astype(jnp.float32),
    )
    grad_qkv = wide_grads[:, : 3 * model_width]
    grad_out = wide_grads[:, 3 * model_width : 4 * model_width]
    grad_up = wide_grads[:, 4 * model_width :]
    small_grads = lax.psum(
        (d_first_gain, d_first_shift, d_second_gain, d_second_shift, d_bias), ("rows", "blk")
    )
    return (
        output[None],
        grad_hidden[None],
        grad_qkv,
        grad_out,
        grad_up,
        down_grads,
        small_grads[0],
        small_grads[1],
        small_grads[2],
        small_grads[3],
        small_grads[4],
    )


MESH = pl.DeviceIdType.MESH
ROWS_Z, ROWS_Y = 4, 2
PAIR = 128


def place_of():
    index = lax.axis_index("rows")
    return index // 4, lax.rem(index // 2, 2), lax.rem(index, 2)


def row_of(z, y, core):
    return (lax.rem(z + ROWS_Z, ROWS_Z) * ROWS_Y + y) * 2 + core


def aligned(index, step):
    return pl.ds(pl.multiple_of(index * step, step), step)


def dot_nt(left, right):
    return lax.dot_general(left, right, (((1,), (1,)), ((), ())), preferred_element_type=jnp.float32)


def dot_nn(left, right):
    return jnp.dot(left, right, preferred_element_type=jnp.float32)


def head_lanes(width):
    lane = lax.broadcasted_iota(jnp.int32, (1, width), 1)
    return (lane < HEAD_DIM, lane >= HEAD_DIM)


def greet(peers):
    barrier = pltpu.get_barrier_semaphore()
    for peer in peers:
        pl.semaphore_signal(barrier, inc=1, device_id=peer, device_id_type=MESH)
    pl.semaphore_wait(barrier, len(peers))


def neighbours():
    z, y, core = place_of()
    return [
        {"rows": row_of(z + 1, y, core)},
        {"rows": row_of(z + 2, y, core)},
        {"rows": row_of(z + 3, y, core)},
        {"rows": row_of(z, 1 - y, core)},
        {"rows": row_of(z, y, 1 - core)},
        {"blk": 1 - lax.axis_index("blk")},
    ]


def write_mask(starts_ref, mask_ref):
    length = mask_ref.shape[0]
    step = 128

    def rows(i, carry):
        key_at = lax.broadcasted_iota(jnp.int32, (step, length), 0) + i * step
        query_at = lax.broadcasted_iota(jnp.int32, (step, length), 1)
        key_seg = jnp.zeros((step, length), jnp.int32)
        query_seg = jnp.zeros((step, length), jnp.int32)
        for cell in range(starts_ref.shape[1]):
            start = starts_ref[0, cell]
            key_seg += (key_at >= start).astype(jnp.int32)
            query_seg += (query_at >= start).astype(jnp.int32)
        mask_ref[aligned(i, step), :] = jnp.where(key_seg == query_seg, 0.0, masked_score)
        return carry

    lax.fori_loop(0, length // step, rows, 0)


def forward_kernel(
    hidden, cot, starts, gain1, shift1, gain2, shift2, bias, q_own, o_own, u_own, d_own,
    q_all, o_all, u_all, d_all, dy_all, normed_t_out, packed_out, lse_out, att_t_out, resid_out,
    second_t_out, act_out, act_t_out, slope_out,
    hid_other, normed, wq, wo, wu, packed, mask, att_part, att_own, resid, second,
    act, act_t, slope, normed_t, att_t, second_t, lse,
    local_sem, send_sem, recv_sem, x_send, x_recv,
):
    bf16 = jnp.bfloat16
    z, y, core = place_of()
    me = row_of(z, y, core)
    piece = lax.axis_index("blk")
    other = 1 - piece
    own_rows, width = hidden.shape
    length = packed.shape[0]
    own = (q_own, o_own, u_own, d_own)
    gathered = (q_all, o_all, u_all, d_all)
    x_peer = {"blk": other}
    peers = neighbours()
    pairs = packed.shape[1] // (3 * PAIR)
    waits = []

    def local(src, dst, index):
        return pltpu.make_async_copy(src, dst, local_sem.at[index])

    def block(w, stage):
        if stage < 3:
            slot, peer = me, peers[stage]
        elif stage < 7:
            slot, peer = row_of(z - (stage - 3), y, core), peers[3]
        elif stage < 11:
            slot, peer = row_of(z - (stage - 7), y, core), peers[4]
        else:
            slot, peer = row_of(z - (stage - 11), 1 - y, core), peers[4]
        src = own[w] if stage in (0, 1, 2, 3, 7) else gathered[w].at[slot]
        index = w * 15 + stage
        return pltpu.make_async_remote_copy(
            src_ref=src, dst_ref=gathered[w].at[slot], send_sem=send_sem.at[index],
            recv_sem=recv_sem.at[index], device_id=peer, device_id_type=MESH,
        )

    def start(w, *stages):
        for stage in stages:
            block(w, stage).start()

    def arrived(w, *stages):
        for stage in stages:
            block(w, stage).wait_recv()

    def to_x(src, dst, index):
        return pltpu.make_async_remote_copy(
            src_ref=src, dst_ref=dst, send_sem=x_send.at[index], recv_sem=x_recv.at[index],
            device_id=x_peer, device_id_type=MESH,
        )

    def relay_z(w, k):
        arrived(w, k - 1)
        start(w, 3 + k, 7 + k)

    def relay_y(w, k):
        arrived(w, 3 + k)
        start(w, 11 + k)

    greet(peers)
    for w in range(4):
        start(w, 0, 2, 1)
        start(w, 7)
        if w == 0:
            start(w, 3)
    hidden_x = to_x(hidden, hid_other, 0)
    hidden_x.start()
    cot_x = to_x(cot, dy_all.at[piece], 1)
    cot_x.start()
    for w in range(4):
        local(own[w], gathered[w].at[me], w).start()
    local(cot, dy_all.at[piece], 4).start()

    def norm_rows(read, half):
        step = 64

        def body(i, carry):
            rows = read(aligned(i, step)).astype(jnp.float32)
            low = layer_norm(rows, gain1[...], shift1[...]).astype(bf16)
            normed[pl.ds(pl.multiple_of(half * own_rows + i * step, step), step), :] = low
            return carry

        lax.fori_loop(0, own_rows // step, body, 0)

    norm_rows(lambda rows: hidden[rows, :], piece)
    relay_z(0, 1)
    relay_z(0, 3)
    start(1, 3)
    write_mask(starts, mask)
    relay_y(0, 0)
    relay_y(0, 1)
    hidden_x.wait_recv()
    norm_rows(lambda rows: hid_other[rows, :], other)
    relay_z(0, 2)
    relay_y(0, 3)

    def flip(i, carry):
        normed_t[aligned(i, 128), :] = normed[:, aligned(i, 128)].T
        return carry

    lax.fori_loop(0, width // 128, flip, 0)
    local(normed_t, normed_t_out, 8).start()
    relay_z(1, 1)
    relay_y(0, 2)
    relay_z(1, 3)
    start(2, 3)
    arrived(0, *range(7, 15))
    local(own[0], gathered[0].at[me], 0).wait()
    local(q_all, wq, 5).start()
    local(q_all, wq, 5).wait()

    def project(i, carry):
        cols = aligned(i, 3 * PAIR)
        weight = wq[:, :, cols].reshape(width, 3 * PAIR)
        value = dot_nn(normed[...], weight).astype(bf16)
        queries = pl.ds(pl.multiple_of(i * 3 * PAIR, PAIR), PAIR)
        rest = pl.ds(pl.multiple_of(i * 3 * PAIR + PAIR, PAIR), 2 * PAIR)
        packed[:, queries] = value[:, :PAIR] * jnp.asarray(HEAD_DIM ** (-0.5), bf16)
        packed[:, rest] = value[:, PAIR:]
        return carry

    lax.fori_loop(0, pairs, project, 0)
    local(packed, packed_out, 9).start()
    first_lanes = head_lanes(PAIR)

    def attend(p):
        base = 3 * PAIR * p
        value_t = packed[:, base + 2 * PAIR : base + 3 * PAIR].T
        step = 256

        def rows(i, carry):
            queries = packed[aligned(i, step), base : base + PAIR]
            keys = packed[:, base + PAIR : base + 2 * PAIR]
            halves = []
            for h in range(2):
                one = jnp.where(first_lanes[h], queries, jnp.zeros_like(queries))
                scores = dot_nt(keys, one) + mask[:, aligned(i, step)]
                top = jnp.max(scores, axis=0, keepdims=True)
                weights = jnp.exp(scores - top)
                total = jnp.sum(weights, axis=0, keepdims=True)
                lse[2 * p + h : 2 * p + h + 1, aligned(i, step)] = top + jnp.log(total)
                summed = dot_nn(value_t[h * HEAD_DIM : (h + 1) * HEAD_DIM], weights.astype(bf16))
                halves.append(summed / total)
            both = jnp.concatenate(halves, axis=0).T.astype(bf16)
            att_part[aligned(i, step), p * PAIR : (p + 1) * PAIR] = both
            return carry

        lax.fori_loop(0, length // step, rows, 0)

    def att_cols(half, p):
        return pl.ds(pl.multiple_of(half * pairs * PAIR + p * PAIR, PAIR), PAIR)

    att_x = []
    for p in range(pairs):
        attend(p)
        part = att_part.at[pl.ds(pl.multiple_of(other * own_rows, 128), own_rows), pl.ds(p * PAIR, PAIR)]
        att_x.append(to_x(part, att_own.at[:, att_cols(piece, p)], 2 + p))
        att_x[-1].start()
        mine = att_part[pl.ds(pl.multiple_of(piece * own_rows, 128), own_rows), p * PAIR : (p + 1) * PAIR]
        att_own[:, att_cols(piece, p)] = mine
        if p == 0:
            relay_y(1, 0)
            relay_y(1, 1)
        elif p == 1:
            relay_z(1, 2)
        elif p == 2:
            relay_y(1, 3)
        elif p == 3:
            relay_z(2, 1)
        elif p == 4:
            relay_y(1, 2)
    local(lse, lse_out, 10).start()
    for copy in att_x:
        copy.wait_recv()
    arrived(1, *range(7, 15))
    local(own[1], gathered[1].at[me], 1).wait()
    local(o_all, wo, 6).start()

    def flip_att(i, carry):
        att_t[aligned(i, 128), :] = att_own[:, aligned(i, 128)].T
        return carry

    lax.fori_loop(0, width // 128, flip_att, 0)
    local(att_t, att_t_out, 11).start()
    relay_z(2, 3)
    start(3, 3)
    local(o_all, wo, 6).wait()

    def merge(i, carry):
        cols = aligned(i, 256)
        weight = wo[:, :, cols].reshape(width, 256)
        resid[:, cols] = hidden[:, cols].astype(jnp.float32) + dot_nn(att_own[...], weight)
        return carry

    lax.fori_loop(0, width // 256, merge, 0)
    local(resid, resid_out, 12).start()

    def second_rows(i, carry):
        rows = aligned(i, 64)
        second[piece, rows, :] = layer_norm(resid[rows, :], gain2[...], shift2[...]).astype(bf16)
        return carry

    lax.fori_loop(0, own_rows // 64, second_rows, 0)
    second_x = to_x(second.at[piece], second.at[piece], 2 + pairs)
    second_x.start()
    relay_y(2, 0)
    relay_y(2, 1)
    relay_z(2, 2)
    second_x.wait_recv()

    def flip_second(i, carry):
        cols = aligned(i, 128)
        second_t[cols, :] = second[:, :, cols].reshape(length, 128).T
        return carry

    lax.fori_loop(0, width // 128, flip_second, 0)
    local(second_t, second_t_out, 13).start()
    relay_y(2, 3)
    relay_z(3, 1)
    relay_y(2, 2)
    arrived(2, *range(7, 15))
    local(own[2], gathered[2].at[me], 2).wait()
    local(u_all, wu, 7).start()
    local(u_all, wu, 7).wait()
    relay_z(3, 3)
    unit = 256
    steps = act.shape[1] // unit

    def expand(i, carry):
        cols = aligned(i // 2, unit)
        rows = aligned(lax.rem(i, 2), own_rows)
        weight = wu[:, :, cols].reshape(width, unit)
        up = dot_nn(second[lax.rem(i, 2)], weight) + bias[:, cols]
        cdf = 0.5 * (1.0 + lax.erf(up * (0.5 ** 0.5)))
        pdf = jnp.exp(up * up * -0.5) * ((2.0 * math.pi) ** -0.5)
        value = (up * cdf).astype(bf16)
        act[rows, cols] = value
        act_t[cols, rows] = value.T
        slope[rows, cols] = (cdf + up * pdf).astype(bf16)
        return carry

    lax.fori_loop(0, steps, expand, 0)
    relay_y(3, 0)
    relay_y(3, 1)
    lax.fori_loop(steps, 2 * steps, expand, 0)
    local(act, act_out, 14).start()
    local(act_t, act_t_out, 15).start()
    local(slope, slope_out, 16).start()
    relay_z(3, 2)
    relay_y(3, 3)
    relay_y(3, 2)
    arrived(3, *range(7, 15))
    cot_x.wait_recv()
    local(own[3], gathered[3].at[me], 3).wait()
    local(cot, dy_all.at[piece], 4).wait()
    local(normed_t, normed_t_out, 8).wait()
    local(packed, packed_out, 9).wait()
    local(lse, lse_out, 10).wait()
    local(att_t, att_t_out, 11).wait()
    local(resid, resid_out, 12).wait()
    local(second_t, second_t_out, 13).wait()
    local(act, act_out, 14).wait()
    local(act_t, act_t_out, 15).wait()
    local(slope, slope_out, 16).wait()
    for w in range(4):
        for stage in range(15):
            block(w, stage).wait_send()
    for copy in [hidden_x, cot_x, second_x] + att_x:
        copy.wait_send()


def forward(hidden, cot, starts, gain1, shift1, gain2, shift2, bias, q_own, o_own, u_own, d_own):
    own_rows, width = hidden.shape
    length = 2 * own_rows
    cols = q_own.shape[1]
    units = u_own.shape[1]
    bf16, f32 = jnp.bfloat16, jnp.float32
    shards = lax.axis_size("rows")
    weights = (q_own, o_own, u_own, d_own)
    head_rows = 16
    outs = [((shards,) + w.shape, bf16) for w in weights] + [
        ((2, own_rows, width), bf16),
        ((width, length), bf16),
        ((length, cols), bf16),
        ((head_rows, length), f32),
        ((width, own_rows), bf16),
        ((own_rows, width), f32),
        ((width, length), bf16),
        ((length, units), bf16),
        ((units, length), bf16),
        ((length, units), bf16),
    ]
    scratch = [
        ((own_rows, width), bf16),
        ((length, width), bf16),
        ((shards,) + q_own.shape, bf16),
        ((shards,) + o_own.shape, bf16),
        ((shards,) + u_own.shape, bf16),
        ((length, cols), bf16),
        ((length, length), f32),
        ((length, cols // 3), bf16),
        ((own_rows, width), bf16),
        ((own_rows, width), f32),
        ((2, own_rows, width), bf16),
        ((length, units), bf16),
        ((units, length), bf16),
        ((length, units), bf16),
        ((width, length), bf16),
        ((width, own_rows), bf16),
        ((width, length), bf16),
        ((head_rows, length), f32),
    ]
    vmem = pl.BlockSpec(memory_space=pltpu.VMEM)
    anywhere = pl.BlockSpec(memory_space=pl.ANY)
    smem = pl.BlockSpec(memory_space=pltpu.SMEM)
    dma = pltpu.SemaphoreType.DMA
    x_copies = 3 + cols // (3 * PAIR)
    return pl.pallas_call(
        forward_kernel,
        out_shape=[jax.ShapeDtypeStruct(shape, kind) for shape, kind in outs],
        in_specs=[vmem, anywhere, smem] + [vmem] * 5 + [anywhere] * 4,
        out_specs=[anywhere] * len(outs),
        scratch_shapes=[pltpu.VMEM(shape, kind) for shape, kind in scratch]
        + [dma((17,)), dma((60,)), dma((60,)), dma((x_copies,)), dma((x_copies,))],
        compiler_params=pltpu.CompilerParams(
            collective_id=1, has_side_effects=True, vmem_limit_bytes=60 * 1024 * 1024
        ),
        name="forward",
    )(hidden, cot, starts, gain1, shift1, gain2, shift2, bias, *weights)


def own_shares(qkv_weight, up_weight, hidden_bias, down_weight, piece, pieces, shards, cols, units):
    pairs = cols // PAIR
    qkv_own = lax.dynamic_index_in_dim(
        qkv_weight.reshape(-1, 3, pieces, pairs, PAIR), piece, 2, keepdims=False
    )
    qkv_own = qkv_own.transpose(0, 2, 1, 3).reshape(-1, 3 * cols)
    up_own = lax.dynamic_index_in_dim(
        up_weight.reshape(-1, shards, pieces, units), piece, 2, keepdims=False
    ).reshape(-1, shards * units)
    bias_own = lax.dynamic_index_in_dim(
        hidden_bias.reshape(shards, pieces, units), piece, 1, keepdims=False
    ).reshape(1, -1)
    down_own = lax.dynamic_slice_in_dim(down_weight, piece * units, units, 0)
    return qkv_own, up_own, bias_own, down_own


def split_layer(
    hidden, starts, first_gain, first_shift, qkv_weight, out_weight, second_gain, second_shift,
    up_weight, hidden_bias, down_weight, cotangent,
):
    own_rows, width = hidden.shape[1], hidden.shape[2]
    pieces = lax.axis_size("blk")
    piece = lax.axis_index("blk")
    shards = lax.axis_size("rows")
    heads = HEADS // pieces
    cols = heads * HEAD_DIM
    pairs = cols // PAIR
    length = own_rows * pieces
    units = down_weight.shape[0] // pieces
    scale = HEAD_DIM ** (-0.5)
    f32 = jnp.float32
    bf16 = jnp.bfloat16
    qkv_own, up_own, bias_own, down_own = own_shares(
        qkv_weight, up_weight, hidden_bias, down_weight, piece, pieces, shards, cols, units
    )
    flat = lambda v: v.reshape(1, -1)
    (
        qkv_all, out_all, up_all, down_all, dy_all, normed_t, packed, lse, att_t, residual, second_t,
        activated, activated_t, slope,
    ) = forward(
        hidden[0], cotangent[0], starts, flat(first_gain), flat(first_shift), flat(second_gain),
        flat(second_shift), bias_own, qkv_own, out_weight, up_own, down_own,
    )
    qkv_all, out_all, up_all, down_all = (
        w.reshape(-1, w.shape[-1]) for w in (qkv_all, out_all, up_all, down_all)
    )
    dy_all = dy_all.reshape(length, width)
    triple = packed.reshape(length, pairs, 3, 2, HEAD_DIM)
    q, k, v = (triple[:, :, i].reshape(length, heads, HEAD_DIM).transpose(1, 0, 2) for i in range(3))
    seg = segment_of(starts[0], jnp.arange(length, dtype=jnp.int32))
    allowed = (seg[:, None] == seg[None, :])[None]
    inputs = hidden[0].astype(f32)
    down_part = jnp.dot(activated, down_all, preferred_element_type=f32).astype(bf16)
    output = residual + lax.psum_scatter(
        down_part, "blk", scatter_dimension=0, tiled=True
    ).astype(f32)

    grad_down = jnp.dot(activated_t, dy_all, preferred_element_type=f32)
    d_act = jnp.einsum("tc,fc->tf", dy_all, down_all, preferred_element_type=f32)
    d_up = (d_act * slope.astype(f32)).astype(bf16)
    grad_up = jnp.dot(second_t, d_up, preferred_element_type=f32)
    d_second_part = jnp.einsum("tf,cf->tc", d_up, up_all, preferred_element_type=f32)
    d_second = lax.psum_scatter(
        d_second_part.astype(bf16), "blk", scatter_dimension=0, tiled=True
    ).astype(f32)
    _, second_pull = jax.vjp(layer_norm, residual, second_gain, second_shift)
    d_norm_two, d_second_gain, d_second_shift = second_pull(d_second)
    d_residual = cotangent[0].astype(f32) + d_norm_two
    d_branch = d_residual.astype(bf16)
    grad_out = jnp.dot(att_t, d_branch, preferred_element_type=f32)
    d_att_own = jnp.einsum("tc,kc->tk", d_branch, out_all, preferred_element_type=f32)
    d_att = lax.all_to_all(d_att_own.astype(bf16), "blk", 1, 0, tiled=True)
    d_att3 = d_att.reshape(length, heads, HEAD_DIM).transpose(1, 0, 2)
    scores = jnp.einsum("hqe,hke->hqk", q, k, preferred_element_type=f32)
    probs = jnp.where(allowed, jnp.exp(scores - lse[:heads, :, None]), 0.0)
    d_probs = jnp.einsum("hqe,hke->hqk", d_att3, v, preferred_element_type=f32)
    row_dots = jnp.sum(probs * d_probs, axis=-1, keepdims=True)
    d_scores = (probs * (d_probs - row_dots)).astype(bf16)
    dq = jnp.einsum("hqk,hke->qhe", d_scores, k, preferred_element_type=f32) * scale
    dk = jnp.einsum("hqk,hqe->khe", d_scores, q, preferred_element_type=f32)
    dv = jnp.einsum("hqk,hqe->khe", probs.astype(bf16), d_att3, preferred_element_type=f32)
    d_packed = jnp.stack([t.reshape(length, pairs, PAIR) for t in (dq, dk, dv)], axis=2)
    d_packed = d_packed.reshape(length, 3 * cols).astype(bf16)
    grad_qkv = jnp.dot(normed_t, d_packed, preferred_element_type=f32)
    d_normed_part = jnp.einsum("tn,cn->tc", d_packed, qkv_all, preferred_element_type=f32)
    d_normed = lax.psum_scatter(
        d_normed_part.astype(bf16), "blk", scatter_dimension=0, tiled=True
    ).astype(f32)
    _, first_pull = jax.vjp(layer_norm, inputs, first_gain, first_shift)
    d_norm_one, d_first_gain, d_first_shift = first_pull(d_normed)
    grad_hidden = d_residual + d_norm_one

    def scattered(grad):
        return lax.psum_scatter(grad.astype(bf16), "rows", scatter_dimension=0, tiled=True)

    def both(part):
        return lax.all_gather(part, "blk", axis=0).astype(f32)

    down_share = both(scattered(grad_down)).reshape(pieces * units, width)
    up_share = both(scattered(grad_up)).reshape(pieces, -1, shards, units)
    up_share = up_share.transpose(1, 2, 0, 3).reshape(-1, pieces * shards * units)
    qkv_share = both(scattered(grad_qkv)).reshape(pieces, -1, pairs, 3, PAIR)
    qkv_share = qkv_share.transpose(1, 3, 0, 2, 4).reshape(-1, 3 * pieces * cols)
    out_share = lax.psum(scattered(grad_out), "blk").astype(f32)
    d_bias_own = jnp.sum(d_up.astype(f32), axis=0)
    slots = jnp.zeros((shards, pieces, units), f32)
    d_bias = lax.dynamic_update_index_in_dim(slots, d_bias_own.reshape(shards, units), piece, 1)
    small = lax.psum(
        (d_first_gain, d_first_shift, d_second_gain, d_second_shift, d_bias.reshape(-1)),
        ("rows", "blk"),
    )
    return (output[None], grad_hidden[None], qkv_share, out_share, up_share, down_share) + small


def splits_evenly(mesh):
    pieces = mesh.shape["blk"]
    return pieces == 2 and mesh.shape["rows"] == 2 * ROWS_Z * ROWS_Y and HEADS % (2 * pieces) == 0


def solution(mesh):
    in_specs = (
        P("rows", "blk", None),
        P("rows", None),
        P(),
        P(),
        P("rows", None),
        P("rows", None),
        P(),
        P(),
        P("rows", None),
        P(),
        P("rows", None),
        P("rows", "blk", None),
    )
    out_specs = (
        P("rows", "blk", None),
        P("rows", "blk", None),
        P("rows", None),
        P("rows", None),
        P("rows", None),
        P("rows", None),
        P(),
        P(),
        P(),
        P(),
        P(),
    )
    layer = split_layer if splits_evenly(mesh) else on_device
    return jax.shard_map(
        layer, mesh=mesh, in_specs=in_specs, out_specs=out_specs, check_vma=False
    )
```

```python
import math

import jax
import jax.numpy as jnp
from jax import lax
from jax.experimental import pallas as pl
from jax.experimental.pallas import tpu as pltpu
from jax.sharding import PartitionSpec as P

HEADS = 20
HEAD_DIM = 64


masked_score = -1e30
block_limit = 512


def layer_norm(values, gain, shift):
    mean_value = jnp.mean(values, axis=-1, keepdims=True)
    centred = values - mean_value
    variance = jnp.mean(centred * centred, axis=-1, keepdims=True)
    return centred * lax.rsqrt(variance + 1e-05) * gain + shift


def segment_of(starts_row, positions):
    reached = starts_row[None, :] <= positions[:, None]
    return jnp.sum(reached.astype(jnp.int32), axis=1) - 1


def scores_with_mask(queries, key_block, query_seg, key_seg):
    products = jnp.einsum("qhe,khe->hqk", queries, key_block, preferred_element_type=jnp.float32)
    products = products * queries.shape[2] ** (-0.5)
    allowed = (query_seg[:, None] == key_seg[None, :])[None, :, :]
    return (jnp.where(allowed, products, masked_score), allowed)


def attend_rows(running, key_rows, value_rows, queries, query_seg, starts_row):
    piece_rows = key_rows.shape[0]
    step_rows = math.gcd(piece_rows, block_limit)
    head_count = queries.shape[1]
    head_width = queries.shape[2]

    def one_block(block_index, state):
        row_top, denominator, weighted = state
        block_start = block_index * step_rows
        key_block = lax.dynamic_slice_in_dim(key_rows, block_start, step_rows, 0).reshape(
            step_rows, head_count, head_width
        )
        value_block = lax.dynamic_slice_in_dim(value_rows, block_start, step_rows, 0).reshape(
            step_rows, head_count, head_width
        )
        key_seg = segment_of(starts_row, block_start + jnp.arange(step_rows, dtype=jnp.int32))
        scores, allowed = scores_with_mask(queries, key_block, query_seg, key_seg)
        new_top = jnp.maximum(row_top, jnp.max(scores, axis=-1))
        factor = jnp.exp(row_top - new_top)
        weights = jnp.where(allowed, jnp.exp(scores - new_top[:, :, None]), 0.0)
        denominator = denominator * factor + jnp.sum(weights, axis=-1)
        weighted = weighted * factor[:, :, None] + jnp.einsum(
            "hqk,khe->hqe",
            weights.astype(jnp.bfloat16),
            value_block,
            preferred_element_type=jnp.float32,
        )
        return (new_top, denominator, weighted)

    return lax.fori_loop(0, piece_rows // step_rows, one_block, running)


def on_device(
    hidden,
    starts,
    first_gain,
    first_shift,
    qkv_weight,
    out_weight,
    second_gain,
    second_shift,
    up_weight,
    hidden_bias,
    down_weight,
    cotangent,
):
    rows_here = hidden.shape[1]
    model_width = hidden.shape[2]
    head_count = HEADS
    head_width = HEAD_DIM
    score_scale = head_width ** (-0.5)
    inputs = hidden[0].astype(jnp.float32)
    starts_row = starts[0]
    offset = lax.axis_index("blk") * rows_here
    query_seg = segment_of(starts_row, offset + jnp.arange(rows_here, dtype=jnp.int32))
    qkv_full, out_full, up_full, down_full = (
        lax.all_gather(qkv_weight, "rows", axis=0, tiled=True),
        lax.all_gather(out_weight, "rows", axis=0, tiled=True),
        lax.all_gather(up_weight, "rows", axis=0, tiled=True),
        lax.all_gather(down_weight, "rows", axis=0, tiled=True),
    )
    normed_low = layer_norm(inputs, first_gain, first_shift).astype(jnp.bfloat16)
    packed = jnp.dot(normed_low, qkv_full, preferred_element_type=jnp.float32).astype(jnp.bfloat16)
    queries = packed[:, :model_width].reshape(rows_here, head_count, head_width)
    key_rows = packed[:, model_width : 2 * model_width]
    value_rows = packed[:, 2 * model_width :]
    initial = (
        jnp.full((head_count, rows_here), masked_score, jnp.float32),
        jnp.zeros((head_count, rows_here), jnp.float32),
        jnp.zeros((head_count, rows_here, head_width), jnp.float32),
    )
    row_top, denominator, weighted = attend_rows(
        initial,
        lax.all_gather(key_rows, "blk", axis=0, tiled=True),
        lax.all_gather(value_rows, "blk", axis=0, tiled=True),
        queries,
        query_seg,
        starts_row,
    )
    log_total = row_top + jnp.log(denominator)
    attended = jnp.transpose(weighted / denominator[:, :, None], (1, 0, 2))
    attended_low = attended.reshape(rows_here, model_width).astype(jnp.bfloat16)
    residual = inputs + jnp.dot(attended_low, out_full, preferred_element_type=jnp.float32)
    second_low = layer_norm(residual, second_gain, second_shift).astype(jnp.bfloat16)
    up_values = jnp.dot(second_low, up_full, preferred_element_type=jnp.float32) + hidden_bias
    activated_low = jax.nn.gelu(up_values, approximate=False).astype(jnp.bfloat16)
    output = residual + jnp.dot(activated_low, down_full, preferred_element_type=jnp.float32)
    cot_low = cotangent[0]
    d_activated = jnp.einsum("tc,fc->tf", cot_low, down_full, preferred_element_type=jnp.float32)
    unused_gelu, gelu_pull = jax.vjp(
        lambda values: jax.nn.gelu(values, approximate=False), up_values
    )
    d_up_low = gelu_pull(d_activated)[0].astype(jnp.bfloat16)
    d_second = jnp.einsum("tf,cf->tc", d_up_low, up_full, preferred_element_type=jnp.float32)
    unused_second, second_pull = jax.vjp(layer_norm, residual, second_gain, second_shift)
    d_norm_two, d_second_gain, d_second_shift = second_pull(d_second)
    d_residual = cot_low.astype(jnp.float32) + d_norm_two
    d_branch_low = d_residual.astype(jnp.bfloat16)
    d_attended_low = jnp.einsum(
        "tc,kc->tk", d_branch_low, out_full, preferred_element_type=jnp.float32
    ).astype(jnp.bfloat16)
    d_attended3 = d_attended_low.reshape(rows_here, head_count, head_width)
    row_dots = jnp.einsum("qhe,qhe->hq", d_attended3.astype(jnp.float32), attended)
    keys_all, values_all = (
        lax.all_gather(key_rows, "blk", axis=0, tiled=True),
        lax.all_gather(value_rows, "blk", axis=0, tiled=True),
    )
    length = keys_all.shape[0]
    step_rows = math.gcd(length, block_limit)

    def block_terms(block_index):
        block_start = block_index * step_rows
        key_block = lax.dynamic_slice_in_dim(keys_all, block_start, step_rows, 0).reshape(
            step_rows, head_count, head_width
        )
        value_block = lax.dynamic_slice_in_dim(values_all, block_start, step_rows, 0).reshape(
            step_rows, head_count, head_width
        )
        key_seg = segment_of(starts_row, block_start + jnp.arange(step_rows, dtype=jnp.int32))
        scores, allowed = scores_with_mask(queries, key_block, query_seg, key_seg)
        probability = jnp.where(allowed, jnp.exp(scores - log_total[:, :, None]), 0.0)
        d_probs = jnp.einsum(
            "qhe,khe->hqk", d_attended3, value_block, preferred_element_type=jnp.float32
        )
        d_scores = (probability * (d_probs - row_dots[:, :, None])).astype(jnp.bfloat16)
        return (key_block, probability, d_scores)

    dq_start = jnp.zeros((rows_here, head_count, head_width), jnp.float32)

    def back_block(dq_sum, block_index):
        key_block, probability, d_scores = block_terms(block_index)
        dq_sum = dq_sum + jnp.einsum(
            "hqk,khe->qhe", d_scores, key_block, preferred_element_type=jnp.float32
        )
        dk_block = (
            jnp.einsum("hqk,qhe->khe", d_scores, queries, preferred_element_type=jnp.float32)
            * score_scale
        )
        dv_block = jnp.einsum(
            "hqk,qhe->khe",
            probability.astype(jnp.bfloat16),
            d_attended3,
            preferred_element_type=jnp.float32,
        )
        return (
            dq_sum,
            (dk_block.reshape(step_rows, model_width), dv_block.reshape(step_rows, model_width)),
        )

    dq_sum, (dk_terms, dv_terms) = lax.scan(back_block, dq_start, jnp.arange(length // step_rows))
    dk_rows, dv_rows = (
        lax.psum_scatter(
            dk_terms.reshape(length, model_width).astype(jnp.bfloat16),
            "blk",
            scatter_dimension=0,
            tiled=True,
        ).astype(jnp.float32),
        lax.psum_scatter(
            dv_terms.reshape(length, model_width).astype(jnp.bfloat16),
            "blk",
            scatter_dimension=0,
            tiled=True,
        ).astype(jnp.float32),
    )
    d_packed = jnp.concatenate(
        [(dq_sum * score_scale).reshape(rows_here, model_width), dk_rows, dv_rows], axis=1
    ).astype(jnp.bfloat16)
    d_normed = jnp.einsum("tn,cn->tc", d_packed, qkv_full, preferred_element_type=jnp.float32)
    unused_first, first_pull = jax.vjp(layer_norm, inputs, first_gain, first_shift)
    d_norm_one, d_first_gain, d_first_shift = first_pull(d_normed)
    grad_hidden = d_residual + d_norm_one
    d_bias = jnp.sum(d_up_low, axis=0, dtype=jnp.float32)
    wide_share = lax.psum_scatter(
        jnp.concatenate(
            [
                jnp.einsum("tc,tn->cn", normed_low, d_packed, preferred_element_type=jnp.float32),
                jnp.einsum(
                    "tc,tn->cn", attended_low, d_branch_low, preferred_element_type=jnp.float32
                ),
                jnp.einsum("tc,tn->cn", second_low, d_up_low, preferred_element_type=jnp.float32),
            ],
            axis=1,
        ).astype(jnp.bfloat16),
        "rows",
        scatter_dimension=0,
        tiled=True,
    )
    down_share = lax.psum_scatter(
        jnp.einsum("tf,tn->fn", activated_low, cot_low, preferred_element_type=jnp.float32).astype(
            jnp.bfloat16
        ),
        "rows",
        scatter_dimension=0,
        tiled=True,
    )
    wide_grads, down_grads = (
        lax.psum(wide_share, "blk").astype(jnp.float32),
        lax.psum(down_share, "blk").astype(jnp.float32),
    )
    grad_qkv = wide_grads[:, : 3 * model_width]
    grad_out = wide_grads[:, 3 * model_width : 4 * model_width]
    grad_up = wide_grads[:, 4 * model_width :]
    small_grads = lax.psum(
        (d_first_gain, d_first_shift, d_second_gain, d_second_shift, d_bias), ("rows", "blk")
    )
    return (
        output[None],
        grad_hidden[None],
        grad_qkv,
        grad_out,
        grad_up,
        down_grads,
        small_grads[0],
        small_grads[1],
        small_grads[2],
        small_grads[3],
        small_grads[4],
    )


MESH = pl.DeviceIdType.MESH
ROWS_Z, ROWS_Y = 4, 2
PAIR = 128


def place_of():
    index = lax.axis_index("rows")
    return index // 4, lax.rem(index // 2, 2), lax.rem(index, 2)


def row_of(z, y, core):
    return (lax.rem(z + ROWS_Z, ROWS_Z) * ROWS_Y + y) * 2 + core


def aligned(index, step):
    return pl.ds(pl.multiple_of(index * step, step), step)


def dot_nt(left, right):
    return lax.dot_general(left, right, (((1,), (1,)), ((), ())), preferred_element_type=jnp.float32)


def dot_nn(left, right):
    return jnp.dot(left, right, preferred_element_type=jnp.float32)


def head_lanes(width):
    lane = lax.broadcasted_iota(jnp.int32, (1, width), 1)
    return (lane < HEAD_DIM, lane >= HEAD_DIM)


def greet(peers):
    barrier = pltpu.get_barrier_semaphore()
    for peer in peers:
        pl.semaphore_signal(barrier, inc=1, device_id=peer, device_id_type=MESH)
    pl.semaphore_wait(barrier, len(peers))


def neighbours():
    z, y, core = place_of()
    return [
        {"rows": row_of(z + 1, y, core)},
        {"rows": row_of(z + 2, y, core)},
        {"rows": row_of(z + 3, y, core)},
        {"rows": row_of(z, 1 - y, core)},
        {"rows": row_of(z, y, 1 - core)},
        {"blk": 1 - lax.axis_index("blk")},
    ]


def write_mask(starts_ref, mask_ref):
    blocks, step, length = mask_ref.shape

    def rows(i, carry):
        key_at = lax.broadcasted_iota(jnp.int32, (step, length), 0) + i * step
        query_at = lax.broadcasted_iota(jnp.int32, (step, length), 1)
        key_seg = jnp.zeros((step, length), jnp.int32)
        query_seg = jnp.zeros((step, length), jnp.int32)
        for cell in range(starts_ref.shape[1]):
            start = starts_ref[0, cell]
            key_seg += (key_at >= start).astype(jnp.int32)
            query_seg += (query_at >= start).astype(jnp.int32)
        mask_ref[i] = jnp.where(key_seg == query_seg, 0.0, masked_score).astype(mask_ref.dtype)
        return carry

    lax.fori_loop(0, blocks, rows, 0)


def forward_kernel(
    hidden, cot, starts, gain1, shift1, gain2, shift2, bias, q_own, o_own, u_own, d_own,
    q_all, o_all, u_all, d_all, dy_all, normed_t_out, packed_out, lse_out, att_t_out, resid_out,
    second_t_out, act_out, act_t_out, slope_out,
    hid_other, normed, wq, wo, wu, packed, mask, att_part, att_own, resid, second,
    act, act_t, slope, normed_t, att_t, second_t, lse,
    local_sem, send_sem, recv_sem, x_send, x_recv,
):
    bf16 = jnp.bfloat16
    z, y, core = place_of()
    me = row_of(z, y, core)
    piece = lax.axis_index("blk")
    other = 1 - piece
    own_rows, width = hidden.shape
    length = packed.shape[0]
    own = (q_own, o_own, u_own, d_own)
    gathered = (q_all, o_all, u_all, d_all)
    x_peer = {"blk": other}
    peers = neighbours()
    pairs = packed.shape[1] // (3 * PAIR)
    waits = []

    def local(src, dst, index):
        return pltpu.make_async_copy(src, dst, local_sem.at[index])

    def block(w, stage):
        if stage < 3:
            slot, peer = me, peers[stage]
        elif stage < 7:
            slot, peer = row_of(z - (stage - 3), y, core), peers[3]
        elif stage < 11:
            slot, peer = row_of(z - (stage - 7), y, core), peers[4]
        else:
            slot, peer = row_of(z - (stage - 11), 1 - y, core), peers[4]
        src = own[w] if stage in (0, 1, 2, 3, 7) else gathered[w].at[slot]
        index = w * 15 + stage
        return pltpu.make_async_remote_copy(
            src_ref=src, dst_ref=gathered[w].at[slot], send_sem=send_sem.at[index],
            recv_sem=recv_sem.at[index], device_id=peer, device_id_type=MESH,
        )

    def start(w, *stages):
        for stage in stages:
            block(w, stage).start()

    def arrived(w, *stages):
        for stage in stages:
            block(w, stage).wait_recv()

    def to_x(src, dst, index):
        return pltpu.make_async_remote_copy(
            src_ref=src, dst_ref=dst, send_sem=x_send.at[index], recv_sem=x_recv.at[index],
            device_id=x_peer, device_id_type=MESH,
        )

    def relay_z(w, k):
        arrived(w, k - 1)
        start(w, 3 + k, 7 + k)

    def relay_y(w, k):
        arrived(w, 3 + k)
        start(w, 11 + k)

    greet(peers)
    for w in range(4):
        start(w, 0, 2, 1)
        start(w, 7)
        if w == 0:
            start(w, 3)
    hidden_x = to_x(hidden, hid_other, 0)
    hidden_x.start()
    cot_x = to_x(cot, dy_all.at[piece], 1)
    cot_x.start()
    for w in range(4):
        local(own[w], gathered[w].at[me], w).start()
    local(cot, dy_all.at[piece], 4).start()

    def norm_rows(read, half):
        step = 64

        def body(i, carry):
            rows = read(aligned(i, step)).astype(jnp.float32)
            low = layer_norm(rows, gain1[...], shift1[...]).astype(bf16)
            normed[pl.ds(pl.multiple_of(half * own_rows + i * step, step), step), :] = low
            return carry

        lax.fori_loop(0, own_rows // step, body, 0)

    norm_rows(lambda rows: hidden[rows, :], piece)
    relay_z(0, 1)
    relay_z(0, 3)
    start(1, 3)
    write_mask(starts, mask)
    relay_y(0, 0)
    relay_y(0, 1)
    hidden_x.wait_recv()
    norm_rows(lambda rows: hid_other[rows, :], other)
    relay_z(0, 2)
    relay_y(0, 3)

    def flip(i, carry):
        normed_t[aligned(i, 128), :] = normed[:, aligned(i, 128)].T
        return carry

    lax.fori_loop(0, width // 128, flip, 0)
    local(normed_t, normed_t_out, 8).start()
    relay_z(1, 1)
    relay_y(0, 2)
    relay_z(1, 3)
    start(2, 3)
    arrived(0, *range(7, 15))
    local(own[0], gathered[0].at[me], 0).wait()
    local(q_all, wq, 5).start()
    local(q_all, wq, 5).wait()

    def project(i, carry):
        cols = aligned(i, 3 * PAIR)
        weight = wq[:, :, cols].reshape(width, 3 * PAIR)
        value = dot_nn(normed[...], weight).astype(bf16)
        queries = pl.ds(pl.multiple_of(i * 3 * PAIR, PAIR), PAIR)
        rest = pl.ds(pl.multiple_of(i * 3 * PAIR + PAIR, PAIR), 2 * PAIR)
        packed[:, queries] = value[:, :PAIR] * jnp.asarray(HEAD_DIM ** (-0.5), bf16)
        packed[:, rest] = value[:, PAIR:]
        return carry

    lax.fori_loop(0, pairs, project, 0)
    local(packed, packed_out, 9).start()
    first_lanes = head_lanes(PAIR)

    def attend(p):
        base = 3 * PAIR * p
        value_t = packed[:, base + 2 * PAIR : base + 3 * PAIR].T
        step = 256

        def rows(i, carry):
            queries = packed[aligned(i, step), base : base + PAIR]
            keys = packed[:, base + PAIR : base + 2 * PAIR]
            halves = []
            for h in range(2):
                one = jnp.where(first_lanes[h], queries, jnp.zeros_like(queries))
                scores = dot_nt(keys, one) + mask[:, :, aligned(i, step)].reshape(length, step)
                top = jnp.max(scores, axis=0, keepdims=True)
                weights = jnp.exp(scores - top)
                total = jnp.sum(weights, axis=0, keepdims=True)
                lse[2 * p + h : 2 * p + h + 1, aligned(i, step)] = top + jnp.log(total)
                summed = dot_nn(value_t[h * HEAD_DIM : (h + 1) * HEAD_DIM], weights.astype(bf16))
                halves.append(summed / total)
            both = jnp.concatenate(halves, axis=0).T.astype(bf16)
            att_part[aligned(i, step), p * PAIR : (p + 1) * PAIR] = both
            return carry

        lax.fori_loop(0, length // step, rows, 0)

    def att_cols(half, p):
        return pl.ds(pl.multiple_of(half * pairs * PAIR + p * PAIR, PAIR), PAIR)

    att_x = []
    for p in range(pairs):
        attend(p)
        part = att_part.at[pl.ds(pl.multiple_of(other * own_rows, 128), own_rows), pl.ds(p * PAIR, PAIR)]
        att_x.append(to_x(part, att_own.at[:, att_cols(piece, p)], 2 + p))
        att_x[-1].start()
        mine = att_part[pl.ds(pl.multiple_of(piece * own_rows, 128), own_rows), p * PAIR : (p + 1) * PAIR]
        att_own[:, att_cols(piece, p)] = mine
        if p == 0:
            relay_y(1, 0)
            relay_y(1, 1)
        elif p == 1:
            relay_z(1, 2)
        elif p == 2:
            relay_y(1, 3)
        elif p == 3:
            relay_z(2, 1)
        elif p == 4:
            relay_y(1, 2)
    local(lse, lse_out, 10).start()
    for copy in att_x:
        copy.wait_recv()
    arrived(1, *range(7, 15))
    local(own[1], gathered[1].at[me], 1).wait()
    local(o_all, wo, 6).start()

    def flip_att(i, carry):
        att_t[aligned(i, 128), :] = att_own[:, aligned(i, 128)].T
        return carry

    lax.fori_loop(0, width // 128, flip_att, 0)
    local(att_t, att_t_out, 11).start()
    relay_z(2, 3)
    start(3, 3)
    local(o_all, wo, 6).wait()

    def merge(i, carry):
        cols = aligned(i, 256)
        weight = wo[:, :, cols].reshape(width, 256)
        resid[:, cols] = hidden[:, cols].astype(jnp.float32) + dot_nn(att_own[...], weight)
        return carry

    lax.fori_loop(0, width // 256, merge, 0)
    local(resid, resid_out, 12).start()

    def second_rows(i, carry):
        rows = aligned(i, 64)
        second[piece, rows, :] = layer_norm(resid[rows, :], gain2[...], shift2[...]).astype(bf16)
        return carry

    lax.fori_loop(0, own_rows // 64, second_rows, 0)
    second_x = to_x(second.at[piece], second.at[piece], 2 + pairs)
    second_x.start()
    relay_y(2, 0)
    relay_y(2, 1)
    relay_z(2, 2)
    second_x.wait_recv()

    def flip_second(i, carry):
        cols = aligned(i, 128)
        second_t[cols, :] = second[:, :, cols].reshape(length, 128).T
        return carry

    lax.fori_loop(0, width // 128, flip_second, 0)
    local(second_t, second_t_out, 13).start()
    relay_y(2, 3)
    relay_z(3, 1)
    relay_y(2, 2)
    arrived(2, *range(7, 15))
    local(own[2], gathered[2].at[me], 2).wait()
    local(u_all, wu, 7).start()
    local(u_all, wu, 7).wait()
    relay_z(3, 3)
    unit = 256
    steps = act.shape[1] // unit

    def expand(i, carry):
        cols = aligned(i // 2, unit)
        rows = aligned(lax.rem(i, 2), own_rows)
        weight = wu[:, :, cols].reshape(width, unit)
        up = dot_nn(second[lax.rem(i, 2)], weight) + bias[:, cols]
        cdf = 0.5 * (1.0 + lax.erf(up * (0.5 ** 0.5)))
        pdf = jnp.exp(up * up * -0.5) * ((2.0 * math.pi) ** -0.5)
        value = (up * cdf).astype(bf16)
        act[rows, cols] = value
        act_t[cols, rows] = value.T
        slope[rows, cols] = (cdf + up * pdf).astype(bf16)
        return carry

    lax.fori_loop(0, steps, expand, 0)
    relay_y(3, 0)
    relay_y(3, 1)
    lax.fori_loop(steps, 2 * steps, expand, 0)
    local(act, act_out, 14).start()
    local(act_t, act_t_out, 15).start()
    local(slope, slope_out, 16).start()
    relay_z(3, 2)
    relay_y(3, 3)
    relay_y(3, 2)
    arrived(3, *range(7, 15))
    cot_x.wait_recv()
    local(own[3], gathered[3].at[me], 3).wait()
    local(cot, dy_all.at[piece], 4).wait()
    local(normed_t, normed_t_out, 8).wait()
    local(packed, packed_out, 9).wait()
    local(lse, lse_out, 10).wait()
    local(att_t, att_t_out, 11).wait()
    local(resid, resid_out, 12).wait()
    local(second_t, second_t_out, 13).wait()
    local(act, act_out, 14).wait()
    local(act_t, act_t_out, 15).wait()
    local(slope, slope_out, 16).wait()
    for w in range(4):
        for stage in range(15):
            block(w, stage).wait_send()
    for copy in [hidden_x, cot_x, second_x] + att_x:
        copy.wait_send()


def forward(hidden, cot, starts, gain1, shift1, gain2, shift2, bias, q_own, o_own, u_own, d_own):
    own_rows, width = hidden.shape
    length = 2 * own_rows
    cols = q_own.shape[1]
    units = u_own.shape[1]
    bf16, f32 = jnp.bfloat16, jnp.float32
    shards = lax.axis_size("rows")
    weights = (q_own, o_own, u_own, d_own)
    head_rows = 16
    outs = [((shards,) + w.shape, bf16) for w in weights] + [
        ((2, own_rows, width), bf16),
        ((width, length), bf16),
        ((length, cols), bf16),
        ((head_rows, length), f32),
        ((width, own_rows), bf16),
        ((own_rows, width), f32),
        ((width, length), bf16),
        ((length, units), bf16),
        ((units, length), bf16),
        ((length, units), bf16),
    ]
    scratch = [
        ((own_rows, width), bf16),
        ((length, width), bf16),
        ((shards,) + q_own.shape, bf16),
        ((shards,) + o_own.shape, bf16),
        ((shards,) + u_own.shape, bf16),
        ((length, cols), bf16),
        ((length // 48, 48, length), f32),
        ((length, cols // 3), bf16),
        ((own_rows, width), bf16),
        ((own_rows, width), f32),
        ((2, own_rows, width), bf16),
        ((length, units), bf16),
        ((units, length), bf16),
        ((length, units), bf16),
        ((width, length), bf16),
        ((width, own_rows), bf16),
        ((width, length), bf16),
        ((head_rows, length), f32),
    ]
    vmem = pl.BlockSpec(memory_space=pltpu.VMEM)
    anywhere = pl.BlockSpec(memory_space=pl.ANY)
    smem = pl.BlockSpec(memory_space=pltpu.SMEM)
    dma = pltpu.SemaphoreType.DMA
    x_copies = 3 + cols // (3 * PAIR)
    return pl.pallas_call(
        forward_kernel,
        out_shape=[jax.ShapeDtypeStruct(shape, kind) for shape, kind in outs],
        in_specs=[vmem, anywhere, smem] + [vmem] * 5 + [anywhere] * 4,
        out_specs=[anywhere] * len(outs),
        scratch_shapes=[pltpu.VMEM(shape, kind) for shape, kind in scratch]
        + [dma((17,)), dma((60,)), dma((60,)), dma((x_copies,)), dma((x_copies,))],
        compiler_params=pltpu.CompilerParams(
            collective_id=1, has_side_effects=True, vmem_limit_bytes=60 * 1024 * 1024
        ),
        name="forward",
    )(hidden, cot, starts, gain1, shift1, gain2, shift2, bias, *weights)


UNIT = 640
SLOTS = 2


def norm_back(values, gain, grad):
    centred = values - jnp.mean(values, axis=-1, keepdims=True)
    scale = lax.rsqrt(jnp.mean(centred * centred, axis=-1, keepdims=True) + 1e-05)
    unit = centred * scale
    scaled = grad * gain
    mean_one = jnp.mean(scaled, axis=-1, keepdims=True)
    mean_two = jnp.mean(scaled * unit, axis=-1, keepdims=True)
    d_values = scale * (scaled - mean_one - unit * mean_two)
    d_gain = jnp.sum(grad * unit, axis=0, keepdims=True)
    d_shift = jnp.sum(grad, axis=0, keepdims=True)
    return d_values, d_gain, d_shift


def backward_kernel(
    starts, gain1, gain2, hidden, dy_all, q_all, o_all, u_all, d_all, normed_t, packed, lse_in, att_t,
    resid, second_t, act, act_t, slope,
    output, grad_hidden, units_out, pairs_out, small_out,
    lhs, half_act, wide, wd, wu, dy, first, second, d_att, x_in0, x_in1, x_out0, x_out1,
    down_own, parts, core_in, core_in_q, y_in, y_in_q, z_in, z_in_q, lse, acc_k, acc_v,
    bias_sum, small, small_core, small_y, small_z,
    local_sem, a_send, a_recv, b_send, b_recv, c_send, c_recv, g_send, g_recv, x_send, x_recv,
    s_send, s_recv, keep_sem,
):
    bf16, f32 = jnp.bfloat16, jnp.float32
    z, y, core = place_of()
    piece = lax.axis_index("blk")
    other = 1 - piece
    own_rows, width = first.shape
    length = 2 * own_rows
    branch = half_act.at[:, pl.ds(0, width)]
    units = wide.shape[1]
    cols = 3 * d_att.shape[1]
    pairs = d_att.shape[1] // PAIR
    peers = neighbours()
    wide_chunks = core_in.shape[0]
    half_rows = lambda half: pl.ds(pl.multiple_of(half * own_rows, 128), own_rows)

    def remote(src, dst, sends, recvs, index, peer):
        return pltpu.make_async_remote_copy(
            src_ref=src, dst_ref=dst, send_sem=sends.at[index], recv_sem=recvs.at[index],
            device_id=peer, device_id_type=MESH,
        )

    loads = {
        "act_t": (act_t, lhs, 0),
        "dy": (dy_all, dy, 1),
        "down": (d_all, wd, 2),
        "slope": (slope, wide, 3),
        "up": (u_all, wu, 4),
        "act_other": (act.at[half_rows(other)], half_act, 5),
        "act_own": (act.at[half_rows(piece)], half_act, 6),
        "resid": (resid, second, 7),
        "lse": (lse_in, lse, 8),
        "second_t": (second_t, lhs.at[:, pl.ds(0, lhs.shape[1] // 2)], 9),
        "att_t": (att_t, lhs.at[:, pl.ds(lhs.shape[1] // 2, lhs.shape[1] // 2), pl.ds(0, own_rows)], 10),
        "out": (o_all, wd.at[pl.ds(0, width)], 11),
        "normed_t": (normed_t, wd.at[pl.ds(width, width), pl.ds(0, length)], 12),
        "qkv": (q_all, wu.at[:, pl.ds(0, cols)], 13),
        "packed": (packed, wide.at[:, pl.ds(0, cols)], 14),
        "hidden": (hidden, branch, 15),
        "output": (second, output, 16),
        "grad_hidden": (first, grad_hidden, 17),
    }

    def local(name):
        src, dst, index = loads[name]
        return pltpu.make_async_copy(src, dst, local_sem.at[index])

    def buffers(i):
        if i < wide_chunks:
            return core_in.at[i], y_in.at[i], z_in.at[i], z_in.at[i, 0], units_out.at[:, i], UNIT
        i -= wide_chunks
        return core_in_q.at[i], y_in_q.at[i], z_in_q.at[i], z_in_q.at[i, 0], pairs_out.at[:, i], 3 * PAIR

    def copy_a(i):
        into, _, _, _, _, n = buffers(i)
        return remote(parts.at[i % SLOTS, 1 - core, :, :, :, pl.ds(0, n)], into, a_send, a_recv, i, peers[4])

    def copy_b(i):
        sums, into, _, _, _, _ = buffers(i)
        return remote(sums.at[1 - y], into, b_send, b_recv, i, peers[3])

    def copy_c(i, k):
        _, sums, into, _, _, _ = buffers(i)
        return remote(sums.at[lax.rem(z + k, ROWS_Z)], into.at[k - 1], c_send, c_recv, 3 * i + k - 1, peers[k - 1])

    def copy_g(i):
        _, _, _, share, out, _ = buffers(i)
        return remote(share, out.at[piece], g_send, g_recv, i, peers[5])

    def keep_g(i):
        _, _, _, share, out, _ = buffers(i)
        return pltpu.make_async_copy(share, out.at[piece], keep_sem.at[i])

    def finish_a(i):
        sums, _, _, _, _, n = buffers(i)
        copy_a(i).wait_recv()
        slot = i % SLOTS
        sums[1 - y] += parts[slot, core, 1 - y, :, :, :n]
        copy_b(i).start()
        sums[y] += parts[slot, core, y, :, :, :n]
        copy_a(i).wait_send()

    def finish_b(i):
        mine, sums, _, _, _, _ = buffers(i)
        copy_b(i).wait_recv()
        sums[...] += mine[y]
        for k in (1, 3, 2):
            copy_c(i, k).start()

    def finish_c(i):
        _, sums, terms, share, _, _ = buffers(i)
        for k in (1, 3, 2):
            copy_c(i, k).wait_recv()
        total = sums[z].astype(f32)
        for k in range(3):
            total += terms[k].astype(f32)
        share[...] = total.astype(bf16)
        copy_g(i).start()
        keep_g(i).start()

    def grad_chunk(i, left, right):
        slot = i % SLOTS

        def one_z(to_z, carry):
            value = dot_nn(left(to_z), right()).astype(bf16)
            n = value.shape[1]
            rows = value.shape[0] // 4
            for block in range(4):
                to_y, to_core = divmod(block, 2)
                parts[slot, to_core, to_y, to_z, :, :n] = value[block * rows : (block + 1) * rows]
            return carry

        lax.fori_loop(0, ROWS_Z, one_z, 0)
        copy_a(i).start()

    for name in ("act_t", "dy", "down", "slope", "act_other", "up", "resid", "lse"):
        local(name).start()
    greet(peers)
    local("act_t").wait()
    local("dy").wait()
    block_rows = parts.shape[4]

    def grad_down(i):
        h, column = divmod(i, 2)

        def left(to_z):
            rows = lhs[pl.ds(to_z * 4, 4), h * block_rows : (h + 1) * block_rows, :]
            return rows.reshape(4 * block_rows, length)

        grad_chunk(i, left, lambda: dy[:, :, column * UNIT : (column + 1) * UNIT].reshape(length, UNIT))

    grad_down(0)
    grad_down(1)
    finish_a(0)
    grad_down(2)
    finish_a(1)
    grad_down(3)
    local("second_t").start()
    local("att_t").start()
    local("down").wait()
    local("slope").wait()

    tile = 256

    def d_units(i, carry):
        at = aligned(i, tile)
        sums = jnp.zeros((1, tile), f32)
        for half in range(2):
            rows = slice(half * own_rows, (half + 1) * own_rows)
            value = dot_nt(dy[half], wd[at, :]) * wide[rows, at].astype(f32)
            low = value.astype(bf16)
            wide[rows, at] = low
            sums += jnp.sum(low.astype(f32), axis=0, keepdims=True)
        bias_sum[:, at] = sums
        return carry

    lax.fori_loop(0, 4, d_units, 0)
    finish_a(2)
    finish_a(3)
    lax.fori_loop(4, units // tile, d_units, 0)
    local("up").wait()

    def d_second(half, write):
        def body(i, carry):
            at = aligned(i, tile)
            write(at, dot_nt(wide[half_rows(half), :], wu[at, :]))
            return carry

        lax.fori_loop(0, width // tile, body, 0)

    def write_out0(at, value):
        x_out0[:, at] = value.astype(bf16)

    def write_first(at, value):
        first[:, at] = value

    d_second(other, write_out0)
    second_x = remote(x_out0, x_in0, x_send, x_recv, 0, peers[5])
    second_x.start()
    d_second(piece, write_first)
    local("qkv").start()
    finish_b(0)
    local("act_other").wait()

    def down_part(target):
        def body(i, carry):
            at = aligned(i, tile)
            target[:, at] = dot_nn(half_act[...], wd[:, at]).astype(bf16)
            return carry

        lax.fori_loop(0, width // tile, body, 0)

    down_part(x_out1)
    local("act_own").start()
    local("second_t").wait()

    def grad_up(i):
        def left(to_z):
            rows = lhs[pl.ds(to_z * 4, 4), :block_rows, :]
            return rows.reshape(4 * block_rows, length)

        grad_chunk(4 + i, left, lambda: wide[:, i * UNIT : (i + 1) * UNIT])

    grad_up(0)
    grad_up(1)
    local("act_own").wait()
    finish_a(4)
    finish_b(1)
    down_part(down_own)
    local("out").start()
    local("normed_t").start()
    finish_a(5)
    grad_up(2)
    grad_up(3)
    local("packed").start()
    mask = lhs.at[:, pl.ds(0, length // lhs.shape[0]), :]
    write_mask(starts, mask)
    finish_a(6)
    finish_a(7)
    finish_c(0)
    finish_b(2)
    local("resid").wait()
    second_x.wait_recv()
    step = 64

    def back_two(i, carry):
        rows = aligned(i, step)
        grad = first[rows, :] + x_in0[rows, :].astype(f32)
        d_values, d_gain, d_shift = norm_back(second[rows, :], gain2[...], grad)
        total = dy[piece, rows, :].astype(f32) + d_values
        first[rows, :] = total
        branch[rows, :] = total.astype(bf16)
        return carry[0] + d_gain, carry[1] + d_shift

    zeros = jnp.zeros((1, width), f32)
    gain_two, shift_two = lax.fori_loop(0, own_rows // step, back_two, (zeros, zeros))
    small[2:3, :] = gain_two
    small[3:4, :] = shift_two
    local("out").wait()
    second_x.wait_send()
    d_width = d_att.shape[1]

    def d_attended(half):
        rows = pl.ds(pl.multiple_of(half * d_width, 128), d_width)
        return dot_nt(branch[...], wd[rows, :]).astype(bf16)

    x_out0[:, :d_width] = d_attended(other)
    att_x = remote(x_out0.at[:, pl.ds(0, d_width)], d_att.at[half_rows(piece)], x_send, x_recv, 1, peers[5])
    att_x.start()
    down_x = remote(x_out1, x_in1, x_send, x_recv, 2, peers[5])
    down_x.start()
    d_att[half_rows(piece), :] = d_attended(piece)
    local("att_t").wait()

    def grad_out(i):
        def left(to_z):
            rows = lhs[pl.ds(to_z * 4, 4), block_rows : 2 * block_rows, :own_rows]
            return rows.reshape(4 * block_rows, own_rows)

        grad_chunk(8 + i, left, lambda: branch[:, i * UNIT : (i + 1) * UNIT])

    grad_out(0)
    grad_out(1)
    finish_c(1)
    finish_b(3)
    finish_a(8)
    finish_a(9)
    local("hidden").start()
    local("lse").wait()
    local("packed").wait()
    local("normed_t").wait()
    att_x.wait_recv()
    first_lanes = head_lanes(PAIR)

    def attend_back(p):
        base = 3 * PAIR * p
        keys_t = wide[:, base + PAIR : base + 2 * PAIR].T
        acc_k[...] = jnp.zeros_like(acc_k)
        acc_v[...] = jnp.zeros_like(acc_v)
        chunk = 256

        def body(i, carry):
            rows = aligned(i, chunk)
            keys = wide[:, base + PAIR : base + 2 * PAIR]
            values = wide[:, base + 2 * PAIR : base + 3 * PAIR]
            queries = wide[rows, base : base + PAIR]
            grads = d_att[rows, p * PAIR : (p + 1) * PAIR]
            blocked = mask[:, :, rows].reshape(length, chunk).astype(f32)
            parts_q = []
            for h in range(2):
                one_q = jnp.where(first_lanes[h], queries, jnp.zeros_like(queries))
                one_g = jnp.where(first_lanes[h], grads, jnp.zeros_like(grads))
                scores = dot_nt(keys, one_q) + (blocked - lse[2 * p + h : 2 * p + h + 1, rows])
                probs = jnp.exp(scores)
                d_probs = dot_nt(values, one_g)
                dots = jnp.sum(probs * d_probs, axis=0, keepdims=True)
                d_scores = (probs * (d_probs - dots)).astype(bf16)
                acc_v[...] += dot_nn(probs.astype(bf16), one_g)
                acc_k[...] += dot_nn(d_scores, one_q)
                parts_q.append(dot_nn(keys_t[h * HEAD_DIM : (h + 1) * HEAD_DIM], d_scores))
            d_queries = jnp.concatenate(parts_q, axis=0).T * HEAD_DIM ** (-0.5)
            wide[rows, base : base + PAIR] = d_queries.astype(bf16)
            return carry

        lax.fori_loop(0, length // chunk, body, 0)
        wide[:, base + PAIR : base + 2 * PAIR] = acc_k[...].astype(bf16)
        wide[:, base + 2 * PAIR : base + 3 * PAIR] = acc_v[...].astype(bf16)

    def grad_pair(p):
        def left(to_z):
            return wd[pl.ds(pl.multiple_of(width + to_z * 4 * block_rows, 64), 4 * block_rows), :length]

        grad_chunk(10 + p, left, lambda: wide[:, 3 * PAIR * p : 3 * PAIR * (p + 1)])

    def write_output():
        down_x.wait_recv()

        def body(i, carry):
            rows = aligned(i, step)
            second[rows, :] += down_own[rows, :].astype(f32) + x_in1[rows, :].astype(f32)
            return carry

        lax.fori_loop(0, own_rows // step, body, 0)
        local("output").start()

    ticks = {
        0: lambda: (finish_c(2), finish_b(4)),
        1: lambda: (finish_a(10), finish_c(3), finish_b(5)),
        2: lambda: (finish_a(11), finish_c(4), finish_b(6)),
        3: lambda: (finish_a(12), write_output(), finish_c(5), finish_b(7)),
        4: lambda: (finish_a(13), finish_c(6)),
    }
    for p in range(pairs):
        attend_back(p)
        grad_pair(p)
        ticks[p]()
    finish_a(14)
    local("qkv").wait()
    local("output").wait()
    att_x.wait_send()

    def d_normed(half, write):
        def body(i, carry):
            at = aligned(i, tile)
            write(at, dot_nt(wide[half_rows(half), :cols], wu[at, :cols]))
            return carry

        lax.fori_loop(0, width // tile, body, 0)

    def write_second(at, value):
        second[:, at] = value

    d_normed(other, write_out0)
    normed_x = remote(x_out0, x_in0, x_send, x_recv, 3, peers[5])
    normed_x.start()
    finish_b(8)
    d_normed(piece, write_second)
    finish_c(7)
    finish_b(9)
    local("hidden").wait()
    finish_c(8)
    finish_b(10)
    normed_x.wait_recv()

    def back_one(i, carry):
        rows = aligned(i, step)
        grad = second[rows, :] + x_in0[rows, :].astype(f32)
        d_values, d_gain, d_shift = norm_back(branch[rows, :].astype(f32), gain1[...], grad)
        first[rows, :] += d_values
        return carry[0] + d_gain, carry[1] + d_shift

    gain_one, shift_one = lax.fori_loop(0, own_rows // step, back_one, (zeros, zeros))
    local("grad_hidden").start()
    small[0:1, :] = gain_one
    small[1:2, :] = shift_one
    small[4:5, :] = bias_sum[:, :width]
    small[5:6, :] = bias_sum[:, width:]
    small[6:8, :] = jnp.zeros((2, width), f32)
    core_x = remote(small, small_core, s_send, s_recv, 0, peers[4])
    core_x.start()
    finish_b(11)
    core_x.wait()
    small[...] += small_core[...]
    y_x = remote(small, small_y, s_send, s_recv, 1, peers[3])
    y_x.start()
    finish_c(9)
    finish_b(12)
    finish_c(10)
    finish_b(13)
    finish_c(11)
    finish_b(14)
    y_x.wait()
    small_z[z] = small[...] + small_y[...]
    z_x = [remote(small_z.at[z], small_z.at[z], s_send, s_recv, 1 + k, peers[k - 1]) for k in (1, 2, 3)]
    for copy in z_x:
        copy.start()
    finish_c(12)
    finish_c(13)
    for copy in z_x:
        copy.wait()
    small[...] = ((small_z[0] + small_z[1]) + small_z[2]) + small_z[3]
    share_x = remote(small, small_out.at[piece], s_send, s_recv, 5, peers[5])
    share_x.start()
    share_keep = pltpu.make_async_copy(small, small_out.at[piece], keep_sem.at[15])
    share_keep.start()
    finish_c(14)
    for i in range(15):
        copy_b(i).wait_send()
        for k in (1, 2, 3):
            copy_c(i, k).wait_send()
        copy_g(i).wait()
        keep_g(i).wait()
    share_x.wait()
    share_keep.wait()
    down_x.wait_send()
    normed_x.wait_send()
    local("grad_hidden").wait()


def backward(starts, gain1, gain2, hidden, dy_all, q_all, o_all, u_all, d_all, *kept):
    bf16, f32 = jnp.bfloat16, jnp.float32
    _, own_rows, width = dy_all.shape
    length = 2 * own_rows
    cols, units = q_all.shape[1], u_all.shape[1]
    rows = width // 16
    wide_units, pairs = 10, cols // (3 * PAIR)
    pair_cols = 3 * PAIR
    outs = [
        ((own_rows, width), f32),
        ((own_rows, width), f32),
        ((2, wide_units, rows, UNIT), bf16),
        ((2, pairs, rows, pair_cols), bf16),
        ((2, 8, width), f32),
    ]
    token = ((own_rows, width), bf16)
    scratch = [
        ((16, 2 * rows, length), bf16),
        ((own_rows, units), bf16),
        ((length, units), bf16),
        ((units, width), bf16),
        ((width, units), bf16),
        ((2, own_rows, width), bf16),
        ((own_rows, width), f32),
        ((own_rows, width), f32),
        ((length, cols // 3), bf16),
        token, token, token, token, token,
        ((SLOTS, 2, 2, ROWS_Z, rows, UNIT), bf16),
        ((wide_units, 2, ROWS_Z, rows, UNIT), bf16),
        ((pairs, 2, ROWS_Z, rows, pair_cols), bf16),
        ((wide_units, ROWS_Z, rows, UNIT), bf16),
        ((pairs, ROWS_Z, rows, pair_cols), bf16),
        ((wide_units, 3, rows, UNIT), bf16),
        ((pairs, 3, rows, pair_cols), bf16),
        ((16, length), f32),
        ((length, PAIR), f32),
        ((length, PAIR), f32),
        ((1, units), f32),
        ((8, width), f32),
        ((8, width), f32),
        ((8, width), f32),
        ((ROWS_Z, 8, width), f32),
    ]
    vmem = pl.BlockSpec(memory_space=pltpu.VMEM)
    anywhere = pl.BlockSpec(memory_space=pl.ANY)
    smem = pl.BlockSpec(memory_space=pltpu.SMEM)
    chunks = wide_units + pairs
    dma = lambda n: pltpu.SemaphoreType.DMA((n,))
    sems = [18] + [chunks] * 4 + [3 * chunks] * 2 + [chunks] * 2 + [4, 4, 6, 6, chunks + 1]
    return pl.pallas_call(
        backward_kernel,
        out_shape=[jax.ShapeDtypeStruct(shape, kind) for shape, kind in outs],
        in_specs=[smem, vmem, vmem] + [anywhere] * (6 + len(kept)),
        out_specs=[anywhere] * len(outs),
        scratch_shapes=[pltpu.VMEM(shape, kind) for shape, kind in scratch] + [dma(n) for n in sems],
        compiler_params=pltpu.CompilerParams(
            collective_id=2, has_side_effects=True, vmem_limit_bytes=60 * 1024 * 1024
        ),
        name="backward",
    )(starts, gain1, gain2, hidden, dy_all, q_all, o_all, u_all, d_all, *kept)


def own_shares(qkv_weight, up_weight, hidden_bias, down_weight, piece, pieces, shards, cols, units):
    pairs = cols // PAIR
    qkv_own = lax.dynamic_index_in_dim(
        qkv_weight.reshape(-1, 3, pieces, pairs, PAIR), piece, 2, keepdims=False
    )
    qkv_own = qkv_own.transpose(0, 2, 1, 3).reshape(-1, 3 * cols)
    up_own = lax.dynamic_index_in_dim(
        up_weight.reshape(-1, shards, pieces, units), piece, 2, keepdims=False
    ).reshape(-1, shards * units)
    bias_own = lax.dynamic_index_in_dim(
        hidden_bias.reshape(shards, pieces, units), piece, 1, keepdims=False
    ).reshape(1, -1)
    down_own = lax.dynamic_slice_in_dim(down_weight, piece * units, units, 0)
    return qkv_own, up_own, bias_own, down_own


def split_layer(
    hidden, starts, first_gain, first_shift, qkv_weight, out_weight, second_gain, second_shift,
    up_weight, hidden_bias, down_weight, cotangent,
):
    width = hidden.shape[2]
    pieces = lax.axis_size("blk")
    piece = lax.axis_index("blk")
    shards = lax.axis_size("rows")
    cols = HEADS // pieces * HEAD_DIM
    pairs = cols // PAIR
    rows = width // shards
    units = down_weight.shape[0] // pieces
    f32 = jnp.float32
    qkv_own, up_own, bias_own, down_own = own_shares(
        qkv_weight, up_weight, hidden_bias, down_weight, piece, pieces, shards, cols, units
    )
    flat = lambda v: v.reshape(1, -1)
    (
        qkv_all, out_all, up_all, down_all, dy_all, normed_t, packed, lse, att_t, residual, second_t,
        activated, activated_t, slope,
    ) = forward(
        hidden[0], cotangent[0], starts, flat(first_gain), flat(first_shift), flat(second_gain),
        flat(second_shift), bias_own, qkv_own, out_weight, up_own, down_own,
    )
    whole = lambda w: w.reshape(-1, w.shape[-1])
    blocks = lambda w: w.reshape(shards, -1, w.shape[-1])
    output, grad_hidden, unit_grads, pair_grads, small = backward(
        starts, flat(first_gain), flat(second_gain), hidden[0], dy_all, whole(qkv_all), whole(out_all),
        whole(up_all), whole(down_all), normed_t, packed, lse, blocks(att_t), residual,
        blocks(second_t), activated, blocks(activated_t), slope,
    )
    down = unit_grads[:, :4].reshape(pieces, 2, 2, rows, UNIT).transpose(0, 1, 3, 2, 4)
    grad_down = down.reshape(pieces * units, width).astype(f32)
    up = unit_grads[:, 4:8].transpose(2, 0, 1, 3).reshape(rows, pieces, shards, units)
    grad_up = up.transpose(0, 2, 1, 3).reshape(rows, -1).astype(f32)
    out = unit_grads[0, 8:].astype(f32) + unit_grads[1, 8:].astype(f32)
    grad_out = out.transpose(1, 0, 2).reshape(rows, width)
    qkv = pair_grads.reshape(pieces, pairs, rows, 3, PAIR).transpose(2, 3, 0, 1, 4)
    grad_qkv = qkv.reshape(rows, -1).astype(f32)
    norms = small[0, :4] + small[1, :4]
    d_bias = small[:, 4:6].reshape(pieces, shards, units).transpose(1, 0, 2).reshape(-1)
    return (
        output[None], grad_hidden[None], grad_qkv, grad_out, grad_up, grad_down,
        norms[0], norms[1], norms[2], norms[3], d_bias,
    )


def splits_evenly(mesh):
    pieces = mesh.shape["blk"]
    return pieces == 2 and mesh.shape["rows"] == 2 * ROWS_Z * ROWS_Y and HEADS % (2 * pieces) == 0


def solution(mesh):
    in_specs = (
        P("rows", "blk", None),
        P("rows", None),
        P(),
        P(),
        P("rows", None),
        P("rows", None),
        P(),
        P(),
        P("rows", None),
        P(),
        P("rows", None),
        P("rows", "blk", None),
    )
    out_specs = (
        P("rows", "blk", None),
        P("rows", "blk", None),
        P("rows", None),
        P("rows", None),
        P("rows", None),
        P("rows", None),
        P(),
        P(),
        P(),
        P(),
        P(),
    )
    layer = split_layer if splits_evenly(mesh) else on_device
    return jax.shard_map(
        layer, mesh=mesh, in_specs=in_specs, out_specs=out_specs, check_vma=False
    )
```

```python
import math

import jax
import jax.numpy as jnp
from jax import lax
from jax.experimental import pallas as pl
from jax.experimental.pallas import tpu as pltpu
from jax.sharding import PartitionSpec as P

HEADS = 20
HEAD_DIM = 64


masked_score = -1e30
block_limit = 512


def layer_norm(values, gain, shift):
    mean_value = jnp.mean(values, axis=-1, keepdims=True)
    centred = values - mean_value
    variance = jnp.mean(centred * centred, axis=-1, keepdims=True)
    return centred * lax.rsqrt(variance + 1e-05) * gain + shift


def segment_of(starts_row, positions):
    reached = starts_row[None, :] <= positions[:, None]
    return jnp.sum(reached.astype(jnp.int32), axis=1) - 1


def scores_with_mask(queries, key_block, query_seg, key_seg):
    products = jnp.einsum("qhe,khe->hqk", queries, key_block, preferred_element_type=jnp.float32)
    products = products * queries.shape[2] ** (-0.5)
    allowed = (query_seg[:, None] == key_seg[None, :])[None, :, :]
    return (jnp.where(allowed, products, masked_score), allowed)


def attend_rows(running, key_rows, value_rows, queries, query_seg, starts_row):
    piece_rows = key_rows.shape[0]
    step_rows = math.gcd(piece_rows, block_limit)
    head_count = queries.shape[1]
    head_width = queries.shape[2]

    def one_block(block_index, state):
        row_top, denominator, weighted = state
        block_start = block_index * step_rows
        key_block = lax.dynamic_slice_in_dim(key_rows, block_start, step_rows, 0).reshape(
            step_rows, head_count, head_width
        )
        value_block = lax.dynamic_slice_in_dim(value_rows, block_start, step_rows, 0).reshape(
            step_rows, head_count, head_width
        )
        key_seg = segment_of(starts_row, block_start + jnp.arange(step_rows, dtype=jnp.int32))
        scores, allowed = scores_with_mask(queries, key_block, query_seg, key_seg)
        new_top = jnp.maximum(row_top, jnp.max(scores, axis=-1))
        factor = jnp.exp(row_top - new_top)
        weights = jnp.where(allowed, jnp.exp(scores - new_top[:, :, None]), 0.0)
        denominator = denominator * factor + jnp.sum(weights, axis=-1)
        weighted = weighted * factor[:, :, None] + jnp.einsum(
            "hqk,khe->hqe",
            weights.astype(jnp.bfloat16),
            value_block,
            preferred_element_type=jnp.float32,
        )
        return (new_top, denominator, weighted)

    return lax.fori_loop(0, piece_rows // step_rows, one_block, running)


def on_device(
    hidden,
    starts,
    first_gain,
    first_shift,
    qkv_weight,
    out_weight,
    second_gain,
    second_shift,
    up_weight,
    hidden_bias,
    down_weight,
    cotangent,
):
    rows_here = hidden.shape[1]
    model_width = hidden.shape[2]
    head_count = HEADS
    head_width = HEAD_DIM
    score_scale = head_width ** (-0.5)
    inputs = hidden[0].astype(jnp.float32)
    starts_row = starts[0]
    offset = lax.axis_index("blk") * rows_here
    query_seg = segment_of(starts_row, offset + jnp.arange(rows_here, dtype=jnp.int32))
    qkv_full, out_full, up_full, down_full = (
        lax.all_gather(qkv_weight, "rows", axis=0, tiled=True),
        lax.all_gather(out_weight, "rows", axis=0, tiled=True),
        lax.all_gather(up_weight, "rows", axis=0, tiled=True),
        lax.all_gather(down_weight, "rows", axis=0, tiled=True),
    )
    normed_low = layer_norm(inputs, first_gain, first_shift).astype(jnp.bfloat16)
    packed = jnp.dot(normed_low, qkv_full, preferred_element_type=jnp.float32).astype(jnp.bfloat16)
    queries = packed[:, :model_width].reshape(rows_here, head_count, head_width)
    key_rows = packed[:, model_width : 2 * model_width]
    value_rows = packed[:, 2 * model_width :]
    initial = (
        jnp.full((head_count, rows_here), masked_score, jnp.float32),
        jnp.zeros((head_count, rows_here), jnp.float32),
        jnp.zeros((head_count, rows_here, head_width), jnp.float32),
    )
    row_top, denominator, weighted = attend_rows(
        initial,
        lax.all_gather(key_rows, "blk", axis=0, tiled=True),
        lax.all_gather(value_rows, "blk", axis=0, tiled=True),
        queries,
        query_seg,
        starts_row,
    )
    log_total = row_top + jnp.log(denominator)
    attended = jnp.transpose(weighted / denominator[:, :, None], (1, 0, 2))
    attended_low = attended.reshape(rows_here, model_width).astype(jnp.bfloat16)
    residual = inputs + jnp.dot(attended_low, out_full, preferred_element_type=jnp.float32)
    second_low = layer_norm(residual, second_gain, second_shift).astype(jnp.bfloat16)
    up_values = jnp.dot(second_low, up_full, preferred_element_type=jnp.float32) + hidden_bias
    activated_low = jax.nn.gelu(up_values, approximate=False).astype(jnp.bfloat16)
    output = residual + jnp.dot(activated_low, down_full, preferred_element_type=jnp.float32)
    cot_low = cotangent[0]
    d_activated = jnp.einsum("tc,fc->tf", cot_low, down_full, preferred_element_type=jnp.float32)
    unused_gelu, gelu_pull = jax.vjp(
        lambda values: jax.nn.gelu(values, approximate=False), up_values
    )
    d_up_low = gelu_pull(d_activated)[0].astype(jnp.bfloat16)
    d_second = jnp.einsum("tf,cf->tc", d_up_low, up_full, preferred_element_type=jnp.float32)
    unused_second, second_pull = jax.vjp(layer_norm, residual, second_gain, second_shift)
    d_norm_two, d_second_gain, d_second_shift = second_pull(d_second)
    d_residual = cot_low.astype(jnp.float32) + d_norm_two
    d_branch_low = d_residual.astype(jnp.bfloat16)
    d_attended_low = jnp.einsum(
        "tc,kc->tk", d_branch_low, out_full, preferred_element_type=jnp.float32
    ).astype(jnp.bfloat16)
    d_attended3 = d_attended_low.reshape(rows_here, head_count, head_width)
    row_dots = jnp.einsum("qhe,qhe->hq", d_attended3.astype(jnp.float32), attended)
    keys_all, values_all = (
        lax.all_gather(key_rows, "blk", axis=0, tiled=True),
        lax.all_gather(value_rows, "blk", axis=0, tiled=True),
    )
    length = keys_all.shape[0]
    step_rows = math.gcd(length, block_limit)

    def block_terms(block_index):
        block_start = block_index * step_rows
        key_block = lax.dynamic_slice_in_dim(keys_all, block_start, step_rows, 0).reshape(
            step_rows, head_count, head_width
        )
        value_block = lax.dynamic_slice_in_dim(values_all, block_start, step_rows, 0).reshape(
            step_rows, head_count, head_width
        )
        key_seg = segment_of(starts_row, block_start + jnp.arange(step_rows, dtype=jnp.int32))
        scores, allowed = scores_with_mask(queries, key_block, query_seg, key_seg)
        probability = jnp.where(allowed, jnp.exp(scores - log_total[:, :, None]), 0.0)
        d_probs = jnp.einsum(
            "qhe,khe->hqk", d_attended3, value_block, preferred_element_type=jnp.float32
        )
        d_scores = (probability * (d_probs - row_dots[:, :, None])).astype(jnp.bfloat16)
        return (key_block, probability, d_scores)

    dq_start = jnp.zeros((rows_here, head_count, head_width), jnp.float32)

    def back_block(dq_sum, block_index):
        key_block, probability, d_scores = block_terms(block_index)
        dq_sum = dq_sum + jnp.einsum(
            "hqk,khe->qhe", d_scores, key_block, preferred_element_type=jnp.float32
        )
        dk_block = (
            jnp.einsum("hqk,qhe->khe", d_scores, queries, preferred_element_type=jnp.float32)
            * score_scale
        )
        dv_block = jnp.einsum(
            "hqk,qhe->khe",
            probability.astype(jnp.bfloat16),
            d_attended3,
            preferred_element_type=jnp.float32,
        )
        return (
            dq_sum,
            (dk_block.reshape(step_rows, model_width), dv_block.reshape(step_rows, model_width)),
        )

    dq_sum, (dk_terms, dv_terms) = lax.scan(back_block, dq_start, jnp.arange(length // step_rows))
    dk_rows, dv_rows = (
        lax.psum_scatter(
            dk_terms.reshape(length, model_width).astype(jnp.bfloat16),
            "blk",
            scatter_dimension=0,
            tiled=True,
        ).astype(jnp.float32),
        lax.psum_scatter(
            dv_terms.reshape(length, model_width).astype(jnp.bfloat16),
            "blk",
            scatter_dimension=0,
            tiled=True,
        ).astype(jnp.float32),
    )
    d_packed = jnp.concatenate(
        [(dq_sum * score_scale).reshape(rows_here, model_width), dk_rows, dv_rows], axis=1
    ).astype(jnp.bfloat16)
    d_normed = jnp.einsum("tn,cn->tc", d_packed, qkv_full, preferred_element_type=jnp.float32)
    unused_first, first_pull = jax.vjp(layer_norm, inputs, first_gain, first_shift)
    d_norm_one, d_first_gain, d_first_shift = first_pull(d_normed)
    grad_hidden = d_residual + d_norm_one
    d_bias = jnp.sum(d_up_low, axis=0, dtype=jnp.float32)
    wide_share = lax.psum_scatter(
        jnp.concatenate(
            [
                jnp.einsum("tc,tn->cn", normed_low, d_packed, preferred_element_type=jnp.float32),
                jnp.einsum(
                    "tc,tn->cn", attended_low, d_branch_low, preferred_element_type=jnp.float32
                ),
                jnp.einsum("tc,tn->cn", second_low, d_up_low, preferred_element_type=jnp.float32),
            ],
            axis=1,
        ).astype(jnp.bfloat16),
        "rows",
        scatter_dimension=0,
        tiled=True,
    )
    down_share = lax.psum_scatter(
        jnp.einsum("tf,tn->fn", activated_low, cot_low, preferred_element_type=jnp.float32).astype(
            jnp.bfloat16
        ),
        "rows",
        scatter_dimension=0,
        tiled=True,
    )
    wide_grads, down_grads = (
        lax.psum(wide_share, "blk").astype(jnp.float32),
        lax.psum(down_share, "blk").astype(jnp.float32),
    )
    grad_qkv = wide_grads[:, : 3 * model_width]
    grad_out = wide_grads[:, 3 * model_width : 4 * model_width]
    grad_up = wide_grads[:, 4 * model_width :]
    small_grads = lax.psum(
        (d_first_gain, d_first_shift, d_second_gain, d_second_shift, d_bias), ("rows", "blk")
    )
    return (
        output[None],
        grad_hidden[None],
        grad_qkv,
        grad_out,
        grad_up,
        down_grads,
        small_grads[0],
        small_grads[1],
        small_grads[2],
        small_grads[3],
        small_grads[4],
    )


MESH = pl.DeviceIdType.MESH
ROWS_Z, ROWS_Y = 4, 2
PAIR = 128


def place_of():
    index = lax.axis_index("rows")
    return index // 4, lax.rem(index // 2, 2), lax.rem(index, 2)


def row_of(z, y, core):
    return (lax.rem(z + ROWS_Z, ROWS_Z) * ROWS_Y + y) * 2 + core


def aligned(index, step):
    return pl.ds(pl.multiple_of(index * step, step), step)


def dot_nt(left, right):
    return lax.dot_general(left, right, (((1,), (1,)), ((), ())), preferred_element_type=jnp.float32)


def dot_nn(left, right):
    return jnp.dot(left, right, preferred_element_type=jnp.float32)


def head_lanes(width):
    lane = lax.broadcasted_iota(jnp.int32, (1, width), 1)
    return (lane < HEAD_DIM, lane >= HEAD_DIM)


def greet(peers):
    barrier = pltpu.get_barrier_semaphore()
    for peer in peers:
        pl.semaphore_signal(barrier, inc=1, device_id=peer, device_id_type=MESH)
    pl.semaphore_wait(barrier, len(peers))


def neighbours():
    z, y, core = place_of()
    return [
        {"rows": row_of(z + 1, y, core)},
        {"rows": row_of(z + 2, y, core)},
        {"rows": row_of(z + 3, y, core)},
        {"rows": row_of(z, 1 - y, core)},
        {"rows": row_of(z, y, 1 - core)},
        {"blk": 1 - lax.axis_index("blk")},
    ]


def write_mask(starts_ref, mask_ref):
    blocks, step, length = mask_ref.shape

    def rows(i, carry):
        key_at = lax.broadcasted_iota(jnp.int32, (step, length), 0) + i * step
        query_at = lax.broadcasted_iota(jnp.int32, (step, length), 1)
        key_seg = jnp.zeros((step, length), jnp.int32)
        query_seg = jnp.zeros((step, length), jnp.int32)
        for cell in range(starts_ref.shape[1]):
            start = starts_ref[0, cell]
            key_seg += (key_at >= start).astype(jnp.int32)
            query_seg += (query_at >= start).astype(jnp.int32)
        mask_ref[i] = jnp.where(key_seg == query_seg, 0.0, masked_score).astype(mask_ref.dtype)
        return carry

    lax.fori_loop(0, blocks, rows, 0)


def forward_kernel(
    hidden, cot, starts, gain1, shift1, gain2, shift2, bias_in, q_in, o_own, u_in, d_in,
    q_all, o_all, u_all, d_all, dy_all, normed_t_out, packed_out, lse_out, att_t_out, resid_out,
    second_t_out, act_out, act_t_out, slope_out,
    hid_other, normed, wq, wo, wu, packed, mask, att_part, att_own, resid, second,
    act, act_t, slope, normed_t, att_t, second_t, lse, u_wide, u_own, bias,
    local_sem, send_sem, recv_sem, x_send, x_recv,
):
    bf16 = jnp.bfloat16
    z, y, core = place_of()
    me = row_of(z, y, core)
    piece = lax.axis_index("blk")
    other = 1 - piece
    own_rows, width = hidden.shape
    length = packed.shape[0]
    d_own = d_in.at[pl.ds(piece * d_all.shape[1], d_all.shape[1])]
    own = (q_all.at[me], o_own, u_own, d_own)
    gathered = (q_all, o_all, u_all, d_all)
    x_peer = {"blk": other}
    peers = neighbours()
    pairs = packed.shape[1] // (3 * PAIR)
    first_gain, first_shift, second_gain, second_shift = (
        ref[...].reshape(1, width) for ref in (gain1, shift1, gain2, shift2)
    )

    def local(src, dst, index):
        return pltpu.make_async_copy(src, dst, local_sem.at[index])

    def block(w, stage):
        if stage < 3:
            slot, peer = me, peers[stage]
        elif stage < 7:
            slot, peer = row_of(z - (stage - 3), y, core), peers[3]
        elif stage < 11:
            slot, peer = row_of(z - (stage - 7), y, core), peers[4]
        else:
            slot, peer = row_of(z - (stage - 11), 1 - y, core), peers[4]
        src = own[w] if stage in (0, 1, 2, 3, 7) else gathered[w].at[slot]
        index = w * 15 + stage
        return pltpu.make_async_remote_copy(
            src_ref=src, dst_ref=gathered[w].at[slot], send_sem=send_sem.at[index],
            recv_sem=recv_sem.at[index], device_id=peer, device_id_type=MESH,
        )

    def start(w, *stages):
        for stage in stages:
            block(w, stage).start()

    def arrived(w, *stages):
        for stage in stages:
            block(w, stage).wait_recv()

    def to_x(src, dst, index):
        return pltpu.make_async_remote_copy(
            src_ref=src, dst_ref=dst, send_sem=x_send.at[index], recv_sem=x_recv.at[index],
            device_id=x_peer, device_id_type=MESH,
        )

    def relay_z(w, k):
        arrived(w, k - 1)
        start(w, 3 + k, 7 + k)

    def relay_y(w, k):
        arrived(w, 3 + k)
        start(w, 11 + k)

    third = q_in.shape[1] // 3
    share = third // 2
    q_picks = []
    for part in range(3):
        picked = q_in.at[:, pl.ds(pl.multiple_of(part * third + piece * share, 128), share)]
        q_picks.append(local(picked, q_all.at[me, :, pl.ds(part * share, share)], 17 + part))
        q_picks[-1].start()
    local(u_in, u_wide, 2).start()
    greet(peers)
    for copy in q_picks:
        copy.wait()
    start(0, 0, 2, 1)
    start(0, 3, 7)
    start(1, 0, 2, 1)
    start(1, 7)
    hidden_x = to_x(hidden, hid_other, 0)
    hidden_x.start()
    cot_x = to_x(cot, dy_all.at[piece], 1)
    cot_x.start()
    local(o_own, o_all.at[me], 1).start()
    local(d_own, d_all.at[me], 3).start()
    local(cot, dy_all.at[piece], 4).start()

    def norm_rows(read, half):
        step = 64

        def body(i, carry):
            rows = read(aligned(i, step)).astype(jnp.float32)
            low = layer_norm(rows, first_gain, first_shift).astype(bf16)
            normed[pl.ds(pl.multiple_of(half * own_rows + i * step, step), step), :] = low
            return carry

        lax.fori_loop(0, own_rows // step, body, 0)

    units_each = d_all.shape[1]
    group = 8 * units_each

    def mine(block):
        wide = block.astype(jnp.float32)
        halves = []
        for half in range(2):
            at = [slice((2 * j + half) * units_each, (2 * j + half + 1) * units_each) for j in range(4)]
            halves.append(jnp.concatenate([wide[:, cols] for cols in at], axis=1))
        return jnp.where(piece == 0, halves[0], halves[1])

    local(u_in, u_wide, 2).wait()
    for g in range(u_own.shape[1] // (group // 2)):
        cols = slice(g * group // 2, (g + 1) * group // 2)
        u_own[:, cols] = mine(u_wide[:, g * group : (g + 1) * group]).astype(bf16)
        bias[:, cols] = mine(bias_in[g * group : (g + 1) * group].reshape(1, group))
    start(2, 0, 2, 1)
    start(2, 7)
    start(3, 0, 2, 1)
    start(3, 7)
    local(u_own, u_all.at[me], 2).start()
    norm_rows(lambda rows: hidden[rows, :], piece)
    relay_z(0, 1)
    relay_z(0, 3)
    start(1, 3)
    write_mask(starts, mask)
    relay_y(0, 0)
    relay_y(0, 1)
    hidden_x.wait_recv()
    norm_rows(lambda rows: hid_other[rows, :], other)
    relay_z(0, 2)
    relay_y(0, 3)

    def flip(i, carry):
        normed_t[aligned(i, 128), :] = normed[:, aligned(i, 128)].T
        return carry

    lax.fori_loop(0, width // 128, flip, 0)
    local(normed_t, normed_t_out, 8).start()
    relay_z(1, 1)
    relay_y(0, 2)
    relay_z(1, 3)
    start(2, 3)
    arrived(0, *range(7, 15))
    local(q_all, wq, 5).start()
    local(q_all, wq, 5).wait()

    column = lax.broadcasted_iota(jnp.int32, (1, 3 * PAIR), 1)

    def project(i, carry):
        cols = aligned(i, 3 * PAIR)
        weight = wq[:, :, cols].reshape(width, 3 * PAIR)
        value = dot_nn(normed[...], weight).astype(bf16)
        factor = jnp.where(i * 3 * PAIR + column < share, HEAD_DIM ** (-0.5), 1.0).astype(bf16)
        packed[:, cols] = value * factor
        return carry

    lax.fori_loop(0, pairs, project, 0)
    local(packed, packed_out, 9).start()
    first_lanes = head_lanes(PAIR)

    def attend(p):
        at_q, at_k, at_v = (slice(t * share + PAIR * p, t * share + PAIR * (p + 1)) for t in range(3))
        value_t = packed[:, at_v].T
        step = 256

        def rows(i, carry):
            queries = packed[aligned(i, step), at_q]
            keys = packed[:, at_k]
            halves = []
            for h in range(2):
                one = jnp.where(first_lanes[h], queries, jnp.zeros_like(queries))
                scores = dot_nt(keys, one) + mask[:, :, aligned(i, step)].reshape(length, step)
                top = jnp.max(scores, axis=0, keepdims=True)
                weights = jnp.exp(scores - top)
                total = jnp.sum(weights, axis=0, keepdims=True)
                lse[2 * p + h : 2 * p + h + 1, aligned(i, step)] = top + jnp.log(total)
                summed = dot_nn(value_t[h * HEAD_DIM : (h + 1) * HEAD_DIM], weights.astype(bf16))
                halves.append(summed / total)
            both = jnp.concatenate(halves, axis=0).T.astype(bf16)
            att_part[aligned(i, step), p * PAIR : (p + 1) * PAIR] = both
            return carry

        lax.fori_loop(0, length // step, rows, 0)

    def att_cols(half, p):
        return pl.ds(pl.multiple_of(half * pairs * PAIR + p * PAIR, PAIR), PAIR)

    att_x = []
    for p in range(pairs):
        attend(p)
        part = att_part.at[pl.ds(pl.multiple_of(other * own_rows, 128), own_rows), pl.ds(p * PAIR, PAIR)]
        att_x.append(to_x(part, att_own.at[:, att_cols(piece, p)], 2 + p))
        att_x[-1].start()
        mine = att_part[pl.ds(pl.multiple_of(piece * own_rows, 128), own_rows), p * PAIR : (p + 1) * PAIR]
        att_own[:, att_cols(piece, p)] = mine
        if p == 0:
            relay_y(1, 0)
            relay_y(1, 1)
        elif p == 1:
            relay_z(1, 2)
        elif p == 2:
            relay_y(1, 3)
        elif p == 3:
            relay_z(2, 1)
        elif p == 4:
            relay_y(1, 2)
    local(lse, lse_out, 10).start()
    for copy in att_x:
        copy.wait_recv()
    arrived(1, *range(7, 15))
    local(own[1], gathered[1].at[me], 1).wait()
    local(o_all, wo, 6).start()

    def flip_att(i, carry):
        att_t[aligned(i, 128), :] = att_own[:, aligned(i, 128)].T
        return carry

    lax.fori_loop(0, width // 128, flip_att, 0)
    local(att_t, att_t_out, 11).start()
    relay_z(2, 3)
    start(3, 3)
    local(o_all, wo, 6).wait()

    def merge(i, carry):
        cols = aligned(i, 256)
        weight = wo[:, :, cols].reshape(width, 256)
        resid[:, cols] = hidden[:, cols].astype(jnp.float32) + dot_nn(att_own[...], weight)
        return carry

    lax.fori_loop(0, width // 256, merge, 0)
    local(resid, resid_out, 12).start()

    def second_rows(i, carry):
        rows = aligned(i, 64)
        second[piece, rows, :] = layer_norm(resid[rows, :], second_gain, second_shift).astype(bf16)
        return carry

    lax.fori_loop(0, own_rows // 64, second_rows, 0)
    second_x = to_x(second.at[piece], second.at[piece], 2 + pairs)
    second_x.start()
    relay_y(2, 0)
    relay_y(2, 1)
    relay_z(2, 2)
    second_x.wait_recv()

    def flip_second(i, carry):
        cols = aligned(i, 128)
        second_t[cols, :] = second[:, :, cols].reshape(length, 128).T
        return carry

    lax.fori_loop(0, width // 128, flip_second, 0)
    local(second_t, second_t_out, 13).start()
    relay_y(2, 3)
    relay_z(3, 1)
    relay_y(2, 2)
    arrived(2, *range(7, 15))
    local(own[2], gathered[2].at[me], 2).wait()
    local(u_all, wu, 7).start()
    local(u_all, wu, 7).wait()
    relay_z(3, 3)
    unit = 256
    steps = act.shape[1] // unit

    def expand(i, carry):
        cols = aligned(i // 2, unit)
        rows = aligned(lax.rem(i, 2), own_rows)
        weight = wu[:, :, cols].reshape(width, unit)
        up = dot_nn(second[lax.rem(i, 2)], weight) + bias[:, cols]
        cdf = 0.5 * (1.0 + lax.erf(up * (0.5 ** 0.5)))
        pdf = jnp.exp(up * up * -0.5) * ((2.0 * math.pi) ** -0.5)
        value = (up * cdf).astype(bf16)
        act[rows, cols] = value
        act_t[cols, rows] = value.T
        slope[rows, cols] = (cdf + up * pdf).astype(bf16)
        return carry

    lax.fori_loop(0, steps, expand, 0)
    relay_y(3, 0)
    relay_y(3, 1)
    lax.fori_loop(steps, 2 * steps, expand, 0)
    local(act, act_out, 14).start()
    local(act_t, act_t_out, 15).start()
    local(slope, slope_out, 16).start()
    relay_z(3, 2)
    relay_y(3, 3)
    relay_y(3, 2)
    arrived(3, *range(7, 15))
    cot_x.wait_recv()
    local(own[3], gathered[3].at[me], 3).wait()
    local(cot, dy_all.at[piece], 4).wait()
    local(normed_t, normed_t_out, 8).wait()
    local(packed, packed_out, 9).wait()
    local(lse, lse_out, 10).wait()
    local(att_t, att_t_out, 11).wait()
    local(resid, resid_out, 12).wait()
    local(second_t, second_t_out, 13).wait()
    local(act, act_out, 14).wait()
    local(act_t, act_t_out, 15).wait()
    local(slope, slope_out, 16).wait()
    for w in range(4):
        for stage in range(15):
            block(w, stage).wait_send()
    for copy in [hidden_x, cot_x, second_x] + att_x:
        copy.wait_send()


def forward(hidden, cot, starts, gain1, shift1, gain2, shift2, bias, qkv, out, up, down):
    own_rows, width = hidden.shape
    length = 2 * own_rows
    cols = qkv.shape[1] // 2
    units = up.shape[1] // 2
    rows = up.shape[0]
    bf16, f32 = jnp.bfloat16, jnp.float32
    shards = lax.axis_size("rows")
    head_rows = 16
    outs = [
        ((shards, rows, cols), bf16),
        ((shards, rows, width), bf16),
        ((shards, rows, units), bf16),
        ((shards, down.shape[0] // 2, width), bf16),
        ((2, own_rows, width), bf16),
        ((width, length), bf16),
        ((length, cols), bf16),
        ((head_rows, length), f32),
        ((width, own_rows), bf16),
        ((own_rows, width), f32),
        ((width, length), bf16),
        ((length, units), bf16),
        ((units, length), bf16),
        ((length, units), bf16),
    ]
    scratch = [
        ((own_rows, width), bf16),
        ((length, width), bf16),
        ((shards, rows, cols), bf16),
        ((shards, rows, width), bf16),
        ((shards, rows, units), bf16),
        ((length, cols), bf16),
        ((length // 48, 48, length), f32),
        ((length, cols // 3), bf16),
        ((own_rows, width), bf16),
        ((own_rows, width), f32),
        ((2, own_rows, width), bf16),
        ((length, units), bf16),
        ((units, length), bf16),
        ((length, units), bf16),
        ((width, length), bf16),
        ((width, own_rows), bf16),
        ((width, length), bf16),
        ((head_rows, length), f32),
        ((rows, 2 * units), bf16),
        ((rows, units), bf16),
        ((1, units), f32),
    ]
    vmem = pl.BlockSpec(memory_space=pltpu.VMEM)
    anywhere = pl.BlockSpec(memory_space=pl.ANY)
    smem = pl.BlockSpec(memory_space=pltpu.SMEM)
    dma = pltpu.SemaphoreType.DMA
    x_copies = 3 + cols // (3 * PAIR)
    return pl.pallas_call(
        forward_kernel,
        out_shape=[jax.ShapeDtypeStruct(shape, kind) for shape, kind in outs],
        in_specs=[vmem, anywhere, smem] + [vmem] * 5 + [anywhere] * 4,
        out_specs=[anywhere] * len(outs),
        scratch_shapes=[pltpu.VMEM(shape, kind) for shape, kind in scratch]
        + [dma((20,)), dma((60,)), dma((60,)), dma((x_copies,)), dma((x_copies,))],
        compiler_params=pltpu.CompilerParams(
            collective_id=1, has_side_effects=True, vmem_limit_bytes=60 * 1024 * 1024
        ),
        name="forward",
    )(hidden, cot, starts, gain1, shift1, gain2, shift2, bias, qkv, out, up, down)


UNIT = 640
SLOTS = 2


def norm_back(values, gain, grad):
    centred = values - jnp.mean(values, axis=-1, keepdims=True)
    scale = lax.rsqrt(jnp.mean(centred * centred, axis=-1, keepdims=True) + 1e-05)
    unit = centred * scale
    scaled = grad * gain
    mean_one = jnp.mean(scaled, axis=-1, keepdims=True)
    mean_two = jnp.mean(scaled * unit, axis=-1, keepdims=True)
    d_values = scale * (scaled - mean_one - unit * mean_two)
    d_gain = jnp.sum(grad * unit, axis=0, keepdims=True)
    d_shift = jnp.sum(grad, axis=0, keepdims=True)
    return d_values, d_gain, d_shift


def backward_kernel(
    starts, gain1, gain2, hidden, dy_all, q_all, o_all, u_all, d_all, normed_t, packed, lse_in, att_t,
    resid, second_t, act, act_t, slope,
    output, grad_hidden, units_out, pairs_out, small_out,
    lhs, half_act, wide, wd, wu, dy, first, second, d_att, x_in0, x_in1, x_out0, x_out1,
    down_own, parts, core_in, core_in_q, y_in, y_in_q, z_in, z_in_q, lse, acc_k, acc_v,
    bias_sum, small, small_core, small_y, small_z,
    local_sem, a_send, a_recv, b_send, b_recv, c_send, c_recv, g_send, g_recv, x_send, x_recv,
    s_send, s_recv, keep_sem,
):
    bf16, f32 = jnp.bfloat16, jnp.float32
    z, y, core = place_of()
    piece = lax.axis_index("blk")
    other = 1 - piece
    own_rows, width = first.shape
    length = 2 * own_rows
    branch = half_act.at[:, pl.ds(0, width)]
    units = wide.shape[1]
    cols = 3 * d_att.shape[1]
    pairs = d_att.shape[1] // PAIR
    peers = neighbours()
    wide_chunks = core_in.shape[0]
    first_gain, second_gain = gain1[...].reshape(1, width), gain2[...].reshape(1, width)
    half_rows = lambda half: pl.ds(pl.multiple_of(half * own_rows, 128), own_rows)

    def remote(src, dst, sends, recvs, index, peer):
        return pltpu.make_async_remote_copy(
            src_ref=src, dst_ref=dst, send_sem=sends.at[index], recv_sem=recvs.at[index],
            device_id=peer, device_id_type=MESH,
        )

    loads = {
        "act_t": (act_t, lhs, 0),
        "dy": (dy_all, dy, 1),
        "down": (d_all, wd, 2),
        "slope": (slope, wide, 3),
        "up": (u_all, wu, 4),
        "act_other": (act.at[half_rows(other)], half_act, 5),
        "act_own": (act.at[half_rows(piece)], half_act, 6),
        "resid": (resid, second, 7),
        "lse": (lse_in, lse, 8),
        "second_t": (second_t, lhs.at[:, pl.ds(0, lhs.shape[1] // 2)], 9),
        "att_t": (att_t, lhs.at[:, pl.ds(lhs.shape[1] // 2, lhs.shape[1] // 2), pl.ds(0, own_rows)], 10),
        "out": (o_all, wd.at[pl.ds(0, width)], 11),
        "normed_t": (normed_t, wd.at[pl.ds(width, width), pl.ds(0, length)], 12),
        "qkv": (q_all, wu.at[:, pl.ds(0, cols)], 13),
        "packed": (packed, wide.at[:, pl.ds(0, cols)], 14),
        "hidden": (hidden, branch, 15),
        "output": (second, output, 16),
        "grad_hidden": (first, grad_hidden, 17),
    }

    def local(name):
        src, dst, index = loads[name]
        return pltpu.make_async_copy(src, dst, local_sem.at[index])

    def buffers(i):
        if i < wide_chunks:
            return core_in.at[i], y_in.at[i], z_in.at[i], z_in.at[i, 0], units_out.at[:, i], UNIT
        i -= wide_chunks
        return core_in_q.at[i], y_in_q.at[i], z_in_q.at[i], z_in_q.at[i, 0], pairs_out.at[:, i], 3 * PAIR

    def copy_a(i):
        into, _, _, _, _, n = buffers(i)
        return remote(parts.at[i % SLOTS, 1 - core, :, :, :, pl.ds(0, n)], into, a_send, a_recv, i, peers[4])

    def copy_b(i):
        sums, into, _, _, _, _ = buffers(i)
        return remote(sums.at[1 - y], into, b_send, b_recv, i, peers[3])

    def copy_c(i, k):
        _, sums, into, _, _, _ = buffers(i)
        return remote(sums.at[lax.rem(z + k, ROWS_Z)], into.at[k - 1], c_send, c_recv, 3 * i + k - 1, peers[k - 1])

    def copy_g(i):
        _, _, _, share, out, _ = buffers(i)
        return remote(share, out.at[piece], g_send, g_recv, i, peers[5])

    def keep_g(i):
        _, _, _, share, out, _ = buffers(i)
        return pltpu.make_async_copy(share, out.at[piece], keep_sem.at[i])

    def finish_a(i):
        sums, _, _, _, _, n = buffers(i)
        copy_a(i).wait_recv()
        slot = i % SLOTS
        sums[1 - y] += parts[slot, core, 1 - y, :, :, :n]
        copy_b(i).start()
        sums[y] += parts[slot, core, y, :, :, :n]
        copy_a(i).wait_send()

    def finish_b(i):
        mine, sums, _, _, _, _ = buffers(i)
        copy_b(i).wait_recv()
        sums[...] += mine[y]
        for k in (1, 3, 2):
            copy_c(i, k).start()

    def finish_c(i):
        _, sums, terms, share, _, _ = buffers(i)
        for k in (1, 3, 2):
            copy_c(i, k).wait_recv()
        total = sums[z].astype(f32)
        for k in range(3):
            total += terms[k].astype(f32)
        share[...] = total.astype(bf16)
        copy_g(i).start()
        keep_g(i).start()

    def grad_chunk(i, left, right):
        slot = i % SLOTS

        def one_z(to_z, carry):
            value = dot_nn(left(to_z), right()).astype(bf16)
            n = value.shape[1]
            rows = value.shape[0] // 4
            for block in range(4):
                to_y, to_core = divmod(block, 2)
                parts[slot, to_core, to_y, to_z, :, :n] = value[block * rows : (block + 1) * rows]
            return carry

        lax.fori_loop(0, ROWS_Z, one_z, 0)
        copy_a(i).start()

    for name in ("act_t", "dy", "down", "slope", "act_other", "up", "resid", "lse"):
        local(name).start()
    greet(peers)
    local("act_t").wait()
    local("dy").wait()
    block_rows = parts.shape[4]

    def grad_down(i):
        h, column = divmod(i, 2)

        def left(to_z):
            rows = lhs[pl.ds(to_z * 4, 4), h * block_rows : (h + 1) * block_rows, :]
            return rows.reshape(4 * block_rows, length)

        grad_chunk(i, left, lambda: dy[:, :, column * UNIT : (column + 1) * UNIT].reshape(length, UNIT))

    grad_down(0)
    grad_down(1)
    finish_a(0)
    grad_down(2)
    finish_a(1)
    grad_down(3)
    local("second_t").start()
    local("att_t").start()
    local("down").wait()
    local("slope").wait()

    tile = 256

    def d_units(i, carry):
        at = aligned(i, tile)
        sums = jnp.zeros((1, tile), f32)
        for half in range(2):
            rows = slice(half * own_rows, (half + 1) * own_rows)
            value = dot_nt(dy[half], wd[at, :]) * wide[rows, at].astype(f32)
            low = value.astype(bf16)
            wide[rows, at] = low
            sums += jnp.sum(low.astype(f32), axis=0, keepdims=True)
        bias_sum[:, at] = sums
        return carry

    lax.fori_loop(0, 4, d_units, 0)
    finish_a(2)
    finish_a(3)
    lax.fori_loop(4, units // tile, d_units, 0)
    local("up").wait()

    def d_second(half, write):
        def body(i, carry):
            at = aligned(i, tile)
            write(at, dot_nt(wide[half_rows(half), :], wu[at, :]))
            return carry

        lax.fori_loop(0, width // tile, body, 0)

    def write_out0(at, value):
        x_out0[:, at] = value.astype(bf16)

    def write_first(at, value):
        first[:, at] = value

    d_second(other, write_out0)
    second_x = remote(x_out0, x_in0, x_send, x_recv, 0, peers[5])
    second_x.start()
    d_second(piece, write_first)
    local("qkv").start()
    finish_b(0)
    local("act_other").wait()

    def down_part(target):
        def body(i, carry):
            at = aligned(i, tile)
            target[:, at] = dot_nn(half_act[...], wd[:, at]).astype(bf16)
            return carry

        lax.fori_loop(0, width // tile, body, 0)

    down_part(x_out1)
    local("act_own").start()
    local("second_t").wait()

    def grad_up(i):
        def left(to_z):
            rows = lhs[pl.ds(to_z * 4, 4), :block_rows, :]
            return rows.reshape(4 * block_rows, length)

        grad_chunk(4 + i, left, lambda: wide[:, i * UNIT : (i + 1) * UNIT])

    grad_up(0)
    grad_up(1)
    local("act_own").wait()
    finish_a(4)
    finish_b(1)
    down_part(down_own)
    local("out").start()
    local("normed_t").start()
    finish_a(5)
    grad_up(2)
    grad_up(3)
    local("packed").start()
    mask = lhs.at[:, pl.ds(0, length // lhs.shape[0]), :]
    write_mask(starts, mask)
    finish_a(6)
    finish_a(7)
    finish_c(0)
    finish_b(2)
    local("resid").wait()
    second_x.wait_recv()
    step = 64

    def back_two(i, carry):
        rows = aligned(i, step)
        grad = first[rows, :] + x_in0[rows, :].astype(f32)
        d_values, d_gain, d_shift = norm_back(second[rows, :], second_gain, grad)
        total = dy[piece, rows, :].astype(f32) + d_values
        first[rows, :] = total
        branch[rows, :] = total.astype(bf16)
        return carry[0] + d_gain, carry[1] + d_shift

    zeros = jnp.zeros((1, width), f32)
    gain_two, shift_two = lax.fori_loop(0, own_rows // step, back_two, (zeros, zeros))
    small[2:3, :] = gain_two
    small[3:4, :] = shift_two
    local("out").wait()
    second_x.wait_send()
    d_width = d_att.shape[1]

    def d_attended(half):
        rows = pl.ds(pl.multiple_of(half * d_width, 128), d_width)
        return dot_nt(branch[...], wd[rows, :]).astype(bf16)

    x_out0[:, :d_width] = d_attended(other)
    att_x = remote(x_out0.at[:, pl.ds(0, d_width)], d_att.at[half_rows(piece)], x_send, x_recv, 1, peers[5])
    att_x.start()
    down_x = remote(x_out1, x_in1, x_send, x_recv, 2, peers[5])
    down_x.start()
    d_att[half_rows(piece), :] = d_attended(piece)
    local("att_t").wait()

    def grad_out(i):
        def left(to_z):
            rows = lhs[pl.ds(to_z * 4, 4), block_rows : 2 * block_rows, :own_rows]
            return rows.reshape(4 * block_rows, own_rows)

        grad_chunk(8 + i, left, lambda: branch[:, i * UNIT : (i + 1) * UNIT])

    grad_out(0)
    grad_out(1)
    finish_c(1)
    finish_b(3)
    finish_a(8)
    finish_a(9)
    local("hidden").start()
    local("lse").wait()
    local("packed").wait()
    local("normed_t").wait()
    att_x.wait_recv()
    first_lanes = head_lanes(PAIR)

    def pair_cols(p):
        return tuple(slice(t * d_width + PAIR * p, t * d_width + PAIR * (p + 1)) for t in range(3))

    def attend_back(p):
        at_q, at_k, at_v = pair_cols(p)
        keys_t = wide[:, at_k].T
        acc_k[...] = jnp.zeros_like(acc_k)
        acc_v[...] = jnp.zeros_like(acc_v)
        chunk = 256

        def body(i, carry):
            rows = aligned(i, chunk)
            keys = wide[:, at_k]
            values = wide[:, at_v]
            queries = wide[rows, at_q]
            grads = d_att[rows, p * PAIR : (p + 1) * PAIR]
            blocked = mask[:, :, rows].reshape(length, chunk).astype(f32)
            parts_q = []
            for h in range(2):
                one_q = jnp.where(first_lanes[h], queries, jnp.zeros_like(queries))
                one_g = jnp.where(first_lanes[h], grads, jnp.zeros_like(grads))
                scores = dot_nt(keys, one_q) + (blocked - lse[2 * p + h : 2 * p + h + 1, rows])
                probs = jnp.exp(scores)
                d_probs = dot_nt(values, one_g)
                dots = jnp.sum(probs * d_probs, axis=0, keepdims=True)
                d_scores = (probs * (d_probs - dots)).astype(bf16)
                acc_v[...] += dot_nn(probs.astype(bf16), one_g)
                acc_k[...] += dot_nn(d_scores, one_q)
                parts_q.append(dot_nn(keys_t[h * HEAD_DIM : (h + 1) * HEAD_DIM], d_scores))
            d_queries = jnp.concatenate(parts_q, axis=0).T * HEAD_DIM ** (-0.5)
            wide[rows, at_q] = d_queries.astype(bf16)
            return carry

        lax.fori_loop(0, length // chunk, body, 0)
        wide[:, at_k] = acc_k[...].astype(bf16)
        wide[:, at_v] = acc_v[...].astype(bf16)

    def grad_pair(p):
        def left(to_z):
            return wd[pl.ds(pl.multiple_of(width + to_z * 4 * block_rows, 64), 4 * block_rows), :length]

        grad_chunk(10 + p, left, lambda: jnp.concatenate([wide[:, at] for at in pair_cols(p)], axis=1))

    def write_output():
        down_x.wait_recv()

        def body(i, carry):
            rows = aligned(i, step)
            second[rows, :] += down_own[rows, :].astype(f32) + x_in1[rows, :].astype(f32)
            return carry

        lax.fori_loop(0, own_rows // step, body, 0)
        local("output").start()

    ticks = {
        0: lambda: (finish_c(2), finish_b(4)),
        1: lambda: (finish_a(10), finish_c(3), finish_b(5)),
        2: lambda: (finish_a(11), finish_c(4), finish_b(6)),
        3: lambda: (finish_a(12), write_output(), finish_c(5), finish_b(7)),
        4: lambda: (finish_a(13), finish_c(6)),
    }
    for p in range(pairs):
        attend_back(p)
        grad_pair(p)
        ticks[p]()
    finish_a(14)
    local("qkv").wait()
    local("output").wait()
    att_x.wait_send()

    def d_normed(half, write):
        def body(i, carry):
            at = aligned(i, tile)
            write(at, dot_nt(wide[half_rows(half), :cols], wu[at, :cols]))
            return carry

        lax.fori_loop(0, width // tile, body, 0)

    def write_second(at, value):
        second[:, at] = value

    d_normed(other, write_out0)
    normed_x = remote(x_out0, x_in0, x_send, x_recv, 3, peers[5])
    normed_x.start()
    finish_b(8)
    d_normed(piece, write_second)
    finish_c(7)
    finish_b(9)
    local("hidden").wait()
    finish_c(8)
    finish_b(10)
    normed_x.wait_recv()

    def back_one(i, carry):
        rows = aligned(i, step)
        grad = second[rows, :] + x_in0[rows, :].astype(f32)
        d_values, d_gain, d_shift = norm_back(branch[rows, :].astype(f32), first_gain, grad)
        first[rows, :] += d_values
        return carry[0] + d_gain, carry[1] + d_shift

    gain_one, shift_one = lax.fori_loop(0, own_rows // step, back_one, (zeros, zeros))
    local("grad_hidden").start()
    small[0:1, :] = gain_one
    small[1:2, :] = shift_one
    small[4:5, :] = bias_sum[:, :width]
    small[5:6, :] = bias_sum[:, width:]
    small[6:8, :] = jnp.zeros((2, width), f32)
    core_x = remote(small, small_core, s_send, s_recv, 0, peers[4])
    core_x.start()
    finish_b(11)
    core_x.wait()
    small[...] += small_core[...]
    y_x = remote(small, small_y, s_send, s_recv, 1, peers[3])
    y_x.start()
    finish_c(9)
    finish_b(12)
    finish_c(10)
    finish_b(13)
    finish_c(11)
    finish_b(14)
    y_x.wait()
    small_z[z] = small[...] + small_y[...]
    z_x = [remote(small_z.at[z], small_z.at[z], s_send, s_recv, 1 + k, peers[k - 1]) for k in (1, 2, 3)]
    for copy in z_x:
        copy.start()
    finish_c(12)
    finish_c(13)
    for copy in z_x:
        copy.wait()
    small[...] = ((small_z[0] + small_z[1]) + small_z[2]) + small_z[3]
    share_x = remote(small, small_out.at[piece], s_send, s_recv, 5, peers[5])
    share_x.start()
    share_keep = pltpu.make_async_copy(small, small_out.at[piece], keep_sem.at[15])
    share_keep.start()
    finish_c(14)
    for i in range(15):
        copy_b(i).wait_send()
        for k in (1, 2, 3):
            copy_c(i, k).wait_send()
        copy_g(i).wait()
        keep_g(i).wait()
    share_x.wait()
    share_keep.wait()
    down_x.wait_send()
    normed_x.wait_send()
    local("grad_hidden").wait()


def backward(starts, gain1, gain2, hidden, dy_all, q_all, o_all, u_all, d_all, *kept):
    bf16, f32 = jnp.bfloat16, jnp.float32
    _, own_rows, width = dy_all.shape
    length = 2 * own_rows
    cols, units = q_all.shape[1], u_all.shape[1]
    rows = width // 16
    wide_units, pairs = 10, cols // (3 * PAIR)
    pair_cols = 3 * PAIR
    outs = [
        ((own_rows, width), f32),
        ((own_rows, width), f32),
        ((2, wide_units, rows, UNIT), bf16),
        ((2, pairs, rows, pair_cols), bf16),
        ((2, 8, width), f32),
    ]
    token = ((own_rows, width), bf16)
    scratch = [
        ((16, 2 * rows, length), bf16),
        ((own_rows, units), bf16),
        ((length, units), bf16),
        ((units, width), bf16),
        ((width, units), bf16),
        ((2, own_rows, width), bf16),
        ((own_rows, width), f32),
        ((own_rows, width), f32),
        ((length, cols // 3), bf16),
        token, token, token, token, token,
        ((SLOTS, 2, 2, ROWS_Z, rows, UNIT), bf16),
        ((wide_units, 2, ROWS_Z, rows, UNIT), bf16),
        ((pairs, 2, ROWS_Z, rows, pair_cols), bf16),
        ((wide_units, ROWS_Z, rows, UNIT), bf16),
        ((pairs, ROWS_Z, rows, pair_cols), bf16),
        ((wide_units, 3, rows, UNIT), bf16),
        ((pairs, 3, rows, pair_cols), bf16),
        ((16, length), f32),
        ((length, PAIR), f32),
        ((length, PAIR), f32),
        ((1, units), f32),
        ((8, width), f32),
        ((8, width), f32),
        ((8, width), f32),
        ((ROWS_Z, 8, width), f32),
    ]
    vmem = pl.BlockSpec(memory_space=pltpu.VMEM)
    anywhere = pl.BlockSpec(memory_space=pl.ANY)
    smem = pl.BlockSpec(memory_space=pltpu.SMEM)
    chunks = wide_units + pairs
    dma = lambda n: pltpu.SemaphoreType.DMA((n,))
    sems = [18] + [chunks] * 4 + [3 * chunks] * 2 + [chunks] * 2 + [4, 4, 6, 6, chunks + 1]
    return pl.pallas_call(
        backward_kernel,
        out_shape=[jax.ShapeDtypeStruct(shape, kind) for shape, kind in outs],
        in_specs=[smem, vmem, vmem] + [anywhere] * (6 + len(kept)),
        out_specs=[anywhere] * len(outs),
        scratch_shapes=[pltpu.VMEM(shape, kind) for shape, kind in scratch] + [dma(n) for n in sems],
        compiler_params=pltpu.CompilerParams(
            collective_id=2, has_side_effects=True, vmem_limit_bytes=60 * 1024 * 1024
        ),
        name="backward",
    )(starts, gain1, gain2, hidden, dy_all, q_all, o_all, u_all, d_all, *kept)


def finish_kernel(
    raw_output, raw_grad, units_lo, units_hi, pairs_in, small,
    output, grad_hidden, qkv, out, up, down, gain1, shift1, gain2, shift2, bias,
):
    f32 = jnp.float32
    step = pl.program_id(0)
    output[0] = raw_output[...]
    grad_hidden[0] = raw_grad[...]
    rows = out.shape[0]
    width = small.shape[2]
    units_in = (units_lo, units_hi)

    def mixed(first, second):
        each = first.shape[1] // 4
        blocks = []
        for j in range(4):
            at = slice(j * each, (j + 1) * each)
            blocks += [first[:, at].astype(f32), second[:, at].astype(f32)]
        return jnp.concatenate(blocks, axis=1)

    for now in range(2):

        @pl.when(step == now)
        def _():
            for i in range(4):
                h, column = divmod(i, 2)
                at = slice(column * UNIT, (column + 1) * UNIT)
                down[h * rows : (h + 1) * rows, at] = units_in[now][0, i].astype(f32)
            for i in range(2):
                chunk = 4 + 2 * now + i
                at = slice(i * 2 * UNIT, (i + 1) * 2 * UNIT)
                up[:, at] = mixed(units_lo[0, chunk], units_hi[0, chunk])
            out[...] = units_lo[0, 8 + now].astype(f32) + units_hi[0, 8 + now].astype(f32)
            pairs = pairs_in.shape[1]
            for block in range(3 * now, 3 * now + 3):
                part, piece = divmod(block, 2)
                for p in range(pairs):
                    at = (block - 3 * now) * pairs * PAIR + p * PAIR
                    chunk = pairs_in[piece, p, :, part * PAIR : (part + 1) * PAIR]
                    qkv[:, at : at + PAIR] = chunk.astype(f32)

    @pl.when(step == 0)
    def _():
        for i, ref in enumerate((gain1, shift1, gain2, shift2)):
            ref[...] = (small[0, i : i + 1, :] + small[1, i : i + 1, :]).reshape(width)
        for g in range(2):
            for j in range(2):
                at = slice(j * UNIT, (j + 1) * UNIT)
                lo, hi = small[0, 4 + g : 5 + g, at], small[1, 4 + g : 5 + g, at]
                begin = (2 * g + j) * 2 * UNIT
                bias[begin : begin + 2 * UNIT] = mixed(lo, hi).reshape(2 * UNIT)


def finish(raw_output, raw_grad, units_in, pairs_in, small):
    f32 = jnp.float32
    own_rows, width = raw_output.shape
    rows = units_in.shape[2]
    shapes = [
        (1, own_rows, width), (1, own_rows, width), (rows, 3 * width), (rows, width), (rows, 8 * UNIT),
        (4 * rows, width), (width,), (width,), (width,), (width,), (8 * UNIT,),
    ]
    token = pl.BlockSpec((own_rows // 2, width), lambda s: (s, 0))
    token_out = pl.BlockSpec((1, own_rows // 2, width), lambda s: (0, s, 0))
    columns = lambda n: pl.BlockSpec((rows, n // 2), lambda s: (0, s))
    fixed = lambda shape: pl.BlockSpec(shape, lambda s: (0,) * len(shape))
    half = lambda i: pl.BlockSpec((1,) + units_in.shape[1:], lambda s: (i, 0, 0, 0))
    return pl.pallas_call(
        finish_kernel,
        grid=(2,),
        out_shape=[jax.ShapeDtypeStruct(shape, f32) for shape in shapes],
        in_specs=[token, token, half(0), half(1), fixed(pairs_in.shape), fixed(small.shape)],
        out_specs=[
            token_out, token_out, columns(3 * width), columns(width), columns(8 * UNIT),
            pl.BlockSpec((2 * rows, width), lambda s: (s, 0)),
        ] + [fixed(shape) for shape in shapes[6:]],
        compiler_params=pltpu.CompilerParams(vmem_limit_bytes=60 * 1024 * 1024),
        name="finish",
    )(raw_output, raw_grad, units_in, units_in, pairs_in, small)


def split_layer(
    hidden, starts, first_gain, first_shift, qkv_weight, out_weight, second_gain, second_shift,
    up_weight, hidden_bias, down_weight, cotangent,
):
    shards = lax.axis_size("rows")
    (
        qkv_all, out_all, up_all, down_all, dy_all, normed_t, packed, lse, att_t, residual, second_t,
        activated, activated_t, slope,
    ) = forward(
        hidden[0], cotangent[0], starts, first_gain, first_shift, second_gain, second_shift, hidden_bias,
        qkv_weight, out_weight, up_weight, down_weight,
    )
    whole = lambda w: w.reshape(-1, w.shape[-1])
    blocks = lambda w: w.reshape(shards, -1, w.shape[-1])
    shares = backward(
        starts, first_gain, second_gain, hidden[0], dy_all, whole(qkv_all), whole(out_all),
        whole(up_all), whole(down_all), normed_t, packed, lse, blocks(att_t), residual,
        blocks(second_t), activated, blocks(activated_t), slope,
    )
    return tuple(finish(*shares))


def splits_evenly(mesh):
    pieces = mesh.shape["blk"]
    return pieces == 2 and mesh.shape["rows"] == 2 * ROWS_Z * ROWS_Y and HEADS % (2 * pieces) == 0


def solution(mesh):
    in_specs = (
        P("rows", "blk", None),
        P("rows", None),
        P(),
        P(),
        P("rows", None),
        P("rows", None),
        P(),
        P(),
        P("rows", None),
        P(),
        P("rows", None),
        P("rows", "blk", None),
    )
    out_specs = (
        P("rows", "blk", None),
        P("rows", "blk", None),
        P("rows", None),
        P("rows", None),
        P("rows", None),
        P("rows", None),
        P(),
        P(),
        P(),
        P(),
        P(),
    )
    layer = split_layer if splits_evenly(mesh) else on_device
    return jax.shard_map(
        layer, mesh=mesh, in_specs=in_specs, out_specs=out_specs, check_vma=False
    )
```

```python
import math

import jax
import jax.numpy as jnp
from jax import lax
from jax.experimental import pallas as pl
from jax.experimental.pallas import tpu as pltpu
from jax.sharding import PartitionSpec as P

HEADS = 20
HEAD_DIM = 64


masked_score = -1e30
block_limit = 512


def layer_norm(values, gain, shift):
    mean_value = jnp.mean(values, axis=-1, keepdims=True)
    centred = values - mean_value
    variance = jnp.mean(centred * centred, axis=-1, keepdims=True)
    return centred * lax.rsqrt(variance + 1e-05) * gain + shift


def segment_of(starts_row, positions):
    reached = starts_row[None, :] <= positions[:, None]
    return jnp.sum(reached.astype(jnp.int32), axis=1) - 1


def scores_with_mask(queries, key_block, query_seg, key_seg):
    products = jnp.einsum("qhe,khe->hqk", queries, key_block, preferred_element_type=jnp.float32)
    products = products * queries.shape[2] ** (-0.5)
    allowed = (query_seg[:, None] == key_seg[None, :])[None, :, :]
    return (jnp.where(allowed, products, masked_score), allowed)


def attend_rows(running, key_rows, value_rows, queries, query_seg, starts_row):
    piece_rows = key_rows.shape[0]
    step_rows = math.gcd(piece_rows, block_limit)
    head_count = queries.shape[1]
    head_width = queries.shape[2]

    def one_block(block_index, state):
        row_top, denominator, weighted = state
        block_start = block_index * step_rows
        key_block = lax.dynamic_slice_in_dim(key_rows, block_start, step_rows, 0).reshape(
            step_rows, head_count, head_width
        )
        value_block = lax.dynamic_slice_in_dim(value_rows, block_start, step_rows, 0).reshape(
            step_rows, head_count, head_width
        )
        key_seg = segment_of(starts_row, block_start + jnp.arange(step_rows, dtype=jnp.int32))
        scores, allowed = scores_with_mask(queries, key_block, query_seg, key_seg)
        new_top = jnp.maximum(row_top, jnp.max(scores, axis=-1))
        factor = jnp.exp(row_top - new_top)
        weights = jnp.where(allowed, jnp.exp(scores - new_top[:, :, None]), 0.0)
        denominator = denominator * factor + jnp.sum(weights, axis=-1)
        weighted = weighted * factor[:, :, None] + jnp.einsum(
            "hqk,khe->hqe",
            weights.astype(jnp.bfloat16),
            value_block,
            preferred_element_type=jnp.float32,
        )
        return (new_top, denominator, weighted)

    return lax.fori_loop(0, piece_rows // step_rows, one_block, running)


def on_device(
    hidden,
    starts,
    first_gain,
    first_shift,
    qkv_weight,
    out_weight,
    second_gain,
    second_shift,
    up_weight,
    hidden_bias,
    down_weight,
    cotangent,
):
    rows_here = hidden.shape[1]
    model_width = hidden.shape[2]
    head_count = HEADS
    head_width = HEAD_DIM
    score_scale = head_width ** (-0.5)
    inputs = hidden[0].astype(jnp.float32)
    starts_row = starts[0]
    offset = lax.axis_index("blk") * rows_here
    query_seg = segment_of(starts_row, offset + jnp.arange(rows_here, dtype=jnp.int32))
    qkv_full, out_full, up_full, down_full = (
        lax.all_gather(qkv_weight, "rows", axis=0, tiled=True),
        lax.all_gather(out_weight, "rows", axis=0, tiled=True),
        lax.all_gather(up_weight, "rows", axis=0, tiled=True),
        lax.all_gather(down_weight, "rows", axis=0, tiled=True),
    )
    normed_low = layer_norm(inputs, first_gain, first_shift).astype(jnp.bfloat16)
    packed = jnp.dot(normed_low, qkv_full, preferred_element_type=jnp.float32).astype(jnp.bfloat16)
    queries = packed[:, :model_width].reshape(rows_here, head_count, head_width)
    key_rows = packed[:, model_width : 2 * model_width]
    value_rows = packed[:, 2 * model_width :]
    initial = (
        jnp.full((head_count, rows_here), masked_score, jnp.float32),
        jnp.zeros((head_count, rows_here), jnp.float32),
        jnp.zeros((head_count, rows_here, head_width), jnp.float32),
    )
    row_top, denominator, weighted = attend_rows(
        initial,
        lax.all_gather(key_rows, "blk", axis=0, tiled=True),
        lax.all_gather(value_rows, "blk", axis=0, tiled=True),
        queries,
        query_seg,
        starts_row,
    )
    log_total = row_top + jnp.log(denominator)
    attended = jnp.transpose(weighted / denominator[:, :, None], (1, 0, 2))
    attended_low = attended.reshape(rows_here, model_width).astype(jnp.bfloat16)
    residual = inputs + jnp.dot(attended_low, out_full, preferred_element_type=jnp.float32)
    second_low = layer_norm(residual, second_gain, second_shift).astype(jnp.bfloat16)
    up_values = jnp.dot(second_low, up_full, preferred_element_type=jnp.float32) + hidden_bias
    activated_low = jax.nn.gelu(up_values, approximate=False).astype(jnp.bfloat16)
    output = residual + jnp.dot(activated_low, down_full, preferred_element_type=jnp.float32)
    cot_low = cotangent[0]
    d_activated = jnp.einsum("tc,fc->tf", cot_low, down_full, preferred_element_type=jnp.float32)
    unused_gelu, gelu_pull = jax.vjp(
        lambda values: jax.nn.gelu(values, approximate=False), up_values
    )
    d_up_low = gelu_pull(d_activated)[0].astype(jnp.bfloat16)
    d_second = jnp.einsum("tf,cf->tc", d_up_low, up_full, preferred_element_type=jnp.float32)
    unused_second, second_pull = jax.vjp(layer_norm, residual, second_gain, second_shift)
    d_norm_two, d_second_gain, d_second_shift = second_pull(d_second)
    d_residual = cot_low.astype(jnp.float32) + d_norm_two
    d_branch_low = d_residual.astype(jnp.bfloat16)
    d_attended_low = jnp.einsum(
        "tc,kc->tk", d_branch_low, out_full, preferred_element_type=jnp.float32
    ).astype(jnp.bfloat16)
    d_attended3 = d_attended_low.reshape(rows_here, head_count, head_width)
    row_dots = jnp.einsum("qhe,qhe->hq", d_attended3.astype(jnp.float32), attended)
    keys_all, values_all = (
        lax.all_gather(key_rows, "blk", axis=0, tiled=True),
        lax.all_gather(value_rows, "blk", axis=0, tiled=True),
    )
    length = keys_all.shape[0]
    step_rows = math.gcd(length, block_limit)

    def block_terms(block_index):
        block_start = block_index * step_rows
        key_block = lax.dynamic_slice_in_dim(keys_all, block_start, step_rows, 0).reshape(
            step_rows, head_count, head_width
        )
        value_block = lax.dynamic_slice_in_dim(values_all, block_start, step_rows, 0).reshape(
            step_rows, head_count, head_width
        )
        key_seg = segment_of(starts_row, block_start + jnp.arange(step_rows, dtype=jnp.int32))
        scores, allowed = scores_with_mask(queries, key_block, query_seg, key_seg)
        probability = jnp.where(allowed, jnp.exp(scores - log_total[:, :, None]), 0.0)
        d_probs = jnp.einsum(
            "qhe,khe->hqk", d_attended3, value_block, preferred_element_type=jnp.float32
        )
        d_scores = (probability * (d_probs - row_dots[:, :, None])).astype(jnp.bfloat16)
        return (key_block, probability, d_scores)

    dq_start = jnp.zeros((rows_here, head_count, head_width), jnp.float32)

    def back_block(dq_sum, block_index):
        key_block, probability, d_scores = block_terms(block_index)
        dq_sum = dq_sum + jnp.einsum(
            "hqk,khe->qhe", d_scores, key_block, preferred_element_type=jnp.float32
        )
        dk_block = (
            jnp.einsum("hqk,qhe->khe", d_scores, queries, preferred_element_type=jnp.float32)
            * score_scale
        )
        dv_block = jnp.einsum(
            "hqk,qhe->khe",
            probability.astype(jnp.bfloat16),
            d_attended3,
            preferred_element_type=jnp.float32,
        )
        return (
            dq_sum,
            (dk_block.reshape(step_rows, model_width), dv_block.reshape(step_rows, model_width)),
        )

    dq_sum, (dk_terms, dv_terms) = lax.scan(back_block, dq_start, jnp.arange(length // step_rows))
    dk_rows, dv_rows = (
        lax.psum_scatter(
            dk_terms.reshape(length, model_width).astype(jnp.bfloat16),
            "blk",
            scatter_dimension=0,
            tiled=True,
        ).astype(jnp.float32),
        lax.psum_scatter(
            dv_terms.reshape(length, model_width).astype(jnp.bfloat16),
            "blk",
            scatter_dimension=0,
            tiled=True,
        ).astype(jnp.float32),
    )
    d_packed = jnp.concatenate(
        [(dq_sum * score_scale).reshape(rows_here, model_width), dk_rows, dv_rows], axis=1
    ).astype(jnp.bfloat16)
    d_normed = jnp.einsum("tn,cn->tc", d_packed, qkv_full, preferred_element_type=jnp.float32)
    unused_first, first_pull = jax.vjp(layer_norm, inputs, first_gain, first_shift)
    d_norm_one, d_first_gain, d_first_shift = first_pull(d_normed)
    grad_hidden = d_residual + d_norm_one
    d_bias = jnp.sum(d_up_low, axis=0, dtype=jnp.float32)
    wide_share = lax.psum_scatter(
        jnp.concatenate(
            [
                jnp.einsum("tc,tn->cn", normed_low, d_packed, preferred_element_type=jnp.float32),
                jnp.einsum(
                    "tc,tn->cn", attended_low, d_branch_low, preferred_element_type=jnp.float32
                ),
                jnp.einsum("tc,tn->cn", second_low, d_up_low, preferred_element_type=jnp.float32),
            ],
            axis=1,
        ).astype(jnp.bfloat16),
        "rows",
        scatter_dimension=0,
        tiled=True,
    )
    down_share = lax.psum_scatter(
        jnp.einsum("tf,tn->fn", activated_low, cot_low, preferred_element_type=jnp.float32).astype(
            jnp.bfloat16
        ),
        "rows",
        scatter_dimension=0,
        tiled=True,
    )
    wide_grads, down_grads = (
        lax.psum(wide_share, "blk").astype(jnp.float32),
        lax.psum(down_share, "blk").astype(jnp.float32),
    )
    grad_qkv = wide_grads[:, : 3 * model_width]
    grad_out = wide_grads[:, 3 * model_width : 4 * model_width]
    grad_up = wide_grads[:, 4 * model_width :]
    small_grads = lax.psum(
        (d_first_gain, d_first_shift, d_second_gain, d_second_shift, d_bias), ("rows", "blk")
    )
    return (
        output[None],
        grad_hidden[None],
        grad_qkv,
        grad_out,
        grad_up,
        down_grads,
        small_grads[0],
        small_grads[1],
        small_grads[2],
        small_grads[3],
        small_grads[4],
    )


MESH = pl.DeviceIdType.MESH
ROWS_Z, ROWS_Y = 4, 2
PAIR = 128


def place_of():
    index = lax.axis_index("rows")
    return index // 4, lax.rem(index // 2, 2), lax.rem(index, 2)


def row_of(z, y, core):
    return (lax.rem(z + ROWS_Z, ROWS_Z) * ROWS_Y + y) * 2 + core


def aligned(index, step):
    return pl.ds(pl.multiple_of(index * step, step), step)


def dot_nt(left, right):
    return lax.dot_general(left, right, (((1,), (1,)), ((), ())), preferred_element_type=jnp.float32)


def dot_nn(left, right):
    return jnp.dot(left, right, preferred_element_type=jnp.float32)


def head_lanes(width):
    lane = lax.broadcasted_iota(jnp.int32, (1, width), 1)
    return (lane < HEAD_DIM, lane >= HEAD_DIM)


def greet(peers):
    barrier = pltpu.get_barrier_semaphore()
    for peer in peers:
        pl.semaphore_signal(barrier, inc=1, device_id=peer, device_id_type=MESH)
    pl.semaphore_wait(barrier, len(peers))


def neighbours():
    z, y, core = place_of()
    return [
        {"rows": row_of(z + 1, y, core)},
        {"rows": row_of(z + 2, y, core)},
        {"rows": row_of(z + 3, y, core)},
        {"rows": row_of(z, 1 - y, core)},
        {"rows": row_of(z, y, 1 - core)},
        {"blk": 1 - lax.axis_index("blk")},
    ]


def write_mask(starts_ref, mask_ref):
    blocks, step, length = mask_ref.shape

    def rows(i, carry):
        key_at = lax.broadcasted_iota(jnp.int32, (step, length), 0) + i * step
        query_at = lax.broadcasted_iota(jnp.int32, (step, length), 1)
        key_seg = jnp.zeros((step, length), jnp.int32)
        query_seg = jnp.zeros((step, length), jnp.int32)
        for cell in range(starts_ref.shape[1]):
            start = starts_ref[0, cell]
            key_seg += (key_at >= start).astype(jnp.int32)
            query_seg += (query_at >= start).astype(jnp.int32)
        mask_ref[i] = jnp.where(key_seg == query_seg, 0.0, masked_score).astype(mask_ref.dtype)
        return carry

    lax.fori_loop(0, blocks, rows, 0)


def forward_kernel(
    hidden, cot, starts, gain1, shift1, gain2, shift2, bias_in, q_in, o_in, u_in, d_in,
    q_all, o_all, u_all, d_all, dy_all, normed_t_out, packed_out, lse_out, att_t_out, resid_out,
    second_t_out, act_out, act_t_out, slope_out,
    hid_other, normed, wq, wo, wu, packed, mask, att_part, att_own, resid, second,
    act, act_t, slope, normed_t, att_t, second_t, lse, u_wide, q_own, o_own, u_own, d_own, cot_own, bias,
    local_sem, send_sem, recv_sem, x_send, x_recv,
):
    bf16 = jnp.bfloat16
    z, y, core = place_of()
    me = row_of(z, y, core)
    piece = lax.axis_index("blk")
    other = 1 - piece
    own_rows, width = hidden.shape
    length = packed.shape[0]
    rows = o_own.shape[0]
    d_rows = lambda ref, half: ref.at[pl.ds(half * rows, rows)]
    own = (q_own, o_own, u_own, d_rows(d_own, 0), d_rows(d_own, 1))

    def slot_of(w, at_z, at_y, at_core):
        slot = row_of(at_z, at_y, at_core)
        if w < 3:
            return (q_all, o_all, u_all)[w].at[slot]
        return d_rows(d_all.at[slot], w - 3)

    x_peer = {"blk": other}
    peers = neighbours()
    pairs = packed.shape[1] // (3 * PAIR)
    first_gain, first_shift, second_gain, second_shift = (
        ref[...].reshape(1, width) for ref in (gain1, shift1, gain2, shift2)
    )

    def local(src, dst, index):
        return pltpu.make_async_copy(src, dst, local_sem.at[index])

    peer_up, peer_down, peer_y, peer_core = peers[0], peers[2], peers[3], peers[4]

    def send(w, at_z, v, place, peer, first=False):
        block = slot_of(w, at_z, y if v == 0 else 1 - y, core)
        index = w * 24 + place
        return pltpu.make_async_remote_copy(
            src_ref=own[w] if first else block, dst_ref=block, send_sem=send_sem.at[index],
            recv_sem=recv_sem.at[index], device_id=peer, device_id_type=MESH,
        )

    def along(w, side, a, v):
        at_z = z - (a - 1) if side == 0 else z + (a - 1)
        return send(w, at_z, v, (side * 3 + a - 1) * 2 + v, peer_up if side == 0 else peer_down, a == 1 and v == 0)

    def to_y(w, at_z, first=False):
        return send(w, at_z, 0, 12 + at_z, peer_y, first)

    def to_core(w, at_z, v, first=False):
        return send(w, at_z, v, 16 + 2 * at_z + v, peer_core, first)

    def pass_on(w, a, v):
        @pl.when(z < ROWS_Z - 1)
        def _():
            along(w, 0, a, v).start()

        @pl.when(z > 0)
        def _():
            along(w, 1, a, v).start()

    def from_z(a, action):
        @pl.when(z >= a)
        def _():
            action(0, z - a)

        @pl.when(z + a < ROWS_Z)
        def _():
            action(1, z + a)

    def start_own(w):
        pass_on(w, 1, 0)
        to_y(w, z, True).start()
        to_core(w, z, 0, True).start()

    def relay_z(w, a, v=0):
        def action(side, at_z):
            along(w, side, a, v).wait_recv()
            if a < ROWS_Z - 1:
                @pl.when(z < ROWS_Z - 1 if side == 0 else z > 0)
                def _():
                    along(w, side, a + 1, v).start()

            if w < 4:
                to_y(w, at_z).start()
            to_core(w, at_z, v).start()

        from_z(a, action)

    def relay_y(w, a):
        def action(side, at_z):
            to_y(w, at_z).wait_recv()
            to_core(w, at_z, 1).start()

        if a == 0:
            action(0, z)
            if w == 4:
                pass_on(w, 1, 1)
        else:
            from_z(a, action)

    def all_here(w):
        for at_z in range(ROWS_Z):
            for v in range(2):
                to_core(w, at_z, v).wait_recv()

    def all_gone(w):
        for v in range(1 if w < 4 else 2):
            for a in range(1, ROWS_Z):
                @pl.when((z < ROWS_Z - 1) & (z >= a - 1))
                def _():
                    along(w, 0, a, v).wait_send()

                @pl.when((z > 0) & (z + a - 1 < ROWS_Z))
                def _():
                    along(w, 1, a, v).wait_send()

        for at_z in range(ROWS_Z):
            if w < 4:
                to_y(w, at_z).wait_send()
            for v in range(2):
                to_core(w, at_z, v).wait_send()
        if w == 4:
            to_y(w, z).wait_send()

    def to_x(src, dst, index):
        return pltpu.make_async_remote_copy(
            src_ref=src, dst_ref=dst, send_sem=x_send.at[index], recv_sem=x_recv.at[index],
            device_id=x_peer, device_id_type=MESH,
        )

    third = q_in.shape[1] // 3
    share = third // 2
    q_picks = []
    for part in range(3):
        picked = q_in.at[:, pl.ds(pl.multiple_of(part * third + piece * share, 128), share)]
        q_picks.append(local(picked, q_own.at[:, pl.ds(part * share, share)], 17 + part))
        q_picks[-1].start()
    d_mine = d_in.at[pl.ds(piece * 2 * rows, 2 * rows)]
    local(o_in, o_own, 1).start()
    local(u_in, u_wide, 2).start()
    local(d_mine, d_own, 3).start()
    local(cot, cot_own, 4).start()
    greet(peers)
    for copy in q_picks:
        copy.wait()
    start_own(0)
    hidden_x = to_x(hidden, hid_other, 0)
    hidden_x.start()
    cot_x = to_x(cot, dy_all.at[piece], 1)
    cot_x.start()
    local(q_own, q_all.at[me], 0).start()
    local(o_in, o_own, 1).wait()
    local(o_own, o_all.at[me], 1).start()
    local(d_mine, d_own, 3).wait()
    local(d_own, d_all.at[me], 3).start()
    local(cot, cot_own, 4).wait()
    local(cot_own, dy_all.at[piece], 4).start()

    def norm_rows(read, half):
        step = 64

        def body(i, carry):
            rows = read(aligned(i, step)).astype(jnp.float32)
            low = layer_norm(rows, first_gain, first_shift).astype(bf16)
            normed[pl.ds(pl.multiple_of(half * own_rows + i * step, step), step), :] = low
            return carry

        lax.fori_loop(0, own_rows // step, body, 0)

    units_each = 2 * rows
    group = 8 * units_each

    def mine(block):
        wide = block.astype(jnp.float32)
        halves = []
        for half in range(2):
            at = [slice((2 * j + half) * units_each, (2 * j + half + 1) * units_each) for j in range(4)]
            halves.append(jnp.concatenate([wide[:, cols] for cols in at], axis=1))
        return jnp.where(piece == 0, halves[0], halves[1])

    local(u_in, u_wide, 2).wait()
    for g in range(u_own.shape[1] // (group // 2)):
        cols = slice(g * group // 2, (g + 1) * group // 2)
        u_own[:, cols] = mine(u_wide[:, g * group : (g + 1) * group]).astype(bf16)
        bias[:, cols] = mine(bias_in[g * group : (g + 1) * group].reshape(1, group))
    local(u_own, u_all.at[me], 2).start()
    norm_rows(lambda rows: hidden[rows, :], piece)
    relay_z(0, 1)
    start_own(1)
    relay_y(0, 0)
    write_mask(starts, mask)
    relay_z(0, 2)
    relay_y(0, 1)
    relay_z(0, 3)
    relay_y(0, 2)
    hidden_x.wait_recv()
    norm_rows(lambda rows: hid_other[rows, :], other)
    relay_z(1, 1)
    start_own(2)

    def flip(i, carry):
        normed_t[aligned(i, 128), :] = normed[:, aligned(i, 128)].T
        return carry

    lax.fori_loop(0, width // 128, flip, 0)
    local(normed_t, normed_t_out, 8).start()
    relay_y(0, 3)
    relay_z(1, 2)
    all_here(0)
    local(q_own, q_all.at[me], 0).wait()
    local(q_all, wq, 5).start()
    local(q_all, wq, 5).wait()

    column = lax.broadcasted_iota(jnp.int32, (1, 3 * PAIR), 1)

    def project(i, carry):
        cols = aligned(i, 3 * PAIR)
        weight = wq[:, :, cols].reshape(width, 3 * PAIR)
        value = dot_nn(normed[...], weight).astype(bf16)
        factor = jnp.where(i * 3 * PAIR + column < share, HEAD_DIM ** (-0.5), 1.0).astype(bf16)
        packed[:, cols] = value * factor
        return carry

    relay_z(1, 3)
    relay_y(1, 0)
    lax.fori_loop(0, pairs, project, 0)
    relay_y(1, 1)
    local(packed, packed_out, 9).start()
    first_lanes = head_lanes(PAIR)

    def attend(p):
        at_q, at_k, at_v = (slice(t * share + PAIR * p, t * share + PAIR * (p + 1)) for t in range(3))
        value_t = packed[:, at_v].T
        step = 256

        def rows(i, carry):
            queries = packed[aligned(i, step), at_q]
            keys = packed[:, at_k]
            halves = []
            for h in range(2):
                one = jnp.where(first_lanes[h], queries, jnp.zeros_like(queries))
                scores = dot_nt(keys, one) + mask[:, :, aligned(i, step)].reshape(length, step)
                top = jnp.max(scores, axis=0, keepdims=True)
                weights = jnp.exp(scores - top)
                total = jnp.sum(weights, axis=0, keepdims=True)
                lse[2 * p + h : 2 * p + h + 1, aligned(i, step)] = top + jnp.log(total)
                summed = dot_nn(value_t[h * HEAD_DIM : (h + 1) * HEAD_DIM], weights.astype(bf16))
                halves.append(summed / total)
            both = jnp.concatenate(halves, axis=0).T.astype(bf16)
            att_part[aligned(i, step), p * PAIR : (p + 1) * PAIR] = both
            return carry

        lax.fori_loop(0, length // step, rows, 0)

    def att_cols(half, p):
        return pl.ds(pl.multiple_of(half * pairs * PAIR + p * PAIR, PAIR), PAIR)

    att_x = []
    for p in range(pairs):
        attend(p)
        part = att_part.at[pl.ds(pl.multiple_of(other * own_rows, 128), own_rows), pl.ds(p * PAIR, PAIR)]
        att_x.append(to_x(part, att_own.at[:, att_cols(piece, p)], 2 + p))
        att_x[-1].start()
        mine = att_part[pl.ds(pl.multiple_of(piece * own_rows, 128), own_rows), p * PAIR : (p + 1) * PAIR]
        att_own[:, att_cols(piece, p)] = mine
        if p == 0:
            relay_y(1, 2)
            start_own(3)
        elif p == 1:
            relay_z(2, 1)
            start_own(4)
            relay_y(1, 3)
        elif p == 2:
            relay_y(2, 0)
        elif p == 3:
            relay_z(2, 2)
        elif p == 4:
            relay_y(4, 0)
    local(lse, lse_out, 10).start()
    for copy in att_x:
        copy.wait_recv()
    all_here(1)
    local(o_own, o_all.at[me], 1).wait()
    local(o_all, wo, 6).start()

    def flip_att(i, carry):
        att_t[aligned(i, 128), :] = att_own[:, aligned(i, 128)].T
        return carry

    lax.fori_loop(0, width // 128, flip_att, 0)
    local(att_t, att_t_out, 11).start()
    relay_y(2, 1)
    local(o_all, wo, 6).wait()

    def merge(i, carry):
        cols = aligned(i, 256)
        weight = wo[:, :, cols].reshape(width, 256)
        resid[:, cols] = hidden[:, cols].astype(jnp.float32) + dot_nn(att_own[...], weight)
        return carry

    lax.fori_loop(0, width // 256, merge, 0)
    local(resid, resid_out, 12).start()

    def second_rows(i, carry):
        rows = aligned(i, 64)
        second[piece, rows, :] = layer_norm(resid[rows, :], second_gain, second_shift).astype(bf16)
        return carry

    lax.fori_loop(0, own_rows // 64, second_rows, 0)
    second_x = to_x(second.at[piece], second.at[piece], 2 + pairs)
    second_x.start()
    relay_z(2, 3)
    relay_y(2, 2)
    relay_z(3, 1)
    relay_z(3, 2)
    relay_y(2, 3)
    relay_y(3, 0)
    relay_z(3, 3)
    second_x.wait_recv()

    def flip_second(i, carry):
        cols = aligned(i, 128)
        second_t[cols, :] = second[:, :, cols].reshape(length, 128).T
        return carry

    lax.fori_loop(0, width // 128, flip_second, 0)
    local(second_t, second_t_out, 13).start()
    relay_z(4, 1, 0)
    relay_y(3, 1)
    all_here(2)
    local(u_own, u_all.at[me], 2).wait()
    local(u_all, wu, 7).start()
    relay_z(4, 1, 1)
    local(u_all, wu, 7).wait()
    unit = 256
    steps = act.shape[1] // unit

    def expand(i, carry):
        cols = aligned(i // 2, unit)
        rows = aligned(lax.rem(i, 2), own_rows)
        weight = wu[:, :, cols].reshape(width, unit)
        up = dot_nn(second[lax.rem(i, 2)], weight) + bias[:, cols]
        cdf = 0.5 * (1.0 + lax.erf(up * (0.5 ** 0.5)))
        pdf = jnp.exp(up * up * -0.5) * ((2.0 * math.pi) ** -0.5)
        value = (up * cdf).astype(bf16)
        act[rows, cols] = value
        act_t[cols, rows] = value.T
        slope[rows, cols] = (cdf + up * pdf).astype(bf16)
        return carry

    lax.fori_loop(0, steps // 2, expand, 0)
    relay_z(4, 2, 0)
    relay_y(3, 2)
    lax.fori_loop(steps // 2, steps, expand, 0)
    relay_z(4, 2, 1)
    lax.fori_loop(steps, 3 * steps // 2, expand, 0)
    relay_z(4, 3, 0)
    relay_y(3, 3)
    lax.fori_loop(3 * steps // 2, 2 * steps, expand, 0)
    local(act, act_out, 14).start()
    local(act_t, act_t_out, 15).start()
    local(slope, slope_out, 16).start()
    relay_z(4, 3, 1)
    all_here(3)
    all_here(4)
    cot_x.wait_recv()
    local(d_own, d_all.at[me], 3).wait()
    local(cot_own, dy_all.at[piece], 4).wait()
    local(normed_t, normed_t_out, 8).wait()
    local(packed, packed_out, 9).wait()
    local(lse, lse_out, 10).wait()
    local(att_t, att_t_out, 11).wait()
    local(resid, resid_out, 12).wait()
    local(second_t, second_t_out, 13).wait()
    local(act, act_out, 14).wait()
    local(act_t, act_t_out, 15).wait()
    local(slope, slope_out, 16).wait()
    for w in range(5):
        all_gone(w)
    for copy in [hidden_x, cot_x, second_x] + att_x:
        copy.wait_send()


def forward(hidden, cot, starts, gain1, shift1, gain2, shift2, bias, qkv, out, up, down):
    own_rows, width = hidden.shape
    length = 2 * own_rows
    cols = qkv.shape[1] // 2
    units = up.shape[1] // 2
    rows = up.shape[0]
    bf16, f32 = jnp.bfloat16, jnp.float32
    shards = lax.axis_size("rows")
    head_rows = 16
    outs = [
        ((shards, rows, cols), bf16),
        ((shards, rows, width), bf16),
        ((shards, rows, units), bf16),
        ((shards, down.shape[0] // 2, width), bf16),
        ((2, own_rows, width), bf16),
        ((width, length), bf16),
        ((length, cols), bf16),
        ((head_rows, length), f32),
        ((width, own_rows), bf16),
        ((own_rows, width), f32),
        ((width, length), bf16),
        ((length, units), bf16),
        ((units, length), bf16),
        ((length, units), bf16),
    ]
    scratch = [
        ((own_rows, width), bf16),
        ((length, width), bf16),
        ((shards, rows, cols), bf16),
        ((shards, rows, width), bf16),
        ((shards, rows, units), bf16),
        ((length, cols), bf16),
        ((length // 48, 48, length), f32),
        ((length, cols // 3), bf16),
        ((own_rows, width), bf16),
        ((own_rows, width), f32),
        ((2, own_rows, width), bf16),
        ((length, units), bf16),
        ((units, length), bf16),
        ((length, units), bf16),
        ((width, length), bf16),
        ((width, own_rows), bf16),
        ((width, length), bf16),
        ((head_rows, length), f32),
        ((rows, 2 * units), bf16),
        ((rows, cols), bf16),
        ((rows, width), bf16),
        ((rows, units), bf16),
        ((2 * rows, width), bf16),
        ((own_rows, width), bf16),
        ((1, units), f32),
    ]
    vmem = pl.BlockSpec(memory_space=pltpu.VMEM)
    anywhere = pl.BlockSpec(memory_space=pl.ANY)
    smem = pl.BlockSpec(memory_space=pltpu.SMEM)
    dma = pltpu.SemaphoreType.DMA
    x_copies = 3 + cols // (3 * PAIR)
    return pl.pallas_call(
        forward_kernel,
        out_shape=[jax.ShapeDtypeStruct(shape, kind) for shape, kind in outs],
        in_specs=[vmem, anywhere, smem] + [vmem] * 5 + [anywhere] * 4,
        out_specs=[anywhere] * len(outs),
        scratch_shapes=[pltpu.VMEM(shape, kind) for shape, kind in scratch]
        + [dma((20,)), dma((120,)), dma((120,)), dma((x_copies,)), dma((x_copies,))],
        compiler_params=pltpu.CompilerParams(
            collective_id=1, has_side_effects=True, vmem_limit_bytes=60 * 1024 * 1024
        ),
        name="forward",
    )(hidden, cot, starts, gain1, shift1, gain2, shift2, bias, qkv, out, up, down)


UNIT = 640
SLOTS = 2


def norm_back(values, gain, grad):
    centred = values - jnp.mean(values, axis=-1, keepdims=True)
    scale = lax.rsqrt(jnp.mean(centred * centred, axis=-1, keepdims=True) + 1e-05)
    unit = centred * scale
    scaled = grad * gain
    mean_one = jnp.mean(scaled, axis=-1, keepdims=True)
    mean_two = jnp.mean(scaled * unit, axis=-1, keepdims=True)
    d_values = scale * (scaled - mean_one - unit * mean_two)
    d_gain = jnp.sum(grad * unit, axis=0, keepdims=True)
    d_shift = jnp.sum(grad, axis=0, keepdims=True)
    return d_values, d_gain, d_shift


def backward_kernel(
    starts, gain1, gain2, hidden, dy_all, q_all, o_all, u_all, d_all, normed_t, packed, lse_in, att_t,
    resid, second_t, act, act_t, slope,
    output, grad_hidden, units_out, pairs_out, small_out,
    lhs, half_act, wide, wd, wu, dy, first, second, d_att, x_in0, x_in1, x_out0, x_out1,
    down_own, parts, core_in, core_in_q, y_in, y_in_q, z_in, z_in_q, lse, acc_k, acc_v,
    bias_sum, small, small_core, small_y, small_z,
    local_sem, a_send, a_recv, b_send, b_recv, c_send, c_recv, g_send, g_recv, x_send, x_recv,
    s_send, s_recv, keep_sem,
):
    bf16, f32 = jnp.bfloat16, jnp.float32
    z, y, core = place_of()
    piece = lax.axis_index("blk")
    other = 1 - piece
    own_rows, width = first.shape
    length = 2 * own_rows
    branch = half_act.at[:, pl.ds(0, width)]
    units = wide.shape[1]
    cols = 3 * d_att.shape[1]
    pairs = d_att.shape[1] // PAIR
    peers = neighbours()
    wide_chunks = core_in.shape[0]
    first_gain, second_gain = gain1[...].reshape(1, width), gain2[...].reshape(1, width)
    half_rows = lambda half: pl.ds(pl.multiple_of(half * own_rows, 128), own_rows)

    def remote(src, dst, sends, recvs, index, peer):
        return pltpu.make_async_remote_copy(
            src_ref=src, dst_ref=dst, send_sem=sends.at[index], recv_sem=recvs.at[index],
            device_id=peer, device_id_type=MESH,
        )

    loads = {
        "act_t": (act_t, lhs, 0),
        "dy": (dy_all, dy, 1),
        "down": (d_all, wd, 2),
        "slope": (slope, wide, 3),
        "up": (u_all, wu, 4),
        "act_other": (act.at[half_rows(other)], half_act, 5),
        "act_own": (act.at[half_rows(piece)], half_act, 6),
        "resid": (resid, second, 7),
        "lse": (lse_in, lse, 8),
        "second_t": (second_t, lhs.at[:, pl.ds(0, lhs.shape[1] // 2)], 9),
        "att_t": (att_t, lhs.at[:, pl.ds(lhs.shape[1] // 2, lhs.shape[1] // 2), pl.ds(0, own_rows)], 10),
        "out": (o_all, wd.at[pl.ds(0, width)], 11),
        "normed_t": (normed_t, wd.at[pl.ds(width, width), pl.ds(0, length)], 12),
        "qkv": (q_all, wu.at[:, pl.ds(0, cols)], 13),
        "packed": (packed, wide.at[:, pl.ds(0, cols)], 14),
        "hidden": (hidden, branch, 15),
        "output": (second, output, 16),
        "grad_hidden": (first, grad_hidden, 17),
    }

    def local(name):
        src, dst, index = loads[name]
        return pltpu.make_async_copy(src, dst, local_sem.at[index])

    def buffers(i):
        if i < wide_chunks:
            return core_in.at[i], y_in.at[i], z_in.at[i], z_in.at[i, 0], units_out.at[:, i], UNIT
        i -= wide_chunks
        return core_in_q.at[i], y_in_q.at[i], z_in_q.at[i], z_in_q.at[i, 0], pairs_out.at[:, i], 3 * PAIR

    def copy_a(i):
        into, _, _, _, _, n = buffers(i)
        return remote(parts.at[i % SLOTS, 1 - core, :, :, :, pl.ds(0, n)], into, a_send, a_recv, i, peers[4])

    def copy_b(i):
        sums, into, _, _, _, _ = buffers(i)
        return remote(sums.at[1 - y], into, b_send, b_recv, i, peers[3])

    def copy_c(i, k):
        _, sums, into, _, _, _ = buffers(i)
        return remote(sums.at[lax.rem(z + k, ROWS_Z)], into.at[k - 1], c_send, c_recv, 3 * i + k - 1, peers[k - 1])

    def copy_g(i):
        _, _, _, share, out, _ = buffers(i)
        return remote(share, out.at[piece], g_send, g_recv, i, peers[5])

    def keep_g(i):
        _, _, _, share, out, _ = buffers(i)
        return pltpu.make_async_copy(share, out.at[piece], keep_sem.at[i])

    def finish_a(i):
        sums, _, _, _, _, n = buffers(i)
        copy_a(i).wait_recv()
        slot = i % SLOTS
        sums[1 - y] += parts[slot, core, 1 - y, :, :, :n]
        copy_b(i).start()
        sums[y] += parts[slot, core, y, :, :, :n]
        copy_a(i).wait_send()

    def finish_b(i):
        mine, sums, _, _, _, _ = buffers(i)
        copy_b(i).wait_recv()
        sums[...] += mine[y]
        for k in (1, 3, 2):
            copy_c(i, k).start()

    def finish_c(i):
        _, sums, terms, share, _, _ = buffers(i)
        for k in (1, 3, 2):
            copy_c(i, k).wait_recv()
        total = sums[z].astype(f32)
        for k in range(3):
            total += terms[k].astype(f32)
        share[...] = total.astype(bf16)
        copy_g(i).start()
        keep_g(i).start()

    def grad_chunk(i, left, right):
        slot = i % SLOTS

        def one_z(to_z, carry):
            value = dot_nn(left(to_z), right()).astype(bf16)
            n = value.shape[1]
            rows = value.shape[0] // 4
            for block in range(4):
                to_y, to_core = divmod(block, 2)
                parts[slot, to_core, to_y, to_z, :, :n] = value[block * rows : (block + 1) * rows]
            return carry

        lax.fori_loop(0, ROWS_Z, one_z, 0)
        copy_a(i).start()

    for name in ("act_t", "dy", "down", "slope", "act_other", "up", "resid", "lse"):
        local(name).start()
    greet(peers)
    local("act_t").wait()
    local("dy").wait()
    block_rows = parts.shape[4]

    def grad_down(i):
        h, column = divmod(i, 2)

        def left(to_z):
            rows = lhs[pl.ds(to_z * 4, 4), h * block_rows : (h + 1) * block_rows, :]
            return rows.reshape(4 * block_rows, length)

        grad_chunk(i, left, lambda: dy[:, :, column * UNIT : (column + 1) * UNIT].reshape(length, UNIT))

    grad_down(0)
    grad_down(1)
    finish_a(0)
    grad_down(2)
    finish_a(1)
    grad_down(3)
    local("second_t").start()
    local("att_t").start()
    local("down").wait()
    local("slope").wait()

    tile = 256

    def d_units(i, carry):
        at = aligned(i, tile)
        sums = jnp.zeros((1, tile), f32)
        for half in range(2):
            rows = slice(half * own_rows, (half + 1) * own_rows)
            value = dot_nt(dy[half], wd[at, :]) * wide[rows, at].astype(f32)
            low = value.astype(bf16)
            wide[rows, at] = low
            sums += jnp.sum(low.astype(f32), axis=0, keepdims=True)
        bias_sum[:, at] = sums
        return carry

    lax.fori_loop(0, 4, d_units, 0)
    finish_a(2)
    finish_a(3)
    lax.fori_loop(4, units // tile, d_units, 0)
    local("up").wait()

    def d_second(half, write):
        def body(i, carry):
            at = aligned(i, tile)
            write(at, dot_nt(wide[half_rows(half), :], wu[at, :]))
            return carry

        lax.fori_loop(0, width // tile, body, 0)

    def write_out0(at, value):
        x_out0[:, at] = value.astype(bf16)

    def write_first(at, value):
        first[:, at] = value

    d_second(other, write_out0)
    second_x = remote(x_out0, x_in0, x_send, x_recv, 0, peers[5])
    second_x.start()
    d_second(piece, write_first)
    local("qkv").start()
    finish_b(0)
    local("act_other").wait()

    def down_part(target):
        def body(i, carry):
            at = aligned(i, tile)
            target[:, at] = dot_nn(half_act[...], wd[:, at]).astype(bf16)
            return carry

        lax.fori_loop(0, width // tile, body, 0)

    down_part(x_out1)
    local("act_own").start()
    local("second_t").wait()

    def grad_up(i):
        def left(to_z):
            rows = lhs[pl.ds(to_z * 4, 4), :block_rows, :]
            return rows.reshape(4 * block_rows, length)

        grad_chunk(4 + i, left, lambda: wide[:, i * UNIT : (i + 1) * UNIT])

    grad_up(0)
    grad_up(1)
    local("act_own").wait()
    finish_a(4)
    finish_b(1)
    down_part(down_own)
    local("out").start()
    local("normed_t").start()
    finish_a(5)
    grad_up(2)
    grad_up(3)
    local("packed").start()
    mask = lhs.at[:, pl.ds(0, length // lhs.shape[0]), :]
    write_mask(starts, mask)
    finish_a(6)
    finish_a(7)
    finish_c(0)
    finish_b(2)
    local("resid").wait()
    second_x.wait_recv()
    step = 64

    def back_two(i, carry):
        rows = aligned(i, step)
        grad = first[rows, :] + x_in0[rows, :].astype(f32)
        d_values, d_gain, d_shift = norm_back(second[rows, :], second_gain, grad)
        total = dy[piece, rows, :].astype(f32) + d_values
        first[rows, :] = total
        branch[rows, :] = total.astype(bf16)
        return carry[0] + d_gain, carry[1] + d_shift

    zeros = jnp.zeros((1, width), f32)
    gain_two, shift_two = lax.fori_loop(0, own_rows // step, back_two, (zeros, zeros))
    small[2:3, :] = gain_two
    small[3:4, :] = shift_two
    local("out").wait()
    second_x.wait_send()
    d_width = d_att.shape[1]

    def d_attended(half):
        rows = pl.ds(pl.multiple_of(half * d_width, 128), d_width)
        return dot_nt(branch[...], wd[rows, :]).astype(bf16)

    x_out0[:, :d_width] = d_attended(other)
    att_x = remote(x_out0.at[:, pl.ds(0, d_width)], d_att.at[half_rows(piece)], x_send, x_recv, 1, peers[5])
    att_x.start()
    down_x = remote(x_out1, x_in1, x_send, x_recv, 2, peers[5])
    down_x.start()
    d_att[half_rows(piece), :] = d_attended(piece)
    local("att_t").wait()

    def grad_out(i):
        def left(to_z):
            rows = lhs[pl.ds(to_z * 4, 4), block_rows : 2 * block_rows, :own_rows]
            return rows.reshape(4 * block_rows, own_rows)

        grad_chunk(8 + i, left, lambda: branch[:, i * UNIT : (i + 1) * UNIT])

    grad_out(0)
    grad_out(1)
    finish_c(1)
    finish_b(3)
    finish_a(8)
    finish_a(9)
    local("hidden").start()
    local("lse").wait()
    local("packed").wait()
    local("normed_t").wait()
    att_x.wait_recv()
    first_lanes = head_lanes(PAIR)

    def pair_cols(p):
        return tuple(slice(t * d_width + PAIR * p, t * d_width + PAIR * (p + 1)) for t in range(3))

    def attend_back(p):
        at_q, at_k, at_v = pair_cols(p)
        keys_t = wide[:, at_k].T
        acc_k[...] = jnp.zeros_like(acc_k)
        acc_v[...] = jnp.zeros_like(acc_v)
        chunk = 256

        def body(i, carry):
            rows = aligned(i, chunk)
            keys = wide[:, at_k]
            values = wide[:, at_v]
            queries = wide[rows, at_q]
            grads = d_att[rows, p * PAIR : (p + 1) * PAIR]
            blocked = mask[:, :, rows].reshape(length, chunk).astype(f32)
            parts_q = []
            for h in range(2):
                one_q = jnp.where(first_lanes[h], queries, jnp.zeros_like(queries))
                one_g = jnp.where(first_lanes[h], grads, jnp.zeros_like(grads))
                scores = dot_nt(keys, one_q) + (blocked - lse[2 * p + h : 2 * p + h + 1, rows])
                probs = jnp.exp(scores)
                d_probs = dot_nt(values, one_g)
                dots = jnp.sum(probs * d_probs, axis=0, keepdims=True)
                d_scores = (probs * (d_probs - dots)).astype(bf16)
                acc_v[...] += dot_nn(probs.astype(bf16), one_g)
                acc_k[...] += dot_nn(d_scores, one_q)
                parts_q.append(dot_nn(keys_t[h * HEAD_DIM : (h + 1) * HEAD_DIM], d_scores))
            d_queries = jnp.concatenate(parts_q, axis=0).T * HEAD_DIM ** (-0.5)
            wide[rows, at_q] = d_queries.astype(bf16)
            return carry

        lax.fori_loop(0, length // chunk, body, 0)
        wide[:, at_k] = acc_k[...].astype(bf16)
        wide[:, at_v] = acc_v[...].astype(bf16)

    def grad_pair(p):
        def left(to_z):
            return wd[pl.ds(pl.multiple_of(width + to_z * 4 * block_rows, 64), 4 * block_rows), :length]

        grad_chunk(10 + p, left, lambda: jnp.concatenate([wide[:, at] for at in pair_cols(p)], axis=1))

    def write_output():
        down_x.wait_recv()

        def body(i, carry):
            rows = aligned(i, step)
            second[rows, :] += down_own[rows, :].astype(f32) + x_in1[rows, :].astype(f32)
            return carry

        lax.fori_loop(0, own_rows // step, body, 0)
        local("output").start()

    ticks = {
        0: lambda: (finish_c(2), finish_b(4)),
        1: lambda: (finish_a(10), finish_c(3), finish_b(5)),
        2: lambda: (finish_a(11), finish_c(4), finish_b(6)),
        3: lambda: (finish_a(12), write_output(), finish_c(5), finish_b(7)),
        4: lambda: (finish_a(13), finish_c(6)),
    }
    for p in range(pairs):
        attend_back(p)
        grad_pair(p)
        ticks[p]()
    finish_a(14)
    local("qkv").wait()
    local("output").wait()
    att_x.wait_send()

    def d_normed(half, write):
        def body(i, carry):
            at = aligned(i, tile)
            write(at, dot_nt(wide[half_rows(half), :cols], wu[at, :cols]))
            return carry

        lax.fori_loop(0, width // tile, body, 0)

    def write_second(at, value):
        second[:, at] = value

    d_normed(other, write_out0)
    normed_x = remote(x_out0, x_in0, x_send, x_recv, 3, peers[5])
    normed_x.start()
    finish_b(8)
    d_normed(piece, write_second)
    finish_c(7)
    finish_b(9)
    local("hidden").wait()
    finish_c(8)
    finish_b(10)
    normed_x.wait_recv()

    def back_one(i, carry):
        rows = aligned(i, step)
        grad = second[rows, :] + x_in0[rows, :].astype(f32)
        d_values, d_gain, d_shift = norm_back(branch[rows, :].astype(f32), first_gain, grad)
        first[rows, :] += d_values
        return carry[0] + d_gain, carry[1] + d_shift

    gain_one, shift_one = lax.fori_loop(0, own_rows // step, back_one, (zeros, zeros))
    local("grad_hidden").start()
    small[0:1, :] = gain_one
    small[1:2, :] = shift_one
    small[4:5, :] = bias_sum[:, :width]
    small[5:6, :] = bias_sum[:, width:]
    small[6:8, :] = jnp.zeros((2, width), f32)
    core_x = remote(small, small_core, s_send, s_recv, 0, peers[4])
    core_x.start()
    finish_b(11)
    core_x.wait()
    small[...] += small_core[...]
    y_x = remote(small, small_y, s_send, s_recv, 1, peers[3])
    y_x.start()
    finish_c(9)
    finish_b(12)
    finish_c(10)
    finish_b(13)
    finish_c(11)
    finish_b(14)
    y_x.wait()
    small_z[z] = small[...] + small_y[...]
    z_x = [remote(small_z.at[z], small_z.at[z], s_send, s_recv, 1 + k, peers[k - 1]) for k in (1, 2, 3)]
    for copy in z_x:
        copy.start()
    finish_c(12)
    finish_c(13)
    for copy in z_x:
        copy.wait()
    small[...] = ((small_z[0] + small_z[1]) + small_z[2]) + small_z[3]
    share_x = remote(small, small_out.at[piece], s_send, s_recv, 5, peers[5])
    share_x.start()
    share_keep = pltpu.make_async_copy(small, small_out.at[piece], keep_sem.at[15])
    share_keep.start()
    finish_c(14)
    for i in range(15):
        copy_b(i).wait_send()
        for k in (1, 2, 3):
            copy_c(i, k).wait_send()
        copy_g(i).wait()
        keep_g(i).wait()
    share_x.wait()
    share_keep.wait()
    down_x.wait_send()
    normed_x.wait_send()
    local("grad_hidden").wait()


def backward(starts, gain1, gain2, hidden, dy_all, q_all, o_all, u_all, d_all, *kept):
    bf16, f32 = jnp.bfloat16, jnp.float32
    _, own_rows, width = dy_all.shape
    length = 2 * own_rows
    cols, units = q_all.shape[1], u_all.shape[1]
    rows = width // 16
    wide_units, pairs = 10, cols // (3 * PAIR)
    pair_cols = 3 * PAIR
    outs = [
        ((own_rows, width), f32),
        ((own_rows, width), f32),
        ((2, wide_units, rows, UNIT), bf16),
        ((2, pairs, rows, pair_cols), bf16),
        ((2, 8, width), f32),
    ]
    token = ((own_rows, width), bf16)
    scratch = [
        ((16, 2 * rows, length), bf16),
        ((own_rows, units), bf16),
        ((length, units), bf16),
        ((units, width), bf16),
        ((width, units), bf16),
        ((2, own_rows, width), bf16),
        ((own_rows, width), f32),
        ((own_rows, width), f32),
        ((length, cols // 3), bf16),
        token, token, token, token, token,
        ((SLOTS, 2, 2, ROWS_Z, rows, UNIT), bf16),
        ((wide_units, 2, ROWS_Z, rows, UNIT), bf16),
        ((pairs, 2, ROWS_Z, rows, pair_cols), bf16),
        ((wide_units, ROWS_Z, rows, UNIT), bf16),
        ((pairs, ROWS_Z, rows, pair_cols), bf16),
        ((wide_units, 3, rows, UNIT), bf16),
        ((pairs, 3, rows, pair_cols), bf16),
        ((16, length), f32),
        ((length, PAIR), f32),
        ((length, PAIR), f32),
        ((1, units), f32),
        ((8, width), f32),
        ((8, width), f32),
        ((8, width), f32),
        ((ROWS_Z, 8, width), f32),
    ]
    vmem = pl.BlockSpec(memory_space=pltpu.VMEM)
    anywhere = pl.BlockSpec(memory_space=pl.ANY)
    smem = pl.BlockSpec(memory_space=pltpu.SMEM)
    chunks = wide_units + pairs
    dma = lambda n: pltpu.SemaphoreType.DMA((n,))
    sems = [18] + [chunks] * 4 + [3 * chunks] * 2 + [chunks] * 2 + [4, 4, 6, 6, chunks + 1]
    return pl.pallas_call(
        backward_kernel,
        out_shape=[jax.ShapeDtypeStruct(shape, kind) for shape, kind in outs],
        in_specs=[smem, vmem, vmem] + [anywhere] * (6 + len(kept)),
        out_specs=[anywhere] * len(outs),
        scratch_shapes=[pltpu.VMEM(shape, kind) for shape, kind in scratch] + [dma(n) for n in sems],
        compiler_params=pltpu.CompilerParams(
            collective_id=2, has_side_effects=True, vmem_limit_bytes=60 * 1024 * 1024
        ),
        name="backward",
    )(starts, gain1, gain2, hidden, dy_all, q_all, o_all, u_all, d_all, *kept)


def finish_kernel(
    raw_output, raw_grad, units_lo, units_hi, pairs_in, small,
    output, grad_hidden, qkv, out, up, down, gain1, shift1, gain2, shift2, bias,
):
    f32 = jnp.float32
    step = pl.program_id(0)
    output[0] = raw_output[...]
    grad_hidden[0] = raw_grad[...]
    rows = out.shape[0]
    width = small.shape[2]
    units_in = (units_lo, units_hi)

    def mixed(first, second):
        each = first.shape[1] // 4
        blocks = []
        for j in range(4):
            at = slice(j * each, (j + 1) * each)
            blocks += [first[:, at].astype(f32), second[:, at].astype(f32)]
        return jnp.concatenate(blocks, axis=1)

    for now in range(2):

        @pl.when(step == now)
        def _():
            for i in range(4):
                h, column = divmod(i, 2)
                at = slice(column * UNIT, (column + 1) * UNIT)
                down[h * rows : (h + 1) * rows, at] = units_in[now][0, i].astype(f32)
            for i in range(2):
                chunk = 4 + 2 * now + i
                at = slice(i * 2 * UNIT, (i + 1) * 2 * UNIT)
                up[:, at] = mixed(units_lo[0, chunk], units_hi[0, chunk])
            out[...] = units_lo[0, 8 + now].astype(f32) + units_hi[0, 8 + now].astype(f32)
            pairs = pairs_in.shape[1]
            for block in range(3 * now, 3 * now + 3):
                part, piece = divmod(block, 2)
                for p in range(pairs):
                    at = (block - 3 * now) * pairs * PAIR + p * PAIR
                    chunk = pairs_in[piece, p, :, part * PAIR : (part + 1) * PAIR]
                    qkv[:, at : at + PAIR] = chunk.astype(f32)

    @pl.when(step == 0)
    def _():
        for i, ref in enumerate((gain1, shift1, gain2, shift2)):
            ref[...] = (small[0, i : i + 1, :] + small[1, i : i + 1, :]).reshape(width)
        for g in range(2):
            for j in range(2):
                at = slice(j * UNIT, (j + 1) * UNIT)
                lo, hi = small[0, 4 + g : 5 + g, at], small[1, 4 + g : 5 + g, at]
                begin = (2 * g + j) * 2 * UNIT
                bias[begin : begin + 2 * UNIT] = mixed(lo, hi).reshape(2 * UNIT)


def finish(raw_output, raw_grad, units_in, pairs_in, small):
    f32 = jnp.float32
    own_rows, width = raw_output.shape
    rows = units_in.shape[2]
    shapes = [
        (1, own_rows, width), (1, own_rows, width), (rows, 3 * width), (rows, width), (rows, 8 * UNIT),
        (4 * rows, width), (width,), (width,), (width,), (width,), (8 * UNIT,),
    ]
    token = pl.BlockSpec((own_rows // 2, width), lambda s: (s, 0))
    token_out = pl.BlockSpec((1, own_rows // 2, width), lambda s: (0, s, 0))
    columns = lambda n: pl.BlockSpec((rows, n // 2), lambda s: (0, s))
    fixed = lambda shape: pl.BlockSpec(shape, lambda s: (0,) * len(shape))
    half = lambda i: pl.BlockSpec((1,) + units_in.shape[1:], lambda s: (i, 0, 0, 0))
    return pl.pallas_call(
        finish_kernel,
        grid=(2,),
        out_shape=[jax.ShapeDtypeStruct(shape, f32) for shape in shapes],
        in_specs=[token, token, half(0), half(1), fixed(pairs_in.shape), fixed(small.shape)],
        out_specs=[
            token_out, token_out, columns(3 * width), columns(width), columns(8 * UNIT),
            pl.BlockSpec((2 * rows, width), lambda s: (s, 0)),
        ] + [fixed(shape) for shape in shapes[6:]],
        compiler_params=pltpu.CompilerParams(vmem_limit_bytes=60 * 1024 * 1024),
        name="finish",
    )(raw_output, raw_grad, units_in, units_in, pairs_in, small)


def split_layer(
    hidden, starts, first_gain, first_shift, qkv_weight, out_weight, second_gain, second_shift,
    up_weight, hidden_bias, down_weight, cotangent,
):
    shards = lax.axis_size("rows")
    (
        qkv_all, out_all, up_all, down_all, dy_all, normed_t, packed, lse, att_t, residual, second_t,
        activated, activated_t, slope,
    ) = forward(
        hidden[0], cotangent[0], starts, first_gain, first_shift, second_gain, second_shift, hidden_bias,
        qkv_weight, out_weight, up_weight, down_weight,
    )
    whole = lambda w: w.reshape(-1, w.shape[-1])
    blocks = lambda w: w.reshape(shards, -1, w.shape[-1])
    shares = backward(
        starts, first_gain, second_gain, hidden[0], dy_all, whole(qkv_all), whole(out_all),
        whole(up_all), whole(down_all), normed_t, packed, lse, blocks(att_t), residual,
        blocks(second_t), activated, blocks(activated_t), slope,
    )
    return tuple(finish(*shares))


def splits_evenly(mesh):
    pieces = mesh.shape["blk"]
    return pieces == 2 and mesh.shape["rows"] == 2 * ROWS_Z * ROWS_Y and HEADS % (2 * pieces) == 0


def solution(mesh):
    in_specs = (
        P("rows", "blk", None),
        P("rows", None),
        P(),
        P(),
        P("rows", None),
        P("rows", None),
        P(),
        P(),
        P("rows", None),
        P(),
        P("rows", None),
        P("rows", "blk", None),
    )
    out_specs = (
        P("rows", "blk", None),
        P("rows", "blk", None),
        P("rows", None),
        P("rows", None),
        P("rows", None),
        P("rows", None),
        P(),
        P(),
        P(),
        P(),
        P(),
    )
    layer = split_layer if splits_evenly(mesh) else on_device
    return jax.shard_map(
        layer, mesh=mesh, in_specs=in_specs, out_specs=out_specs, check_vma=False
    )
```

```python
import functools
import math

import jax
import jax.numpy as jnp
from jax import lax
from jax.experimental import pallas as pl
from jax.experimental.pallas import tpu as pltpu
from jax.sharding import PartitionSpec as P

HEADS = 20
HEAD_DIM = 64


masked_score = -1e30
block_limit = 512


def layer_norm(values, gain, shift):
    mean_value = jnp.mean(values, axis=-1, keepdims=True)
    centred = values - mean_value
    variance = jnp.mean(centred * centred, axis=-1, keepdims=True)
    return centred * lax.rsqrt(variance + 1e-05) * gain + shift


def segment_of(starts_row, positions):
    reached = starts_row[None, :] <= positions[:, None]
    return jnp.sum(reached.astype(jnp.int32), axis=1) - 1


def scores_with_mask(queries, key_block, query_seg, key_seg):
    products = jnp.einsum("qhe,khe->hqk", queries, key_block, preferred_element_type=jnp.float32)
    products = products * queries.shape[2] ** (-0.5)
    allowed = (query_seg[:, None] == key_seg[None, :])[None, :, :]
    return (jnp.where(allowed, products, masked_score), allowed)


def attend_rows(running, key_rows, value_rows, queries, query_seg, starts_row):
    piece_rows = key_rows.shape[0]
    step_rows = math.gcd(piece_rows, block_limit)
    head_count = queries.shape[1]
    head_width = queries.shape[2]

    def one_block(block_index, state):
        row_top, denominator, weighted = state
        block_start = block_index * step_rows
        key_block = lax.dynamic_slice_in_dim(key_rows, block_start, step_rows, 0).reshape(
            step_rows, head_count, head_width
        )
        value_block = lax.dynamic_slice_in_dim(value_rows, block_start, step_rows, 0).reshape(
            step_rows, head_count, head_width
        )
        key_seg = segment_of(starts_row, block_start + jnp.arange(step_rows, dtype=jnp.int32))
        scores, allowed = scores_with_mask(queries, key_block, query_seg, key_seg)
        new_top = jnp.maximum(row_top, jnp.max(scores, axis=-1))
        factor = jnp.exp(row_top - new_top)
        weights = jnp.where(allowed, jnp.exp(scores - new_top[:, :, None]), 0.0)
        denominator = denominator * factor + jnp.sum(weights, axis=-1)
        weighted = weighted * factor[:, :, None] + jnp.einsum(
            "hqk,khe->hqe",
            weights.astype(jnp.bfloat16),
            value_block,
            preferred_element_type=jnp.float32,
        )
        return (new_top, denominator, weighted)

    return lax.fori_loop(0, piece_rows // step_rows, one_block, running)


def on_device(
    hidden,
    starts,
    first_gain,
    first_shift,
    qkv_weight,
    out_weight,
    second_gain,
    second_shift,
    up_weight,
    hidden_bias,
    down_weight,
    cotangent,
):
    rows_here = hidden.shape[1]
    model_width = hidden.shape[2]
    head_count = HEADS
    head_width = HEAD_DIM
    score_scale = head_width ** (-0.5)
    inputs = hidden[0].astype(jnp.float32)
    starts_row = starts[0]
    offset = lax.axis_index("blk") * rows_here
    query_seg = segment_of(starts_row, offset + jnp.arange(rows_here, dtype=jnp.int32))
    qkv_full, out_full, up_full, down_full = (
        lax.all_gather(qkv_weight, "rows", axis=0, tiled=True),
        lax.all_gather(out_weight, "rows", axis=0, tiled=True),
        lax.all_gather(up_weight, "rows", axis=0, tiled=True),
        lax.all_gather(down_weight, "rows", axis=0, tiled=True),
    )
    normed_low = layer_norm(inputs, first_gain, first_shift).astype(jnp.bfloat16)
    packed = jnp.dot(normed_low, qkv_full, preferred_element_type=jnp.float32).astype(jnp.bfloat16)
    queries = packed[:, :model_width].reshape(rows_here, head_count, head_width)
    key_rows = packed[:, model_width : 2 * model_width]
    value_rows = packed[:, 2 * model_width :]
    initial = (
        jnp.full((head_count, rows_here), masked_score, jnp.float32),
        jnp.zeros((head_count, rows_here), jnp.float32),
        jnp.zeros((head_count, rows_here, head_width), jnp.float32),
    )
    row_top, denominator, weighted = attend_rows(
        initial,
        lax.all_gather(key_rows, "blk", axis=0, tiled=True),
        lax.all_gather(value_rows, "blk", axis=0, tiled=True),
        queries,
        query_seg,
        starts_row,
    )
    log_total = row_top + jnp.log(denominator)
    attended = jnp.transpose(weighted / denominator[:, :, None], (1, 0, 2))
    attended_low = attended.reshape(rows_here, model_width).astype(jnp.bfloat16)
    residual = inputs + jnp.dot(attended_low, out_full, preferred_element_type=jnp.float32)
    second_low = layer_norm(residual, second_gain, second_shift).astype(jnp.bfloat16)
    up_values = jnp.dot(second_low, up_full, preferred_element_type=jnp.float32) + hidden_bias
    activated_low = jax.nn.gelu(up_values, approximate=False).astype(jnp.bfloat16)
    output = residual + jnp.dot(activated_low, down_full, preferred_element_type=jnp.float32)
    cot_low = cotangent[0]
    d_activated = jnp.einsum("tc,fc->tf", cot_low, down_full, preferred_element_type=jnp.float32)
    unused_gelu, gelu_pull = jax.vjp(
        lambda values: jax.nn.gelu(values, approximate=False), up_values
    )
    d_up_low = gelu_pull(d_activated)[0].astype(jnp.bfloat16)
    d_second = jnp.einsum("tf,cf->tc", d_up_low, up_full, preferred_element_type=jnp.float32)
    unused_second, second_pull = jax.vjp(layer_norm, residual, second_gain, second_shift)
    d_norm_two, d_second_gain, d_second_shift = second_pull(d_second)
    d_residual = cot_low.astype(jnp.float32) + d_norm_two
    d_branch_low = d_residual.astype(jnp.bfloat16)
    d_attended_low = jnp.einsum(
        "tc,kc->tk", d_branch_low, out_full, preferred_element_type=jnp.float32
    ).astype(jnp.bfloat16)
    d_attended3 = d_attended_low.reshape(rows_here, head_count, head_width)
    row_dots = jnp.einsum("qhe,qhe->hq", d_attended3.astype(jnp.float32), attended)
    keys_all, values_all = (
        lax.all_gather(key_rows, "blk", axis=0, tiled=True),
        lax.all_gather(value_rows, "blk", axis=0, tiled=True),
    )
    length = keys_all.shape[0]
    step_rows = math.gcd(length, block_limit)

    def block_terms(block_index):
        block_start = block_index * step_rows
        key_block = lax.dynamic_slice_in_dim(keys_all, block_start, step_rows, 0).reshape(
            step_rows, head_count, head_width
        )
        value_block = lax.dynamic_slice_in_dim(values_all, block_start, step_rows, 0).reshape(
            step_rows, head_count, head_width
        )
        key_seg = segment_of(starts_row, block_start + jnp.arange(step_rows, dtype=jnp.int32))
        scores, allowed = scores_with_mask(queries, key_block, query_seg, key_seg)
        probability = jnp.where(allowed, jnp.exp(scores - log_total[:, :, None]), 0.0)
        d_probs = jnp.einsum(
            "qhe,khe->hqk", d_attended3, value_block, preferred_element_type=jnp.float32
        )
        d_scores = (probability * (d_probs - row_dots[:, :, None])).astype(jnp.bfloat16)
        return (key_block, probability, d_scores)

    dq_start = jnp.zeros((rows_here, head_count, head_width), jnp.float32)

    def back_block(dq_sum, block_index):
        key_block, probability, d_scores = block_terms(block_index)
        dq_sum = dq_sum + jnp.einsum(
            "hqk,khe->qhe", d_scores, key_block, preferred_element_type=jnp.float32
        )
        dk_block = (
            jnp.einsum("hqk,qhe->khe", d_scores, queries, preferred_element_type=jnp.float32)
            * score_scale
        )
        dv_block = jnp.einsum(
            "hqk,qhe->khe",
            probability.astype(jnp.bfloat16),
            d_attended3,
            preferred_element_type=jnp.float32,
        )
        return (
            dq_sum,
            (dk_block.reshape(step_rows, model_width), dv_block.reshape(step_rows, model_width)),
        )

    dq_sum, (dk_terms, dv_terms) = lax.scan(back_block, dq_start, jnp.arange(length // step_rows))
    dk_rows, dv_rows = (
        lax.psum_scatter(
            dk_terms.reshape(length, model_width).astype(jnp.bfloat16),
            "blk",
            scatter_dimension=0,
            tiled=True,
        ).astype(jnp.float32),
        lax.psum_scatter(
            dv_terms.reshape(length, model_width).astype(jnp.bfloat16),
            "blk",
            scatter_dimension=0,
            tiled=True,
        ).astype(jnp.float32),
    )
    d_packed = jnp.concatenate(
        [(dq_sum * score_scale).reshape(rows_here, model_width), dk_rows, dv_rows], axis=1
    ).astype(jnp.bfloat16)
    d_normed = jnp.einsum("tn,cn->tc", d_packed, qkv_full, preferred_element_type=jnp.float32)
    unused_first, first_pull = jax.vjp(layer_norm, inputs, first_gain, first_shift)
    d_norm_one, d_first_gain, d_first_shift = first_pull(d_normed)
    grad_hidden = d_residual + d_norm_one
    d_bias = jnp.sum(d_up_low, axis=0, dtype=jnp.float32)
    wide_share = lax.psum_scatter(
        jnp.concatenate(
            [
                jnp.einsum("tc,tn->cn", normed_low, d_packed, preferred_element_type=jnp.float32),
                jnp.einsum(
                    "tc,tn->cn", attended_low, d_branch_low, preferred_element_type=jnp.float32
                ),
                jnp.einsum("tc,tn->cn", second_low, d_up_low, preferred_element_type=jnp.float32),
            ],
            axis=1,
        ).astype(jnp.bfloat16),
        "rows",
        scatter_dimension=0,
        tiled=True,
    )
    down_share = lax.psum_scatter(
        jnp.einsum("tf,tn->fn", activated_low, cot_low, preferred_element_type=jnp.float32).astype(
            jnp.bfloat16
        ),
        "rows",
        scatter_dimension=0,
        tiled=True,
    )
    wide_grads, down_grads = (
        lax.psum(wide_share, "blk").astype(jnp.float32),
        lax.psum(down_share, "blk").astype(jnp.float32),
    )
    grad_qkv = wide_grads[:, : 3 * model_width]
    grad_out = wide_grads[:, 3 * model_width : 4 * model_width]
    grad_up = wide_grads[:, 4 * model_width :]
    small_grads = lax.psum(
        (d_first_gain, d_first_shift, d_second_gain, d_second_shift, d_bias), ("rows", "blk")
    )
    return (
        output[None],
        grad_hidden[None],
        grad_qkv,
        grad_out,
        grad_up,
        down_grads,
        small_grads[0],
        small_grads[1],
        small_grads[2],
        small_grads[3],
        small_grads[4],
    )


MESH = pl.DeviceIdType.MESH
FORWARD_MOVES = (
    ((0, 0), (1, 0), (2, 0), (0, 1), (1, 1), (2, 1),),
    (),
    (),
    (),
    (),
    (),
    (),
    (),
    (),
    (),
    ((3, 0, 1, 0), (4, 0, 0), (4, 1, 0), (3, 0, 0, 0), (0, 2), (3, 1, 1, 0), (4, 0, 2), (3, 1, 0, 0), (4, 0, 1), (3, 0, 2, 0), (4, 1, 2), (4, 1, 1), (3, 2, 1, 0), (2, 4),),
    (),
    (),
    ((4, 0, 3), (3, 2, 0, 0), (0, 3), (4, 2, 2), (3, 1, 2, 0), (1, 2), (4, 2, 1), (3, 2, 2, 0), (1, 3), (4, 1, 3),),
    (),
    (),
    ((4, 2, 0), (3, 3, 1, 0), (0, 5), (2, 5),),
    ((4, 2, 3),),
    (),
    (),
    (),
    (),
    (),
    ((3, 3, 0, 0),),
    (),
    (),
    ((4, 3, 0), (2, 2), (2, 3), (0, 4),),
    (),
    ((3, 5, 1, 0),),
    (),
    (),
    (),
    ((3, 5, 0, 0),),
    (),
    (),
    ((4, 3, 2),),
    (),
    (),
    (),
    (),
    ((3, 3, 2, 0), (1, 5), (4, 3, 1), (1, 4), (3, 4, 1, 0), (3, 4, 0, 0), (4, 3, 3), (3, 5, 2, 0),),
    (),
    ((4, 5, 0),),
    ((3, 4, 2, 0),),
    (),
    ((4, 4, 0),),
    (),
    ((3, 5, 1, 1),),
    (),
    (),
    ((4, 4, 2),),
    (),
    ((3, 5, 0, 1),),
    (),
    ((4, 4, 1),),
    ((3, 5, 2, 1), (4, 4, 3),),
)
ROWS_Z, ROWS_Y = 4, 2
PAIR = 128


def place_of():
    index = lax.axis_index("rows")
    return index // 4, lax.rem(index // 2, 2), lax.rem(index, 2)


def row_of(z, y, core):
    return (lax.rem(z + ROWS_Z, ROWS_Z) * ROWS_Y + y) * 2 + core


def aligned(index, step):
    return pl.ds(pl.multiple_of(index * step, step), step)


def dot_nt(left, right):
    return lax.dot_general(left, right, (((1,), (1,)), ((), ())), preferred_element_type=jnp.float32)


def dot_nn(left, right):
    return jnp.dot(left, right, preferred_element_type=jnp.float32)


def head_lanes(width):
    lane = lax.broadcasted_iota(jnp.int32, (1, width), 1)
    return (lane < HEAD_DIM, lane >= HEAD_DIM)


def greet(peers):
    barrier = pltpu.get_barrier_semaphore()
    for peer in peers:
        pl.semaphore_signal(barrier, inc=1, device_id=peer, device_id_type=MESH)
    pl.semaphore_wait(barrier, len(peers))


def neighbours():
    z, y, core = place_of()
    return [
        {"rows": row_of(z + 1, y, core)},
        {"rows": row_of(z + 2, y, core)},
        {"rows": row_of(z + 3, y, core)},
        {"rows": row_of(z, 1 - y, core)},
        {"rows": row_of(z, y, 1 - core)},
        {"blk": 1 - lax.axis_index("blk")},
    ]


def write_mask(starts_ref, mask_ref, part=0, parts=1):
    blocks, step, length = mask_ref.shape

    def rows(i, carry):
        key_at = lax.broadcasted_iota(jnp.int32, (step, length), 0) + i * step
        query_at = lax.broadcasted_iota(jnp.int32, (step, length), 1)
        key_seg = jnp.zeros((step, length), jnp.int32)
        query_seg = jnp.zeros((step, length), jnp.int32)
        for cell in range(starts_ref.shape[1]):
            start = starts_ref[0, cell]
            key_seg += (key_at >= start).astype(jnp.int32)
            query_seg += (query_at >= start).astype(jnp.int32)
        mask_ref[i] = jnp.where(key_seg == query_seg, 0.0, masked_score).astype(mask_ref.dtype)
        return carry

    lax.fori_loop(blocks * part // parts, blocks * (part + 1) // parts, rows, 0)


def forward_kernel(
    hidden, cot, starts, gain1, shift1, gain2, shift2, bias_in, q_in, o_in, u_in, d_in,
    q_all, o_all, u_all, d_all, dy_all, normed_t_out, packed_out, lse_out, att_t_out, resid_out,
    second_t_out, act_out, act_t_out, slope_out,
    hid_other, normed, wq, wo, wu, packed, mask, att_part, att_own, resid, second,
    act, act_t, slope, normed_t, att_t, second_t, lse, u_wide, q_own, o_own, u_own, d_own, cot_own, bias,
    local_sem, send_sem, recv_sem, x_send, x_recv,
):
    bf16 = jnp.bfloat16
    z, y, core = place_of()
    me = row_of(z, y, core)
    piece = lax.axis_index("blk")
    other = 1 - piece
    own_rows, width = hidden.shape
    length = packed.shape[0]
    rows = o_own.shape[0]
    early = rows * 3 // 5
    d_half = lambda half: pl.ds(half * rows, rows)
    own = (
        q_own.at[pl.ds(0, early)], q_own.at[pl.ds(early, rows - early)], o_own, u_own,
        d_own.at[d_half(0)], d_own.at[d_half(1)],
    )
    last = len(own) - 1

    def slot_of(w, at_z, at_y, at_core):
        slot = row_of(at_z, at_y, at_core)
        if w < 2:
            return q_all.at[slot, pl.ds(w * early, own[w].shape[0])]
        if w < 4:
            return (o_all, u_all)[w - 2].at[slot]
        return d_all.at[slot, d_half(w - 4)]

    x_peer = {"blk": other}
    peers = neighbours()
    pairs = packed.shape[1] // (3 * PAIR)
    first_gain, first_shift, second_gain, second_shift = (
        ref[...].reshape(1, width) for ref in (gain1, shift1, gain2, shift2)
    )

    def local(src, dst, index):
        return pltpu.make_async_copy(src, dst, local_sem.at[index])

    near = z + 1 - 2 * lax.rem(z, 2)
    far = lax.rem(z + 2, ROWS_Z)
    spread = (z, far, near, ROWS_Z - 1 - z)

    def send(w, at_z, v, place, peer, first=False):
        block = slot_of(w, at_z, y if v == 0 else 1 - y, core)
        index = w * 18 + place
        return pltpu.make_async_remote_copy(
            src_ref=own[w] if first else block, dst_ref=block, send_sem=send_sem.at[index],
            recv_sem=recv_sem.at[index], device_id=peer, device_id_type=MESH,
        )

    def along(w, k, v):
        peer = {"rows": row_of(far if k == 0 else near, y, core)}
        return send(w, far if k == 2 else z, v, 2 * k + v, peer, k < 2 and v == 0)

    def to_y(w, at_z, first=False):
        return send(w, at_z, 0, 6 + at_z, peers[3], first)

    def to_core(w, at_z, v, first=False):
        return send(w, at_z, v, 10 + 2 * at_z + v, peers[4], first)

    def pass_on(w, v):
        inner = (z == 1) | (z == 2)

        @pl.when(inner)
        def _():
            along(w, 0, v).start()

        along(w, 1, v).start()

        @pl.when(jnp.logical_not(inner))
        def _():
            along(w, 0, v).start()

    def relay_z(w, k, v):
        along(w, k, v).wait_recv()
        if k == 0:
            along(w, 2, v).start()
        at_z = spread[k + 1]
        if w < last:
            to_y(w, at_z).start()
        to_core(w, at_z, v).start()

    def relay_y(w, k):
        to_y(w, spread[k]).wait_recv()
        to_core(w, spread[k], 1).start()
        if w == last:
            pass_on(w, 1)

    def all_here(ws):
        for w in ws:
            for at_z in range(ROWS_Z):
                for v in range(2):
                    to_core(w, at_z, v).wait_recv()

    def all_here_load(ws, source, target, first):
        for i, at_z in enumerate(spread):
            for v in range(2):
                for w in ws:
                    to_core(w, at_z, v).wait_recv()
                chip = pl.ds(row_of(at_z, y if v == 0 else 1 - y, 0), 2)
                local(source.at[chip], target.at[chip], first + 2 * i + v).start()

    def loaded(source, target, first):
        for i in range(2 * ROWS_Z):
            chip = pl.ds(0, 2)
            local(source.at[chip], target.at[chip], first + i).wait()

    def all_gone(w):
        for v in range(1 if w < last else 2):
            for k in range(3):
                along(w, k, v).wait_send()
        for at_z in range(ROWS_Z) if w < last else (z,):
            to_y(w, at_z).wait_send()
        for at_z in range(ROWS_Z):
            for v in range(2):
                to_core(w, at_z, v).wait_send()

    def to_x(src, dst, index):
        return pltpu.make_async_remote_copy(
            src_ref=src, dst_ref=dst, send_sem=x_send.at[index], recv_sem=x_recv.at[index],
            device_id=x_peer, device_id_type=MESH,
        )

    third = q_in.shape[1] // 3
    share = third // 2
    q_picks = []
    for part in range(3):
        picked = q_in.at[:, pl.ds(pl.multiple_of(part * third + piece * share, 128), share)]
        q_picks.append(local(picked, q_own.at[:, pl.ds(part * share, share)], 17 + part))
        q_picks[-1].start()
    d_mine = d_in.at[pl.ds(piece * 2 * rows, 2 * rows)]
    local(o_in, o_own, 1).start()
    local(u_in, u_wide, 2).start()
    local(d_mine, d_own, 3).start()
    local(cot, cot_own, 4).start()
    greet(peers)
    for copy in q_picks:
        copy.wait()
    hidden_x = to_x(hidden, hid_other, 0)
    cot_x = to_x(cot, dy_all.at[piece], 1)
    local(o_in, o_own, 1).wait()
    local(d_mine, d_own, 3).wait()
    local(u_in, u_wide, 2).wait()
    half_rows = lambda half: pl.ds(pl.multiple_of(half * own_rows, 128), own_rows)

    def first_copies():
        local(q_own, q_all.at[me], 0).start()
        local(o_own, o_all.at[me], 1).start()
        local(d_own, d_all.at[me], 3).start()
        local(cot, cot_own, 4).wait()
        local(cot_own, dy_all.at[piece], 4).start()

    units_each = 2 * rows
    group = 8 * units_each

    def mine(block):
        wide = block.astype(jnp.float32)
        halves = []
        for half in range(2):
            at = [slice((2 * j + half) * units_each, (2 * j + half + 1) * units_each) for j in range(4)]
            halves.append(jnp.concatenate([wide[:, cols] for cols in at], axis=1))
        return jnp.where(piece == 0, halves[0], halves[1])

    def pick_units(g):
        cols = slice(g * group // 2, (g + 1) * group // 2)
        u_own[:, cols] = mine(u_wide[:, g * group : (g + 1) * group]).astype(bf16)
        bias[:, cols] = mine(bias_in[g * group : (g + 1) * group].reshape(1, group))
        if g == u_own.shape[1] * 2 // group - 1:
            local(u_own, u_all.at[me], 2).start()

    def norm_rows(source, half, part):
        step = 64
        steps = own_rows // step

        def body(i, carry):
            value = source[aligned(i, step), :].astype(jnp.float32)
            low = layer_norm(value, first_gain, first_shift).astype(bf16)
            normed[pl.ds(pl.multiple_of(half * own_rows + i * step, step), step), :] = low
            return carry

        lax.fori_loop(steps * part // 2, steps * (part + 1) // 2, body, 0)

    def q_here():
        local(q_own, q_all.at[me], 0).wait()
        all_here_load((0, 1), q_all, wq, 20)

    column = lax.broadcasted_iota(jnp.int32, (1, 3 * PAIR), 1)

    def project(begin, end):
        def body(i, carry):
            cols = aligned(i, 3 * PAIR)
            weight = wq[:, :, cols].reshape(width, 3 * PAIR)
            value = dot_nn(normed[...], weight).astype(bf16)
            factor = jnp.where(i * 3 * PAIR + column < share, HEAD_DIM ** (-0.5), 1.0).astype(bf16)
            packed[:, cols] = value * factor
            return carry

        lax.fori_loop(begin, end, body, 0)
        if end == pairs:
            local(packed, packed_out, 9).start()

    first_lanes = head_lanes(PAIR)

    def att_cols(half, p):
        return pl.ds(pl.multiple_of(half * pairs * PAIR + p * PAIR, PAIR), PAIR)

    def attend(p, half):
        at_q, at_k, at_v = (slice(t * share + PAIR * p, t * share + PAIR * (p + 1)) for t in range(3))
        value_t = packed[:, at_v].T
        at = half_rows(half)
        queries = packed[at, at_q]
        keys = packed[:, at_k]
        halves = []
        for h in range(2):
            one = jnp.where(first_lanes[h], queries, jnp.zeros_like(queries))
            scores = dot_nt(keys, one) + mask[:, :, at].reshape(length, own_rows)
            top = jnp.max(scores, axis=0, keepdims=True)
            weights = jnp.exp(scores - top)
            total = jnp.sum(weights, axis=0, keepdims=True)
            lse[2 * p + h : 2 * p + h + 1, at] = top + jnp.log(total)
            summed = dot_nn(value_t[h * HEAD_DIM : (h + 1) * HEAD_DIM], weights.astype(bf16))
            halves.append(summed / total)
        return jnp.concatenate(halves, axis=0).T.astype(bf16)

    def attend_other(p):
        att_part[:, p * PAIR : (p + 1) * PAIR] = attend(p, other)

    def attend_own(p):
        att_own[:, att_cols(piece, p)] = attend(p, piece)
        if p == pairs - 1:
            local(lse, lse_out, 10).start()

    att_x = [
        to_x(att_part.at[:, pl.ds(p * PAIR, PAIR)], att_own.at[:, att_cols(piece, p)], 2 + p) for p in range(pairs)
    ]

    def o_here():
        local(o_own, o_all.at[me], 1).wait()
        all_here_load((2,), o_all, wo, 28)

    def att_here():
        for copy in att_x:
            copy.wait_recv()
        loaded(o_all, wo, 28)

    part_rows = own_rows // 2
    second_x = [
        to_x(second.at[piece, pl.ds(i * part_rows, part_rows)], second.at[piece, pl.ds(i * part_rows, part_rows)], 2 + pairs + i)
        for i in range(2)
    ]

    def merge(part):
        at = slice(part * part_rows, (part + 1) * part_rows)

        def body(i, carry):
            cols = aligned(i, 256)
            weight = wo[:, :, cols].reshape(width, 256)
            resid[at, cols] = hidden[at, cols].astype(jnp.float32) + dot_nn(att_own[at, :], weight)
            return carry

        lax.fori_loop(0, width // 256, body, 0)

        def second_rows(i, carry):
            rows = aligned(i, 64)
            second[piece, rows, :] = layer_norm(resid[rows, :], second_gain, second_shift).astype(bf16)
            return carry

        lax.fori_loop(part * part_rows // 64, (part + 1) * part_rows // 64, second_rows, 0)
        if part == 1:
            local(resid, resid_out, 12).start()

    def flip_normed():
        def body(i, carry):
            normed_t[aligned(i, 128), :] = normed[:, aligned(i, 128)].T
            return carry

        lax.fori_loop(0, width // 128, body, 0)
        local(normed_t, normed_t_out, 8).start()

    def flip_second(half):
        def body(i, carry):
            second_t[aligned(i, 128), half_rows(half)] = second[half, :, aligned(i, 128)].T
            return carry

        lax.fori_loop(0, width // 128, body, 0)

    def flip_att():
        def body(i, carry):
            att_t[aligned(i, 128), :] = att_own[:, aligned(i, 128)].T
            return carry

        lax.fori_loop(0, width // 128, body, 0)
        local(att_t, att_t_out, 11).start()
        flip_second(piece)

    def u_here():
        local(u_own, u_all.at[me], 2).wait()
        all_here_load((3,), u_all, wu, 36)

    unit = 256
    fifth = act.shape[1] // unit // 5

    def expand(half, begin):
        at = half_rows(half)

        def body(i, carry):
            cols = aligned(i, unit)
            weight = wu[:, :, cols].reshape(width, unit)
            up = dot_nn(second[half], weight) + bias[:, cols]
            cdf = 0.5 * (1.0 + lax.erf(up * (0.5 ** 0.5)))
            pdf = jnp.exp(up * up * -0.5) * ((2.0 * math.pi) ** -0.5)
            value = (up * cdf).astype(bf16)
            act[at, cols] = value
            act_t[cols, at] = value.T
            slope[at, cols] = (cdf + up * pdf).astype(bf16)
            return carry

        lax.fori_loop(begin * fifth, (begin + 1) * fifth, body, 0)
        if begin == 4:
            for copy in halves_out(half):
                copy.start()

    def halves_out(half):
        base = 44 if half is piece else 47
        at = half_rows(half)
        return (
            local(act.at[at], act_out.at[at], base),
            local(act_t.at[:, at], act_t_out.at[:, at], base + 1),
            local(slope.at[at], slope_out.at[at], base + 2),
        )

    def second_here():
        for copy in second_x:
            copy.wait_recv()

    def flip_last():
        flip_second(other)
        local(second_t, second_t_out, 13).start()

    def outputs():
        local(cot_own, dy_all.at[piece], 4).wait()
        local(d_own, d_all.at[me], 3).wait()
        local(normed_t, normed_t_out, 8).wait()
        local(packed, packed_out, 9).wait()
        local(lse, lse_out, 10).wait()
        local(att_t, att_t_out, 11).wait()
        local(resid, resid_out, 12).wait()
        local(second_t, second_t_out, 13).wait()
        for half in (piece, other):
            for copy in halves_out(half):
                copy.wait()

    act_now = functools.partial
    steps = [hidden_x.start, cot_x.start]
    steps += [act_now(pick_units, g) for g in range(4)]
    steps += [act_now(norm_rows, hidden, piece, part) for part in range(2)]
    steps += [act_now(write_mask, starts, mask, part, 2) for part in range(2)]
    steps += [hidden_x.wait_recv]
    steps += [act_now(norm_rows, hid_other, other, part) for part in range(2)]
    steps += [q_here, act_now(loaded, q_all, wq, 20), act_now(project, 0, 2), act_now(project, 2, pairs)]
    for p in range(pairs):
        steps += [act_now(attend_other, p), att_x[p].start]
    steps += [act_now(attend_own, p) for p in range(pairs - 1)]
    steps += [o_here, act_now(attend_own, pairs - 1), att_here]
    steps += [act_now(merge, 0), second_x[0].start, act_now(merge, 1), second_x[1].start]
    steps += [flip_normed, flip_att, u_here, act_now(loaded, u_all, wu, 36)]
    steps += [act_now(expand, piece, i) for i in range(5)]
    steps += [second_here, flip_last]
    steps += [act_now(expand, other, i) for i in range(5)]
    steps += [outputs, act_now(all_here, (4, 5))]
    moves = (
        lambda w: pass_on(w, 0),
        lambda w: to_y(w, z, True).start(),
        lambda w: to_core(w, z, 0, True).start(),
        relay_z,
        relay_y,
    )
    for i, step in enumerate(steps):
        for kind, *where in FORWARD_MOVES[i]:
            moves[kind](*where)
        step()
        if i == 1:
            first_copies()
    cot_x.wait_recv()
    for w in range(len(own)):
        all_gone(w)
    for copy in [hidden_x, cot_x] + second_x + att_x:
        copy.wait_send()


def forward(hidden, cot, starts, gain1, shift1, gain2, shift2, bias, qkv, out, up, down):
    own_rows, width = hidden.shape
    length = 2 * own_rows
    cols = qkv.shape[1] // 2
    units = up.shape[1] // 2
    rows = up.shape[0]
    bf16, f32 = jnp.bfloat16, jnp.float32
    shards = lax.axis_size("rows")
    head_rows = 16
    outs = [
        ((shards, rows, cols), bf16),
        ((shards, rows, width), bf16),
        ((shards, rows, units), bf16),
        ((shards, down.shape[0] // 2, width), bf16),
        ((2, own_rows, width), bf16),
        ((width, length), bf16),
        ((length, cols), bf16),
        ((head_rows, length), f32),
        ((width, own_rows), bf16),
        ((own_rows, width), f32),
        ((width, length), bf16),
        ((length, units), bf16),
        ((units, length), bf16),
        ((length, units), bf16),
    ]
    scratch = [
        ((own_rows, width), bf16),
        ((length, width), bf16),
        ((shards, rows, cols), bf16),
        ((shards, rows, width), bf16),
        ((shards, rows, units), bf16),
        ((length, cols), bf16),
        ((length // 48, 48, length), f32),
        ((own_rows, cols // 3), bf16),
        ((own_rows, width), bf16),
        ((own_rows, width), f32),
        ((2, own_rows, width), bf16),
        ((length, units), bf16),
        ((units, length), bf16),
        ((length, units), bf16),
        ((width, length), bf16),
        ((width, own_rows), bf16),
        ((width, length), bf16),
        ((head_rows, length), f32),
        ((rows, 2 * units), bf16),
        ((rows, cols), bf16),
        ((rows, width), bf16),
        ((rows, units), bf16),
        ((2 * rows, width), bf16),
        ((own_rows, width), bf16),
        ((1, units), f32),
    ]
    vmem = pl.BlockSpec(memory_space=pltpu.VMEM)
    anywhere = pl.BlockSpec(memory_space=pl.ANY)
    smem = pl.BlockSpec(memory_space=pltpu.SMEM)
    dma = pltpu.SemaphoreType.DMA
    x_copies = 4 + cols // (3 * PAIR)
    return pl.pallas_call(
        forward_kernel,
        out_shape=[jax.ShapeDtypeStruct(shape, kind) for shape, kind in outs],
        in_specs=[vmem, anywhere, smem] + [vmem] * 5 + [anywhere] * 4,
        out_specs=[anywhere] * len(outs),
        scratch_shapes=[pltpu.VMEM(shape, kind) for shape, kind in scratch]
        + [dma((50,)), dma((108,)), dma((108,)), dma((x_copies,)), dma((x_copies,))],
        compiler_params=pltpu.CompilerParams(
            collective_id=1, has_side_effects=True, vmem_limit_bytes=60 * 1024 * 1024
        ),
        name="forward",
    )(hidden, cot, starts, gain1, shift1, gain2, shift2, bias, qkv, out, up, down)


UNIT = 640
SLOTS = 2


def norm_back(values, gain, grad):
    centred = values - jnp.mean(values, axis=-1, keepdims=True)
    scale = lax.rsqrt(jnp.mean(centred * centred, axis=-1, keepdims=True) + 1e-05)
    unit = centred * scale
    scaled = grad * gain
    mean_one = jnp.mean(scaled, axis=-1, keepdims=True)
    mean_two = jnp.mean(scaled * unit, axis=-1, keepdims=True)
    d_values = scale * (scaled - mean_one - unit * mean_two)
    d_gain = jnp.sum(grad * unit, axis=0, keepdims=True)
    d_shift = jnp.sum(grad, axis=0, keepdims=True)
    return d_values, d_gain, d_shift


def backward_kernel(
    starts, gain1, gain2, hidden, dy_all, q_all, o_all, u_all, d_all, normed_t, packed, lse_in, att_t,
    resid, second_t, act, act_t, slope,
    output, grad_hidden, units_out, pairs_out, small_out,
    lhs, half_act, wide, wd, wu, dy, first, second, d_att, x_in0, x_in1, x_out0, x_out1,
    down_own, parts, core_in, core_in_q, y_in, y_in_q, z_in, z_in_q, lse, acc_k, acc_v,
    bias_sum, small, small_core, small_y, small_z,
    local_sem, a_send, a_recv, b_send, b_recv, c_send, c_recv, g_send, g_recv, x_send, x_recv,
    s_send, s_recv, keep_sem,
):
    bf16, f32 = jnp.bfloat16, jnp.float32
    z, y, core = place_of()
    piece = lax.axis_index("blk")
    other = 1 - piece
    own_rows, width = first.shape
    length = 2 * own_rows
    branch = half_act.at[:, pl.ds(0, width)]
    units = wide.shape[1]
    cols = 3 * d_att.shape[1]
    pairs = d_att.shape[1] // PAIR
    peers = neighbours()
    wide_chunks = core_in.shape[0]
    first_gain, second_gain = gain1[...].reshape(1, width), gain2[...].reshape(1, width)
    half_rows = lambda half: pl.ds(pl.multiple_of(half * own_rows, 128), own_rows)

    def remote(src, dst, sends, recvs, index, peer):
        return pltpu.make_async_remote_copy(
            src_ref=src, dst_ref=dst, send_sem=sends.at[index], recv_sem=recvs.at[index],
            device_id=peer, device_id_type=MESH,
        )

    loads = {
        "act_t": (act_t, lhs, 0),
        "dy": (dy_all, dy, 1),
        "down": (d_all, wd, 2),
        "slope": (slope, wide, 3),
        "up": (u_all, wu, 4),
        "act_other": (act.at[half_rows(other)], half_act, 5),
        "act_own": (act.at[half_rows(piece)], half_act, 6),
        "resid": (resid, second, 7),
        "lse": (lse_in, lse, 8),
        "second_t": (second_t, lhs.at[:, pl.ds(0, lhs.shape[1] // 2)], 9),
        "att_t": (att_t, lhs.at[:, pl.ds(lhs.shape[1] // 2, lhs.shape[1] // 2), pl.ds(0, own_rows)], 10),
        "out": (o_all, wd.at[pl.ds(0, width)], 11),
        "normed_t": (normed_t, wd.at[pl.ds(width, width), pl.ds(0, length)], 12),
        "qkv": (q_all, wu.at[:, pl.ds(0, cols)], 13),
        "packed": (packed, wide.at[:, pl.ds(0, cols)], 14),
        "hidden": (hidden, branch, 15),
        "output": (second, output, 16),
        "grad_hidden": (first, grad_hidden, 17),
    }

    def local(name):
        src, dst, index = loads[name]
        return pltpu.make_async_copy(src, dst, local_sem.at[index])

    def buffers(i):
        if i < wide_chunks:
            return core_in.at[i], y_in.at[i], z_in.at[i], z_in.at[i, 0], units_out.at[:, i], UNIT
        i -= wide_chunks
        return core_in_q.at[i], y_in_q.at[i], z_in_q.at[i], z_in_q.at[i, 0], pairs_out.at[:, i], 3 * PAIR

    def copy_a(i):
        into, _, _, _, _, n = buffers(i)
        return remote(parts.at[i % SLOTS, 1 - core, :, :, :, pl.ds(0, n)], into, a_send, a_recv, i, peers[4])

    def copy_b(i):
        sums, into, _, _, _, _ = buffers(i)
        return remote(sums.at[1 - y], into, b_send, b_recv, i, peers[3])

    def copy_c(i, k):
        _, sums, into, _, _, _ = buffers(i)
        return remote(sums.at[lax.rem(z + k, ROWS_Z)], into.at[k - 1], c_send, c_recv, 3 * i + k - 1, peers[k - 1])

    def copy_g(i):
        _, _, _, share, out, _ = buffers(i)
        return remote(share, out.at[piece], g_send, g_recv, i, peers[5])

    def keep_g(i):
        _, _, _, share, out, _ = buffers(i)
        return pltpu.make_async_copy(share, out.at[piece], keep_sem.at[i])

    def finish_a(i):
        sums, _, _, _, _, n = buffers(i)
        copy_a(i).wait_recv()
        slot = i % SLOTS
        sums[1 - y] += parts[slot, core, 1 - y, :, :, :n]
        copy_b(i).start()
        sums[y] += parts[slot, core, y, :, :, :n]
        copy_a(i).wait_send()

    def finish_b(i):
        mine, sums, _, _, _, _ = buffers(i)
        copy_b(i).wait_recv()
        sums[...] += mine[y]
        for k in (1, 3, 2):
            copy_c(i, k).start()

    def finish_c(i):
        _, sums, terms, share, _, _ = buffers(i)
        for k in (1, 3, 2):
            copy_c(i, k).wait_recv()
        total = sums[z].astype(f32)
        for k in range(3):
            total += terms[k].astype(f32)
        share[...] = total.astype(bf16)
        copy_g(i).start()
        keep_g(i).start()

    def grad_chunk(i, left, right):
        slot = i % SLOTS

        def one_z(to_z, carry):
            value = dot_nn(left(to_z), right()).astype(bf16)
            n = value.shape[1]
            rows = value.shape[0] // 4
            for block in range(4):
                to_y, to_core = divmod(block, 2)
                parts[slot, to_core, to_y, to_z, :, :n] = value[block * rows : (block + 1) * rows]
            return carry

        lax.fori_loop(0, ROWS_Z, one_z, 0)
        copy_a(i).start()

    for name in ("act_t", "dy", "down", "slope", "act_other", "up", "resid", "lse"):
        local(name).start()
    greet(peers)
    local("act_t").wait()
    local("dy").wait()
    block_rows = parts.shape[4]

    def grad_down(i):
        h, column = divmod(i, 2)

        def left(to_z):
            rows = lhs[pl.ds(to_z * 4, 4), h * block_rows : (h + 1) * block_rows, :]
            return rows.reshape(4 * block_rows, length)

        grad_chunk(i, left, lambda: dy[:, :, column * UNIT : (column + 1) * UNIT].reshape(length, UNIT))

    grad_down(0)
    grad_down(1)
    finish_a(0)
    grad_down(2)
    finish_a(1)
    grad_down(3)
    local("second_t").start()
    local("att_t").start()
    local("down").wait()
    local("slope").wait()

    tile = 256

    def d_units(i, carry):
        at = aligned(i, tile)
        sums = jnp.zeros((1, tile), f32)
        for half in range(2):
            rows = slice(half * own_rows, (half + 1) * own_rows)
            value = dot_nt(dy[half], wd[at, :]) * wide[rows, at].astype(f32)
            low = value.astype(bf16)
            wide[rows, at] = low
            sums += jnp.sum(low.astype(f32), axis=0, keepdims=True)
        bias_sum[:, at] = sums
        return carry

    lax.fori_loop(0, 4, d_units, 0)
    finish_a(2)
    finish_a(3)
    lax.fori_loop(4, units // tile, d_units, 0)
    local("up").wait()

    def d_second(half, write):
        def body(i, carry):
            at = aligned(i, tile)
            write(at, dot_nt(wide[half_rows(half), :], wu[at, :]))
            return carry

        lax.fori_loop(0, width // tile, body, 0)

    def write_out0(at, value):
        x_out0[:, at] = value.astype(bf16)

    def write_first(at, value):
        first[:, at] = value

    d_second(other, write_out0)
    second_x = remote(x_out0, x_in0, x_send, x_recv, 0, peers[5])
    second_x.start()
    d_second(piece, write_first)
    local("qkv").start()
    finish_b(0)
    local("act_other").wait()

    def down_part(target):
        def body(i, carry):
            at = aligned(i, tile)
            target[:, at] = dot_nn(half_act[...], wd[:, at]).astype(bf16)
            return carry

        lax.fori_loop(0, width // tile, body, 0)

    down_part(x_out1)
    local("act_own").start()
    local("second_t").wait()

    def grad_up(i):
        def left(to_z):
            rows = lhs[pl.ds(to_z * 4, 4), :block_rows, :]
            return rows.reshape(4 * block_rows, length)

        grad_chunk(4 + i, left, lambda: wide[:, i * UNIT : (i + 1) * UNIT])

    grad_up(0)
    grad_up(1)
    local("act_own").wait()
    finish_a(4)
    finish_b(1)
    down_part(down_own)
    local("out").start()
    local("normed_t").start()
    finish_a(5)
    grad_up(2)
    grad_up(3)
    local("packed").start()
    mask = lhs.at[:, pl.ds(0, length // lhs.shape[0]), :]
    write_mask(starts, mask)
    finish_a(6)
    finish_a(7)
    finish_c(0)
    finish_b(2)
    local("resid").wait()
    second_x.wait_recv()
    step = 64

    def back_two(i, carry):
        rows = aligned(i, step)
        grad = first[rows, :] + x_in0[rows, :].astype(f32)
        d_values, d_gain, d_shift = norm_back(second[rows, :], second_gain, grad)
        total = dy[piece, rows, :].astype(f32) + d_values
        first[rows, :] = total
        branch[rows, :] = total.astype(bf16)
        return carry[0] + d_gain, carry[1] + d_shift

    zeros = jnp.zeros((1, width), f32)
    gain_two, shift_two = lax.fori_loop(0, own_rows // step, back_two, (zeros, zeros))
    small[2:3, :] = gain_two
    small[3:4, :] = shift_two
    local("out").wait()
    second_x.wait_send()
    d_width = d_att.shape[1]

    def d_attended(half):
        rows = pl.ds(pl.multiple_of(half * d_width, 128), d_width)
        return dot_nt(branch[...], wd[rows, :]).astype(bf16)

    x_out0[:, :d_width] = d_attended(other)
    att_x = remote(x_out0.at[:, pl.ds(0, d_width)], d_att.at[half_rows(piece)], x_send, x_recv, 1, peers[5])
    att_x.start()
    down_x = remote(x_out1, x_in1, x_send, x_recv, 2, peers[5])
    down_x.start()
    d_att[half_rows(piece), :] = d_attended(piece)
    local("att_t").wait()

    def grad_out(i):
        def left(to_z):
            rows = lhs[pl.ds(to_z * 4, 4), block_rows : 2 * block_rows, :own_rows]
            return rows.reshape(4 * block_rows, own_rows)

        grad_chunk(8 + i, left, lambda: branch[:, i * UNIT : (i + 1) * UNIT])

    grad_out(0)
    grad_out(1)
    finish_c(1)
    finish_b(3)
    finish_a(8)
    finish_a(9)
    local("hidden").start()
    local("lse").wait()
    local("packed").wait()
    local("normed_t").wait()
    att_x.wait_recv()
    first_lanes = head_lanes(PAIR)

    def pair_cols(p):
        return tuple(slice(t * d_width + PAIR * p, t * d_width + PAIR * (p + 1)) for t in range(3))

    def attend_back(p):
        at_q, at_k, at_v = pair_cols(p)
        keys_t = wide[:, at_k].T
        acc_k[...] = jnp.zeros_like(acc_k)
        acc_v[...] = jnp.zeros_like(acc_v)
        chunk = 256

        def body(i, carry):
            rows = aligned(i, chunk)
            keys = wide[:, at_k]
            values = wide[:, at_v]
            queries = wide[rows, at_q]
            grads = d_att[rows, p * PAIR : (p + 1) * PAIR]
            blocked = mask[:, :, rows].reshape(length, chunk).astype(f32)
            parts_q = []
            for h in range(2):
                one_q = jnp.where(first_lanes[h], queries, jnp.zeros_like(queries))
                one_g = jnp.where(first_lanes[h], grads, jnp.zeros_like(grads))
                scores = dot_nt(keys, one_q) + (blocked - lse[2 * p + h : 2 * p + h + 1, rows])
                probs = jnp.exp(scores)
                d_probs = dot_nt(values, one_g)
                dots = jnp.sum(probs * d_probs, axis=0, keepdims=True)
                d_scores = (probs * (d_probs - dots)).astype(bf16)
                acc_v[...] += dot_nn(probs.astype(bf16), one_g)
                acc_k[...] += dot_nn(d_scores, one_q)
                parts_q.append(dot_nn(keys_t[h * HEAD_DIM : (h + 1) * HEAD_DIM], d_scores))
            d_queries = jnp.concatenate(parts_q, axis=0).T * HEAD_DIM ** (-0.5)
            wide[rows, at_q] = d_queries.astype(bf16)
            return carry

        lax.fori_loop(0, length // chunk, body, 0)
        wide[:, at_k] = acc_k[...].astype(bf16)
        wide[:, at_v] = acc_v[...].astype(bf16)

    def grad_pair(p):
        def left(to_z):
            return wd[pl.ds(pl.multiple_of(width + to_z * 4 * block_rows, 64), 4 * block_rows), :length]

        grad_chunk(10 + p, left, lambda: jnp.concatenate([wide[:, at] for at in pair_cols(p)], axis=1))

    def write_output():
        down_x.wait_recv()

        def body(i, carry):
            rows = aligned(i, step)
            second[rows, :] += down_own[rows, :].astype(f32) + x_in1[rows, :].astype(f32)
            return carry

        lax.fori_loop(0, own_rows // step, body, 0)
        local("output").start()

    ticks = {
        0: lambda: (finish_c(2), finish_b(4)),
        1: lambda: (finish_a(10), finish_c(3), finish_b(5)),
        2: lambda: (finish_a(11), finish_c(4), finish_b(6)),
        3: lambda: (finish_a(12), write_output(), finish_c(5), finish_b(7)),
        4: lambda: (finish_a(13), finish_c(6)),
    }
    for p in range(pairs):
        attend_back(p)
        grad_pair(p)
        ticks[p]()
    finish_a(14)
    local("qkv").wait()
    local("output").wait()
    att_x.wait_send()

    def d_normed(half, write):
        def body(i, carry):
            at = aligned(i, tile)
            write(at, dot_nt(wide[half_rows(half), :cols], wu[at, :cols]))
            return carry

        lax.fori_loop(0, width // tile, body, 0)

    def write_second(at, value):
        second[:, at] = value

    d_normed(other, write_out0)
    normed_x = remote(x_out0, x_in0, x_send, x_recv, 3, peers[5])
    normed_x.start()
    finish_b(8)
    d_normed(piece, write_second)
    finish_c(7)
    finish_b(9)
    local("hidden").wait()
    finish_c(8)
    finish_b(10)
    normed_x.wait_recv()

    def back_one(i, carry):
        rows = aligned(i, step)
        grad = second[rows, :] + x_in0[rows, :].astype(f32)
        d_values, d_gain, d_shift = norm_back(branch[rows, :].astype(f32), first_gain, grad)
        first[rows, :] += d_values
        return carry[0] + d_gain, carry[1] + d_shift

    gain_one, shift_one = lax.fori_loop(0, own_rows // step, back_one, (zeros, zeros))
    local("grad_hidden").start()
    small[0:1, :] = gain_one
    small[1:2, :] = shift_one
    small[4:5, :] = bias_sum[:, :width]
    small[5:6, :] = bias_sum[:, width:]
    small[6:8, :] = jnp.zeros((2, width), f32)
    core_x = remote(small, small_core, s_send, s_recv, 0, peers[4])
    core_x.start()
    finish_b(11)
    core_x.wait()
    small[...] += small_core[...]
    y_x = remote(small, small_y, s_send, s_recv, 1, peers[3])
    y_x.start()
    finish_c(9)
    finish_b(12)
    finish_c(10)
    finish_b(13)
    finish_c(11)
    finish_b(14)
    y_x.wait()
    small_z[z] = small[...] + small_y[...]
    z_x = [remote(small_z.at[z], small_z.at[z], s_send, s_recv, 1 + k, peers[k - 1]) for k in (1, 2, 3)]
    for copy in z_x:
        copy.start()
    finish_c(12)
    finish_c(13)
    for copy in z_x:
        copy.wait()
    small[...] = ((small_z[0] + small_z[1]) + small_z[2]) + small_z[3]
    share_x = remote(small, small_out.at[piece], s_send, s_recv, 5, peers[5])
    share_x.start()
    share_keep = pltpu.make_async_copy(small, small_out.at[piece], keep_sem.at[15])
    share_keep.start()
    finish_c(14)
    for i in range(15):
        copy_b(i).wait_send()
        for k in (1, 2, 3):
            copy_c(i, k).wait_send()
        copy_g(i).wait()
        keep_g(i).wait()
    share_x.wait()
    share_keep.wait()
    down_x.wait_send()
    normed_x.wait_send()
    local("grad_hidden").wait()


def backward(starts, gain1, gain2, hidden, dy_all, q_all, o_all, u_all, d_all, *kept):
    bf16, f32 = jnp.bfloat16, jnp.float32
    _, own_rows, width = dy_all.shape
    length = 2 * own_rows
    cols, units = q_all.shape[1], u_all.shape[1]
    rows = width // 16
    wide_units, pairs = 10, cols // (3 * PAIR)
    pair_cols = 3 * PAIR
    outs = [
        ((own_rows, width), f32),
        ((own_rows, width), f32),
        ((2, wide_units, rows, UNIT), bf16),
        ((2, pairs, rows, pair_cols), bf16),
        ((2, 8, width), f32),
    ]
    token = ((own_rows, width), bf16)
    scratch = [
        ((16, 2 * rows, length), bf16),
        ((own_rows, units), bf16),
        ((length, units), bf16),
        ((units, width), bf16),
        ((width, units), bf16),
        ((2, own_rows, width), bf16),
        ((own_rows, width), f32),
        ((own_rows, width), f32),
        ((length, cols // 3), bf16),
        token, token, token, token, token,
        ((SLOTS, 2, 2, ROWS_Z, rows, UNIT), bf16),
        ((wide_units, 2, ROWS_Z, rows, UNIT), bf16),
        ((pairs, 2, ROWS_Z, rows, pair_cols), bf16),
        ((wide_units, ROWS_Z, rows, UNIT), bf16),
        ((pairs, ROWS_Z, rows, pair_cols), bf16),
        ((wide_units, 3, rows, UNIT), bf16),
        ((pairs, 3, rows, pair_cols), bf16),
        ((16, length), f32),
        ((length, PAIR), f32),
        ((length, PAIR), f32),
        ((1, units), f32),
        ((8, width), f32),
        ((8, width), f32),
        ((8, width), f32),
        ((ROWS_Z, 8, width), f32),
    ]
    vmem = pl.BlockSpec(memory_space=pltpu.VMEM)
    anywhere = pl.BlockSpec(memory_space=pl.ANY)
    smem = pl.BlockSpec(memory_space=pltpu.SMEM)
    chunks = wide_units + pairs
    dma = lambda n: pltpu.SemaphoreType.DMA((n,))
    sems = [18] + [chunks] * 4 + [3 * chunks] * 2 + [chunks] * 2 + [4, 4, 6, 6, chunks + 1]
    return pl.pallas_call(
        backward_kernel,
        out_shape=[jax.ShapeDtypeStruct(shape, kind) for shape, kind in outs],
        in_specs=[smem, vmem, vmem] + [anywhere] * (6 + len(kept)),
        out_specs=[anywhere] * len(outs),
        scratch_shapes=[pltpu.VMEM(shape, kind) for shape, kind in scratch] + [dma(n) for n in sems],
        compiler_params=pltpu.CompilerParams(
            collective_id=2, has_side_effects=True, vmem_limit_bytes=60 * 1024 * 1024
        ),
        name="backward",
    )(starts, gain1, gain2, hidden, dy_all, q_all, o_all, u_all, d_all, *kept)


def finish_kernel(
    raw_output, raw_grad, units_lo, units_hi, pairs_in, small,
    output, grad_hidden, qkv, out, up, down, gain1, shift1, gain2, shift2, bias,
):
    f32 = jnp.float32
    step = pl.program_id(0)
    output[0] = raw_output[...]
    grad_hidden[0] = raw_grad[...]
    rows = out.shape[0]
    width = small.shape[2]
    units_in = (units_lo, units_hi)

    def mixed(first, second):
        each = first.shape[1] // 4
        blocks = []
        for j in range(4):
            at = slice(j * each, (j + 1) * each)
            blocks += [first[:, at].astype(f32), second[:, at].astype(f32)]
        return jnp.concatenate(blocks, axis=1)

    for now in range(2):

        @pl.when(step == now)
        def _():
            for i in range(4):
                h, column = divmod(i, 2)
                at = slice(column * UNIT, (column + 1) * UNIT)
                down[h * rows : (h + 1) * rows, at] = units_in[now][0, i].astype(f32)
            for i in range(2):
                chunk = 4 + 2 * now + i
                at = slice(i * 2 * UNIT, (i + 1) * 2 * UNIT)
                up[:, at] = mixed(units_lo[0, chunk], units_hi[0, chunk])
            out[...] = units_lo[0, 8 + now].astype(f32) + units_hi[0, 8 + now].astype(f32)
            pairs = pairs_in.shape[1]
            for block in range(3 * now, 3 * now + 3):
                part, piece = divmod(block, 2)
                for p in range(pairs):
                    at = (block - 3 * now) * pairs * PAIR + p * PAIR
                    chunk = pairs_in[piece, p, :, part * PAIR : (part + 1) * PAIR]
                    qkv[:, at : at + PAIR] = chunk.astype(f32)

    @pl.when(step == 0)
    def _():
        for i, ref in enumerate((gain1, shift1, gain2, shift2)):
            ref[...] = (small[0, i : i + 1, :] + small[1, i : i + 1, :]).reshape(width)
        for g in range(2):
            for j in range(2):
                at = slice(j * UNIT, (j + 1) * UNIT)
                lo, hi = small[0, 4 + g : 5 + g, at], small[1, 4 + g : 5 + g, at]
                begin = (2 * g + j) * 2 * UNIT
                bias[begin : begin + 2 * UNIT] = mixed(lo, hi).reshape(2 * UNIT)


def finish(raw_output, raw_grad, units_in, pairs_in, small):
    f32 = jnp.float32
    own_rows, width = raw_output.shape
    rows = units_in.shape[2]
    shapes = [
        (1, own_rows, width), (1, own_rows, width), (rows, 3 * width), (rows, width), (rows, 8 * UNIT),
        (4 * rows, width), (width,), (width,), (width,), (width,), (8 * UNIT,),
    ]
    token = pl.BlockSpec((own_rows // 2, width), lambda s: (s, 0))
    token_out = pl.BlockSpec((1, own_rows // 2, width), lambda s: (0, s, 0))
    columns = lambda n: pl.BlockSpec((rows, n // 2), lambda s: (0, s))
    fixed = lambda shape: pl.BlockSpec(shape, lambda s: (0,) * len(shape))
    half = lambda i: pl.BlockSpec((1,) + units_in.shape[1:], lambda s: (i, 0, 0, 0))
    return pl.pallas_call(
        finish_kernel,
        grid=(2,),
        out_shape=[jax.ShapeDtypeStruct(shape, f32) for shape in shapes],
        in_specs=[token, token, half(0), half(1), fixed(pairs_in.shape), fixed(small.shape)],
        out_specs=[
            token_out, token_out, columns(3 * width), columns(width), columns(8 * UNIT),
            pl.BlockSpec((2 * rows, width), lambda s: (s, 0)),
        ] + [fixed(shape) for shape in shapes[6:]],
        compiler_params=pltpu.CompilerParams(vmem_limit_bytes=60 * 1024 * 1024),
        name="finish",
    )(raw_output, raw_grad, units_in, units_in, pairs_in, small)


def split_layer(
    hidden, starts, first_gain, first_shift, qkv_weight, out_weight, second_gain, second_shift,
    up_weight, hidden_bias, down_weight, cotangent,
):
    shards = lax.axis_size("rows")
    (
        qkv_all, out_all, up_all, down_all, dy_all, normed_t, packed, lse, att_t, residual, second_t,
        activated, activated_t, slope,
    ) = forward(
        hidden[0], cotangent[0], starts, first_gain, first_shift, second_gain, second_shift, hidden_bias,
        qkv_weight, out_weight, up_weight, down_weight,
    )
    whole = lambda w: w.reshape(-1, w.shape[-1])
    blocks = lambda w: w.reshape(shards, -1, w.shape[-1])
    shares = backward(
        starts, first_gain, second_gain, hidden[0], dy_all, whole(qkv_all), whole(out_all),
        whole(up_all), whole(down_all), normed_t, packed, lse, blocks(att_t), residual,
        blocks(second_t), activated, blocks(activated_t), slope,
    )
    return tuple(finish(*shares))


def splits_evenly(mesh):
    pieces = mesh.shape["blk"]
    return pieces == 2 and mesh.shape["rows"] == 2 * ROWS_Z * ROWS_Y and HEADS % (2 * pieces) == 0


def solution(mesh):
    in_specs = (
        P("rows", "blk", None),
        P("rows", None),
        P(),
        P(),
        P("rows", None),
        P("rows", None),
        P(),
        P(),
        P("rows", None),
        P(),
        P("rows", None),
        P("rows", "blk", None),
    )
    out_specs = (
        P("rows", "blk", None),
        P("rows", "blk", None),
        P("rows", None),
        P("rows", None),
        P("rows", None),
        P("rows", None),
        P(),
        P(),
        P(),
        P(),
        P(),
    )
    layer = split_layer if splits_evenly(mesh) else on_device
    return jax.shard_map(
        layer, mesh=mesh, in_specs=in_specs, out_specs=out_specs, check_vma=False
    )
```

```python
import functools
import math

import jax
import jax.numpy as jnp
from jax import lax
from jax.experimental import pallas as pl
from jax.experimental.pallas import tpu as pltpu
from jax.sharding import PartitionSpec as P

HEADS = 20
HEAD_DIM = 64


masked_score = -1e30
block_limit = 512


def layer_norm(values, gain, shift):
    mean_value = jnp.mean(values, axis=-1, keepdims=True)
    centred = values - mean_value
    variance = jnp.mean(centred * centred, axis=-1, keepdims=True)
    return centred * lax.rsqrt(variance + 1e-05) * gain + shift


def segment_of(starts_row, positions):
    reached = starts_row[None, :] <= positions[:, None]
    return jnp.sum(reached.astype(jnp.int32), axis=1) - 1


def scores_with_mask(queries, key_block, query_seg, key_seg):
    products = jnp.einsum("qhe,khe->hqk", queries, key_block, preferred_element_type=jnp.float32)
    products = products * queries.shape[2] ** (-0.5)
    allowed = (query_seg[:, None] == key_seg[None, :])[None, :, :]
    return (jnp.where(allowed, products, masked_score), allowed)


def attend_rows(running, key_rows, value_rows, queries, query_seg, starts_row):
    piece_rows = key_rows.shape[0]
    step_rows = math.gcd(piece_rows, block_limit)
    head_count = queries.shape[1]
    head_width = queries.shape[2]

    def one_block(block_index, state):
        row_top, denominator, weighted = state
        block_start = block_index * step_rows
        key_block = lax.dynamic_slice_in_dim(key_rows, block_start, step_rows, 0).reshape(
            step_rows, head_count, head_width
        )
        value_block = lax.dynamic_slice_in_dim(value_rows, block_start, step_rows, 0).reshape(
            step_rows, head_count, head_width
        )
        key_seg = segment_of(starts_row, block_start + jnp.arange(step_rows, dtype=jnp.int32))
        scores, allowed = scores_with_mask(queries, key_block, query_seg, key_seg)
        new_top = jnp.maximum(row_top, jnp.max(scores, axis=-1))
        factor = jnp.exp(row_top - new_top)
        weights = jnp.where(allowed, jnp.exp(scores - new_top[:, :, None]), 0.0)
        denominator = denominator * factor + jnp.sum(weights, axis=-1)
        weighted = weighted * factor[:, :, None] + jnp.einsum(
            "hqk,khe->hqe",
            weights.astype(jnp.bfloat16),
            value_block,
            preferred_element_type=jnp.float32,
        )
        return (new_top, denominator, weighted)

    return lax.fori_loop(0, piece_rows // step_rows, one_block, running)


def on_device(
    hidden,
    starts,
    first_gain,
    first_shift,
    qkv_weight,
    out_weight,
    second_gain,
    second_shift,
    up_weight,
    hidden_bias,
    down_weight,
    cotangent,
):
    rows_here = hidden.shape[1]
    model_width = hidden.shape[2]
    head_count = HEADS
    head_width = HEAD_DIM
    score_scale = head_width ** (-0.5)
    inputs = hidden[0].astype(jnp.float32)
    starts_row = starts[0]
    offset = lax.axis_index("blk") * rows_here
    query_seg = segment_of(starts_row, offset + jnp.arange(rows_here, dtype=jnp.int32))
    qkv_full, out_full, up_full, down_full = (
        lax.all_gather(qkv_weight, "rows", axis=0, tiled=True),
        lax.all_gather(out_weight, "rows", axis=0, tiled=True),
        lax.all_gather(up_weight, "rows", axis=0, tiled=True),
        lax.all_gather(down_weight, "rows", axis=0, tiled=True),
    )
    normed_low = layer_norm(inputs, first_gain, first_shift).astype(jnp.bfloat16)
    packed = jnp.dot(normed_low, qkv_full, preferred_element_type=jnp.float32).astype(jnp.bfloat16)
    queries = packed[:, :model_width].reshape(rows_here, head_count, head_width)
    key_rows = packed[:, model_width : 2 * model_width]
    value_rows = packed[:, 2 * model_width :]
    initial = (
        jnp.full((head_count, rows_here), masked_score, jnp.float32),
        jnp.zeros((head_count, rows_here), jnp.float32),
        jnp.zeros((head_count, rows_here, head_width), jnp.float32),
    )
    row_top, denominator, weighted = attend_rows(
        initial,
        lax.all_gather(key_rows, "blk", axis=0, tiled=True),
        lax.all_gather(value_rows, "blk", axis=0, tiled=True),
        queries,
        query_seg,
        starts_row,
    )
    log_total = row_top + jnp.log(denominator)
    attended = jnp.transpose(weighted / denominator[:, :, None], (1, 0, 2))
    attended_low = attended.reshape(rows_here, model_width).astype(jnp.bfloat16)
    residual = inputs + jnp.dot(attended_low, out_full, preferred_element_type=jnp.float32)
    second_low = layer_norm(residual, second_gain, second_shift).astype(jnp.bfloat16)
    up_values = jnp.dot(second_low, up_full, preferred_element_type=jnp.float32) + hidden_bias
    activated_low = jax.nn.gelu(up_values, approximate=False).astype(jnp.bfloat16)
    output = residual + jnp.dot(activated_low, down_full, preferred_element_type=jnp.float32)
    cot_low = cotangent[0]
    d_activated = jnp.einsum("tc,fc->tf", cot_low, down_full, preferred_element_type=jnp.float32)
    unused_gelu, gelu_pull = jax.vjp(
        lambda values: jax.nn.gelu(values, approximate=False), up_values
    )
    d_up_low = gelu_pull(d_activated)[0].astype(jnp.bfloat16)
    d_second = jnp.einsum("tf,cf->tc", d_up_low, up_full, preferred_element_type=jnp.float32)
    unused_second, second_pull = jax.vjp(layer_norm, residual, second_gain, second_shift)
    d_norm_two, d_second_gain, d_second_shift = second_pull(d_second)
    d_residual = cot_low.astype(jnp.float32) + d_norm_two
    d_branch_low = d_residual.astype(jnp.bfloat16)
    d_attended_low = jnp.einsum(
        "tc,kc->tk", d_branch_low, out_full, preferred_element_type=jnp.float32
    ).astype(jnp.bfloat16)
    d_attended3 = d_attended_low.reshape(rows_here, head_count, head_width)
    row_dots = jnp.einsum("qhe,qhe->hq", d_attended3.astype(jnp.float32), attended)
    keys_all, values_all = (
        lax.all_gather(key_rows, "blk", axis=0, tiled=True),
        lax.all_gather(value_rows, "blk", axis=0, tiled=True),
    )
    length = keys_all.shape[0]
    step_rows = math.gcd(length, block_limit)

    def block_terms(block_index):
        block_start = block_index * step_rows
        key_block = lax.dynamic_slice_in_dim(keys_all, block_start, step_rows, 0).reshape(
            step_rows, head_count, head_width
        )
        value_block = lax.dynamic_slice_in_dim(values_all, block_start, step_rows, 0).reshape(
            step_rows, head_count, head_width
        )
        key_seg = segment_of(starts_row, block_start + jnp.arange(step_rows, dtype=jnp.int32))
        scores, allowed = scores_with_mask(queries, key_block, query_seg, key_seg)
        probability = jnp.where(allowed, jnp.exp(scores - log_total[:, :, None]), 0.0)
        d_probs = jnp.einsum(
            "qhe,khe->hqk", d_attended3, value_block, preferred_element_type=jnp.float32
        )
        d_scores = (probability * (d_probs - row_dots[:, :, None])).astype(jnp.bfloat16)
        return (key_block, probability, d_scores)

    dq_start = jnp.zeros((rows_here, head_count, head_width), jnp.float32)

    def back_block(dq_sum, block_index):
        key_block, probability, d_scores = block_terms(block_index)
        dq_sum = dq_sum + jnp.einsum(
            "hqk,khe->qhe", d_scores, key_block, preferred_element_type=jnp.float32
        )
        dk_block = (
            jnp.einsum("hqk,qhe->khe", d_scores, queries, preferred_element_type=jnp.float32)
            * score_scale
        )
        dv_block = jnp.einsum(
            "hqk,qhe->khe",
            probability.astype(jnp.bfloat16),
            d_attended3,
            preferred_element_type=jnp.float32,
        )
        return (
            dq_sum,
            (dk_block.reshape(step_rows, model_width), dv_block.reshape(step_rows, model_width)),
        )

    dq_sum, (dk_terms, dv_terms) = lax.scan(back_block, dq_start, jnp.arange(length // step_rows))
    dk_rows, dv_rows = (
        lax.psum_scatter(
            dk_terms.reshape(length, model_width).astype(jnp.bfloat16),
            "blk",
            scatter_dimension=0,
            tiled=True,
        ).astype(jnp.float32),
        lax.psum_scatter(
            dv_terms.reshape(length, model_width).astype(jnp.bfloat16),
            "blk",
            scatter_dimension=0,
            tiled=True,
        ).astype(jnp.float32),
    )
    d_packed = jnp.concatenate(
        [(dq_sum * score_scale).reshape(rows_here, model_width), dk_rows, dv_rows], axis=1
    ).astype(jnp.bfloat16)
    d_normed = jnp.einsum("tn,cn->tc", d_packed, qkv_full, preferred_element_type=jnp.float32)
    unused_first, first_pull = jax.vjp(layer_norm, inputs, first_gain, first_shift)
    d_norm_one, d_first_gain, d_first_shift = first_pull(d_normed)
    grad_hidden = d_residual + d_norm_one
    d_bias = jnp.sum(d_up_low, axis=0, dtype=jnp.float32)
    wide_share = lax.psum_scatter(
        jnp.concatenate(
            [
                jnp.einsum("tc,tn->cn", normed_low, d_packed, preferred_element_type=jnp.float32),
                jnp.einsum(
                    "tc,tn->cn", attended_low, d_branch_low, preferred_element_type=jnp.float32
                ),
                jnp.einsum("tc,tn->cn", second_low, d_up_low, preferred_element_type=jnp.float32),
            ],
            axis=1,
        ).astype(jnp.bfloat16),
        "rows",
        scatter_dimension=0,
        tiled=True,
    )
    down_share = lax.psum_scatter(
        jnp.einsum("tf,tn->fn", activated_low, cot_low, preferred_element_type=jnp.float32).astype(
            jnp.bfloat16
        ),
        "rows",
        scatter_dimension=0,
        tiled=True,
    )
    wide_grads, down_grads = (
        lax.psum(wide_share, "blk").astype(jnp.float32),
        lax.psum(down_share, "blk").astype(jnp.float32),
    )
    grad_qkv = wide_grads[:, : 3 * model_width]
    grad_out = wide_grads[:, 3 * model_width : 4 * model_width]
    grad_up = wide_grads[:, 4 * model_width :]
    small_grads = lax.psum(
        (d_first_gain, d_first_shift, d_second_gain, d_second_shift, d_bias), ("rows", "blk")
    )
    return (
        output[None],
        grad_hidden[None],
        grad_qkv,
        grad_out,
        grad_up,
        down_grads,
        small_grads[0],
        small_grads[1],
        small_grads[2],
        small_grads[3],
        small_grads[4],
    )


MESH = pl.DeviceIdType.MESH
FORWARD_MOVES = (
    ((0, 0), (1, 0), (2, 0), (0, 1), (1, 1), (2, 1),),
    (),
    (),
    (),
    (),
    (),
    (),
    (),
    (),
    (),
    ((4, 0, 0), (3, 0, 1, 0), (2, 2), (2, 3), (4, 1, 0), (3, 0, 0, 0), (3, 1, 1, 0), (4, 0, 2), (3, 1, 0, 0), (4, 0, 1), (3, 0, 2, 0), (4, 1, 2), (0, 2), (3, 1, 2, 0), (4, 1, 1),),
    (),
    (),
    ((4, 0, 3), (3, 2, 1, 0), (4, 1, 3), (3, 2, 0, 0),),
    (),
    ((4, 2, 2), (1, 2), (0, 3),),
    (),
    ((4, 2, 1), (3, 2, 2, 0),),
    (),
    ((4, 2, 0), (1, 3), (2, 5),),
    (),
    (),
    (),
    (),
    ((3, 3, 1, 0), (4, 2, 3),),
    (),
    (),
    (),
    (),
    (),
    (),
    (),
    (),
    ((3, 3, 0, 0), (4, 3, 0), (0, 5),),
    (),
    (),
    (),
    (),
    (),
    (),
    ((4, 3, 2), (3, 3, 2, 0), (0, 4), (2, 4), (1, 5), (3, 5, 1, 0), (4, 3, 1), (1, 4), (3, 5, 0, 0), (3, 4, 1, 0), (4, 3, 3), (3, 4, 0, 0),),
    (),
    ((4, 5, 0), (3, 5, 2, 0),),
    (),
    (),
    ((4, 4, 0),),
    ((3, 4, 2, 0),),
    (),
    (),
    (),
    ((4, 4, 2),),
    ((3, 5, 1, 1),),
    (),
    (),
    ((3, 5, 0, 1), (4, 4, 1),),
    (),
    (),
    (),
    ((4, 4, 3),),
    ((3, 5, 2, 1),),
    (),
    (),
    (),
    (),
    (),
    (),
    (),
    (),
    (),
    (),
    (),
    (),
    (),
)
ROWS_Z, ROWS_Y = 4, 2
PAIR = 128
UNIT = 640
SLOTS = 2


def place_of():
    index = lax.axis_index("rows")
    return index // 4, lax.rem(index // 2, 2), lax.rem(index, 2)


def row_of(z, y, core):
    return (lax.rem(z + ROWS_Z, ROWS_Z) * ROWS_Y + y) * 2 + core


def aligned(index, step):
    return pl.ds(pl.multiple_of(index * step, step), step)


def dot_nt(left, right):
    return lax.dot_general(left, right, (((1,), (1,)), ((), ())), preferred_element_type=jnp.float32)


def dot_nn(left, right):
    return jnp.dot(left, right, preferred_element_type=jnp.float32)


def head_lanes(width):
    lane = lax.broadcasted_iota(jnp.int32, (1, width), 1)
    return (lane < HEAD_DIM, lane >= HEAD_DIM)


def greet(peers):
    barrier = pltpu.get_barrier_semaphore()
    for peer in peers:
        pl.semaphore_signal(barrier, inc=1, device_id=peer, device_id_type=MESH)
    pl.semaphore_wait(barrier, len(peers))


def neighbours():
    z, y, core = place_of()
    return [
        {"rows": row_of(z + 1, y, core)},
        {"rows": row_of(z + 2, y, core)},
        {"rows": row_of(z + 3, y, core)},
        {"rows": row_of(z, 1 - y, core)},
        {"rows": row_of(z, y, 1 - core)},
        {"blk": 1 - lax.axis_index("blk")},
    ]


def write_mask(starts_ref, mask_ref, part=0, parts=1):
    blocks, step, length = mask_ref.shape

    def rows(i, carry):
        key_at = lax.broadcasted_iota(jnp.int32, (step, length), 0) + i * step
        query_at = lax.broadcasted_iota(jnp.int32, (step, length), 1)
        key_seg = jnp.zeros((step, length), jnp.int32)
        query_seg = jnp.zeros((step, length), jnp.int32)
        for cell in range(starts_ref.shape[1]):
            start = starts_ref[0, cell]
            key_seg += (key_at >= start).astype(jnp.int32)
            query_seg += (query_at >= start).astype(jnp.int32)
        mask_ref[i] = jnp.where(key_seg == query_seg, 0.0, masked_score).astype(mask_ref.dtype)
        return carry

    lax.fori_loop(blocks * part // parts, blocks * (part + 1) // parts, rows, 0)


def z_place(z):
    return 2 * lax.rem(z, 2) + z // 2


def grad_chunk(target, left, right):
    def half(j, carry):
        value = dot_nn(left(j), right()).astype(jnp.bfloat16)
        n = value.shape[1]
        rows = value.shape[0] // 8
        for block in range(8):
            to_z, to_y, to_core = block // 4, block // 2 % 2, block % 2
            target[to_core, to_y, 2 * to_z + j, :, :n] = value[block * rows : (block + 1) * rows]
        return carry

    lax.fori_loop(0, 2, half, 0)


def forward_kernel(
    hidden, cot, starts, gain1, shift1, gain2, shift2, bias_in, q_in, o_in, u_in, d_in,
    q_all, o_all, u_all, d_all, dy_all, down_sums, normed_t_out, packed_out, lse_out, att_t_out, resid_out,
    second_t_out, act_out, slope_out,
    hid_other, normed, wq, wo, wu, packed, mask, att_part, att_own, resid, second,
    act, act_t, slope, normed_t, att_t, second_t, lse, u_wide, q_own, o_own, u_own, d_own, dy, bias, parts, core_in,
    local_sem, send_sem, recv_sem, x_send, x_recv,
):
    bf16 = jnp.bfloat16
    z, y, core = place_of()
    me = row_of(z, y, core)
    piece = lax.axis_index("blk")
    other = 1 - piece
    own_rows, width = hidden.shape
    length = packed.shape[0]
    rows = o_own.shape[0]
    early = rows * 3 // 5
    d_half = lambda half: pl.ds(half * rows, rows)
    own = (
        q_own.at[pl.ds(0, early)], q_own.at[pl.ds(early, rows - early)], o_own, u_own,
        d_own.at[d_half(0)], d_own.at[d_half(1)],
    )
    last = len(own) - 1

    def slot_of(w, at_z, at_y, at_core):
        slot = row_of(at_z, at_y, at_core)
        if w < 2:
            return q_all.at[slot, pl.ds(w * early, own[w].shape[0])]
        if w < 4:
            return (o_all, u_all)[w - 2].at[slot]
        return d_all.at[slot, d_half(w - 4)]

    x_peer = {"blk": other}
    peers = neighbours()
    pairs = packed.shape[1] // (3 * PAIR)
    first_gain, first_shift, second_gain, second_shift = (
        ref[...].reshape(1, width) for ref in (gain1, shift1, gain2, shift2)
    )

    def local(src, dst, index):
        return pltpu.make_async_copy(src, dst, local_sem.at[index])

    near = z + 1 - 2 * lax.rem(z, 2)
    far = lax.rem(z + 2, ROWS_Z)
    spread = (z, far, near, ROWS_Z - 1 - z)

    def send(w, at_z, v, place, peer, first=False):
        block = slot_of(w, at_z, y if v == 0 else 1 - y, core)
        index = w * 18 + place
        return pltpu.make_async_remote_copy(
            src_ref=own[w] if first else block, dst_ref=block, send_sem=send_sem.at[index],
            recv_sem=recv_sem.at[index], device_id=peer, device_id_type=MESH,
        )

    def along(w, k, v):
        peer = {"rows": row_of(far if k == 0 else near, y, core)}
        return send(w, far if k == 2 else z, v, 2 * k + v, peer, k < 2 and v == 0)

    def to_y(w, at_z, first=False):
        return send(w, at_z, 0, 6 + at_z, peers[3], first)

    def to_core(w, at_z, v, first=False):
        return send(w, at_z, v, 10 + 2 * at_z + v, peers[4], first)

    def pass_on(w, v):
        inner = (z == 1) | (z == 2)

        @pl.when(inner)
        def _():
            along(w, 0, v).start()

        along(w, 1, v).start()

        @pl.when(jnp.logical_not(inner))
        def _():
            along(w, 0, v).start()

    def relay_z(w, k, v):
        along(w, k, v).wait_recv()
        if k == 0:
            along(w, 2, v).start()
        at_z = spread[k + 1]
        if w < last:
            to_y(w, at_z).start()
        to_core(w, at_z, v).start()

    def relay_y(w, k):
        to_y(w, spread[k]).wait_recv()
        to_core(w, spread[k], 1).start()
        if w == last:
            pass_on(w, 1)

    def all_here(ws):
        for w in ws:
            for at_z in range(ROWS_Z):
                for v in range(2):
                    to_core(w, at_z, v).wait_recv()

    def all_here_load(ws, source, target, first):
        for i, at_z in enumerate(spread):
            for v in range(2):
                for w in ws:
                    to_core(w, at_z, v).wait_recv()
                chip = pl.ds(row_of(at_z, y if v == 0 else 1 - y, 0), 2)
                local(source.at[chip], target.at[chip], first + 2 * i + v).start()

    def loaded(source, target, first):
        for i in range(2 * ROWS_Z):
            chip = pl.ds(0, 2)
            local(source.at[chip], target.at[chip], first + i).wait()

    def all_gone(w):
        for v in range(1 if w < last else 2):
            for k in range(3):
                along(w, k, v).wait_send()
        for at_z in range(ROWS_Z) if w < last else (z,):
            to_y(w, at_z).wait_send()
        for at_z in range(ROWS_Z):
            for v in range(2):
                to_core(w, at_z, v).wait_send()

    def to_x(src, dst, index):
        return pltpu.make_async_remote_copy(
            src_ref=src, dst_ref=dst, send_sem=x_send.at[index], recv_sem=x_recv.at[index],
            device_id=x_peer, device_id_type=MESH,
        )

    third = q_in.shape[1] // 3
    share = third // 2
    q_picks = []
    for part in range(3):
        picked = q_in.at[:, pl.ds(pl.multiple_of(part * third + piece * share, 128), share)]
        q_picks.append(local(picked, q_own.at[:, pl.ds(part * share, share)], 17 + part))
        q_picks[-1].start()
    d_mine = d_in.at[pl.ds(piece * 2 * rows, 2 * rows)]
    local(o_in, o_own, 1).start()
    local(u_in, u_wide, 2).start()
    local(d_mine, d_own, 3).start()
    local(cot, dy.at[piece], 4).start()
    greet(peers)
    for copy in q_picks:
        copy.wait()
    hidden_x = to_x(hidden, hid_other, 0)
    cot_x = to_x(cot, dy.at[piece], 1)
    local(o_in, o_own, 1).wait()
    local(d_mine, d_own, 3).wait()
    local(u_in, u_wide, 2).wait()
    half_rows = lambda half: pl.ds(pl.multiple_of(half * own_rows, 128), own_rows)

    def first_copies():
        local(q_own, q_all.at[me], 0).start()
        local(o_own, o_all.at[me], 1).start()
        local(d_own, d_all.at[me], 3).start()
        local(cot, dy.at[piece], 4).wait()

    units_each = 2 * rows
    group = 8 * units_each

    def mine(block):
        wide = block.astype(jnp.float32)
        halves = []
        for half in range(2):
            at = [slice((2 * j + half) * units_each, (2 * j + half + 1) * units_each) for j in range(4)]
            halves.append(jnp.concatenate([wide[:, cols] for cols in at], axis=1))
        return jnp.where(piece == 0, halves[0], halves[1])

    def pick_units(g):
        cols = slice(g * group // 2, (g + 1) * group // 2)
        u_own[:, cols] = mine(u_wide[:, g * group : (g + 1) * group]).astype(bf16)
        bias[:, cols] = mine(bias_in[g * group : (g + 1) * group].reshape(1, group))
        if g == u_own.shape[1] * 2 // group - 1:
            local(u_own, u_all.at[me], 2).start()

    def norm_rows(source, half, part):
        step = 64
        steps = own_rows // step

        def body(i, carry):
            value = source[aligned(i, step), :].astype(jnp.float32)
            low = layer_norm(value, first_gain, first_shift).astype(bf16)
            normed[pl.ds(pl.multiple_of(half * own_rows + i * step, step), step), :] = low
            return carry

        lax.fori_loop(steps * part // 2, steps * (part + 1) // 2, body, 0)

    def q_here():
        local(q_own, q_all.at[me], 0).wait()
        all_here_load((0, 1), q_all, wq, 20)

    column = lax.broadcasted_iota(jnp.int32, (1, 3 * PAIR), 1)

    def project(begin, end):
        def body(i, carry):
            cols = aligned(i, 3 * PAIR)
            weight = wq[:, :, cols].reshape(width, 3 * PAIR)
            value = dot_nn(normed[...], weight).astype(bf16)
            factor = jnp.where(i * 3 * PAIR + column < share, HEAD_DIM ** (-0.5), 1.0).astype(bf16)
            packed[:, cols] = value * factor
            return carry

        lax.fori_loop(begin, end, body, 0)
        if end == pairs:
            local(packed, packed_out, 9).start()

    first_lanes = head_lanes(PAIR)

    def att_cols(half, p):
        return pl.ds(pl.multiple_of(half * pairs * PAIR + p * PAIR, PAIR), PAIR)

    def attend(p, half):
        at_q, at_k, at_v = (slice(t * share + PAIR * p, t * share + PAIR * (p + 1)) for t in range(3))
        value_t = packed[:, at_v].T
        at = half_rows(half)
        queries = packed[at, at_q]
        keys = packed[:, at_k]
        halves = []
        for h in range(2):
            one = jnp.where(first_lanes[h], queries, jnp.zeros_like(queries))
            scores = dot_nt(keys, one) + mask[:, :, at].reshape(length, own_rows)
            top = jnp.max(scores, axis=0, keepdims=True)
            weights = jnp.exp(scores - top)
            total = jnp.sum(weights, axis=0, keepdims=True)
            lse[2 * p + h : 2 * p + h + 1, at] = top + jnp.log(total)
            summed = dot_nn(value_t[h * HEAD_DIM : (h + 1) * HEAD_DIM], weights.astype(bf16))
            halves.append(summed / total)
        return jnp.concatenate(halves, axis=0).T.astype(bf16)

    def attend_other(p):
        att_part[:, p * PAIR : (p + 1) * PAIR] = attend(p, other)

    def attend_own(p):
        att_own[:, att_cols(piece, p)] = attend(p, piece)
        if p == pairs - 1:
            local(lse, lse_out, 10).start()

    att_x = [
        to_x(att_part.at[:, pl.ds(p * PAIR, PAIR)], att_own.at[:, att_cols(piece, p)], 2 + p) for p in range(pairs)
    ]

    def o_here():
        local(o_own, o_all.at[me], 1).wait()
        all_here_load((2,), o_all, wo, 28)

    def att_here():
        for copy in att_x:
            copy.wait_recv()
        loaded(o_all, wo, 28)

    part_rows = own_rows // 2
    second_x = [
        to_x(second.at[piece, pl.ds(i * part_rows, part_rows)], second.at[piece, pl.ds(i * part_rows, part_rows)], 2 + pairs + i)
        for i in range(2)
    ]

    def merge(part):
        at = slice(part * part_rows, (part + 1) * part_rows)

        def body(i, carry):
            cols = aligned(i, 256)
            weight = wo[:, :, cols].reshape(width, 256)
            resid[at, cols] = hidden[at, cols].astype(jnp.float32) + dot_nn(att_own[at, :], weight)
            return carry

        lax.fori_loop(0, width // 256, body, 0)

        def second_rows(i, carry):
            rows = aligned(i, 64)
            second[piece, rows, :] = layer_norm(resid[rows, :], second_gain, second_shift).astype(bf16)
            return carry

        lax.fori_loop(part * part_rows // 64, (part + 1) * part_rows // 64, second_rows, 0)
        if part == 1:
            local(resid, resid_out, 12).start()

    def flip_normed():
        def body(i, carry):
            normed_t[aligned(i, 128), :] = normed[:, aligned(i, 128)].T
            return carry

        lax.fori_loop(0, width // 128, body, 0)
        local(normed_t, normed_t_out, 8).start()

    def flip_second(half):
        def body(i, carry):
            second_t[aligned(i, 128), half_rows(half)] = second[half, :, aligned(i, 128)].T
            return carry

        lax.fori_loop(0, width // 128, body, 0)

    def flip_att():
        def body(i, carry):
            att_t[aligned(i, 128), :] = att_own[:, aligned(i, 128)].T
            return carry

        lax.fori_loop(0, width // 128, body, 0)
        local(att_t, att_t_out, 11).start()
        flip_second(piece)

    def u_here():
        local(u_own, u_all.at[me], 2).wait()
        all_here_load((3,), u_all, wu, 36)

    unit = 256
    fifth = act.shape[1] // unit // 5

    def expand(half, begin):
        at = half_rows(half)

        def body(i, carry):
            cols = aligned(i, unit)
            weight = wu[:, :, cols].reshape(width, unit)
            up = dot_nn(second[half], weight) + bias[:, cols]
            cdf = 0.5 * (1.0 + lax.erf(up * (0.5 ** 0.5)))
            pdf = jnp.exp(up * up * -0.5) * ((2.0 * math.pi) ** -0.5)
            value = (up * cdf).astype(bf16)
            act[at, cols] = value
            act_t[cols, at] = value.T
            slope[at, cols] = (cdf + up * pdf).astype(bf16)
            return carry

        lax.fori_loop(begin * fifth, (begin + 1) * fifth, body, 0)
        if begin == 4:
            for copy in halves_out(half):
                copy.start()

    def halves_out(half):
        base = 44 if half is piece else 47
        at = half_rows(half)
        return (
            local(act.at[at], act_out.at[at], base),
            local(slope.at[at], slope_out.at[at], base + 1),
        )

    def second_here():
        for copy in second_x:
            copy.wait_recv()

    def flip_last():
        flip_second(other)
        local(second_t, second_t_out, 13).start()

    def dy_here():
        cot_x.wait_recv()
        local(dy, dy_all, 4).start()

    def grad_down(i):
        h, at = i // 2, slice(i % 2 * UNIT, (i % 2 + 1) * UNIT)

        def left(j):
            begin = lambda block: pl.multiple_of((8 * j + block) * 2 * rows + h * rows, 16)
            return jnp.concatenate([act_t[pl.ds(begin(block), rows), :] for block in range(8)], axis=0)

        grad_chunk(parts.at[i % SLOTS], left, lambda: dy[:, :, at].reshape(length, UNIT))

    sums_x = [
        pltpu.make_async_remote_copy(
            src_ref=parts.at[i % SLOTS, 1 - core], dst_ref=core_in.at[i], send_sem=x_send.at[4 + pairs + i],
            recv_sem=x_recv.at[4 + pairs + i], device_id=peers[4], device_id_type=MESH,
        )
        for i in range(4)
    ]

    def sum_down(i):
        core_in[i] += parts[i % SLOTS, core]
        sums_x[i].wait_send()
        local(core_in.at[i], down_sums.at[i], 50 + i).start()

    def outputs():
        for i in range(4):
            local(core_in.at[i], down_sums.at[i], 50 + i).wait()
        local(dy, dy_all, 4).wait()
        local(d_own, d_all.at[me], 3).wait()
        local(normed_t, normed_t_out, 8).wait()
        local(packed, packed_out, 9).wait()
        local(lse, lse_out, 10).wait()
        local(att_t, att_t_out, 11).wait()
        local(resid, resid_out, 12).wait()
        local(second_t, second_t_out, 13).wait()
        for half in (piece, other):
            for copy in halves_out(half):
                copy.wait()

    act_now = functools.partial
    steps = [hidden_x.start, cot_x.start]
    steps += [act_now(pick_units, g) for g in range(4)]
    steps += [act_now(norm_rows, hidden, piece, part) for part in range(2)]
    steps += [act_now(write_mask, starts, mask, part, 2) for part in range(2)]
    steps += [hidden_x.wait_recv]
    steps += [act_now(norm_rows, hid_other, other, part) for part in range(2)]
    steps += [q_here, act_now(loaded, q_all, wq, 20), act_now(project, 0, 2), act_now(project, 2, pairs)]
    for p in range(pairs):
        steps += [act_now(attend_other, p), att_x[p].start]
    steps += [act_now(attend_own, p) for p in range(pairs - 1)]
    steps += [o_here, act_now(attend_own, pairs - 1), att_here]
    steps += [act_now(merge, 0), second_x[0].start, act_now(merge, 1), second_x[1].start]
    steps += [flip_normed, flip_att, u_here, act_now(loaded, u_all, wu, 36)]
    steps += [act_now(expand, piece, i) for i in range(5)]
    steps += [second_here, flip_last]
    steps += [act_now(expand, other, i) for i in range(5)]
    steps += [dy_here]
    for i in range(4):
        steps += [act_now(grad_down, i), sums_x[i].start]
        if i:
            steps += [sums_x[i - 1].wait_recv, act_now(sum_down, i - 1)]
    steps += [sums_x[3].wait_recv, act_now(sum_down, 3), outputs, act_now(all_here, (4, 5))]
    moves = (
        lambda w: pass_on(w, 0),
        lambda w: to_y(w, z, True).start(),
        lambda w: to_core(w, z, 0, True).start(),
        relay_z,
        relay_y,
    )
    for i, step in enumerate(steps):
        for kind, *where in FORWARD_MOVES[i]:
            moves[kind](*where)
        step()
        if i == 1:
            first_copies()
    for w in range(len(own)):
        all_gone(w)
    for copy in [hidden_x, cot_x] + second_x + att_x:
        copy.wait_send()


def forward(hidden, cot, starts, gain1, shift1, gain2, shift2, bias, qkv, out, up, down):
    own_rows, width = hidden.shape
    length = 2 * own_rows
    cols = qkv.shape[1] // 2
    units = up.shape[1] // 2
    rows = up.shape[0]
    bf16, f32 = jnp.bfloat16, jnp.float32
    shards = lax.axis_size("rows")
    head_rows = 16
    outs = [
        ((shards, rows, cols), bf16),
        ((shards, rows, width), bf16),
        ((shards, rows, units), bf16),
        ((shards, down.shape[0] // 2, width), bf16),
        ((2, own_rows, width), bf16),
        ((4, 2, ROWS_Z, rows, UNIT), bf16),
        ((width, length), bf16),
        ((length, cols), bf16),
        ((head_rows, length), f32),
        ((width, own_rows), bf16),
        ((own_rows, width), f32),
        ((width, length), bf16),
        ((length, units), bf16),
        ((length, units), bf16),
    ]
    scratch = [
        ((own_rows, width), bf16),
        ((length, width), bf16),
        ((shards, rows, cols), bf16),
        ((shards, rows, width), bf16),
        ((shards, rows, units), bf16),
        ((length, cols), bf16),
        ((length // 48, 48, length), f32),
        ((own_rows, cols // 3), bf16),
        ((own_rows, width), bf16),
        ((own_rows, width), f32),
        ((2, own_rows, width), bf16),
        ((length, units), bf16),
        ((units, length), bf16),
        ((length, units), bf16),
        ((width, length), bf16),
        ((width, own_rows), bf16),
        ((width, length), bf16),
        ((head_rows, length), f32),
        ((rows, 2 * units), bf16),
        ((rows, cols), bf16),
        ((rows, width), bf16),
        ((rows, units), bf16),
        ((2 * rows, width), bf16),
        ((2, own_rows, width), bf16),
        ((1, units), f32),
        ((SLOTS, 2, 2, ROWS_Z, rows, UNIT), bf16),
        ((4, 2, ROWS_Z, rows, UNIT), bf16),
    ]
    vmem = pl.BlockSpec(memory_space=pltpu.VMEM)
    anywhere = pl.BlockSpec(memory_space=pl.ANY)
    smem = pl.BlockSpec(memory_space=pltpu.SMEM)
    dma = pltpu.SemaphoreType.DMA
    x_copies = 8 + cols // (3 * PAIR)
    return pl.pallas_call(
        forward_kernel,
        out_shape=[jax.ShapeDtypeStruct(shape, kind) for shape, kind in outs],
        in_specs=[vmem, anywhere, smem] + [vmem] * 5 + [anywhere] * 4,
        out_specs=[anywhere] * len(outs),
        scratch_shapes=[pltpu.VMEM(shape, kind) for shape, kind in scratch]
        + [dma((54,)), dma((108,)), dma((108,)), dma((x_copies,)), dma((x_copies,))],
        compiler_params=pltpu.CompilerParams(
            collective_id=1, has_side_effects=True, vmem_limit_bytes=60 * 1024 * 1024
        ),
        name="forward",
    )(hidden, cot, starts, gain1, shift1, gain2, shift2, bias, qkv, out, up, down)


BACKWARD_MOVES = (
    ((2, 0), (3, 0), (1, 0), (0, 0),),
    (),
    (),
    (),
    (),
    (),
    (),
    ((2, 1), (1, 1),),
    (),
    (),
    (),
    ((4, 0), (5, 0), (0, 1), (3, 1),),
    (),
    ((2, 2),),
    (),
    ((1, 2), (6, 0), (7, 0), (4, 1), (0, 2),),
    (),
    (),
    (),
    ((3, 2),),
    ((5, 1),),
    (),
    (),
    (),
    (),
    ((2, 3), (1, 3),),
    (),
    (),
    (),
    ((4, 2),),
    (),
    ((8, 0), (3, 3),),
    ((9, 0), (6, 1),),
    ((5, 2),),
    ((4, 3),),
    (),
    (),
    ((10, 0), (6, 2), (7, 1),),
    ((0, 3), (5, 3),),
    ((6, 3),),
    (),
    (),
    ((11, 0), (7, 2),),
    (),
    ((8, 1),),
    ((7, 3),),
    (),
    ((12, 0),),
    ((8, 2),),
    ((9, 1),),
    (),
    ((8, 3),),
    (),
    ((10, 1), (9, 2),),
    (),
    (),
    (),
    (),
    ((10, 2), (11, 1),),
    ((9, 3), (13, 0), (10, 3),),
    (),
    (),
    ((14, 0), (12, 1), (11, 2), (13, 1), (12, 2), (11, 3),),
    ((14, 1), (13, 2), (12, 3), (14, 2), (13, 3), (14, 3),),
    (),
    (),
    (),
    (),
    (),
)


def norm_back(values, gain, grad):
    centred = values - jnp.mean(values, axis=-1, keepdims=True)
    scale = lax.rsqrt(jnp.mean(centred * centred, axis=-1, keepdims=True) + 1e-05)
    unit = centred * scale
    scaled = grad * gain
    mean_one = jnp.mean(scaled, axis=-1, keepdims=True)
    mean_two = jnp.mean(scaled * unit, axis=-1, keepdims=True)
    d_values = scale * (scaled - mean_one - unit * mean_two)
    d_gain = jnp.sum(grad * unit, axis=0, keepdims=True)
    d_shift = jnp.sum(grad, axis=0, keepdims=True)
    return d_values, d_gain, d_shift


def backward_kernel(
    starts, gain1, gain2, hidden, dy_all, q_all, o_all, u_all, d_all, down_sums, normed_t, packed, lse_in, att_t_in,
    resid, second_t, act, slope,
    output, grad_hidden, units_out, pairs_out, small_out,
    lhs, att_t, half_act, wide, wd, wu, dy, first, second, d_att, x_in0, x_in1, x_out0, down_own,
    parts, core_in, core_in_q, y_in, y_in_q, z_in, z_in_q, lse, acc_k, acc_v, bias_sum, early, late,
    early_near, late_near, early_all, late_all, small,
    local_sem, a_send, a_recv, b_send, b_recv, c_send, c_recv, g_send, g_recv, x_send, x_recv,
    s_send, s_recv, keep_sem,
):
    bf16, f32 = jnp.bfloat16, jnp.float32
    z, y, core = place_of()
    piece = lax.axis_index("blk")
    other = 1 - piece
    own_rows, width = first.shape
    length = 2 * own_rows
    branch = half_act.at[:, pl.ds(0, width)]
    units = wide.shape[1]
    d_width = d_att.shape[1]
    cols = 3 * d_width
    pairs = d_width // PAIR
    near = z + 1 - 2 * lax.rem(z, 2)
    far = lax.rem(z + 2, ROWS_Z)
    peer_core, peer_y = {"rows": row_of(z, y, 1 - core)}, {"rows": row_of(z, 1 - y, core)}
    peer_near, peer_far = {"rows": row_of(near, y, core)}, {"rows": row_of(far, y, core)}
    peer_x = {"blk": other}
    group = [peer_core, peer_y, {"rows": row_of(z, 1 - y, 1 - core)}]
    line = [
        {"rows": row_of(z + k, y, core), "blk": lax.rem(piece + n, 2)} for n in range(2) for k in range(ROWS_Z) if n or k
    ]
    wide_chunks = core_in.shape[0]
    chunks = wide_chunks + pairs
    first_gain, second_gain = gain1[...].reshape(1, width), gain2[...].reshape(1, width)
    half_rows = lambda half: pl.ds(pl.multiple_of(half * own_rows, 128), own_rows)
    part_rows = own_rows // 2
    part_at = lambda part: pl.ds(part * part_rows, part_rows)

    def remote(src, dst, sends, recvs, index, peer):
        return pltpu.make_async_remote_copy(
            src_ref=src, dst_ref=dst, send_sem=sends.at[index], recv_sem=recvs.at[index],
            device_id=peer, device_id_type=MESH,
        )

    loads = {
        "sums": (down_sums, core_in.at[pl.ds(0, 4)], 0),
        "dy": (dy_all, dy, 1),
        "down": (d_all, wd, 2),
        "slope": (slope, wide, 3),
        "up": (u_all, wu, 4),
        "act_other": (act.at[half_rows(other)], half_act, 5),
        "act_own": (act.at[half_rows(piece)], half_act, 6),
        "resid": (resid, second, 7),
        "lse": (lse_in, lse, 8),
        "second_t": (second_t, lhs, 9),
        "att_t": (att_t_in, att_t, 10),
        "out": (o_all, wd.at[pl.ds(0, width)], 11),
        "normed_t": (normed_t, wd.at[pl.ds(width, width), pl.ds(0, length)], 12),
        "qkv": (q_all, wu.at[:, pl.ds(0, cols)], 13),
        "packed": (packed, wide.at[:, pl.ds(0, cols)], 14),
        "hidden": (hidden, branch, 15),
        "output": (second, output, 16),
        "grad_hidden": (first, grad_hidden, 17),
    }

    def local(name):
        src, dst, index = loads[name]
        return pltpu.make_async_copy(src, dst, local_sem.at[index])

    z_first = (0, 1)
    mine, theirs = pl.ds(2 * lax.rem(z, 2), 2), pl.ds(2 - 2 * lax.rem(z, 2), 2)
    place, far_place = z_place(z), z_place(far)
    order = tuple(range(chunks))

    def buffers(i):
        if i < wide_chunks:
            return core_in.at[i], y_in.at[i], z_in.at[i], units_out.at[:, i], UNIT
        i -= wide_chunks
        return core_in_q.at[i], y_in_q.at[i], z_in_q.at[i], pairs_out.at[:, i], 3 * PAIR

    def copy_a(i):
        into, _, _, _, n = buffers(i)
        return remote(parts.at[i % SLOTS, 1 - core, :, :, :, pl.ds(0, n)], into, a_send, a_recv, i, peer_core)

    def copy_b(i):
        sums, by_y, by_z, _, _ = buffers(i)
        if i in z_first:
            return remote(sums.at[1 - y, place], by_z.at[2], b_send, b_recv, i, peer_y)
        return remote(sums.at[1 - y], by_y, b_send, b_recv, i, peer_y)

    def copies_c(i, step):
        sums, by_y, by_z, _, _ = buffers(i)
        index = 4 * i + 2 * step
        if i not in z_first:
            if step == 0:
                return [remote(by_y.at[theirs], by_z.at[pl.ds(0, 2)], c_send, c_recv, index, peer_near)]
            return [remote(by_y.at[far_place], by_z.at[2], c_send, c_recv, index, peer_far)]
        if step == 0:
            return [
                remote(sums.at[v, theirs], by_y.at[pl.ds(2 * v, 2)], c_send, c_recv, index + v, peer_near)
                for v in range(2)
            ]
        return [remote(sums.at[v, far_place], by_z.at[v], c_send, c_recv, index + v, peer_far) for v in range(2)]

    def copy_g(i):
        _, _, by_z, out, _ = buffers(i)
        return remote(by_z.at[0], out.at[piece], g_send, g_recv, i, peer_x)

    def keep_g(i):
        _, _, by_z, out, _ = buffers(i)
        return pltpu.make_async_copy(by_z.at[0], out.at[piece], keep_sem.at[i])

    def move(i, stage):
        sums, by_y, by_z, _, n = buffers(i)
        if stage == 0:
            slot = i % SLOTS
            if i >= 4:
                copy_a(i).wait_recv()
                sums[1 - y] += parts[slot, core, 1 - y, :, :, :n]
            if i in z_first:
                for copy in copies_c(i, 0):
                    copy.start()
            else:
                copy_b(i).start()
            if i >= 4:
                sums[y] += parts[slot, core, y, :, :, :n]
                copy_a(i).wait_send()
        elif i in z_first and stage < 3:
            for v, copy in enumerate(copies_c(i, stage - 1)):
                copy.wait_recv()
                if stage == 1:
                    sums[v, mine] += by_y[2 * v : 2 * v + 2]
                else:
                    sums[v, place] += by_z[v]
            for copy in copies_c(i, 1) if stage == 1 else [copy_b(i)]:
                copy.start()
        elif stage == 1:
            copy_b(i).wait_recv()
            by_y[...] += sums[y]
            copies_c(i, 0)[0].start()
        elif stage == 2:
            copies_c(i, 0)[0].wait_recv()
            by_y[mine] += by_z[0:2]
            copies_c(i, 1)[0].start()
        else:
            if i in z_first:
                copy_b(i).wait_recv()
                total = sums[y, place].astype(f32) + by_z[2].astype(f32)
            else:
                copies_c(i, 1)[0].wait_recv()
                total = by_y[place].astype(f32) + by_z[2].astype(f32)
            by_z[0] = total.astype(bf16)
            copy_g(i).start()
            keep_g(i).start()

    for name in ("sums", "dy", "down", "slope", "up", "act_other", "second_t", "resid", "lse", "att_t"):
        local(name).start()
    greet(group + line)
    local("sums").wait()

    def ready_units():
        for name in ("dy", "down", "slope"):
            local(name).wait()

    tile = 256

    def d_units(begin, end):
        def body(i, carry):
            at = aligned(i, tile)
            value = dot_nt(dy[...].reshape(length, width), wd[at, :]) * wide[:, at].astype(f32)
            low = value.astype(bf16)
            wide[:, at] = low
            bias_sum[:, at] = jnp.sum(low.astype(f32), axis=0, keepdims=True)
            return carry

        lax.fori_loop(begin, end, body, 0)

    def times_up(rows, write):
        def body(i, carry):
            at = aligned(i, tile)
            write(at, dot_nt(wide[rows, :], wu[at, :]))
            return carry

        lax.fori_loop(0, width // tile, body, 0)

    def d_second_other(part):
        if part == 0:
            local("up").wait()

        def write(at, value):
            x_out0[part_at(part), at] = value.astype(bf16)

        times_up(pl.ds(pl.multiple_of(other * own_rows + part * part_rows, 64), part_rows), write)

    def exchange(part, index):
        return remote(x_out0.at[part_at(part)], x_in0.at[part_at(part)], x_send, x_recv, index, peer_x)

    second_x = [exchange(part, part) for part in range(2)]
    normed_x = [exchange(part, 2 + part) for part in range(2)]
    down_x = remote(dy.at[other], x_in1, x_send, x_recv, 4, peer_x)
    att_x = [
        remote(
            x_out0.at[:, pl.ds(p * PAIR, PAIR)], d_att.at[half_rows(piece), pl.ds(p * PAIR, PAIR)],
            x_send, x_recv, 5 + p, peer_x,
        )
        for p in range(pairs)
    ]

    def d_second_own():
        def write(at, value):
            first[:, at] = value

        times_up(half_rows(piece), write)
        local("qkv").start()

    def down_part(target):
        def body(i, carry):
            at = aligned(i, tile)
            target[:, at] = dot_nn(half_act[...], wd[:, at]).astype(bf16)
            return carry

        lax.fori_loop(0, width // tile, body, 0)

    def down_other():
        local("act_other").wait()
        down_part(dy.at[other])
        local("act_own").start()

    def down_mine():
        local("act_own").wait()
        down_part(down_own)
        local("out").start()
        local("normed_t").start()

    def chunk(i, left, right):
        grad_chunk(parts.at[i % SLOTS], left, right)
        copy_a(i).start()

    def grad_up(i):
        if i == 0:
            local("second_t").wait()
        left = lambda j: lhs[pl.ds(8 * j, 8)].reshape(8 * lhs.shape[1], length)
        chunk(4 + i, left, lambda: wide[:, i * UNIT : (i + 1) * UNIT])
        if i == 3:
            local("packed").start()

    mask = lhs.at[:, pl.ds(0, length // lhs.shape[0]), :]
    step = 64

    def back_two(part):
        if part == 0:
            local("resid").wait()
        second_x[part].wait_recv()

        def body(i, carry):
            rows = aligned(i, step)
            grad = first[rows, :] + x_in0[rows, :].astype(f32)
            d_values, d_gain, d_shift = norm_back(second[rows, :], second_gain, grad)
            total = dy[piece, rows, :].astype(f32) + d_values
            first[rows, :] = total
            branch[rows, :] = total.astype(bf16)
            early[0:1, :] += d_gain
            early[1:2, :] += d_shift
            return carry

        steps_each = part_rows // step
        if part == 0:
            early[...] = jnp.zeros_like(early)
        lax.fori_loop(part * steps_each, (part + 1) * steps_each, body, 0)

    def d_attended(half):
        rows = pl.ds(pl.multiple_of(half * d_width, 128), d_width)
        return dot_nt(branch[...], wd[rows, :]).astype(bf16)

    def d_att_other():
        local("out").wait()
        for copy in second_x:
            copy.wait_send()
        x_out0[:, :d_width] = d_attended(other)

    def d_att_own():
        d_att[half_rows(piece), :] = d_attended(piece)

    def grad_out(i):
        if i == 0:
            local("att_t").wait()
        left = lambda j: att_t[pl.ds(8 * j, 8)].reshape(8 * att_t.shape[1], own_rows)
        chunk(8 + i, left, lambda: branch[:, i * UNIT : (i + 1) * UNIT])
        if i == 1:
            local("hidden").start()

    first_lanes = head_lanes(PAIR)
    query_chunk = 256

    def pair_cols(p):
        return tuple(slice(t * d_width + PAIR * p, t * d_width + PAIR * (p + 1)) for t in range(3))

    def att_here(p):
        if p == 0:
            for name in ("lse", "packed", "normed_t"):
                local(name).wait()
        att_x[p].wait_recv()
        acc_k[...] = jnp.zeros_like(acc_k)
        acc_v[...] = jnp.zeros_like(acc_v)

    def attend_back(p, i):
        at_q, at_k, at_v = pair_cols(p)
        keys_t = wide[:, at_k].T
        rows = slice(i * query_chunk, (i + 1) * query_chunk)
        keys = wide[:, at_k]
        values = wide[:, at_v]
        queries = wide[rows, at_q]
        grads = d_att[rows, p * PAIR : (p + 1) * PAIR]
        blocked = mask[:, :, rows].reshape(length, query_chunk).astype(f32)
        parts_q = []
        for h in range(2):
            one_q = jnp.where(first_lanes[h], queries, jnp.zeros_like(queries))
            one_g = jnp.where(first_lanes[h], grads, jnp.zeros_like(grads))
            scores = dot_nt(keys, one_q) + (blocked - lse[2 * p + h : 2 * p + h + 1, rows])
            probs = jnp.exp(scores)
            d_probs = dot_nt(values, one_g)
            dots = jnp.sum(probs * d_probs, axis=0, keepdims=True)
            d_scores = (probs * (d_probs - dots)).astype(bf16)
            acc_v[...] += dot_nn(probs.astype(bf16), one_g)
            acc_k[...] += dot_nn(d_scores, one_q)
            parts_q.append(dot_nn(keys_t[h * HEAD_DIM : (h + 1) * HEAD_DIM], d_scores))
        d_queries = jnp.concatenate(parts_q, axis=0).T * HEAD_DIM ** (-0.5)
        wide[rows, at_q] = d_queries.astype(bf16)
        if i == length // query_chunk - 1:
            wide[:, at_k] = acc_k[...].astype(bf16)
            wide[:, at_v] = acc_v[...].astype(bf16)

    def grad_pair(p):
        n = 8 * parts.shape[4]
        left = lambda j: wd[pl.ds(pl.multiple_of(width + j * n, 64), n), :length]
        chunk(10 + p, left, lambda: jnp.concatenate([wide[:, at] for at in pair_cols(p)], axis=1))

    def write_output():
        def body(i, carry):
            rows = aligned(i, step)
            second[rows, :] += down_own[rows, :].astype(f32) + x_in1[rows, :].astype(f32)
            return carry

        lax.fori_loop(0, own_rows // step, body, 0)
        local("output").start()

    def times_qkv(rows, write):
        def body(i, carry):
            at = aligned(i, tile)
            write(at, dot_nt(wide[rows, :cols], wu[at, :cols]))
            return carry

        lax.fori_loop(0, width // tile, body, 0)

    def d_normed_other(part):
        if part == 0:
            local("qkv").wait()
            for copy in att_x:
                copy.wait_send()

        def write(at, value):
            x_out0[part_at(part), at] = value.astype(bf16)

        times_qkv(pl.ds(pl.multiple_of(other * own_rows + part * part_rows, 64), part_rows), write)

    def d_normed_own():
        local("output").wait()

        def write(at, value):
            second[:, at] = value

        times_qkv(half_rows(piece), write)

    def back_one(part):
        if part == 0:
            local("hidden").wait()
            late[...] = jnp.zeros_like(late)
        normed_x[part].wait_recv()

        def body(i, carry):
            rows = aligned(i, step)
            grad = second[rows, :] + x_in0[rows, :].astype(f32)
            d_values, d_gain, d_shift = norm_back(branch[rows, :].astype(f32), first_gain, grad)
            first[rows, :] += d_values
            late[0:1, :] += d_gain
            late[1:2, :] += d_shift
            return carry

        steps_each = part_rows // step
        lax.fori_loop(part * steps_each, (part + 1) * steps_each, body, 0)
        if part == 1:
            local("grad_hidden").start()

    def small_near(value, near_slots, base):
        own_slot = 2 * y + core
        return [
            remote(value, near_slots.at[own_slot], s_send, s_recv, base + k, peer) for k, peer in enumerate(group)
        ]

    def small_line(all_slots, base):
        own_slot = z * 2 + piece
        return [
            remote(all_slots.at[own_slot], all_slots.at[own_slot], s_send, s_recv, base + 3 + k, peer)
            for k, peer in enumerate(line)
        ]

    def small_one(value, near_slots, base):
        near_slots[2 * y + core] = value[...]
        for copy in small_near(value, near_slots, base):
            copy.start()

    def small_two(value, near_slots, all_slots, base):
        for copy in small_near(value, near_slots, base):
            copy.wait()
        all_slots[z * 2 + piece] = ((near_slots[0] + near_slots[1]) + near_slots[2]) + near_slots[3]
        for copy in small_line(all_slots, base):
            copy.start()

    def small_three(all_slots, base, at):
        for copy in small_line(all_slots, base):
            copy.wait()
        n = all_slots.shape[1]
        for x in range(2):
            total = ((all_slots[x] + all_slots[2 + x]) + all_slots[4 + x]) + all_slots[6 + x]
            small[x, at : at + n, :] = total

    def early_one():
        early[2:3, :] = bias_sum[:, :width]
        early[3:4, :] = bias_sum[:, width:]
        small_one(early, early_near, 0)

    call = functools.partial
    steps = [ready_units, call(d_units, 0, 3), call(d_units, 3, 6), call(d_units, 6, 10)]
    for part in range(2):
        steps += [call(d_second_other, part), second_x[part].start]
    steps += [call(grad_up, 0), call(grad_up, 1), d_second_own, down_other, call(grad_up, 2), call(grad_up, 3), down_mine]
    steps += [call(write_mask, starts, mask), call(back_two, 0), call(back_two, 1), d_att_other]
    steps += [copy.start for copy in att_x]
    steps += [d_att_own, down_x.start, early_one, call(grad_out, 0), call(grad_out, 1)]
    for p in range(pairs):
        steps += [call(att_here, p)] + [call(attend_back, p, i) for i in range(length // query_chunk)]
        if p < 3:
            steps += [call(grad_pair, p)]
        if p == 1:
            steps += [call(small_two, early, early_near, early_all, 0)]
    for part in range(2):
        steps += [call(d_normed_other, part), normed_x[part].start]
    steps += [call(grad_pair, 3), call(grad_pair, 4), down_x.wait_recv, write_output, d_normed_own]
    steps += [call(back_one, 0), call(back_one, 1), call(small_one, late, late_near, 10)]
    steps += [call(small_three, early_all, 0, 2), call(small_two, late, late_near, late_all, 10)]
    steps += [call(small_three, late_all, 10, 0)]
    for i, one in enumerate(steps):
        for where in BACKWARD_MOVES[i]:
            move(*where)
        one()
    small_keep = pltpu.make_async_copy(small, small_out, keep_sem.at[chunks])
    small_keep.start()
    for where in BACKWARD_MOVES[len(steps)]:
        move(*where)
    for i in range(chunks):
        copy_b(i).wait_send()
        for copy in copies_c(i, 0) + copies_c(i, 1):
            copy.wait_send()
        copy_g(i).wait()
        keep_g(i).wait()
    small_keep.wait()
    down_x.wait_send()
    for copy in normed_x:
        copy.wait_send()
    local("grad_hidden").wait()


def backward(starts, gain1, gain2, hidden, dy_all, q_all, o_all, u_all, d_all, *kept):
    bf16, f32 = jnp.bfloat16, jnp.float32
    _, own_rows, width = dy_all.shape
    length = 2 * own_rows
    cols, units = q_all.shape[1], u_all.shape[1]
    rows = width // 16
    wide_units, pairs = 10, cols // (3 * PAIR)
    pair_cols = 3 * PAIR
    outs = [
        ((own_rows, width), f32),
        ((own_rows, width), f32),
        ((2, wide_units, rows, UNIT), bf16),
        ((2, pairs, rows, pair_cols), bf16),
        ((2, 6, width), f32),
    ]
    token = ((own_rows, width), bf16)
    scratch = [
        ((16, rows, length), bf16),
        ((16, rows, own_rows), bf16),
        ((own_rows, units), bf16),
        ((length, units), bf16),
        ((units, width), bf16),
        ((width, units), bf16),
        ((2, own_rows, width), bf16),
        ((own_rows, width), f32),
        ((own_rows, width), f32),
        ((length, cols // 3), bf16),
        token, token, token, token,
        ((SLOTS, 2, 2, ROWS_Z, rows, UNIT), bf16),
        ((wide_units, 2, ROWS_Z, rows, UNIT), bf16),
        ((pairs, 2, ROWS_Z, rows, pair_cols), bf16),
        ((wide_units, ROWS_Z, rows, UNIT), bf16),
        ((pairs, ROWS_Z, rows, pair_cols), bf16),
        ((wide_units, 3, rows, UNIT), bf16),
        ((pairs, 3, rows, pair_cols), bf16),
        ((16, length), f32),
        ((length, PAIR), f32),
        ((length, PAIR), f32),
        ((1, units), f32),
        ((4, width), f32),
        ((2, width), f32),
        ((4, 4, width), f32),
        ((4, 2, width), f32),
        ((8, 4, width), f32),
        ((8, 2, width), f32),
        ((2, 6, width), f32),
    ]
    vmem = pl.BlockSpec(memory_space=pltpu.VMEM)
    anywhere = pl.BlockSpec(memory_space=pl.ANY)
    smem = pl.BlockSpec(memory_space=pltpu.SMEM)
    chunks = wide_units + pairs
    dma = lambda n: pltpu.SemaphoreType.DMA((n,))
    sems = [18] + [chunks] * 4 + [4 * chunks] * 2 + [chunks] * 2 + [5 + pairs] * 2 + [20, 20, chunks + 1]
    return pl.pallas_call(
        backward_kernel,
        out_shape=[jax.ShapeDtypeStruct(shape, kind) for shape, kind in outs],
        in_specs=[smem, vmem, vmem] + [anywhere] * (6 + len(kept)),
        out_specs=[anywhere] * len(outs),
        scratch_shapes=[pltpu.VMEM(shape, kind) for shape, kind in scratch] + [dma(n) for n in sems],
        compiler_params=pltpu.CompilerParams(
            collective_id=2, has_side_effects=True, vmem_limit_bytes=60 * 1024 * 1024
        ),
        name="backward",
    )(starts, gain1, gain2, hidden, dy_all, q_all, o_all, u_all, d_all, *kept)


def finish_kernel(
    raw_output, raw_grad, units_lo, units_hi, pairs_in, small,
    output, grad_hidden, qkv, out, up, down, gain1, shift1, gain2, shift2, bias,
):
    f32 = jnp.float32
    step = pl.program_id(0)
    output[0] = raw_output[...]
    grad_hidden[0] = raw_grad[...]
    rows = out.shape[0]
    width = small.shape[2]
    units_in = (units_lo, units_hi)

    def mixed(first, second):
        each = first.shape[1] // 4
        blocks = []
        for j in range(4):
            at = slice(j * each, (j + 1) * each)
            blocks += [first[:, at].astype(f32), second[:, at].astype(f32)]
        return jnp.concatenate(blocks, axis=1)

    for now in range(2):

        @pl.when(step == now)
        def _():
            for i in range(4):
                h, column = divmod(i, 2)
                at = slice(column * UNIT, (column + 1) * UNIT)
                down[h * rows : (h + 1) * rows, at] = units_in[now][0, i].astype(f32)
            for i in range(2):
                chunk = 4 + 2 * now + i
                at = slice(i * 2 * UNIT, (i + 1) * 2 * UNIT)
                up[:, at] = mixed(units_lo[0, chunk], units_hi[0, chunk])
            out[...] = units_lo[0, 8 + now].astype(f32) + units_hi[0, 8 + now].astype(f32)
            pairs = pairs_in.shape[1]
            for block in range(3 * now, 3 * now + 3):
                part, piece = divmod(block, 2)
                for p in range(pairs):
                    at = (block - 3 * now) * pairs * PAIR + p * PAIR
                    chunk = pairs_in[piece, p, :, part * PAIR : (part + 1) * PAIR]
                    qkv[:, at : at + PAIR] = chunk.astype(f32)

    @pl.when(step == 0)
    def _():
        for i, ref in enumerate((gain1, shift1, gain2, shift2)):
            ref[...] = (small[0, i : i + 1, :] + small[1, i : i + 1, :]).reshape(width)
        for g in range(2):
            for j in range(2):
                at = slice(j * UNIT, (j + 1) * UNIT)
                lo, hi = small[0, 4 + g : 5 + g, at], small[1, 4 + g : 5 + g, at]
                begin = (2 * g + j) * 2 * UNIT
                bias[begin : begin + 2 * UNIT] = mixed(lo, hi).reshape(2 * UNIT)


def finish(raw_output, raw_grad, units_in, pairs_in, small):
    f32 = jnp.float32
    own_rows, width = raw_output.shape
    rows = units_in.shape[2]
    shapes = [
        (1, own_rows, width), (1, own_rows, width), (rows, 3 * width), (rows, width), (rows, 8 * UNIT),
        (4 * rows, width), (width,), (width,), (width,), (width,), (8 * UNIT,),
    ]
    token = pl.BlockSpec((own_rows // 2, width), lambda s: (s, 0))
    token_out = pl.BlockSpec((1, own_rows // 2, width), lambda s: (0, s, 0))
    columns = lambda n: pl.BlockSpec((rows, n // 2), lambda s: (0, s))
    fixed = lambda shape: pl.BlockSpec(shape, lambda s: (0,) * len(shape))
    half = lambda i: pl.BlockSpec((1,) + units_in.shape[1:], lambda s: (i, 0, 0, 0))
    return pl.pallas_call(
        finish_kernel,
        grid=(2,),
        out_shape=[jax.ShapeDtypeStruct(shape, f32) for shape in shapes],
        in_specs=[token, token, half(0), half(1), fixed(pairs_in.shape), fixed(small.shape)],
        out_specs=[
            token_out, token_out, columns(3 * width), columns(width), columns(8 * UNIT),
            pl.BlockSpec((2 * rows, width), lambda s: (s, 0)),
        ] + [fixed(shape) for shape in shapes[6:]],
        compiler_params=pltpu.CompilerParams(vmem_limit_bytes=60 * 1024 * 1024),
        name="finish",
    )(raw_output, raw_grad, units_in, units_in, pairs_in, small)


def split_layer(
    hidden, starts, first_gain, first_shift, qkv_weight, out_weight, second_gain, second_shift,
    up_weight, hidden_bias, down_weight, cotangent,
):
    shards = lax.axis_size("rows")
    (
        qkv_all, out_all, up_all, down_all, dy_all, down_sums, normed_t, packed, lse, att_t, residual, second_t,
        activated, slope,
    ) = forward(
        hidden[0], cotangent[0], starts, first_gain, first_shift, second_gain, second_shift, hidden_bias,
        qkv_weight, out_weight, up_weight, down_weight,
    )
    whole = lambda w: w.reshape(-1, w.shape[-1])
    blocks = lambda w: w.reshape(shards, -1, w.shape[-1])
    shares = backward(
        starts, first_gain, second_gain, hidden[0], dy_all, whole(qkv_all), whole(out_all),
        whole(up_all), whole(down_all), down_sums, normed_t, packed, lse, blocks(att_t), residual,
        blocks(second_t), activated, slope,
    )
    return tuple(finish(*shares))


def splits_evenly(mesh):
    pieces = mesh.shape["blk"]
    return pieces == 2 and mesh.shape["rows"] == 2 * ROWS_Z * ROWS_Y and HEADS % (2 * pieces) == 0


def solution(mesh):
    in_specs = (
        P("rows", "blk", None),
        P("rows", None),
        P(),
        P(),
        P("rows", None),
        P("rows", None),
        P(),
        P(),
        P("rows", None),
        P(),
        P("rows", None),
        P("rows", "blk", None),
    )
    out_specs = (
        P("rows", "blk", None),
        P("rows", "blk", None),
        P("rows", None),
        P("rows", None),
        P("rows", None),
        P("rows", None),
        P(),
        P(),
        P(),
        P(),
        P(),
    )
    layer = split_layer if splits_evenly(mesh) else on_device
    return jax.shard_map(
        layer, mesh=mesh, in_specs=in_specs, out_specs=out_specs, check_vma=False
    )
```

```python
import functools
import math

import jax
import jax.numpy as jnp
from jax import lax
from jax.experimental import pallas as pl
from jax.experimental.pallas import tpu as pltpu
from jax.sharding import PartitionSpec as P

HEADS = 20
HEAD_DIM = 64


masked_score = -1e30
block_limit = 512


def layer_norm(values, gain, shift):
    mean_value = jnp.mean(values, axis=-1, keepdims=True)
    centred = values - mean_value
    variance = jnp.mean(centred * centred, axis=-1, keepdims=True)
    return centred * lax.rsqrt(variance + 1e-05) * gain + shift


def segment_of(starts_row, positions):
    reached = starts_row[None, :] <= positions[:, None]
    return jnp.sum(reached.astype(jnp.int32), axis=1) - 1


def scores_with_mask(queries, key_block, query_seg, key_seg):
    products = jnp.einsum("qhe,khe->hqk", queries, key_block, preferred_element_type=jnp.float32)
    products = products * queries.shape[2] ** (-0.5)
    allowed = (query_seg[:, None] == key_seg[None, :])[None, :, :]
    return (jnp.where(allowed, products, masked_score), allowed)


def attend_rows(running, key_rows, value_rows, queries, query_seg, starts_row):
    piece_rows = key_rows.shape[0]
    step_rows = math.gcd(piece_rows, block_limit)
    head_count = queries.shape[1]
    head_width = queries.shape[2]

    def one_block(block_index, state):
        row_top, denominator, weighted = state
        block_start = block_index * step_rows
        key_block = lax.dynamic_slice_in_dim(key_rows, block_start, step_rows, 0).reshape(
            step_rows, head_count, head_width
        )
        value_block = lax.dynamic_slice_in_dim(value_rows, block_start, step_rows, 0).reshape(
            step_rows, head_count, head_width
        )
        key_seg = segment_of(starts_row, block_start + jnp.arange(step_rows, dtype=jnp.int32))
        scores, allowed = scores_with_mask(queries, key_block, query_seg, key_seg)
        new_top = jnp.maximum(row_top, jnp.max(scores, axis=-1))
        factor = jnp.exp(row_top - new_top)
        weights = jnp.where(allowed, jnp.exp(scores - new_top[:, :, None]), 0.0)
        denominator = denominator * factor + jnp.sum(weights, axis=-1)
        weighted = weighted * factor[:, :, None] + jnp.einsum(
            "hqk,khe->hqe",
            weights.astype(jnp.bfloat16),
            value_block,
            preferred_element_type=jnp.float32,
        )
        return (new_top, denominator, weighted)

    return lax.fori_loop(0, piece_rows // step_rows, one_block, running)


def on_device(
    hidden,
    starts,
    first_gain,
    first_shift,
    qkv_weight,
    out_weight,
    second_gain,
    second_shift,
    up_weight,
    hidden_bias,
    down_weight,
    cotangent,
):
    rows_here = hidden.shape[1]
    model_width = hidden.shape[2]
    head_count = HEADS
    head_width = HEAD_DIM
    score_scale = head_width ** (-0.5)
    inputs = hidden[0].astype(jnp.float32)
    starts_row = starts[0]
    offset = lax.axis_index("blk") * rows_here
    query_seg = segment_of(starts_row, offset + jnp.arange(rows_here, dtype=jnp.int32))
    qkv_full, out_full, up_full, down_full = (
        lax.all_gather(qkv_weight, "rows", axis=0, tiled=True),
        lax.all_gather(out_weight, "rows", axis=0, tiled=True),
        lax.all_gather(up_weight, "rows", axis=0, tiled=True),
        lax.all_gather(down_weight, "rows", axis=0, tiled=True),
    )
    normed_low = layer_norm(inputs, first_gain, first_shift).astype(jnp.bfloat16)
    packed = jnp.dot(normed_low, qkv_full, preferred_element_type=jnp.float32).astype(jnp.bfloat16)
    queries = packed[:, :model_width].reshape(rows_here, head_count, head_width)
    key_rows = packed[:, model_width : 2 * model_width]
    value_rows = packed[:, 2 * model_width :]
    initial = (
        jnp.full((head_count, rows_here), masked_score, jnp.float32),
        jnp.zeros((head_count, rows_here), jnp.float32),
        jnp.zeros((head_count, rows_here, head_width), jnp.float32),
    )
    row_top, denominator, weighted = attend_rows(
        initial,
        lax.all_gather(key_rows, "blk", axis=0, tiled=True),
        lax.all_gather(value_rows, "blk", axis=0, tiled=True),
        queries,
        query_seg,
        starts_row,
    )
    log_total = row_top + jnp.log(denominator)
    attended = jnp.transpose(weighted / denominator[:, :, None], (1, 0, 2))
    attended_low = attended.reshape(rows_here, model_width).astype(jnp.bfloat16)
    residual = inputs + jnp.dot(attended_low, out_full, preferred_element_type=jnp.float32)
    second_low = layer_norm(residual, second_gain, second_shift).astype(jnp.bfloat16)
    up_values = jnp.dot(second_low, up_full, preferred_element_type=jnp.float32) + hidden_bias
    activated_low = jax.nn.gelu(up_values, approximate=False).astype(jnp.bfloat16)
    output = residual + jnp.dot(activated_low, down_full, preferred_element_type=jnp.float32)
    cot_low = cotangent[0]
    d_activated = jnp.einsum("tc,fc->tf", cot_low, down_full, preferred_element_type=jnp.float32)
    unused_gelu, gelu_pull = jax.vjp(
        lambda values: jax.nn.gelu(values, approximate=False), up_values
    )
    d_up_low = gelu_pull(d_activated)[0].astype(jnp.bfloat16)
    d_second = jnp.einsum("tf,cf->tc", d_up_low, up_full, preferred_element_type=jnp.float32)
    unused_second, second_pull = jax.vjp(layer_norm, residual, second_gain, second_shift)
    d_norm_two, d_second_gain, d_second_shift = second_pull(d_second)
    d_residual = cot_low.astype(jnp.float32) + d_norm_two
    d_branch_low = d_residual.astype(jnp.bfloat16)
    d_attended_low = jnp.einsum(
        "tc,kc->tk", d_branch_low, out_full, preferred_element_type=jnp.float32
    ).astype(jnp.bfloat16)
    d_attended3 = d_attended_low.reshape(rows_here, head_count, head_width)
    row_dots = jnp.einsum("qhe,qhe->hq", d_attended3.astype(jnp.float32), attended)
    keys_all, values_all = (
        lax.all_gather(key_rows, "blk", axis=0, tiled=True),
        lax.all_gather(value_rows, "blk", axis=0, tiled=True),
    )
    length = keys_all.shape[0]
    step_rows = math.gcd(length, block_limit)

    def block_terms(block_index):
        block_start = block_index * step_rows
        key_block = lax.dynamic_slice_in_dim(keys_all, block_start, step_rows, 0).reshape(
            step_rows, head_count, head_width
        )
        value_block = lax.dynamic_slice_in_dim(values_all, block_start, step_rows, 0).reshape(
            step_rows, head_count, head_width
        )
        key_seg = segment_of(starts_row, block_start + jnp.arange(step_rows, dtype=jnp.int32))
        scores, allowed = scores_with_mask(queries, key_block, query_seg, key_seg)
        probability = jnp.where(allowed, jnp.exp(scores - log_total[:, :, None]), 0.0)
        d_probs = jnp.einsum(
            "qhe,khe->hqk", d_attended3, value_block, preferred_element_type=jnp.float32
        )
        d_scores = (probability * (d_probs - row_dots[:, :, None])).astype(jnp.bfloat16)
        return (key_block, probability, d_scores)

    dq_start = jnp.zeros((rows_here, head_count, head_width), jnp.float32)

    def back_block(dq_sum, block_index):
        key_block, probability, d_scores = block_terms(block_index)
        dq_sum = dq_sum + jnp.einsum(
            "hqk,khe->qhe", d_scores, key_block, preferred_element_type=jnp.float32
        )
        dk_block = (
            jnp.einsum("hqk,qhe->khe", d_scores, queries, preferred_element_type=jnp.float32)
            * score_scale
        )
        dv_block = jnp.einsum(
            "hqk,qhe->khe",
            probability.astype(jnp.bfloat16),
            d_attended3,
            preferred_element_type=jnp.float32,
        )
        return (
            dq_sum,
            (dk_block.reshape(step_rows, model_width), dv_block.reshape(step_rows, model_width)),
        )

    dq_sum, (dk_terms, dv_terms) = lax.scan(back_block, dq_start, jnp.arange(length // step_rows))
    dk_rows, dv_rows = (
        lax.psum_scatter(
            dk_terms.reshape(length, model_width).astype(jnp.bfloat16),
            "blk",
            scatter_dimension=0,
            tiled=True,
        ).astype(jnp.float32),
        lax.psum_scatter(
            dv_terms.reshape(length, model_width).astype(jnp.bfloat16),
            "blk",
            scatter_dimension=0,
            tiled=True,
        ).astype(jnp.float32),
    )
    d_packed = jnp.concatenate(
        [(dq_sum * score_scale).reshape(rows_here, model_width), dk_rows, dv_rows], axis=1
    ).astype(jnp.bfloat16)
    d_normed = jnp.einsum("tn,cn->tc", d_packed, qkv_full, preferred_element_type=jnp.float32)
    unused_first, first_pull = jax.vjp(layer_norm, inputs, first_gain, first_shift)
    d_norm_one, d_first_gain, d_first_shift = first_pull(d_normed)
    grad_hidden = d_residual + d_norm_one
    d_bias = jnp.sum(d_up_low, axis=0, dtype=jnp.float32)
    wide_share = lax.psum_scatter(
        jnp.concatenate(
            [
                jnp.einsum("tc,tn->cn", normed_low, d_packed, preferred_element_type=jnp.float32),
                jnp.einsum(
                    "tc,tn->cn", attended_low, d_branch_low, preferred_element_type=jnp.float32
                ),
                jnp.einsum("tc,tn->cn", second_low, d_up_low, preferred_element_type=jnp.float32),
            ],
            axis=1,
        ).astype(jnp.bfloat16),
        "rows",
        scatter_dimension=0,
        tiled=True,
    )
    down_share = lax.psum_scatter(
        jnp.einsum("tf,tn->fn", activated_low, cot_low, preferred_element_type=jnp.float32).astype(
            jnp.bfloat16
        ),
        "rows",
        scatter_dimension=0,
        tiled=True,
    )
    wide_grads, down_grads = (
        lax.psum(wide_share, "blk").astype(jnp.float32),
        lax.psum(down_share, "blk").astype(jnp.float32),
    )
    grad_qkv = wide_grads[:, : 3 * model_width]
    grad_out = wide_grads[:, 3 * model_width : 4 * model_width]
    grad_up = wide_grads[:, 4 * model_width :]
    small_grads = lax.psum(
        (d_first_gain, d_first_shift, d_second_gain, d_second_shift, d_bias), ("rows", "blk")
    )
    return (
        output[None],
        grad_hidden[None],
        grad_qkv,
        grad_out,
        grad_up,
        down_grads,
        small_grads[0],
        small_grads[1],
        small_grads[2],
        small_grads[3],
        small_grads[4],
    )


MESH = pl.DeviceIdType.MESH
FORWARD_MOVES = (
    ((0, 0), (1, 0), (2, 0), (0, 1), (1, 1), (2, 1),),
    (),
    (),
    (),
    (),
    (),
    ((2, 3),),
    (),
    (),
    (),
    ((3, 0, 1, 0), (4, 0, 0), (4, 1, 0), (3, 0, 0, 0), (3, 1, 1, 0), (4, 0, 2), (3, 1, 0, 0), (0, 2), (2, 2), (4, 0, 1), (3, 0, 2, 0), (4, 1, 2), (3, 1, 2, 0), (1, 2), (4, 1, 1), (2, 5),),
    (),
    (),
    ((4, 0, 3), (3, 2, 1, 0), (2, 4), (4, 1, 3), (3, 2, 0, 0),),
    (),
    (),
    ((4, 2, 0), (0, 3),),
    ((3, 2, 2, 0), (4, 2, 2), (1, 3),),
    (),
    (),
    (),
    (),
    (),
    (),
    ((4, 2, 1),),
    (),
    (),
    (),
    (),
    (),
    ((3, 3, 1, 0), (4, 2, 3),),
    (),
    (),
    ((3, 3, 0, 0), (4, 3, 0),),
    (),
    (),
    (),
    (),
    (),
    (),
    ((4, 3, 2), (3, 3, 2, 0), (0, 4), (1, 5), (3, 4, 1, 0), (4, 3, 1), (1, 4), (3, 4, 0, 0), (4, 3, 3), (0, 5), (3, 4, 2, 0),),
    (),
    (),
    ((4, 5, 0),),
    ((3, 5, 1, 0),),
    (),
    (),
    ((4, 4, 2),),
    (),
    (),
    ((3, 5, 0, 0),),
    (),
    ((4, 4, 0),),
    (),
    ((3, 5, 1, 1),),
    (),
    ((4, 4, 1),),
    (),
    ((3, 5, 0, 1),),
    ((4, 4, 3),),
    (),
    (),
    ((3, 5, 2, 0),),
    (),
    (),
    (),
    (),
    ((3, 5, 2, 1),),
    (),
    (),
    (),
    (),
    (),
)
ROWS_Z, ROWS_Y = 4, 2
PAIR = 128
UNIT = 640
SLOTS = 2
SPARE = 3


def place_of():
    index = lax.axis_index("rows")
    return index // 4, lax.rem(index // 2, 2), lax.rem(index, 2)


def row_of(z, y, core):
    return (lax.rem(z + ROWS_Z, ROWS_Z) * ROWS_Y + y) * 2 + core


def aligned(index, step):
    return pl.ds(pl.multiple_of(index * step, step), step)


def dot_nt(left, right):
    return lax.dot_general(left, right, (((1,), (1,)), ((), ())), preferred_element_type=jnp.float32)


def dot_nn(left, right):
    return jnp.dot(left, right, preferred_element_type=jnp.float32)


def head_lanes(width):
    lane = lax.broadcasted_iota(jnp.int32, (1, width), 1)
    return (lane < HEAD_DIM, lane >= HEAD_DIM)


def greet(peers):
    barrier = pltpu.get_barrier_semaphore()
    for peer in peers:
        pl.semaphore_signal(barrier, inc=1, device_id=peer, device_id_type=MESH)
    pl.semaphore_wait(barrier, len(peers))


def neighbours():
    z, y, core = place_of()
    return [
        {"rows": row_of(z + 1, y, core)},
        {"rows": row_of(z + 2, y, core)},
        {"rows": row_of(z + 3, y, core)},
        {"rows": row_of(z, 1 - y, core)},
        {"rows": row_of(z, y, 1 - core)},
        {"blk": 1 - lax.axis_index("blk")},
    ]


def write_marks(starts_ref, key_marks, query_marks):
    shape = key_marks.shape
    at = lax.broadcasted_iota(jnp.int32, shape, 0)
    lane = lax.broadcasted_iota(jnp.int32, shape, 1)
    lane = jnp.where(lane < HEAD_DIM, lane, lane - HEAD_DIM) - SPARE
    cell = jnp.zeros(shape, jnp.int32) - 1
    for i in range(starts_ref.shape[1]):
        cell += (at >= starts_ref[0, i]).astype(jnp.int32)
    key_marks[...] = jnp.where((lane == cell) | (lane < 0), 1.0, 0.0).astype(key_marks.dtype)
    blocked = (lane != cell) & (lane >= 0) & (lane < starts_ref.shape[1])
    query_marks[...] = jnp.where(blocked, masked_score, 0.0).astype(query_marks.dtype)


def z_place(z):
    return 2 * lax.rem(z, 2) + z // 2


def grad_chunk(target, left, right):
    def half(j, carry):
        value = dot_nn(left(j), right()).astype(jnp.bfloat16)
        n = value.shape[1]
        rows = value.shape[0] // 8
        for block in range(8):
            to_z, to_y, to_core = block // 4, block // 2 % 2, block % 2
            target[to_core, to_y, 2 * to_z + j, :, :n] = value[block * rows : (block + 1) * rows]
        return carry

    lax.fori_loop(0, 2, half, 0)


def forward_kernel(
    hidden, cot, starts, gain1, shift1, gain2, shift2, bias_in, q_in, o_in, u_in, d_in,
    q_all, o_all, u_all, d_all, dy_all, down_sums, normed_t_out, packed_out, lse_out, att_out, att_t_out, resid_out,
    second_t_out, act_out, slope_out,
    hid_other, normed, wq, wo, wu, packed, key_marks, query_marks, att_part, att_own, resid, second,
    act, act_t, slope, normed_t, att_t, second_t, lse, lse_t, u_wide, q_own, o_own, u_own, d_own, dy, bias, parts, core_in,
    local_sem, send_sem, recv_sem, x_send, x_recv,
):
    bf16 = jnp.bfloat16
    z, y, core = place_of()
    me = row_of(z, y, core)
    piece = lax.axis_index("blk")
    other = 1 - piece
    own_rows, width = hidden.shape
    length = packed.shape[0]
    rows = o_own.shape[0]
    early = rows * 3 // 5
    d_half = lambda half: pl.ds(half * rows, rows)
    own = (
        q_own.at[pl.ds(0, early)], q_own.at[pl.ds(early, rows - early)], o_own, u_own,
        d_own.at[d_half(0)], d_own.at[d_half(1)],
    )
    last = len(own) - 1

    def slot_of(w, at_z, at_y, at_core):
        slot = row_of(at_z, at_y, at_core)
        if w < 2:
            return q_all.at[slot, pl.ds(w * early, own[w].shape[0])]
        if w < 4:
            return (o_all, u_all)[w - 2].at[slot]
        return d_all.at[slot, d_half(w - 4)]

    x_peer = {"blk": other}
    peers = neighbours()
    pairs = packed.shape[1] // (3 * PAIR)
    first_gain, first_shift, second_gain, second_shift = (
        ref[...].reshape(1, width) for ref in (gain1, shift1, gain2, shift2)
    )

    def local(src, dst, index):
        return pltpu.make_async_copy(src, dst, local_sem.at[index])

    near = z + 1 - 2 * lax.rem(z, 2)
    far = lax.rem(z + 2, ROWS_Z)
    spread = (z, far, near, ROWS_Z - 1 - z)

    def send(w, at_z, v, place, peer, first=False):
        block = slot_of(w, at_z, y if v == 0 else 1 - y, core)
        index = w * 18 + place
        return pltpu.make_async_remote_copy(
            src_ref=own[w] if first else block, dst_ref=block, send_sem=send_sem.at[index],
            recv_sem=recv_sem.at[index], device_id=peer, device_id_type=MESH,
        )

    def along(w, k, v):
        peer = {"rows": row_of(far if k == 0 else near, y, core)}
        return send(w, far if k == 2 else z, v, 2 * k + v, peer, k < 2 and v == 0)

    def to_y(w, at_z, first=False):
        return send(w, at_z, 0, 6 + at_z, peers[3], first)

    def to_core(w, at_z, v, first=False):
        return send(w, at_z, v, 10 + 2 * at_z + v, peers[4], first)

    def pass_on(w, v):
        inner = (z == 1) | (z == 2)

        @pl.when(inner)
        def _():
            along(w, 0, v).start()

        along(w, 1, v).start()

        @pl.when(jnp.logical_not(inner))
        def _():
            along(w, 0, v).start()

    def relay_z(w, k, v):
        along(w, k, v).wait_recv()
        if k == 0:
            along(w, 2, v).start()
        at_z = spread[k + 1]
        if w < last:
            to_y(w, at_z).start()
        to_core(w, at_z, v).start()

    def relay_y(w, k):
        to_y(w, spread[k]).wait_recv()
        to_core(w, spread[k], 1).start()
        if w == last:
            pass_on(w, 1)

    def all_here(ws):
        for w in ws:
            for at_z in range(ROWS_Z):
                for v in range(2):
                    to_core(w, at_z, v).wait_recv()

    def all_here_load(ws, source, target, first):
        for i, at_z in enumerate(spread):
            for v in range(2):
                for w in ws:
                    to_core(w, at_z, v).wait_recv()
                chip = pl.ds(row_of(at_z, y if v == 0 else 1 - y, 0), 2)
                local(source.at[chip], target.at[chip], first + 2 * i + v).start()

    def loaded(source, target, first):
        for i in range(2 * ROWS_Z):
            chip = pl.ds(0, 2)
            local(source.at[chip], target.at[chip], first + i).wait()

    def all_gone(w):
        for v in range(1 if w < last else 2):
            for k in range(3):
                along(w, k, v).wait_send()
        for at_z in range(ROWS_Z) if w < last else (z,):
            to_y(w, at_z).wait_send()
        for at_z in range(ROWS_Z):
            for v in range(2):
                to_core(w, at_z, v).wait_send()

    def to_x(src, dst, index):
        return pltpu.make_async_remote_copy(
            src_ref=src, dst_ref=dst, send_sem=x_send.at[index], recv_sem=x_recv.at[index],
            device_id=x_peer, device_id_type=MESH,
        )

    third = q_in.shape[1] // 3
    share = third // 2
    q_picks = []
    for part in range(3):
        picked = q_in.at[:, pl.ds(pl.multiple_of(part * third + piece * share, 128), share)]
        q_picks.append(local(picked, q_own.at[:, pl.ds(part * share, share)], 17 + part))
        q_picks[-1].start()
    d_mine = d_in.at[pl.ds(piece * 2 * rows, 2 * rows)]
    local(o_in, o_own, 1).start()
    local(u_in, u_wide, 2).start()
    local(d_mine, d_own, 3).start()
    local(cot, dy.at[piece], 4).start()
    greet(peers)
    for copy in q_picks:
        copy.wait()
    hidden_x = to_x(hidden, hid_other, 0)
    cot_x = to_x(cot, dy.at[piece], 1)
    local(o_in, o_own, 1).wait()
    local(d_mine, d_own, 3).wait()
    local(u_in, u_wide, 2).wait()
    half_rows = lambda half: pl.ds(pl.multiple_of(half * own_rows, 128), own_rows)

    def first_copies():
        local(q_own, q_all.at[me], 0).start()
        local(o_own, o_all.at[me], 1).start()
        local(d_own, d_all.at[me], 3).start()
        local(cot, dy.at[piece], 4).wait()

    units_each = 2 * rows
    group = 8 * units_each

    def mine(block):
        wide = block.astype(jnp.float32)
        halves = []
        for half in range(2):
            at = [slice((2 * j + half) * units_each, (2 * j + half + 1) * units_each) for j in range(4)]
            halves.append(jnp.concatenate([wide[:, cols] for cols in at], axis=1))
        return jnp.where(piece == 0, halves[0], halves[1])

    def pick_units(g):
        cols = slice(g * group // 2, (g + 1) * group // 2)
        u_own[:, cols] = mine(u_wide[:, g * group : (g + 1) * group]).astype(bf16)
        bias[:, cols] = mine(bias_in[g * group : (g + 1) * group].reshape(1, group))
        if g == u_own.shape[1] * 2 // group - 1:
            local(u_own, u_all.at[me], 2).start()

    def norm_rows(source, half, part):
        step = 64
        steps = own_rows // step

        def body(i, carry):
            value = source[aligned(i, step), :].astype(jnp.float32)
            low = layer_norm(value, first_gain, first_shift).astype(bf16)
            normed[pl.ds(pl.multiple_of(half * own_rows + i * step, step), step), :] = low
            return carry

        lax.fori_loop(steps * part // 2, steps * (part + 1) // 2, body, 0)

    def q_here():
        local(q_own, q_all.at[me], 0).wait()
        all_here_load((0, 1), q_all, wq, 20)

    def project(begin, end):
        for part in range(begin, end):
            cols = slice(part * share, (part + 1) * share)
            value = dot_nn(normed[...], wq[:, :, cols].reshape(width, share)).astype(bf16)
            packed[:, cols] = value * jnp.asarray(HEAD_DIM ** (-0.5), bf16) if part == 0 else value
        if end == 3:
            local(packed, packed_out, 9).start()

    first_lanes = head_lanes(PAIR)

    def att_cols(half, p):
        return pl.ds(pl.multiple_of(half * pairs * PAIR + p * PAIR, PAIR), PAIR)

    def attend(p, half):
        at_q, at_k, at_v = (slice(t * share + PAIR * p, t * share + PAIR * (p + 1)) for t in range(3))
        value_t = packed[:, at_v].T
        at = half_rows(half)
        queries = packed[at, at_q]
        keys = packed[:, at_k]
        halves = []
        for h in range(2):
            one = jnp.where(first_lanes[h], queries, query_marks[at, :])
            scores = dot_nt(jnp.where(first_lanes[h], keys, key_marks[...]), one)
            top = jnp.max(scores, axis=0, keepdims=True)
            weights = jnp.exp(scores - top)
            total = jnp.sum(weights, axis=0, keepdims=True)
            lse[2 * p + h : 2 * p + h + 1, at] = top + jnp.log(total)
            summed = dot_nn(value_t[h * HEAD_DIM : (h + 1) * HEAD_DIM], weights.astype(bf16))
            halves.append(summed / total)
        return jnp.concatenate(halves, axis=0).T.astype(bf16)

    def attend_other(p):
        att_part[:, p * PAIR : (p + 1) * PAIR] = attend(p, other)

    def attend_own(p):
        att_own[:, att_cols(piece, p)] = attend(p, piece)
        if p == pairs - 1:
            for copy in att_outs:
                copy.start()

    att_x = [
        to_x(att_part.at[:, pl.ds(p * PAIR, PAIR)], att_own.at[:, att_cols(piece, p)], 2 + p) for p in range(pairs)
    ]

    att_outs = (
        local(att_part, att_out.at[half_rows(other)], 45),
        local(att_own.at[:, pl.ds(pl.multiple_of(piece * share, 128), share)], att_out.at[half_rows(piece)], 46),
    )

    def o_here():
        local(o_own, o_all.at[me], 1).wait()
        all_here_load((2,), o_all, wo, 28)

    def att_here():
        for copy in att_x:
            copy.wait_recv()
        loaded(o_all, wo, 28)

    part_rows = own_rows // 2
    second_x = [
        to_x(second.at[piece, pl.ds(i * part_rows, part_rows)], second.at[piece, pl.ds(i * part_rows, part_rows)], 2 + pairs + i)
        for i in range(2)
    ]

    def merge(part):
        for cols in (slice(0, 512), slice(512, width)) if part == 0 else ():
            weight = wo[:, :, cols].reshape(width, cols.stop - cols.start)
            resid[:, cols] = hidden[:, cols].astype(jnp.float32) + dot_nn(att_own[...], weight)

        def second_rows(i, carry):
            rows = aligned(i, 64)
            second[piece, rows, :] = layer_norm(resid[rows, :], second_gain, second_shift).astype(bf16)
            return carry

        lax.fori_loop(part * part_rows // 64, (part + 1) * part_rows // 64, second_rows, 0)
        if part == 1:
            local(resid, resid_out, 12).start()

    def flip_normed():
        def body(i, carry):
            normed_t[aligned(i, 128), :] = normed[:, aligned(i, 128)].T
            return carry

        lax.fori_loop(0, width // 128, body, 0)
        local(normed_t, normed_t_out, 8).start()
        lse_t[...] = lse[...].T
        local(lse_t, lse_out, 10).start()

    def flip_second(half):
        def body(i, carry):
            second_t[aligned(i, 128), half_rows(half)] = second[half, :, aligned(i, 128)].T
            return carry

        lax.fori_loop(0, width // 128, body, 0)

    def flip_att():
        def body(i, carry):
            att_t[aligned(i, 128), :] = att_own[:, aligned(i, 128)].T
            return carry

        lax.fori_loop(0, width // 128, body, 0)
        local(att_t, att_t_out, 11).start()
        flip_second(piece)

    def u_here():
        local(u_own, u_all.at[me], 2).wait()
        all_here_load((3,), u_all, wu, 36)

    unit = 512
    fifth = act.shape[1] // unit // 5

    def expand(half, begin):
        at = half_rows(half)

        def body(i, carry):
            cols = aligned(i, unit)
            weight = wu[:, :, cols].reshape(width, unit)
            up = dot_nn(second[half], weight) + bias[:, cols]
            cdf = 0.5 * (1.0 + lax.erf(up * (0.5 ** 0.5)))
            pdf = jnp.exp(up * up * -0.5) * ((2.0 * math.pi) ** -0.5)
            value = (up * cdf).astype(bf16)
            act[at, cols] = value
            act_t[cols, at] = value.T
            slope[at, cols] = (cdf + up * pdf).astype(bf16)
            return carry

        lax.fori_loop(begin * fifth, (begin + 1) * fifth, body, 0)
        if begin == 4:
            for copy in halves_out(half):
                copy.start()

    def halves_out(half):
        base = 54 if half is piece else 56
        at = half_rows(half)
        return (
            local(act.at[at], act_out.at[at], base),
            local(slope.at[at], slope_out.at[at], base + 1),
        )

    def second_here():
        for copy in second_x:
            copy.wait_recv()

    def flip_last():
        flip_second(other)
        local(second_t, second_t_out, 13).start()

    def dy_here():
        cot_x.wait_recv()
        local(dy, dy_all, 4).start()

    def grad_down(i):
        h, at = i // 2, slice(i % 2 * UNIT, (i % 2 + 1) * UNIT)

        def left(j):
            begin = lambda block: pl.multiple_of((8 * j + block) * 2 * rows + h * rows, 16)
            return jnp.concatenate([act_t[pl.ds(begin(block), rows), :] for block in range(8)], axis=0)

        grad_chunk(parts.at[i % SLOTS], left, lambda: dy[:, :, at].reshape(length, UNIT))

    sums_x = [
        pltpu.make_async_remote_copy(
            src_ref=parts.at[i % SLOTS, 1 - core], dst_ref=core_in.at[i], send_sem=x_send.at[4 + pairs + i],
            recv_sem=x_recv.at[4 + pairs + i], device_id=peers[4], device_id_type=MESH,
        )
        for i in range(4)
    ]

    def sum_down(i):
        core_in[i] += parts[i % SLOTS, core]
        sums_x[i].wait_send()
        local(core_in.at[i], down_sums.at[i], 50 + i).start()

    def outputs():
        for i in range(4):
            local(core_in.at[i], down_sums.at[i], 50 + i).wait()
        local(dy, dy_all, 4).wait()
        local(d_own, d_all.at[me], 3).wait()
        local(normed_t, normed_t_out, 8).wait()
        local(packed, packed_out, 9).wait()
        local(lse_t, lse_out, 10).wait()
        for copy in att_outs:
            copy.wait()
        local(att_t, att_t_out, 11).wait()
        local(resid, resid_out, 12).wait()
        local(second_t, second_t_out, 13).wait()
        for half in (piece, other):
            for copy in halves_out(half):
                copy.wait()

    act_now = functools.partial
    steps = [hidden_x.start, cot_x.start]
    steps += [act_now(pick_units, g) for g in range(4)]
    steps += [act_now(norm_rows, hidden, piece, part) for part in range(2)]
    steps += [act_now(write_marks, starts, key_marks, query_marks), lambda: None]
    steps += [hidden_x.wait_recv]
    steps += [act_now(norm_rows, hid_other, other, part) for part in range(2)]
    steps += [q_here, act_now(loaded, q_all, wq, 20), act_now(project, 0, 1), act_now(project, 1, 3)]
    for p in range(pairs):
        steps += [act_now(attend_other, p), att_x[p].start]
    steps += [act_now(attend_own, p) for p in range(pairs - 1)]
    steps += [o_here, act_now(attend_own, pairs - 1), att_here]
    steps += [act_now(merge, 0), second_x[0].start, act_now(merge, 1), second_x[1].start]
    steps += [flip_normed, flip_att, u_here, act_now(loaded, u_all, wu, 36)]
    steps += [act_now(expand, piece, i) for i in range(5)]
    steps += [second_here, flip_last]
    steps += [act_now(expand, other, i) for i in range(5)]
    steps += [dy_here]
    for i in range(4):
        steps += [act_now(grad_down, i), sums_x[i].start]
        if i:
            steps += [sums_x[i - 1].wait_recv, act_now(sum_down, i - 1)]
    steps += [sums_x[3].wait_recv, act_now(sum_down, 3), outputs, act_now(all_here, (4, 5))]
    moves = (
        lambda w: pass_on(w, 0),
        lambda w: to_y(w, z, True).start(),
        lambda w: to_core(w, z, 0, True).start(),
        relay_z,
        relay_y,
    )
    for i, step in enumerate(steps):
        for kind, *where in FORWARD_MOVES[i]:
            moves[kind](*where)
        step()
        if i == 1:
            first_copies()
    for w in range(len(own)):
        all_gone(w)
    for copy in [hidden_x, cot_x] + second_x + att_x:
        copy.wait_send()


def forward(hidden, cot, starts, gain1, shift1, gain2, shift2, bias, qkv, out, up, down):
    own_rows, width = hidden.shape
    length = 2 * own_rows
    cols = qkv.shape[1] // 2
    units = up.shape[1] // 2
    rows = up.shape[0]
    bf16, f32 = jnp.bfloat16, jnp.float32
    shards = lax.axis_size("rows")
    head_rows = 128
    outs = [
        ((shards, rows, cols), bf16),
        ((shards, rows, width), bf16),
        ((shards, rows, units), bf16),
        ((shards, down.shape[0] // 2, width), bf16),
        ((2, own_rows, width), bf16),
        ((4, 2, ROWS_Z, rows, UNIT), bf16),
        ((width, length), bf16),
        ((length, cols), bf16),
        ((length, head_rows), f32),
        ((length, cols // 3), bf16),
        ((width, own_rows), bf16),
        ((own_rows, width), f32),
        ((width, length), bf16),
        ((length, units), bf16),
        ((length, units), bf16),
    ]
    scratch = [
        ((own_rows, width), bf16),
        ((length, width), bf16),
        ((shards, rows, cols), bf16),
        ((shards, rows, width), bf16),
        ((shards, rows, units), bf16),
        ((length, cols), bf16),
        ((length, PAIR), bf16),
        ((length, PAIR), bf16),
        ((own_rows, cols // 3), bf16),
        ((own_rows, width), bf16),
        ((own_rows, width), f32),
        ((2, own_rows, width), bf16),
        ((length, units), bf16),
        ((units, length), bf16),
        ((length, units), bf16),
        ((width, length), bf16),
        ((width, own_rows), bf16),
        ((width, length), bf16),
        ((head_rows, length), f32),
        ((length, head_rows), f32),
        ((rows, 2 * units), bf16),
        ((rows, cols), bf16),
        ((rows, width), bf16),
        ((rows, units), bf16),
        ((2 * rows, width), bf16),
        ((2, own_rows, width), bf16),
        ((1, units), f32),
        ((SLOTS, 2, 2, ROWS_Z, rows, UNIT), bf16),
        ((4, 2, ROWS_Z, rows, UNIT), bf16),
    ]
    vmem = pl.BlockSpec(memory_space=pltpu.VMEM)
    anywhere = pl.BlockSpec(memory_space=pl.ANY)
    smem = pl.BlockSpec(memory_space=pltpu.SMEM)
    dma = pltpu.SemaphoreType.DMA
    x_copies = 8 + cols // (3 * PAIR)
    return pl.pallas_call(
        forward_kernel,
        out_shape=[jax.ShapeDtypeStruct(shape, kind) for shape, kind in outs],
        in_specs=[vmem, anywhere, smem] + [vmem] * 5 + [anywhere] * 4,
        out_specs=[anywhere] * len(outs),
        scratch_shapes=[pltpu.VMEM(shape, kind) for shape, kind in scratch]
        + [dma((58,)), dma((108,)), dma((108,)), dma((x_copies,)), dma((x_copies,))],
        compiler_params=pltpu.CompilerParams(
            collective_id=1, has_side_effects=True, vmem_limit_bytes=60 * 1024 * 1024
        ),
        name="forward",
    )(hidden, cot, starts, gain1, shift1, gain2, shift2, bias, qkv, out, up, down)


BACKWARD_MOVES = (
    ((2, 0), (3, 0), (1, 0), (0, 0),),
    (),
    (),
    (),
    (),
    (),
    (),
    ((2, 1), (1, 1),),
    (),
    (),
    (),
    (),
    (),
    ((4, 0), (3, 1), (0, 1),),
    ((5, 0),),
    ((2, 2),),
    (),
    ((1, 2), (6, 0),),
    ((7, 0), (4, 1), (3, 2),),
    (),
    (),
    ((0, 2),),
    (),
    (),
    (),
    (),
    (),
    (),
    (),
    (),
    ((5, 1), (2, 3),),
    (),
    ((1, 3),),
    (),
    ((4, 2), (8, 0),),
    ((3, 3), (9, 0),),
    (),
    (),
    (),
    ((5, 2), (10, 0), (6, 1),),
    ((4, 3),),
    (),
    ((5, 3),),
    (),
    (),
    ((11, 0),),
    (),
    ((7, 1), (6, 2),),
    (),
    ((0, 3),),
    ((12, 0),),
    (),
    (),
    (),
    ((7, 2),),
    (),
    ((6, 3),),
    (),
    ((8, 1),),
    (),
    (),
    (),
    (),
    ((12, 1),),
    ((14, 0), (7, 3), (13, 0), (9, 1), (8, 2), (12, 2), (10, 1), (9, 2), (11, 1), (8, 3), (10, 2), (9, 3), (14, 1), (11, 2), (10, 3), (13, 1),),
    ((12, 3), (14, 2),),
    ((11, 3),),
    (),
    ((13, 2),),
    ((14, 3), (13, 3),),
    (),
)


def thirds(value):
    high = value.astype(jnp.bfloat16)
    rest = value - high.astype(jnp.float32)
    middle = rest.astype(jnp.bfloat16)
    return high, middle, (rest - middle.astype(jnp.float32)).astype(jnp.bfloat16)


def norm_back(values, gain, grad):
    centred = values - jnp.mean(values, axis=-1, keepdims=True)
    scale = lax.rsqrt(jnp.mean(centred * centred, axis=-1, keepdims=True) + 1e-05)
    unit = centred * scale
    scaled = grad * gain
    mean_one = jnp.mean(scaled, axis=-1, keepdims=True)
    mean_two = jnp.mean(scaled * unit, axis=-1, keepdims=True)
    d_values = scale * (scaled - mean_one - unit * mean_two)
    d_gain = jnp.sum(grad * unit, axis=0, keepdims=True)
    d_shift = jnp.sum(grad, axis=0, keepdims=True)
    return d_values, d_gain, d_shift


def backward_kernel(
    starts, gain1, gain2, hidden, dy_all, q_all, o_all, u_all, d_all, down_sums, normed_t, packed, lse_in, att_in, att_t_in,
    resid, second_t, act, slope,
    output, grad_hidden, units_out, pairs_out, small_out,
    lhs, att_t, half_act, wide, wd, wu, dy, first, second, d_att, x_in0, x_in1, x_out0, down_own,
    parts, core_in, core_in_q, y_in, y_in_q, z_in, z_in_q, down_early, lse, key_marks, query_marks, acc_k, acc_v, bias_sum, early, late,
    early_near, late_near, early_all, late_all, small,
    local_sem, a_send, a_recv, b_send, b_recv, c_send, c_recv, g_send, g_recv, x_send, x_recv,
    s_send, s_recv, keep_sem,
):
    bf16, f32 = jnp.bfloat16, jnp.float32
    z, y, core = place_of()
    piece = lax.axis_index("blk")
    other = 1 - piece
    own_rows, width = first.shape
    length = 2 * own_rows
    branch = half_act.at[:, pl.ds(0, width)]
    units = wide.shape[1]
    d_width = d_att.shape[1]
    cols = 3 * d_width
    pairs = d_width // PAIR
    near = z + 1 - 2 * lax.rem(z, 2)
    far = lax.rem(z + 2, ROWS_Z)
    peer_core, peer_y = {"rows": row_of(z, y, 1 - core)}, {"rows": row_of(z, 1 - y, core)}
    peer_near, peer_far = {"rows": row_of(near, y, core)}, {"rows": row_of(far, y, core)}
    peer_x = {"blk": other}
    group = [peer_core, peer_y, {"rows": row_of(z, 1 - y, 1 - core)}]
    line = [
        {"rows": row_of(z + k, y, core), "blk": lax.rem(piece + n, 2)} for n in range(2) for k in range(ROWS_Z) if n or k
    ]
    wide_chunks = core_in.shape[0]
    chunks = wide_chunks + pairs
    first_gain, second_gain = gain1[...].reshape(1, width), gain2[...].reshape(1, width)
    half_rows = lambda half: pl.ds(pl.multiple_of(half * own_rows, 128), own_rows)
    part_rows = own_rows // 2

    def remote(src, dst, sends, recvs, index, peer):
        return pltpu.make_async_remote_copy(
            src_ref=src, dst_ref=dst, send_sem=sends.at[index], recv_sem=recvs.at[index],
            device_id=peer, device_id_type=MESH,
        )

    loads = {
        "sums": (down_sums, core_in.at[pl.ds(0, 4)], 0),
        "dy": (dy_all, dy, 1),
        "up": (u_all, wu, 4),
        "act_other": (act.at[half_rows(other)], half_act, 5),
        "act_own": (act.at[half_rows(piece)], half_act, 6),
        "resid": (resid, second, 7),
        "lse": (lse_in, lse, 8),
        "second_t": (second_t, lhs, 9),
        "att_t": (att_t_in, att_t, 10),
        "out": (o_all, wd.at[pl.ds(0, width)], 11),
        "normed_t": (normed_t, wd.at[pl.ds(width, width), pl.ds(0, length)], 12),
        "qkv": (q_all, wu.at[:, pl.ds(0, cols)], 13),
        "packed": (packed, wide.at[:, pl.ds(0, cols)], 14),
        "hidden": (hidden, branch, 15),
        "output": (second, output, 16),
        "grad_hidden": (first, grad_hidden, 17),
        "att": (att_in, lhs.at[:, pl.ds(0, length // lhs.shape[0]), pl.ds(0, d_att.shape[1])], 18),
    }

    def local(name):
        src, dst, index = loads[name]
        return pltpu.make_async_copy(src, dst, local_sem.at[index])

    z_first = (0, 1, 12)
    mine, theirs = pl.ds(2 * lax.rem(z, 2), 2), pl.ds(2 - 2 * lax.rem(z, 2), 2)
    place, far_place = z_place(z), z_place(far)
    order = tuple(range(chunks))

    def buffers(i):
        if i < wide_chunks:
            return core_in.at[i], y_in.at[i], z_in.at[i], units_out.at[:, i], UNIT
        i -= wide_chunks
        return core_in_q.at[i], y_in_q.at[i], z_in_q.at[i], pairs_out.at[:, i], 3 * PAIR

    def copy_a(i):
        into, _, _, _, n = buffers(i)
        return remote(parts.at[i % SLOTS, 1 - core, :, :, :, pl.ds(0, n)], into, a_send, a_recv, i, peer_core)

    def copy_b(i):
        sums, by_y, by_z, _, _ = buffers(i)
        if i < 4 and i not in z_first:
            sums = down_sums.at[i]
        if i in z_first:
            return remote(sums.at[1 - y, place], by_z.at[2], b_send, b_recv, i, peer_y)
        return remote(sums.at[1 - y], by_y, b_send, b_recv, i, peer_y)

    def copies_c(i, step):
        sums, by_y, by_z, _, _ = buffers(i)
        index = 4 * i + 2 * step
        if i not in z_first:
            if step == 0:
                return [remote(by_y.at[theirs], by_z.at[pl.ds(0, 2)], c_send, c_recv, index, peer_near)]
            return [remote(by_y.at[far_place], by_z.at[2], c_send, c_recv, index, peer_far)]
        if step == 0:
            sums = down_sums.at[i] if i < 4 else sums
            return [
                remote(sums.at[v, theirs], by_y.at[pl.ds(2 * v, 2)], c_send, c_recv, index + v, peer_near)
                for v in range(2)
            ]
        return [remote(sums.at[v, far_place], by_z.at[v], c_send, c_recv, index + v, peer_far) for v in range(2)]

    def copy_g(i):
        _, _, by_z, out, _ = buffers(i)
        return remote(by_z.at[0], out.at[piece], g_send, g_recv, i, peer_x)

    def keep_g(i):
        _, _, by_z, out, _ = buffers(i)
        return pltpu.make_async_copy(by_z.at[0], out.at[piece], keep_sem.at[i])

    unread = ["sums"]

    def move(i, stage):
        sums, by_y, by_z, _, n = buffers(i)
        if i < 4 and stage and unread:
            local(unread.pop()).wait()
        if stage == 0:
            slot = i % SLOTS
            if i >= 4:
                copy_a(i).wait_recv()
                sums[1 - y] += parts[slot, core, 1 - y, :, :, :n]
                if i in z_first:
                    sums[y] += parts[slot, core, y, :, :, :n]
            if i in z_first:
                for copy in copies_c(i, 0):
                    copy.start()
            else:
                copy_b(i).start()
            if i >= 4:
                if i not in z_first:
                    sums[y] += parts[slot, core, y, :, :, :n]
                copy_a(i).wait_send()
        elif i in z_first and stage < 3:
            for v, copy in enumerate(copies_c(i, stage - 1)):
                copy.wait_recv()
                if stage == 1:
                    sums[v, mine] += by_y[2 * v : 2 * v + 2]
                else:
                    sums[v, place] += by_z[v]
            for copy in copies_c(i, 1) if stage == 1 else [copy_b(i)]:
                copy.start()
        elif stage == 1:
            copy_b(i).wait_recv()
            by_y[...] += sums[y]
            copies_c(i, 0)[0].start()
        elif stage == 2:
            copies_c(i, 0)[0].wait_recv()
            by_y[mine] += by_z[0:2]
            copies_c(i, 1)[0].start()
        else:
            if i in z_first:
                copy_b(i).wait_recv()
                total = sums[y, place].astype(f32) + by_z[2].astype(f32)
            else:
                copies_c(i, 1)[0].wait_recv()
                total = by_y[place].astype(f32) + by_z[2].astype(f32)
            by_z[0] = total.astype(bf16)
            copy_g(i).start()
            keep_g(i).start()

    tile = 512

    def tile_loads(i):
        at = pl.ds(i * tile, tile)
        return (
            pltpu.make_async_copy(d_all.at[at], wd.at[at], local_sem.at[19 + 2 * i]),
            pltpu.make_async_copy(slope.at[:, at], wide.at[:, at], local_sem.at[20 + 2 * i]),
        )

    local("act_other").start()
    for i in range(units // tile):
        tile_loads(i)[0].start()
    local("dy").start()
    for i in range(units // tile):
        tile_loads(i)[1].start()
    greet(group + line)

    def ready_units():
        local("act_other").wait()
        for i in range(units // tile):
            tile_loads(i)[0].wait()
        for name in ("sums", "up", "second_t", "resid", "lse", "att_t"):
            local(name).start()

    halves = (slice(0, 512), slice(512, width))

    def d_units(begin, end):
        for i in range(begin, end):
            at = slice(i * tile, (i + 1) * tile)
            if i == 0:
                local("dy").wait()
            tile_loads(i)[1].wait()
            value = dot_nt(dy[...].reshape(length, width), wd[at, :]) * wide[:, at].astype(f32)
            low = value.astype(bf16)
            wide[:, at] = low
            bias_sum[:, at] = jnp.sum(low.astype(f32), axis=0, keepdims=True)

    def d_second(half, part, target):
        if part == 0 and target is x_out0:
            local("up").wait()
        at = halves[part]
        target[:, at] = dot_nt(wide[half_rows(half), :], wu[at, :]).astype(target.dtype)

    def exchange(part, index):
        at = pl.ds(halves[part].start, halves[part].stop - halves[part].start)
        return remote(x_out0.at[:, at], x_in0.at[:, at], x_send, x_recv, index, peer_x)

    second_x = [exchange(part, part) for part in range(2)]
    normed_x = [exchange(part, 2 + part) for part in range(2)]
    first_cols, rest_cols = (pl.ds(at.start, at.stop - at.start) for at in halves)
    down_x = [
        remote(down_early, x_in1.at[:, first_cols], x_send, x_recv, 4, peer_x),
        remote(dy.at[other, :, rest_cols], x_in1.at[:, rest_cols], x_send, x_recv, 5 + pairs, peer_x),
    ]
    att_x = [
        remote(
            x_out0.at[:, pl.ds(p * PAIR, PAIR)], d_att.at[half_rows(piece), pl.ds(p * PAIR, PAIR)],
            x_send, x_recv, 5 + p, peer_x,
        )
        for p in range(pairs)
    ]

    def d_second_own():
        for part in range(2):
            d_second(piece, part, first)
        local("qkv").start()

    def down_first():
        down_early[...] = dot_nn(half_act[...], wd[:, halves[0]]).astype(bf16)

    def down_other():
        dy[other, :, halves[1]] = dot_nn(half_act[...], wd[:, halves[1]]).astype(bf16)
        local("act_own").start()

    def down_mine():
        local("act_own").wait()
        for at in halves:
            down_own[:, at] = dot_nn(half_act[...], wd[:, at]).astype(bf16)
        local("out").start()
        local("normed_t").start()

    def chunk(i, left, right):
        grad_chunk(parts.at[i % SLOTS], left, right)
        copy_a(i).start()

    def grad_up(i):
        if i == 0:
            local("second_t").wait()
        left = lambda j: lhs[pl.ds(8 * j, 8)].reshape(8 * lhs.shape[1], length)
        chunk(4 + i, left, lambda: wide[:, i * UNIT : (i + 1) * UNIT])
        if i == 3:
            local("packed").start()
            local("att").start()

    step = 64

    def back_two(part):
        if part == 0:
            local("resid").wait()
            for copy in second_x:
                copy.wait_recv()

        def body(i, carry):
            rows = aligned(i, step)
            grad = first[rows, :] + x_in0[rows, :].astype(f32)
            d_values, d_gain, d_shift = norm_back(second[rows, :], second_gain, grad)
            total = dy[piece, rows, :].astype(f32) + d_values
            first[rows, :] = total
            branch[rows, :] = total.astype(bf16)
            early[0:1, :] += d_gain
            early[1:2, :] += d_shift
            return carry

        steps_each = part_rows // step
        if part == 0:
            early[...] = jnp.zeros_like(early)
        lax.fori_loop(part * steps_each, (part + 1) * steps_each, body, 0)

    def d_attended(half):
        rows = pl.ds(pl.multiple_of(half * d_width, 128), d_width)
        return dot_nt(branch[...], wd[rows, :]).astype(bf16)

    def d_att_other():
        local("out").wait()
        for copy in second_x:
            copy.wait_send()
        x_out0[:, :d_width] = d_attended(other)

    def d_att_own():
        d_att[half_rows(piece), :] = d_attended(piece)

    def grad_out(i):
        if i == 0:
            local("att_t").wait()
        left = lambda j: att_t[pl.ds(8 * j, 8)].reshape(8 * att_t.shape[1], own_rows)
        chunk(8 + i, left, lambda: branch[:, i * UNIT : (i + 1) * UNIT])
        if i == 1:
            local("hidden").start()

    first_lanes = head_lanes(PAIR)
    query_chunk = 256

    def pair_cols(p):
        return tuple(slice(t * d_width + PAIR * p, t * d_width + PAIR * (p + 1)) for t in range(3))

    def att_here(p):
        if p == 0:
            for name in ("lse", "packed", "normed_t", "att"):
                local(name).wait()
        att_x[p].wait_recv()
        acc_k[...] = jnp.zeros_like(acc_k)
        acc_v[...] = jnp.zeros_like(acc_v)

    lane = lax.broadcasted_iota(jnp.int32, (1, PAIR), 1)
    lane = jnp.where(lane < HEAD_DIM, lane, lane - HEAD_DIM)

    def marked(value, marks):
        for at, part in enumerate(thirds(value)):
            marks = jnp.where(lane == at, part, marks)
        return marks

    def attend_back(p, i):
        at_q, at_k, at_v = pair_cols(p)
        heads = slice(p * PAIR, (p + 1) * PAIR)
        rows = slice(i * query_chunk, (i + 1) * query_chunk)
        keys, values, queries = wide[:, at_k], wide[:, at_v], wide[rows, at_q]
        keys_t = keys.T
        grads = d_att[rows, heads]
        attended = lhs[:, : length // lhs.shape[0], heads].reshape(length, PAIR)[rows, :]
        products = grads.astype(f32) * attended.astype(f32)
        nothing = jnp.zeros_like(queries)
        parts_q = []
        for h in range(2):
            here = first_lanes[h]
            dots = jnp.sum(jnp.where(here, products, 0.0), axis=1, keepdims=True)
            top = lse[rows, 2 * p + h : 2 * p + h + 1]
            one_q = jnp.where(here, queries, marked(-top, query_marks[rows, :]))
            one_g = jnp.where(here, grads, marked(-dots, nothing))
            probs = jnp.exp(dot_nt(jnp.where(here, keys, key_marks[...]), one_q))
            d_scores = (probs * dot_nt(jnp.where(here, values, key_marks[...]), one_g)).astype(bf16)
            acc_v[...] += dot_nn(probs.astype(bf16), jnp.where(here, grads, nothing))
            acc_k[...] += dot_nn(d_scores, jnp.where(here, queries, nothing))
            parts_q.append(dot_nn(keys_t[h * HEAD_DIM : (h + 1) * HEAD_DIM], d_scores))
        d_queries = jnp.concatenate(parts_q, axis=0).T * HEAD_DIM ** (-0.5)
        wide[rows, at_q] = d_queries.astype(bf16)
        if i == length // query_chunk - 1:
            wide[:, at_k] = acc_k[...].astype(bf16)
            wide[:, at_v] = acc_v[...].astype(bf16)

    def grad_pair(p):
        n = 8 * parts.shape[4]
        left = lambda j: wd[pl.ds(pl.multiple_of(width + j * n, 64), n), :length]
        chunk(10 + p, left, lambda: jnp.concatenate([wide[:, at] for at in pair_cols(p)], axis=1))

    def down_here():
        for copy in down_x:
            copy.wait_recv()

    def write_output():
        def body(i, carry):
            rows = aligned(i, step)
            second[rows, :] += down_own[rows, :].astype(f32) + x_in1[rows, :].astype(f32)
            return carry

        lax.fori_loop(0, own_rows // step, body, 0)
        local("output").start()

    def d_normed(half, part, target):
        if part == 0 and target is x_out0:
            local("qkv").wait()
            for copy in att_x:
                copy.wait_send()
        at = halves[part]
        target[:, at] = dot_nt(wide[half_rows(half), :cols], wu[at, :cols]).astype(target.dtype)

    def d_normed_own():
        local("output").wait()
        for part in range(2):
            d_normed(piece, part, second)

    def back_one(part):
        if part == 0:
            local("hidden").wait()
            late[...] = jnp.zeros_like(late)
            for copy in normed_x:
                copy.wait_recv()

        def body(i, carry):
            rows = aligned(i, step)
            grad = second[rows, :] + x_in0[rows, :].astype(f32)
            d_values, d_gain, d_shift = norm_back(branch[rows, :].astype(f32), first_gain, grad)
            first[rows, :] += d_values
            late[0:1, :] += d_gain
            late[1:2, :] += d_shift
            return carry

        steps_each = part_rows // step
        lax.fori_loop(part * steps_each, (part + 1) * steps_each, body, 0)
        if part == 1:
            local("grad_hidden").start()

    def small_near(value, near_slots, base):
        own_slot = 2 * y + core
        return [
            remote(value, near_slots.at[own_slot], s_send, s_recv, base + k, peer) for k, peer in enumerate(group)
        ]

    def small_line(all_slots, base):
        own_slot = z * 2 + piece
        return [
            remote(all_slots.at[own_slot], all_slots.at[own_slot], s_send, s_recv, base + 3 + k, peer)
            for k, peer in enumerate(line)
        ]

    def small_one(value, near_slots, base):
        near_slots[2 * y + core] = value[...]
        for copy in small_near(value, near_slots, base):
            copy.start()

    def small_two(value, near_slots, all_slots, base):
        for copy in small_near(value, near_slots, base):
            copy.wait()
        all_slots[z * 2 + piece] = ((near_slots[0] + near_slots[1]) + near_slots[2]) + near_slots[3]
        for copy in small_line(all_slots, base):
            copy.start()

    def small_three(all_slots, base, at):
        for copy in small_line(all_slots, base):
            copy.wait()
        n = all_slots.shape[1]
        for x in range(2):
            total = ((all_slots[x] + all_slots[2 + x]) + all_slots[4 + x]) + all_slots[6 + x]
            small[x, at : at + n, :] = total

    def early_one():
        early[2:3, :] = bias_sum[:, :width]
        early[3:4, :] = bias_sum[:, width:]
        small_one(early, early_near, 0)

    call = functools.partial
    steps = [ready_units, down_first, down_x[0].start, call(d_units, 0, 2), call(d_units, 2, 4), call(d_units, 4, 5)]
    for part in range(2):
        steps += [call(d_second, other, part, x_out0), second_x[part].start]
    steps += [call(grad_up, 0), call(grad_up, 1), d_second_own, down_other, call(grad_up, 2), call(grad_up, 3), down_mine]
    steps += [call(write_marks, starts, key_marks, query_marks), call(back_two, 0), call(back_two, 1), d_att_other]
    steps += [copy.start for copy in att_x]
    steps += [d_att_own, down_x[1].start, early_one, call(grad_out, 0), call(grad_out, 1)]
    for p in range(pairs):
        steps += [call(att_here, p)] + [call(attend_back, p, i) for i in range(length // query_chunk)]
        if p < 3:
            steps += [call(grad_pair, p)]
        if p == 1:
            steps += [call(small_two, early, early_near, early_all, 0)]
    for part in range(2):
        steps += [call(d_normed, other, part, x_out0), normed_x[part].start]
    steps += [call(grad_pair, 3), call(grad_pair, 4), down_here, write_output, d_normed_own]
    steps += [call(back_one, 0), call(back_one, 1), call(small_one, late, late_near, 10)]
    steps += [call(small_three, early_all, 0, 2), call(small_two, late, late_near, late_all, 10)]
    steps += [call(small_three, late_all, 10, 0)]
    for i, one in enumerate(steps):
        for where in BACKWARD_MOVES[i]:
            move(*where)
        one()
    small_keep = pltpu.make_async_copy(small, small_out, keep_sem.at[chunks])
    small_keep.start()
    for where in BACKWARD_MOVES[len(steps)]:
        move(*where)
    for i in range(chunks):
        copy_b(i).wait_send()
        for copy in copies_c(i, 0) + copies_c(i, 1):
            copy.wait_send()
        copy_g(i).wait()
        keep_g(i).wait()
    small_keep.wait()
    for copy in down_x + normed_x:
        copy.wait_send()
    local("grad_hidden").wait()


def backward(starts, gain1, gain2, hidden, dy_all, q_all, o_all, u_all, d_all, *kept):
    bf16, f32 = jnp.bfloat16, jnp.float32
    _, own_rows, width = dy_all.shape
    length = 2 * own_rows
    cols, units = q_all.shape[1], u_all.shape[1]
    rows = width // 16
    wide_units, pairs = 10, cols // (3 * PAIR)
    pair_cols = 3 * PAIR
    outs = [
        ((own_rows, width), f32),
        ((own_rows, width), f32),
        ((2, wide_units, rows, UNIT), bf16),
        ((2, pairs, rows, pair_cols), bf16),
        ((2, 6, width), f32),
    ]
    token = ((own_rows, width), bf16)
    scratch = [
        ((16, rows, length), bf16),
        ((16, rows, own_rows), bf16),
        ((own_rows, units), bf16),
        ((length, units), bf16),
        ((units, width), bf16),
        ((width, units), bf16),
        ((2, own_rows, width), bf16),
        ((own_rows, width), f32),
        ((own_rows, width), f32),
        ((length, cols // 3), bf16),
        token, token, token, token,
        ((SLOTS, 2, 2, ROWS_Z, rows, UNIT), bf16),
        ((wide_units, 2, ROWS_Z, rows, UNIT), bf16),
        ((pairs, 2, ROWS_Z, rows, pair_cols), bf16),
        ((wide_units, ROWS_Z, rows, UNIT), bf16),
        ((pairs, ROWS_Z, rows, pair_cols), bf16),
        ((wide_units, 3, rows, UNIT), bf16),
        ((pairs, 3, rows, pair_cols), bf16),
        ((own_rows, 512), bf16),
        ((length, PAIR), f32),
        ((length, PAIR), bf16),
        ((length, PAIR), bf16),
        ((length, PAIR), f32),
        ((length, PAIR), f32),
        ((1, units), f32),
        ((4, width), f32),
        ((2, width), f32),
        ((4, 4, width), f32),
        ((4, 2, width), f32),
        ((8, 4, width), f32),
        ((8, 2, width), f32),
        ((2, 6, width), f32),
    ]
    vmem = pl.BlockSpec(memory_space=pltpu.VMEM)
    anywhere = pl.BlockSpec(memory_space=pl.ANY)
    smem = pl.BlockSpec(memory_space=pltpu.SMEM)
    chunks = wide_units + pairs
    dma = lambda n: pltpu.SemaphoreType.DMA((n,))
    sems = [29] + [chunks] * 4 + [4 * chunks] * 2 + [chunks] * 2 + [6 + pairs] * 2 + [20, 20, chunks + 1]
    return pl.pallas_call(
        backward_kernel,
        out_shape=[jax.ShapeDtypeStruct(shape, kind) for shape, kind in outs],
        in_specs=[smem, vmem, vmem] + [anywhere] * (6 + len(kept)),
        out_specs=[anywhere] * len(outs),
        scratch_shapes=[pltpu.VMEM(shape, kind) for shape, kind in scratch] + [dma(n) for n in sems],
        compiler_params=pltpu.CompilerParams(
            collective_id=2, has_side_effects=True, vmem_limit_bytes=60 * 1024 * 1024
        ),
        name="backward",
    )(starts, gain1, gain2, hidden, dy_all, q_all, o_all, u_all, d_all, *kept)


def finish_kernel(
    raw_output, raw_grad, units_lo, units_hi, pairs_in, small,
    output, grad_hidden, qkv, out, up, down, gain1, shift1, gain2, shift2, bias,
):
    f32 = jnp.float32
    step = pl.program_id(0)
    output[0] = raw_output[...]
    grad_hidden[0] = raw_grad[...]
    rows = out.shape[0]
    width = small.shape[2]
    units_in = (units_lo, units_hi)

    def mixed(first, second):
        each = first.shape[1] // 4
        blocks = []
        for j in range(4):
            at = slice(j * each, (j + 1) * each)
            blocks += [first[:, at].astype(f32), second[:, at].astype(f32)]
        return jnp.concatenate(blocks, axis=1)

    for now in range(2):

        @pl.when(step == now)
        def _():
            for i in range(4):
                h, column = divmod(i, 2)
                at = slice(column * UNIT, (column + 1) * UNIT)
                down[h * rows : (h + 1) * rows, at] = units_in[now][0, i].astype(f32)
            for i in range(2):
                chunk = 4 + 2 * now + i
                at = slice(i * 2 * UNIT, (i + 1) * 2 * UNIT)
                up[:, at] = mixed(units_lo[0, chunk], units_hi[0, chunk])
            out[...] = units_lo[0, 8 + now].astype(f32) + units_hi[0, 8 + now].astype(f32)
            pairs = pairs_in.shape[1]
            for block in range(3 * now, 3 * now + 3):
                part, piece = divmod(block, 2)
                for p in range(pairs):
                    at = (block - 3 * now) * pairs * PAIR + p * PAIR
                    chunk = pairs_in[piece, p, :, part * PAIR : (part + 1) * PAIR]
                    qkv[:, at : at + PAIR] = chunk.astype(f32)

    @pl.when(step == 0)
    def _():
        for i, ref in enumerate((gain1, shift1, gain2, shift2)):
            ref[...] = (small[0, i : i + 1, :] + small[1, i : i + 1, :]).reshape(width)
        for g in range(2):
            for j in range(2):
                at = slice(j * UNIT, (j + 1) * UNIT)
                lo, hi = small[0, 4 + g : 5 + g, at], small[1, 4 + g : 5 + g, at]
                begin = (2 * g + j) * 2 * UNIT
                bias[begin : begin + 2 * UNIT] = mixed(lo, hi).reshape(2 * UNIT)


def finish(raw_output, raw_grad, units_in, pairs_in, small):
    f32 = jnp.float32
    own_rows, width = raw_output.shape
    rows = units_in.shape[2]
    shapes = [
        (1, own_rows, width), (1, own_rows, width), (rows, 3 * width), (rows, width), (rows, 8 * UNIT),
        (4 * rows, width), (width,), (width,), (width,), (width,), (8 * UNIT,),
    ]
    token = pl.BlockSpec((own_rows // 2, width), lambda s: (s, 0))
    token_out = pl.BlockSpec((1, own_rows // 2, width), lambda s: (0, s, 0))
    columns = lambda n: pl.BlockSpec((rows, n // 2), lambda s: (0, s))
    fixed = lambda shape: pl.BlockSpec(shape, lambda s: (0,) * len(shape))
    half = lambda i: pl.BlockSpec((1,) + units_in.shape[1:], lambda s: (i, 0, 0, 0))
    return pl.pallas_call(
        finish_kernel,
        grid=(2,),
        out_shape=[jax.ShapeDtypeStruct(shape, f32) for shape in shapes],
        in_specs=[token, token, half(0), half(1), fixed(pairs_in.shape), fixed(small.shape)],
        out_specs=[
            token_out, token_out, columns(3 * width), columns(width), columns(8 * UNIT),
            pl.BlockSpec((2 * rows, width), lambda s: (s, 0)),
        ] + [fixed(shape) for shape in shapes[6:]],
        compiler_params=pltpu.CompilerParams(vmem_limit_bytes=60 * 1024 * 1024),
        name="finish",
    )(raw_output, raw_grad, units_in, units_in, pairs_in, small)


def split_layer(
    hidden, starts, first_gain, first_shift, qkv_weight, out_weight, second_gain, second_shift,
    up_weight, hidden_bias, down_weight, cotangent,
):
    shards = lax.axis_size("rows")
    (
        qkv_all, out_all, up_all, down_all, dy_all, down_sums, normed_t, packed, lse, att, att_t, residual, second_t,
        activated, slope,
    ) = forward(
        hidden[0], cotangent[0], starts, first_gain, first_shift, second_gain, second_shift, hidden_bias,
        qkv_weight, out_weight, up_weight, down_weight,
    )
    whole = lambda w: w.reshape(-1, w.shape[-1])
    blocks = lambda w: w.reshape(shards, -1, w.shape[-1])
    shares = backward(
        starts, first_gain, second_gain, hidden[0], dy_all, whole(qkv_all), whole(out_all),
        whole(up_all), whole(down_all), down_sums, normed_t, packed, lse, blocks(att), blocks(att_t), residual,
        blocks(second_t), activated, slope,
    )
    return tuple(finish(*shares))


def splits_evenly(mesh):
    pieces = mesh.shape["blk"]
    return pieces == 2 and mesh.shape["rows"] == 2 * ROWS_Z * ROWS_Y and HEADS % (2 * pieces) == 0


def solution(mesh):
    in_specs = (
        P("rows", "blk", None),
        P("rows", None),
        P(),
        P(),
        P("rows", None),
        P("rows", None),
        P(),
        P(),
        P("rows", None),
        P(),
        P("rows", None),
        P("rows", "blk", None),
    )
    out_specs = (
        P("rows", "blk", None),
        P("rows", "blk", None),
        P("rows", None),
        P("rows", None),
        P("rows", None),
        P("rows", None),
        P(),
        P(),
        P(),
        P(),
        P(),
    )
    layer = split_layer if splits_evenly(mesh) else on_device
    return jax.shard_map(
        layer, mesh=mesh, in_specs=in_specs, out_specs=out_specs, check_vma=False
    )
```

```python
import functools
import math

import jax
import jax.numpy as jnp
from jax import lax
from jax.experimental import pallas as pl
from jax.experimental.pallas import tpu as pltpu
from jax.sharding import PartitionSpec as P

HEADS = 20
HEAD_DIM = 64


masked_score = -1e30
block_limit = 512


def layer_norm(values, gain, shift):
    mean_value = jnp.mean(values, axis=-1, keepdims=True)
    centred = values - mean_value
    variance = jnp.mean(centred * centred, axis=-1, keepdims=True)
    return centred * lax.rsqrt(variance + 1e-05) * gain + shift


def segment_of(starts_row, positions):
    reached = starts_row[None, :] <= positions[:, None]
    return jnp.sum(reached.astype(jnp.int32), axis=1) - 1


def scores_with_mask(queries, key_block, query_seg, key_seg):
    products = jnp.einsum("qhe,khe->hqk", queries, key_block, preferred_element_type=jnp.float32)
    products = products * queries.shape[2] ** (-0.5)
    allowed = (query_seg[:, None] == key_seg[None, :])[None, :, :]
    return (jnp.where(allowed, products, masked_score), allowed)


def attend_rows(running, key_rows, value_rows, queries, query_seg, starts_row):
    piece_rows = key_rows.shape[0]
    step_rows = math.gcd(piece_rows, block_limit)
    head_count = queries.shape[1]
    head_width = queries.shape[2]

    def one_block(block_index, state):
        row_top, denominator, weighted = state
        block_start = block_index * step_rows
        key_block = lax.dynamic_slice_in_dim(key_rows, block_start, step_rows, 0).reshape(
            step_rows, head_count, head_width
        )
        value_block = lax.dynamic_slice_in_dim(value_rows, block_start, step_rows, 0).reshape(
            step_rows, head_count, head_width
        )
        key_seg = segment_of(starts_row, block_start + jnp.arange(step_rows, dtype=jnp.int32))
        scores, allowed = scores_with_mask(queries, key_block, query_seg, key_seg)
        new_top = jnp.maximum(row_top, jnp.max(scores, axis=-1))
        factor = jnp.exp(row_top - new_top)
        weights = jnp.where(allowed, jnp.exp(scores - new_top[:, :, None]), 0.0)
        denominator = denominator * factor + jnp.sum(weights, axis=-1)
        weighted = weighted * factor[:, :, None] + jnp.einsum(
            "hqk,khe->hqe",
            weights.astype(jnp.bfloat16),
            value_block,
            preferred_element_type=jnp.float32,
        )
        return (new_top, denominator, weighted)

    return lax.fori_loop(0, piece_rows // step_rows, one_block, running)


def on_device(
    hidden,
    starts,
    first_gain,
    first_shift,
    qkv_weight,
    out_weight,
    second_gain,
    second_shift,
    up_weight,
    hidden_bias,
    down_weight,
    cotangent,
):
    rows_here = hidden.shape[1]
    model_width = hidden.shape[2]
    head_count = HEADS
    head_width = HEAD_DIM
    score_scale = head_width ** (-0.5)
    inputs = hidden[0].astype(jnp.float32)
    starts_row = starts[0]
    offset = lax.axis_index("blk") * rows_here
    query_seg = segment_of(starts_row, offset + jnp.arange(rows_here, dtype=jnp.int32))
    qkv_full, out_full, up_full, down_full = (
        lax.all_gather(qkv_weight, "rows", axis=0, tiled=True),
        lax.all_gather(out_weight, "rows", axis=0, tiled=True),
        lax.all_gather(up_weight, "rows", axis=0, tiled=True),
        lax.all_gather(down_weight, "rows", axis=0, tiled=True),
    )
    normed_low = layer_norm(inputs, first_gain, first_shift).astype(jnp.bfloat16)
    packed = jnp.dot(normed_low, qkv_full, preferred_element_type=jnp.float32).astype(jnp.bfloat16)
    queries = packed[:, :model_width].reshape(rows_here, head_count, head_width)
    key_rows = packed[:, model_width : 2 * model_width]
    value_rows = packed[:, 2 * model_width :]
    initial = (
        jnp.full((head_count, rows_here), masked_score, jnp.float32),
        jnp.zeros((head_count, rows_here), jnp.float32),
        jnp.zeros((head_count, rows_here, head_width), jnp.float32),
    )
    row_top, denominator, weighted = attend_rows(
        initial,
        lax.all_gather(key_rows, "blk", axis=0, tiled=True),
        lax.all_gather(value_rows, "blk", axis=0, tiled=True),
        queries,
        query_seg,
        starts_row,
    )
    log_total = row_top + jnp.log(denominator)
    attended = jnp.transpose(weighted / denominator[:, :, None], (1, 0, 2))
    attended_low = attended.reshape(rows_here, model_width).astype(jnp.bfloat16)
    residual = inputs + jnp.dot(attended_low, out_full, preferred_element_type=jnp.float32)
    second_low = layer_norm(residual, second_gain, second_shift).astype(jnp.bfloat16)
    up_values = jnp.dot(second_low, up_full, preferred_element_type=jnp.float32) + hidden_bias
    activated_low = jax.nn.gelu(up_values, approximate=False).astype(jnp.bfloat16)
    output = residual + jnp.dot(activated_low, down_full, preferred_element_type=jnp.float32)
    cot_low = cotangent[0]
    d_activated = jnp.einsum("tc,fc->tf", cot_low, down_full, preferred_element_type=jnp.float32)
    unused_gelu, gelu_pull = jax.vjp(
        lambda values: jax.nn.gelu(values, approximate=False), up_values
    )
    d_up_low = gelu_pull(d_activated)[0].astype(jnp.bfloat16)
    d_second = jnp.einsum("tf,cf->tc", d_up_low, up_full, preferred_element_type=jnp.float32)
    unused_second, second_pull = jax.vjp(layer_norm, residual, second_gain, second_shift)
    d_norm_two, d_second_gain, d_second_shift = second_pull(d_second)
    d_residual = cot_low.astype(jnp.float32) + d_norm_two
    d_branch_low = d_residual.astype(jnp.bfloat16)
    d_attended_low = jnp.einsum(
        "tc,kc->tk", d_branch_low, out_full, preferred_element_type=jnp.float32
    ).astype(jnp.bfloat16)
    d_attended3 = d_attended_low.reshape(rows_here, head_count, head_width)
    row_dots = jnp.einsum("qhe,qhe->hq", d_attended3.astype(jnp.float32), attended)
    keys_all, values_all = (
        lax.all_gather(key_rows, "blk", axis=0, tiled=True),
        lax.all_gather(value_rows, "blk", axis=0, tiled=True),
    )
    length = keys_all.shape[0]
    step_rows = math.gcd(length, block_limit)

    def block_terms(block_index):
        block_start = block_index * step_rows
        key_block = lax.dynamic_slice_in_dim(keys_all, block_start, step_rows, 0).reshape(
            step_rows, head_count, head_width
        )
        value_block = lax.dynamic_slice_in_dim(values_all, block_start, step_rows, 0).reshape(
            step_rows, head_count, head_width
        )
        key_seg = segment_of(starts_row, block_start + jnp.arange(step_rows, dtype=jnp.int32))
        scores, allowed = scores_with_mask(queries, key_block, query_seg, key_seg)
        probability = jnp.where(allowed, jnp.exp(scores - log_total[:, :, None]), 0.0)
        d_probs = jnp.einsum(
            "qhe,khe->hqk", d_attended3, value_block, preferred_element_type=jnp.float32
        )
        d_scores = (probability * (d_probs - row_dots[:, :, None])).astype(jnp.bfloat16)
        return (key_block, probability, d_scores)

    dq_start = jnp.zeros((rows_here, head_count, head_width), jnp.float32)

    def back_block(dq_sum, block_index):
        key_block, probability, d_scores = block_terms(block_index)
        dq_sum = dq_sum + jnp.einsum(
            "hqk,khe->qhe", d_scores, key_block, preferred_element_type=jnp.float32
        )
        dk_block = (
            jnp.einsum("hqk,qhe->khe", d_scores, queries, preferred_element_type=jnp.float32)
            * score_scale
        )
        dv_block = jnp.einsum(
            "hqk,qhe->khe",
            probability.astype(jnp.bfloat16),
            d_attended3,
            preferred_element_type=jnp.float32,
        )
        return (
            dq_sum,
            (dk_block.reshape(step_rows, model_width), dv_block.reshape(step_rows, model_width)),
        )

    dq_sum, (dk_terms, dv_terms) = lax.scan(back_block, dq_start, jnp.arange(length // step_rows))
    dk_rows, dv_rows = (
        lax.psum_scatter(
            dk_terms.reshape(length, model_width).astype(jnp.bfloat16),
            "blk",
            scatter_dimension=0,
            tiled=True,
        ).astype(jnp.float32),
        lax.psum_scatter(
            dv_terms.reshape(length, model_width).astype(jnp.bfloat16),
            "blk",
            scatter_dimension=0,
            tiled=True,
        ).astype(jnp.float32),
    )
    d_packed = jnp.concatenate(
        [(dq_sum * score_scale).reshape(rows_here, model_width), dk_rows, dv_rows], axis=1
    ).astype(jnp.bfloat16)
    d_normed = jnp.einsum("tn,cn->tc", d_packed, qkv_full, preferred_element_type=jnp.float32)
    unused_first, first_pull = jax.vjp(layer_norm, inputs, first_gain, first_shift)
    d_norm_one, d_first_gain, d_first_shift = first_pull(d_normed)
    grad_hidden = d_residual + d_norm_one
    d_bias = jnp.sum(d_up_low, axis=0, dtype=jnp.float32)
    wide_share = lax.psum_scatter(
        jnp.concatenate(
            [
                jnp.einsum("tc,tn->cn", normed_low, d_packed, preferred_element_type=jnp.float32),
                jnp.einsum(
                    "tc,tn->cn", attended_low, d_branch_low, preferred_element_type=jnp.float32
                ),
                jnp.einsum("tc,tn->cn", second_low, d_up_low, preferred_element_type=jnp.float32),
            ],
            axis=1,
        ).astype(jnp.bfloat16),
        "rows",
        scatter_dimension=0,
        tiled=True,
    )
    down_share = lax.psum_scatter(
        jnp.einsum("tf,tn->fn", activated_low, cot_low, preferred_element_type=jnp.float32).astype(
            jnp.bfloat16
        ),
        "rows",
        scatter_dimension=0,
        tiled=True,
    )
    wide_grads, down_grads = (
        lax.psum(wide_share, "blk").astype(jnp.float32),
        lax.psum(down_share, "blk").astype(jnp.float32),
    )
    grad_qkv = wide_grads[:, : 3 * model_width]
    grad_out = wide_grads[:, 3 * model_width : 4 * model_width]
    grad_up = wide_grads[:, 4 * model_width :]
    small_grads = lax.psum(
        (d_first_gain, d_first_shift, d_second_gain, d_second_shift, d_bias), ("rows", "blk")
    )
    return (
        output[None],
        grad_hidden[None],
        grad_qkv,
        grad_out,
        grad_up,
        down_grads,
        small_grads[0],
        small_grads[1],
        small_grads[2],
        small_grads[3],
        small_grads[4],
    )


MESH = pl.DeviceIdType.MESH
FORWARD_MOVES = (
    ((0, 0), (1, 0), (2, 0), (0, 1), (1, 1), (2, 1),),
    (),
    (),
    (),
    (),
    (),
    ((2, 3),),
    (),
    (),
    (),
    ((3, 0, 1, 0), (4, 0, 0), (4, 1, 0), (3, 0, 0, 0), (3, 1, 1, 0), (4, 0, 2), (3, 1, 0, 0), (0, 2), (2, 2), (4, 0, 1), (3, 0, 2, 0), (4, 1, 2), (3, 1, 2, 0), (1, 2), (4, 1, 1), (2, 5),),
    (),
    (),
    ((4, 0, 3), (3, 2, 1, 0), (2, 4), (4, 1, 3), (3, 2, 0, 0),),
    (),
    (),
    ((4, 2, 0), (0, 3),),
    ((3, 2, 2, 0), (4, 2, 2), (1, 3),),
    (),
    (),
    (),
    (),
    (),
    (),
    ((4, 2, 1),),
    (),
    (),
    (),
    (),
    (),
    ((3, 3, 1, 0), (4, 2, 3),),
    (),
    (),
    ((3, 3, 0, 0), (4, 3, 0),),
    (),
    (),
    (),
    (),
    (),
    (),
    ((4, 3, 2), (3, 3, 2, 0), (0, 4), (1, 5), (3, 4, 1, 0), (4, 3, 1), (1, 4), (3, 4, 0, 0), (4, 3, 3), (0, 5), (3, 4, 2, 0),),
    (),
    (),
    ((4, 5, 0),),
    ((3, 5, 1, 0),),
    (),
    (),
    ((4, 4, 2),),
    (),
    (),
    ((3, 5, 0, 0),),
    (),
    ((4, 4, 0),),
    (),
    ((3, 5, 1, 1),),
    (),
    ((4, 4, 1),),
    (),
    ((3, 5, 0, 1),),
    ((4, 4, 3),),
    (),
    (),
    ((3, 5, 2, 0),),
    (),
    (),
    (),
    (),
    ((3, 5, 2, 1),),
    (),
    (),
    (),
    (),
    (),
)
ROWS_Z, ROWS_Y = 4, 2
PAIR = 128
UNIT = 640
SLOTS = 2
SPARE = 3


def place_of():
    index = lax.axis_index("rows")
    return index // 4, lax.rem(index // 2, 2), lax.rem(index, 2)


def row_of(z, y, core):
    return (lax.rem(z + ROWS_Z, ROWS_Z) * ROWS_Y + y) * 2 + core


def aligned(index, step):
    return pl.ds(pl.multiple_of(index * step, step), step)


def dot_nt(left, right):
    return lax.dot_general(left, right, (((1,), (1,)), ((), ())), preferred_element_type=jnp.float32)


def dot_nn(left, right):
    return jnp.dot(left, right, preferred_element_type=jnp.float32)


def head_lanes(width):
    lane = lax.broadcasted_iota(jnp.int32, (1, width), 1)
    return (lane < HEAD_DIM, lane >= HEAD_DIM)


def greet(peers):
    barrier = pltpu.get_barrier_semaphore()
    for peer in peers:
        pl.semaphore_signal(barrier, inc=1, device_id=peer, device_id_type=MESH)
    pl.semaphore_wait(barrier, len(peers))


def neighbours():
    z, y, core = place_of()
    return [
        {"rows": row_of(z + 1, y, core)},
        {"rows": row_of(z + 2, y, core)},
        {"rows": row_of(z + 3, y, core)},
        {"rows": row_of(z, 1 - y, core)},
        {"rows": row_of(z, y, 1 - core)},
        {"blk": 1 - lax.axis_index("blk")},
    ]


def write_marks(starts_ref, key_marks, query_marks):
    shape = key_marks.shape
    at = lax.broadcasted_iota(jnp.int32, shape, 0)
    lane = lax.broadcasted_iota(jnp.int32, shape, 1)
    lane = jnp.where(lane < HEAD_DIM, lane, lane - HEAD_DIM) - SPARE
    cell = jnp.zeros(shape, jnp.int32) - 1
    for i in range(starts_ref.shape[1]):
        cell += (at >= starts_ref[0, i]).astype(jnp.int32)
    key_marks[...] = jnp.where((lane == cell) | (lane < 0), 1.0, 0.0).astype(key_marks.dtype)
    blocked = (lane != cell) & (lane >= 0) & (lane < starts_ref.shape[1])
    query_marks[...] = jnp.where(blocked, masked_score, 0.0).astype(query_marks.dtype)


def z_place(z):
    return 2 * lax.rem(z, 2) + z // 2


def grad_chunk(target, left, right):
    def half(j, carry):
        value = dot_nn(left(j), right()).astype(jnp.bfloat16)
        n = value.shape[1]
        rows = value.shape[0] // 8
        for block in range(8):
            to_z, to_y, to_core = block // 4, block // 2 % 2, block % 2
            target[to_core, to_y, 2 * to_z + j, :, :n] = value[block * rows : (block + 1) * rows]
        return carry

    lax.fori_loop(0, 2, half, 0)


def forward_kernel(
    hidden, cot, starts, gain1, shift1, gain2, shift2, bias_in, q_in, o_in, u_in, d_in,
    q_all, o_all, u_all, d_all, dy_all, down_sums, normed_t_out, packed_out, lse_out, att_out, att_t_out, resid_out,
    second_t_out, act_out, slope_out,
    hid_other, normed, wq, wo, wu, packed, key_marks, query_marks, att_part, att_own, resid, second,
    act, act_t, slope, normed_t, att_t, second_t, lse, lse_t, u_wide, q_own, o_own, u_own, d_own, dy, bias, parts, core_in,
    local_sem, send_sem, recv_sem, x_send, x_recv,
):
    bf16 = jnp.bfloat16
    z, y, core = place_of()
    me = row_of(z, y, core)
    piece = lax.axis_index("blk")
    other = 1 - piece
    own_rows, width = hidden.shape
    length = packed.shape[0]
    rows = o_own.shape[0]
    early = rows * 3 // 5
    d_half = lambda half: pl.ds(half * rows, rows)
    own = (
        q_own.at[pl.ds(0, early)], q_own.at[pl.ds(early, rows - early)], o_own, u_own,
        d_own.at[d_half(0)], d_own.at[d_half(1)],
    )
    last = len(own) - 1

    def slot_of(w, at_z, at_y, at_core):
        slot = row_of(at_z, at_y, at_core)
        if w < 2:
            return q_all.at[slot, pl.ds(w * early, own[w].shape[0])]
        if w < 4:
            return (o_all, u_all)[w - 2].at[slot]
        return d_all.at[slot, d_half(w - 4)]

    x_peer = {"blk": other}
    peers = neighbours()
    pairs = packed.shape[1] // (3 * PAIR)
    first_gain, first_shift, second_gain, second_shift = (
        ref[...].reshape(1, width) for ref in (gain1, shift1, gain2, shift2)
    )

    def local(src, dst, index):
        return pltpu.make_async_copy(src, dst, local_sem.at[index])

    near = z + 1 - 2 * lax.rem(z, 2)
    far = lax.rem(z + 2, ROWS_Z)
    spread = (z, far, near, ROWS_Z - 1 - z)

    def send(w, at_z, v, place, peer, first=False):
        block = slot_of(w, at_z, y if v == 0 else 1 - y, core)
        index = w * 18 + place
        return pltpu.make_async_remote_copy(
            src_ref=own[w] if first else block, dst_ref=block, send_sem=send_sem.at[index],
            recv_sem=recv_sem.at[index], device_id=peer, device_id_type=MESH,
        )

    def along(w, k, v):
        peer = {"rows": row_of(far if k == 0 else near, y, core)}
        return send(w, far if k == 2 else z, v, 2 * k + v, peer, k < 2 and v == 0)

    def to_y(w, at_z, first=False):
        return send(w, at_z, 0, 6 + at_z, peers[3], first)

    def to_core(w, at_z, v, first=False):
        return send(w, at_z, v, 10 + 2 * at_z + v, peers[4], first)

    def pass_on(w, v):
        inner = (z == 1) | (z == 2)

        @pl.when(inner)
        def _():
            along(w, 0, v).start()

        along(w, 1, v).start()

        @pl.when(jnp.logical_not(inner))
        def _():
            along(w, 0, v).start()

    def relay_z(w, k, v):
        along(w, k, v).wait_recv()
        if k == 0:
            along(w, 2, v).start()
        at_z = spread[k + 1]
        if w < last:
            to_y(w, at_z).start()
        to_core(w, at_z, v).start()

    def relay_y(w, k):
        to_y(w, spread[k]).wait_recv()
        to_core(w, spread[k], 1).start()
        if w == last:
            pass_on(w, 1)

    def all_here(ws):
        for w in ws:
            for at_z in range(ROWS_Z):
                for v in range(2):
                    to_core(w, at_z, v).wait_recv()

    def all_here_load(ws, source, target, first):
        for i, at_z in enumerate(spread):
            for v in range(2):
                for w in ws:
                    to_core(w, at_z, v).wait_recv()
                chip = pl.ds(row_of(at_z, y if v == 0 else 1 - y, 0), 2)
                local(source.at[chip], target.at[chip], first + 2 * i + v).start()

    def loaded(source, target, first):
        for i in range(2 * ROWS_Z):
            chip = pl.ds(0, 2)
            local(source.at[chip], target.at[chip], first + i).wait()

    def all_gone(w):
        for v in range(1 if w < last else 2):
            for k in range(3):
                along(w, k, v).wait_send()
        for at_z in range(ROWS_Z) if w < last else (z,):
            to_y(w, at_z).wait_send()
        for at_z in range(ROWS_Z):
            for v in range(2):
                to_core(w, at_z, v).wait_send()

    def to_x(src, dst, index):
        return pltpu.make_async_remote_copy(
            src_ref=src, dst_ref=dst, send_sem=x_send.at[index], recv_sem=x_recv.at[index],
            device_id=x_peer, device_id_type=MESH,
        )

    third = q_in.shape[1] // 3
    share = third // 2
    q_picks = []
    for part in range(3):
        picked = q_in.at[:, pl.ds(pl.multiple_of(part * third + piece * share, 128), share)]
        q_picks.append(local(picked, q_own.at[:, pl.ds(part * share, share)], 17 + part))
        q_picks[-1].start()
    d_mine = d_in.at[pl.ds(piece * 2 * rows, 2 * rows)]
    local(o_in, o_own, 1).start()
    local(u_in, u_wide, 2).start()
    local(d_mine, d_own, 3).start()
    local(cot, dy.at[piece], 4).start()
    greet(peers)
    for copy in q_picks:
        copy.wait()
    hidden_x = to_x(hidden, hid_other, 0)
    cot_x = to_x(cot, dy.at[piece], 1)
    local(o_in, o_own, 1).wait()
    local(d_mine, d_own, 3).wait()
    local(u_in, u_wide, 2).wait()
    half_rows = lambda half: pl.ds(pl.multiple_of(half * own_rows, 128), own_rows)

    def first_copies():
        local(q_own, q_all.at[me], 0).start()
        local(o_own, o_all.at[me], 1).start()
        local(d_own, d_all.at[me], 3).start()
        local(cot, dy.at[piece], 4).wait()

    units_each = 2 * rows
    group = 8 * units_each

    def mine(block):
        wide = block.astype(jnp.float32)
        halves = []
        for half in range(2):
            at = [slice((2 * j + half) * units_each, (2 * j + half + 1) * units_each) for j in range(4)]
            halves.append(jnp.concatenate([wide[:, cols] for cols in at], axis=1))
        return jnp.where(piece == 0, halves[0], halves[1])

    def pick_units(g):
        cols = slice(g * group // 2, (g + 1) * group // 2)
        u_own[:, cols] = mine(u_wide[:, g * group : (g + 1) * group]).astype(bf16)
        bias[:, cols] = mine(bias_in[g * group : (g + 1) * group].reshape(1, group))
        if g == u_own.shape[1] * 2 // group - 1:
            local(u_own, u_all.at[me], 2).start()

    def norm_rows(source, half, part):
        step = 64
        steps = own_rows // step

        def body(i, carry):
            value = source[aligned(i, step), :].astype(jnp.float32)
            low = layer_norm(value, first_gain, first_shift).astype(bf16)
            normed[pl.ds(pl.multiple_of(half * own_rows + i * step, step), step), :] = low
            return carry

        lax.fori_loop(steps * part // 2, steps * (part + 1) // 2, body, 0)

    def q_here():
        local(q_own, q_all.at[me], 0).wait()
        all_here_load((0, 1), q_all, wq, 20)

    def project(begin, end):
        for part in range(begin, end):
            cols = slice(part * share, (part + 1) * share)
            value = dot_nn(normed[...], wq[:, :, cols].reshape(width, share)).astype(bf16)
            packed[:, cols] = value * jnp.asarray(HEAD_DIM ** (-0.5), bf16) if part == 0 else value
        if end == 3:
            local(packed, packed_out, 9).start()

    first_lanes = head_lanes(PAIR)

    def att_cols(half, p):
        return pl.ds(pl.multiple_of(half * pairs * PAIR + p * PAIR, PAIR), PAIR)

    def attend(p, half):
        at_q, at_k, at_v = (slice(t * share + PAIR * p, t * share + PAIR * (p + 1)) for t in range(3))
        value_t = packed[:, at_v].T
        at = half_rows(half)
        queries = packed[at, at_q]
        keys = packed[:, at_k]
        halves = []
        for h in range(2):
            one = jnp.where(first_lanes[h], queries, query_marks[at, :])
            scores = dot_nt(jnp.where(first_lanes[h], keys, key_marks[...]), one)
            top = jnp.max(scores, axis=0, keepdims=True)
            weights = jnp.exp(scores - top)
            total = jnp.sum(weights, axis=0, keepdims=True)
            lse[2 * p + h : 2 * p + h + 1, at] = top + jnp.log(total)
            summed = dot_nn(value_t[h * HEAD_DIM : (h + 1) * HEAD_DIM], weights.astype(bf16))
            halves.append(summed / total)
        return jnp.concatenate(halves, axis=0).T.astype(bf16)

    def attend_other(p):
        att_part[:, p * PAIR : (p + 1) * PAIR] = attend(p, other)

    def attend_own(p):
        att_own[:, att_cols(piece, p)] = attend(p, piece)
        if p == pairs - 1:
            for copy in att_outs:
                copy.start()

    att_x = [
        to_x(att_part.at[:, pl.ds(p * PAIR, PAIR)], att_own.at[:, att_cols(piece, p)], 2 + p) for p in range(pairs)
    ]

    att_outs = (
        local(att_part, att_out.at[half_rows(other)], 45),
        local(att_own.at[:, pl.ds(pl.multiple_of(piece * share, 128), share)], att_out.at[half_rows(piece)], 46),
    )

    def o_here():
        local(o_own, o_all.at[me], 1).wait()
        all_here_load((2,), o_all, wo, 28)

    def att_here():
        for copy in att_x:
            copy.wait_recv()
        loaded(o_all, wo, 28)

    part_rows = own_rows // 2
    second_x = [
        to_x(second.at[piece, pl.ds(i * part_rows, part_rows)], second.at[piece, pl.ds(i * part_rows, part_rows)], 2 + pairs + i)
        for i in range(2)
    ]

    def merge(part):
        for cols in (slice(0, 512), slice(512, width)) if part == 0 else ():
            weight = wo[:, :, cols].reshape(width, cols.stop - cols.start)
            resid[:, cols] = hidden[:, cols].astype(jnp.float32) + dot_nn(att_own[...], weight)

        def second_rows(i, carry):
            rows = aligned(i, 64)
            second[piece, rows, :] = layer_norm(resid[rows, :], second_gain, second_shift).astype(bf16)
            return carry

        lax.fori_loop(part * part_rows // 64, (part + 1) * part_rows // 64, second_rows, 0)
        if part == 1:
            local(resid, resid_out, 12).start()

    def flip_normed():
        def body(i, carry):
            normed_t[aligned(i, 128), :] = normed[:, aligned(i, 128)].T
            return carry

        lax.fori_loop(0, width // 128, body, 0)
        local(normed_t, normed_t_out, 8).start()
        lse_t[...] = lse[...].T
        local(lse_t, lse_out, 10).start()

    def flip_second(half):
        def body(i, carry):
            second_t[aligned(i, 128), half_rows(half)] = second[half, :, aligned(i, 128)].T
            return carry

        lax.fori_loop(0, width // 128, body, 0)

    def flip_att():
        def body(i, carry):
            att_t[aligned(i, 128), :] = att_own[:, aligned(i, 128)].T
            return carry

        lax.fori_loop(0, width // 128, body, 0)
        local(att_t, att_t_out, 11).start()
        flip_second(piece)

    def u_here():
        local(u_own, u_all.at[me], 2).wait()
        all_here_load((3,), u_all, wu, 36)

    unit = 512
    fifth = act.shape[1] // unit // 5

    def expand(half, begin):
        at = half_rows(half)

        def body(i, carry):
            cols = aligned(i, unit)
            weight = wu[:, :, cols].reshape(width, unit)
            up = dot_nn(second[half], weight) + bias[:, cols]
            cdf = 0.5 * (1.0 + lax.erf(up * (0.5 ** 0.5)))
            pdf = jnp.exp(up * up * -0.5) * ((2.0 * math.pi) ** -0.5)
            value = (up * cdf).astype(bf16)
            act[at, cols] = value
            act_t[cols, at] = value.T
            slope[at, cols] = (cdf + up * pdf).astype(bf16)
            return carry

        lax.fori_loop(begin * fifth, (begin + 1) * fifth, body, 0)
        if begin == 4:
            for copy in halves_out(half):
                copy.start()

    def halves_out(half):
        base = 54 if half is piece else 56
        at = half_rows(half)
        return (
            local(act.at[at], act_out.at[at], base),
            local(slope.at[at], slope_out.at[at], base + 1),
        )

    def second_here():
        for copy in second_x:
            copy.wait_recv()

    def flip_last():
        flip_second(other)
        local(second_t, second_t_out, 13).start()

    def dy_here():
        cot_x.wait_recv()
        local(dy, dy_all, 4).start()

    def grad_down(i):
        h, at = i // 2, slice(i % 2 * UNIT, (i % 2 + 1) * UNIT)

        def left(j):
            begin = lambda block: pl.multiple_of((8 * j + block) * 2 * rows + h * rows, 16)
            return jnp.concatenate([act_t[pl.ds(begin(block), rows), :] for block in range(8)], axis=0)

        grad_chunk(parts.at[i % SLOTS], left, lambda: dy[:, :, at].reshape(length, UNIT))

    sums_x = [
        pltpu.make_async_remote_copy(
            src_ref=parts.at[i % SLOTS, 1 - core], dst_ref=core_in.at[i], send_sem=x_send.at[4 + pairs + i],
            recv_sem=x_recv.at[4 + pairs + i], device_id=peers[4], device_id_type=MESH,
        )
        for i in range(4)
    ]

    def sum_down(i):
        core_in[i] += parts[i % SLOTS, core]
        sums_x[i].wait_send()
        local(core_in.at[i], down_sums.at[i], 50 + i).start()

    def outputs():
        for i in range(4):
            local(core_in.at[i], down_sums.at[i], 50 + i).wait()
        local(dy, dy_all, 4).wait()
        local(d_own, d_all.at[me], 3).wait()
        local(normed_t, normed_t_out, 8).wait()
        local(packed, packed_out, 9).wait()
        local(lse_t, lse_out, 10).wait()
        for copy in att_outs:
            copy.wait()
        local(att_t, att_t_out, 11).wait()
        local(resid, resid_out, 12).wait()
        local(second_t, second_t_out, 13).wait()
        for half in (piece, other):
            for copy in halves_out(half):
                copy.wait()

    act_now = functools.partial
    steps = [hidden_x.start, cot_x.start]
    steps += [act_now(pick_units, g) for g in range(4)]
    steps += [act_now(norm_rows, hidden, piece, part) for part in range(2)]
    steps += [act_now(write_marks, starts, key_marks, query_marks), lambda: None]
    steps += [hidden_x.wait_recv]
    steps += [act_now(norm_rows, hid_other, other, part) for part in range(2)]
    steps += [q_here, act_now(loaded, q_all, wq, 20), act_now(project, 0, 1), act_now(project, 1, 3)]
    for p in range(pairs):
        steps += [act_now(attend_other, p), att_x[p].start]
    steps += [act_now(attend_own, p) for p in range(pairs - 1)]
    steps += [o_here, act_now(attend_own, pairs - 1), att_here]
    steps += [act_now(merge, 0), second_x[0].start, act_now(merge, 1), second_x[1].start]
    steps += [flip_normed, flip_att, u_here, act_now(loaded, u_all, wu, 36)]
    steps += [act_now(expand, piece, i) for i in range(5)]
    steps += [second_here, flip_last]
    steps += [act_now(expand, other, i) for i in range(5)]
    steps += [dy_here]
    for i in range(4):
        steps += [act_now(grad_down, i), sums_x[i].start]
        if i:
            steps += [sums_x[i - 1].wait_recv, act_now(sum_down, i - 1)]
    steps += [sums_x[3].wait_recv, act_now(sum_down, 3), outputs, act_now(all_here, (4, 5))]
    moves = (
        lambda w: pass_on(w, 0),
        lambda w: to_y(w, z, True).start(),
        lambda w: to_core(w, z, 0, True).start(),
        relay_z,
        relay_y,
    )
    for i, step in enumerate(steps):
        for kind, *where in FORWARD_MOVES[i]:
            moves[kind](*where)
        step()
        if i == 1:
            first_copies()
    for w in range(len(own)):
        all_gone(w)
    for copy in [hidden_x, cot_x] + second_x + att_x:
        copy.wait_send()


def forward(hidden, cot, starts, gain1, shift1, gain2, shift2, bias, qkv, out, up, down):
    own_rows, width = hidden.shape
    length = 2 * own_rows
    cols = qkv.shape[1] // 2
    units = up.shape[1] // 2
    rows = up.shape[0]
    bf16, f32 = jnp.bfloat16, jnp.float32
    shards = lax.axis_size("rows")
    head_rows = 128
    outs = [
        ((shards, rows, cols), bf16),
        ((shards, rows, width), bf16),
        ((shards, rows, units), bf16),
        ((shards, down.shape[0] // 2, width), bf16),
        ((2, own_rows, width), bf16),
        ((4, 2, ROWS_Z, rows, UNIT), bf16),
        ((width, length), bf16),
        ((length, cols), bf16),
        ((length, head_rows), f32),
        ((length, cols // 3), bf16),
        ((width, own_rows), bf16),
        ((own_rows, width), f32),
        ((width, length), bf16),
        ((length, units), bf16),
        ((length, units), bf16),
    ]
    scratch = [
        ((own_rows, width), bf16),
        ((length, width), bf16),
        ((shards, rows, cols), bf16),
        ((shards, rows, width), bf16),
        ((shards, rows, units), bf16),
        ((length, cols), bf16),
        ((length, PAIR), bf16),
        ((length, PAIR), bf16),
        ((own_rows, cols // 3), bf16),
        ((own_rows, width), bf16),
        ((own_rows, width), f32),
        ((2, own_rows, width), bf16),
        ((length, units), bf16),
        ((units, length), bf16),
        ((length, units), bf16),
        ((width, length), bf16),
        ((width, own_rows), bf16),
        ((width, length), bf16),
        ((head_rows, length), f32),
        ((length, head_rows), f32),
        ((rows, 2 * units), bf16),
        ((rows, cols), bf16),
        ((rows, width), bf16),
        ((rows, units), bf16),
        ((2 * rows, width), bf16),
        ((2, own_rows, width), bf16),
        ((1, units), f32),
        ((SLOTS, 2, 2, ROWS_Z, rows, UNIT), bf16),
        ((4, 2, ROWS_Z, rows, UNIT), bf16),
    ]
    vmem = pl.BlockSpec(memory_space=pltpu.VMEM)
    anywhere = pl.BlockSpec(memory_space=pl.ANY)
    smem = pl.BlockSpec(memory_space=pltpu.SMEM)
    dma = pltpu.SemaphoreType.DMA
    x_copies = 8 + cols // (3 * PAIR)
    return pl.pallas_call(
        forward_kernel,
        out_shape=[jax.ShapeDtypeStruct(shape, kind) for shape, kind in outs],
        in_specs=[vmem, anywhere, smem] + [vmem] * 5 + [anywhere] * 4,
        out_specs=[anywhere] * len(outs),
        scratch_shapes=[pltpu.VMEM(shape, kind) for shape, kind in scratch]
        + [dma((58,)), dma((108,)), dma((108,)), dma((x_copies,)), dma((x_copies,))],
        compiler_params=pltpu.CompilerParams(
            collective_id=1, has_side_effects=True, vmem_limit_bytes=60 * 1024 * 1024
        ),
        name="forward",
    )(hidden, cot, starts, gain1, shift1, gain2, shift2, bias, qkv, out, up, down)


BACKWARD_MOVES = (
    ((1, 0), (2, 0), (3, 0), (0, 0),),
    (),
    (),
    (),
    (),
    (),
    (),
    ((2, 1), (1, 1),),
    (),
    (),
    (),
    (),
    (),
    ((4, 0), (3, 1), (0, 1),),
    ((5, 0),),
    ((2, 2),),
    (),
    ((6, 0), (1, 2),),
    ((7, 0), (4, 1), (3, 2),),
    (),
    (),
    ((0, 2),),
    (),
    (),
    (),
    (),
    (),
    (),
    (),
    (),
    ((2, 3), (5, 1),),
    (),
    (),
    ((8, 0), (4, 2), (9, 0), (3, 3),),
    (),
    (),
    ((5, 2), (10, 0), (6, 1), (1, 3),),
    (),
    (),
    (),
    ((11, 0),),
    (),
    (),
    ((7, 1), (0, 3), (8, 1), (4, 3), (12, 0), (5, 3),),
    (),
    (),
    ((6, 2),),
    (),
    (),
    (),
    ((9, 1),),
    (),
    (),
    (),
    ((7, 2), (13, 0), (14, 0), (10, 1), (8, 2), (11, 1), (6, 3), (9, 2), (12, 1), (7, 3), (10, 2), (13, 1), (11, 2), (9, 3), (14, 1),),
    ((8, 3), (12, 2), (10, 3),),
    (),
    (),
    ((13, 2),),
    ((11, 3), (14, 2), (12, 3), (13, 3),),
    ((14, 3),),
)


def thirds(value):
    high = value.astype(jnp.bfloat16)
    rest = value - high.astype(jnp.float32)
    middle = rest.astype(jnp.bfloat16)
    return high, middle, (rest - middle.astype(jnp.float32)).astype(jnp.bfloat16)


def norm_back(values, gain, grad):
    centred = values - jnp.mean(values, axis=-1, keepdims=True)
    scale = lax.rsqrt(jnp.mean(centred * centred, axis=-1, keepdims=True) + 1e-05)
    unit = centred * scale
    scaled = grad * gain
    mean_one = jnp.mean(scaled, axis=-1, keepdims=True)
    mean_two = jnp.mean(scaled * unit, axis=-1, keepdims=True)
    d_values = scale * (scaled - mean_one - unit * mean_two)
    d_gain = jnp.sum(grad * unit, axis=0, keepdims=True)
    d_shift = jnp.sum(grad, axis=0, keepdims=True)
    return d_values, d_gain, d_shift


def backward_kernel(
    starts, gain1, gain2, hidden, dy_all, q_all, o_all, u_all, d_all, down_sums, normed_t, packed, lse_in, att_in, att_t_in,
    resid, second_t, act, slope,
    output, grad_hidden, units_out, pairs_out, small_out,
    lhs, att_t, att_own, half_act, wide, wd, wu, dy, first, second, d_att, x_in0, x_in1, x_out0, down_own,
    parts, core_in, core_in_q, y_in, y_in_q, z_in, z_in_q, down_early, lse, key_marks, query_marks, acc_k, acc_v, bias_sum, early, late,
    early_near, late_near, early_all, late_all, small,
    local_sem, a_send, a_recv, b_send, b_recv, c_send, c_recv, g_send, g_recv, x_send, x_recv,
    s_send, s_recv, keep_sem,
):
    bf16, f32 = jnp.bfloat16, jnp.float32
    z, y, core = place_of()
    piece = lax.axis_index("blk")
    other = 1 - piece
    own_rows, width = first.shape
    length = 2 * own_rows
    branch = half_act.at[:, pl.ds(0, width)]
    units = wide.shape[1]
    d_width = d_att.shape[1]
    cols = 3 * d_width
    pairs = d_width // PAIR
    near = z + 1 - 2 * lax.rem(z, 2)
    far = lax.rem(z + 2, ROWS_Z)
    peer_core, peer_y = {"rows": row_of(z, y, 1 - core)}, {"rows": row_of(z, 1 - y, core)}
    peer_near, peer_far = {"rows": row_of(near, y, core)}, {"rows": row_of(far, y, core)}
    peer_x = {"blk": other}
    group = [peer_core, peer_y, {"rows": row_of(z, 1 - y, 1 - core)}]
    line = [
        {"rows": row_of(z + k, y, core), "blk": lax.rem(piece + n, 2)} for n in range(2) for k in range(ROWS_Z) if n or k
    ]
    wide_chunks = core_in.shape[0]
    chunks = wide_chunks + pairs
    first_gain, second_gain = gain1[...].reshape(1, width), gain2[...].reshape(1, width)
    half_rows = lambda half: pl.ds(pl.multiple_of(half * own_rows, 128), own_rows)
    part_rows = own_rows // 2

    def remote(src, dst, sends, recvs, index, peer):
        return pltpu.make_async_remote_copy(
            src_ref=src, dst_ref=dst, send_sem=sends.at[index], recv_sem=recvs.at[index],
            device_id=peer, device_id_type=MESH,
        )

    loads = {
        "sums": (down_sums, core_in.at[pl.ds(0, 4)], 0),
        "dy": (dy_all, dy, 1),
        "up": (u_all, wu, 4),
        "act_other": (act.at[half_rows(other)], half_act, 5),
        "act_own": (act.at[half_rows(piece)], half_act, 6),
        "resid": (resid, second, 7),
        "lse": (lse_in, lse, 8),
        "second_t": (second_t, lhs, 9),
        "att_t": (att_t_in, att_t, 10),
        "out": (o_all, wd.at[pl.ds(0, width)], 11),
        "normed_t": (normed_t, wd.at[pl.ds(width, width), pl.ds(0, length)], 12),
        "qkv": (q_all, wu.at[:, pl.ds(0, cols)], 13),
        "packed": (packed, wide.at[:, pl.ds(0, cols)], 14),
        "hidden": (hidden, branch, 15),
        "output": (second, output, 16),
        "grad_hidden": (first, grad_hidden, 17),
        "att": (att_in, att_own, 18),
    }

    def local(name):
        src, dst, index = loads[name]
        return pltpu.make_async_copy(src, dst, local_sem.at[index])

    z_first = (0, 1, 8)
    mine, theirs = pl.ds(2 * lax.rem(z, 2), 2), pl.ds(2 - 2 * lax.rem(z, 2), 2)
    place, far_place = z_place(z), z_place(far)
    order = tuple(range(chunks))

    def buffers(i):
        if i < wide_chunks:
            return core_in.at[i], y_in.at[i], z_in.at[i], units_out.at[:, i], UNIT
        i -= wide_chunks
        return core_in_q.at[i], y_in_q.at[i], z_in_q.at[i], pairs_out.at[:, i], 3 * PAIR

    def copy_a(i):
        into, _, _, _, n = buffers(i)
        return remote(parts.at[i % SLOTS, 1 - core, :, :, :, pl.ds(0, n)], into, a_send, a_recv, i, peer_core)

    def copy_b(i):
        sums, by_y, by_z, _, _ = buffers(i)
        if i < 4 and i not in z_first:
            sums = down_sums.at[i]
        if i in z_first:
            return remote(sums.at[1 - y, place], by_z.at[2], b_send, b_recv, i, peer_y)
        return remote(sums.at[1 - y], by_y, b_send, b_recv, i, peer_y)

    def copies_c(i, step):
        sums, by_y, by_z, _, _ = buffers(i)
        index = 4 * i + 2 * step
        if i not in z_first:
            if step == 0:
                return [remote(by_y.at[theirs], by_z.at[pl.ds(0, 2)], c_send, c_recv, index, peer_near)]
            return [remote(by_y.at[far_place], by_z.at[2], c_send, c_recv, index, peer_far)]
        if step == 0:
            sums = down_sums.at[i] if i < 4 else sums
            return [
                remote(sums.at[v, theirs], by_y.at[pl.ds(2 * v, 2)], c_send, c_recv, index + v, peer_near)
                for v in range(2)
            ]
        return [remote(sums.at[v, far_place], by_z.at[v], c_send, c_recv, index + v, peer_far) for v in range(2)]

    def copy_g(i):
        _, _, by_z, out, _ = buffers(i)
        return remote(by_z.at[0], out.at[piece], g_send, g_recv, i, peer_x)

    def keep_g(i):
        _, _, by_z, out, _ = buffers(i)
        return pltpu.make_async_copy(by_z.at[0], out.at[piece], keep_sem.at[i])

    unread = ["sums"]

    def move(i, stage):
        sums, by_y, by_z, _, n = buffers(i)
        if i < 4 and stage and unread:
            local(unread.pop()).wait()
        if stage == 0:
            slot = i % SLOTS
            if i >= 4:
                copy_a(i).wait_recv()
                sums[1 - y] += parts[slot, core, 1 - y, :, :, :n]
                if i in z_first:
                    sums[y] += parts[slot, core, y, :, :, :n]
            if i in z_first:
                for copy in copies_c(i, 0):
                    copy.start()
            else:
                copy_b(i).start()
            if i >= 4:
                if i not in z_first:
                    sums[y] += parts[slot, core, y, :, :, :n]
                copy_a(i).wait_send()
        elif i in z_first and stage < 3:
            for v, copy in enumerate(copies_c(i, stage - 1)):
                copy.wait_recv()
                if stage == 1:
                    sums[v, mine] += by_y[2 * v : 2 * v + 2]
                else:
                    sums[v, place] += by_z[v]
            for copy in copies_c(i, 1) if stage == 1 else [copy_b(i)]:
                copy.start()
        elif stage == 1:
            copy_b(i).wait_recv()
            by_y[...] += sums[y]
            copies_c(i, 0)[0].start()
        elif stage == 2:
            copies_c(i, 0)[0].wait_recv()
            by_y[mine] += by_z[0:2]
            copies_c(i, 1)[0].start()
        else:
            if i in z_first:
                copy_b(i).wait_recv()
                total = sums[y, place].astype(f32) + by_z[2].astype(f32)
            else:
                copies_c(i, 1)[0].wait_recv()
                total = by_y[place].astype(f32) + by_z[2].astype(f32)
            by_z[0] = total.astype(bf16)
            copy_g(i).start()
            keep_g(i).start()

    tile = 512

    def tile_loads(i):
        at = aligned(i, tile)
        return (
            pltpu.make_async_copy(d_all.at[at], wd.at[at], local_sem.at[19 + 2 * i]),
            pltpu.make_async_copy(slope.at[:, at], wide.at[:, at], local_sem.at[20 + 2 * i]),
        )

    local("act_other").start()
    for i in range(units // tile):
        tile_loads(i)[0].start()
    local("dy").start()
    for i in range(units // tile):
        tile_loads(i)[1].start()
    greet(group + line)

    def ready_units():
        local("act_other").wait()
        for i in range(units // tile):
            tile_loads(i)[0].wait()
        for name in ("sums", "up", "second_t", "resid", "lse", "att_t"):
            local(name).start()

    halves = (slice(0, 512), slice(512, width))

    def d_units(begin, end):
        if begin == 0:
            local("dy").wait()

        def body(i, carry):
            tile_loads(i)[1].wait()
            at = aligned(i, tile)
            value = dot_nt(dy[...].reshape(length, width), wd[at, :]) * wide[:, at].astype(f32)
            low = value.astype(bf16)
            wide[:, at] = low
            bias_sum[:, at] = jnp.sum(low.astype(f32), axis=0, keepdims=True)
            return carry

        lax.fori_loop(begin, end, body, 0)

    def d_second(half, part, target):
        if part == 0 and target is x_out0:
            local("up").wait()
        at = halves[part]
        target[:, at] = dot_nt(wide[half_rows(half), :], wu[at, :]).astype(target.dtype)

    def exchange(part, index):
        at = pl.ds(halves[part].start, halves[part].stop - halves[part].start)
        return remote(x_out0.at[:, at], x_in0.at[:, at], x_send, x_recv, index, peer_x)

    second_x = [exchange(part, part) for part in range(2)]
    normed_x = [exchange(part, 2 + part) for part in range(2)]
    first_cols, rest_cols = (pl.ds(at.start, at.stop - at.start) for at in halves)
    down_x = [
        remote(down_early, x_in1.at[:, first_cols], x_send, x_recv, 4, peer_x),
        remote(dy.at[other, :, rest_cols], x_in1.at[:, rest_cols], x_send, x_recv, 5 + pairs, peer_x),
    ]
    att_x = [
        remote(
            x_out0.at[:, pl.ds(p * PAIR, PAIR)], d_att.at[half_rows(piece), pl.ds(p * PAIR, PAIR)],
            x_send, x_recv, 5 + p, peer_x,
        )
        for p in range(pairs)
    ]

    def d_second_own():
        for part in range(2):
            d_second(piece, part, first)
        local("qkv").start()

    def down_first():
        down_early[...] = dot_nn(half_act[...], wd[:, halves[0]]).astype(bf16)

    def down_other():
        dy[other, :, halves[1]] = dot_nn(half_act[...], wd[:, halves[1]]).astype(bf16)
        local("act_own").start()

    def down_mine():
        local("act_own").wait()
        for at in halves:
            down_own[:, at] = dot_nn(half_act[...], wd[:, at]).astype(bf16)
        local("out").start()
        local("normed_t").start()

    def chunk(i, left, right):
        grad_chunk(parts.at[i % SLOTS], left, right)
        copy_a(i).start()

    def grad_up(i):
        if i == 0:
            local("second_t").wait()
        left = lambda j: lhs[pl.ds(8 * j, 8)].reshape(8 * lhs.shape[1], length)
        chunk(4 + i, left, lambda: wide[:, i * UNIT : (i + 1) * UNIT])
        if i == 3:
            local("packed").start()
            local("att").start()

    step = 64

    def back_two(part):
        if part == 0:
            local("resid").wait()
            for copy in second_x:
                copy.wait_recv()

        def body(i, carry):
            rows = aligned(i, step)
            grad = first[rows, :] + x_in0[rows, :].astype(f32)
            d_values, d_gain, d_shift = norm_back(second[rows, :], second_gain, grad)
            total = dy[piece, rows, :].astype(f32) + d_values
            first[rows, :] = total
            branch[rows, :] = total.astype(bf16)
            early[0:1, :] += d_gain
            early[1:2, :] += d_shift
            return carry

        steps_each = part_rows // step
        if part == 0:
            early[...] = jnp.zeros_like(early)
        lax.fori_loop(part * steps_each, (part + 1) * steps_each, body, 0)

    def d_attended(half):
        rows = pl.ds(pl.multiple_of(half * d_width, 128), d_width)
        return dot_nt(branch[...], wd[rows, :]).astype(bf16)

    def d_att_other():
        local("out").wait()
        for copy in second_x:
            copy.wait_send()
        x_out0[:, :d_width] = d_attended(other)

    def d_att_own():
        d_att[half_rows(piece), :] = d_attended(piece)

    def grad_out(i):
        if i == 0:
            local("att_t").wait()
        left = lambda j: att_t[pl.ds(8 * j, 8)].reshape(8 * att_t.shape[1], own_rows)
        chunk(8 + i, left, lambda: branch[:, i * UNIT : (i + 1) * UNIT])
        if i == 1:
            local("hidden").start()

    first_lanes = head_lanes(PAIR)
    query_chunk = 256

    def pair_cols(p):
        return tuple(slice(t * d_width + PAIR * p, t * d_width + PAIR * (p + 1)) for t in range(3))

    def att_here(p):
        if p == 0:
            for name in ("lse", "packed", "normed_t", "att"):
                local(name).wait()
        att_x[p].wait_recv()
        acc_k[...] = jnp.zeros_like(acc_k)
        acc_v[...] = jnp.zeros_like(acc_v)

    lane = lax.broadcasted_iota(jnp.int32, (1, PAIR), 1)
    lane = jnp.where(lane < HEAD_DIM, lane, lane - HEAD_DIM)

    def marked(value, marks):
        for at, part in enumerate(thirds(value)):
            marks = jnp.where(lane == at, part, marks)
        return marks

    def attend_back(p):
        at_q, at_k, at_v = pair_cols(p)
        heads = slice(p * PAIR, (p + 1) * PAIR)
        keys_t = wide[:, at_k].T

        def one_chunk(i, carry):
            rows = aligned(i, query_chunk)
            keys, values, queries = wide[:, at_k], wide[:, at_v], wide[rows, at_q]
            grads = d_att[rows, heads]
            attended = att_own[rows, heads]
            products = grads.astype(f32) * attended.astype(f32)
            nothing = jnp.zeros_like(queries)
            parts_q = []
            for h in range(2):
                here = first_lanes[h]
                dots = jnp.sum(jnp.where(here, products, 0.0), axis=1, keepdims=True)
                top = lse[rows, 2 * p + h : 2 * p + h + 1]
                one_q = jnp.where(here, queries, marked(-top, query_marks[rows, :]))
                one_g = jnp.where(here, grads, marked(-dots, nothing))
                probs = jnp.exp(dot_nt(jnp.where(here, keys, key_marks[...]), one_q))
                d_scores = (probs * dot_nt(jnp.where(here, values, key_marks[...]), one_g)).astype(bf16)
                acc_v[...] += dot_nn(probs.astype(bf16), jnp.where(here, grads, nothing))
                acc_k[...] += dot_nn(d_scores, jnp.where(here, queries, nothing))
                parts_q.append(dot_nn(keys_t[h * HEAD_DIM : (h + 1) * HEAD_DIM], d_scores))
            d_queries = jnp.concatenate(parts_q, axis=0).T * HEAD_DIM ** (-0.5)
            wide[rows, at_q] = d_queries.astype(bf16)
            return carry

        lax.fori_loop(0, length // query_chunk, one_chunk, 0)
        wide[:, at_k] = acc_k[...].astype(bf16)
        wide[:, at_v] = acc_v[...].astype(bf16)

    def grad_pair(p):
        n = 8 * parts.shape[4]
        left = lambda j: wd[pl.ds(pl.multiple_of(width + j * n, 64), n), :length]
        chunk(10 + p, left, lambda: jnp.concatenate([wide[:, at] for at in pair_cols(p)], axis=1))

    def down_here():
        for copy in down_x:
            copy.wait_recv()

    def write_output():
        def body(i, carry):
            rows = aligned(i, step)
            second[rows, :] += down_own[rows, :].astype(f32) + x_in1[rows, :].astype(f32)
            return carry

        lax.fori_loop(0, own_rows // step, body, 0)
        local("output").start()

    def d_normed(half, part, target):
        if part == 0 and target is x_out0:
            local("qkv").wait()
            for copy in att_x:
                copy.wait_send()
        at = halves[part]
        target[:, at] = dot_nt(wide[half_rows(half), :cols], wu[at, :cols]).astype(target.dtype)

    def d_normed_own():
        local("output").wait()
        for part in range(2):
            d_normed(piece, part, second)

    def back_one(part):
        if part == 0:
            local("hidden").wait()
            late[...] = jnp.zeros_like(late)
            for copy in normed_x:
                copy.wait_recv()

        def body(i, carry):
            rows = aligned(i, step)
            grad = second[rows, :] + x_in0[rows, :].astype(f32)
            d_values, d_gain, d_shift = norm_back(branch[rows, :].astype(f32), first_gain, grad)
            first[rows, :] += d_values
            late[0:1, :] += d_gain
            late[1:2, :] += d_shift
            return carry

        steps_each = part_rows // step
        lax.fori_loop(part * steps_each, (part + 1) * steps_each, body, 0)
        if part == 1:
            local("grad_hidden").start()

    def small_near(value, near_slots, base):
        own_slot = 2 * y + core
        return [
            remote(value, near_slots.at[own_slot], s_send, s_recv, base + k, peer) for k, peer in enumerate(group)
        ]

    def small_line(all_slots, base):
        own_slot = z * 2 + piece
        return [
            remote(all_slots.at[own_slot], all_slots.at[own_slot], s_send, s_recv, base + 3 + k, peer)
            for k, peer in enumerate(line)
        ]

    def small_one(value, near_slots, base):
        near_slots[2 * y + core] = value[...]
        for copy in small_near(value, near_slots, base):
            copy.start()

    def small_two(value, near_slots, all_slots, base):
        for copy in small_near(value, near_slots, base):
            copy.wait()
        all_slots[z * 2 + piece] = ((near_slots[0] + near_slots[1]) + near_slots[2]) + near_slots[3]
        for copy in small_line(all_slots, base):
            copy.start()

    def small_three(all_slots, base, at):
        for copy in small_line(all_slots, base):
            copy.wait()
        n = all_slots.shape[1]
        for x in range(2):
            total = ((all_slots[x] + all_slots[2 + x]) + all_slots[4 + x]) + all_slots[6 + x]
            small[x, at : at + n, :] = total

    def early_one():
        early[2:3, :] = bias_sum[:, :width]
        early[3:4, :] = bias_sum[:, width:]
        small_one(early, early_near, 0)

    call = functools.partial
    steps = [ready_units, down_first, down_x[0].start, call(d_units, 0, 2), call(d_units, 2, 4), call(d_units, 4, 5)]
    for part in range(2):
        steps += [call(d_second, other, part, x_out0), second_x[part].start]
    steps += [call(grad_up, 0), call(grad_up, 1), d_second_own, down_other, call(grad_up, 2), call(grad_up, 3), down_mine]
    steps += [call(write_marks, starts, key_marks, query_marks), call(back_two, 0), call(back_two, 1), d_att_other]
    steps += [copy.start for copy in att_x]
    steps += [d_att_own, down_x[1].start, early_one, call(grad_out, 0), call(grad_out, 1)]
    for p in range(pairs):
        steps += [call(att_here, p)] + [call(attend_back, p)]
        if p < 3:
            steps += [call(grad_pair, p)]
        if p == 1:
            steps += [call(small_two, early, early_near, early_all, 0)]
    for part in range(2):
        steps += [call(d_normed, other, part, x_out0), normed_x[part].start]
    steps += [call(grad_pair, 3), call(grad_pair, 4), down_here, write_output, d_normed_own]
    steps += [call(back_one, 0), call(back_one, 1), call(small_one, late, late_near, 10)]
    steps += [call(small_three, early_all, 0, 2), call(small_two, late, late_near, late_all, 10)]
    steps += [call(small_three, late_all, 10, 0)]
    for i, one in enumerate(steps):
        for where in BACKWARD_MOVES[i]:
            move(*where)
        one()
    small_keep = pltpu.make_async_copy(small, small_out, keep_sem.at[chunks])
    small_keep.start()
    for where in BACKWARD_MOVES[len(steps)]:
        move(*where)
    for i in range(chunks):
        copy_b(i).wait_send()
        for copy in copies_c(i, 0) + copies_c(i, 1):
            copy.wait_send()
        copy_g(i).wait()
        keep_g(i).wait()
    small_keep.wait()
    for copy in down_x + normed_x:
        copy.wait_send()
    local("grad_hidden").wait()


def backward(starts, gain1, gain2, hidden, dy_all, q_all, o_all, u_all, d_all, *kept):
    bf16, f32 = jnp.bfloat16, jnp.float32
    _, own_rows, width = dy_all.shape
    length = 2 * own_rows
    cols, units = q_all.shape[1], u_all.shape[1]
    rows = width // 16
    wide_units, pairs = 10, cols // (3 * PAIR)
    pair_cols = 3 * PAIR
    outs = [
        ((own_rows, width), f32),
        ((own_rows, width), f32),
        ((2, wide_units, rows, UNIT), bf16),
        ((2, pairs, rows, pair_cols), bf16),
        ((2, 6, width), f32),
    ]
    token = ((own_rows, width), bf16)
    scratch = [
        ((16, rows, length), bf16),
        ((16, rows, own_rows), bf16),
        ((length, cols // 3), bf16),
        ((own_rows, units), bf16),
        ((length, units), bf16),
        ((units, width), bf16),
        ((width, units), bf16),
        ((2, own_rows, width), bf16),
        ((own_rows, width), f32),
        ((own_rows, width), f32),
        ((length, cols // 3), bf16),
        token, token, token, token,
        ((SLOTS, 2, 2, ROWS_Z, rows, UNIT), bf16),
        ((wide_units, 2, ROWS_Z, rows, UNIT), bf16),
        ((pairs, 2, ROWS_Z, rows, pair_cols), bf16),
        ((wide_units, ROWS_Z, rows, UNIT), bf16),
        ((pairs, ROWS_Z, rows, pair_cols), bf16),
        ((wide_units, 3, rows, UNIT), bf16),
        ((pairs, 3, rows, pair_cols), bf16),
        ((own_rows, 512), bf16),
        ((length, PAIR), f32),
        ((length, PAIR), bf16),
        ((length, PAIR), bf16),
        ((length, PAIR), f32),
        ((length, PAIR), f32),
        ((1, units), f32),
        ((4, width), f32),
        ((2, width), f32),
        ((4, 4, width), f32),
        ((4, 2, width), f32),
        ((8, 4, width), f32),
        ((8, 2, width), f32),
        ((2, 6, width), f32),
    ]
    vmem = pl.BlockSpec(memory_space=pltpu.VMEM)
    anywhere = pl.BlockSpec(memory_space=pl.ANY)
    smem = pl.BlockSpec(memory_space=pltpu.SMEM)
    chunks = wide_units + pairs
    dma = lambda n: pltpu.SemaphoreType.DMA((n,))
    sems = [29] + [chunks] * 4 + [4 * chunks] * 2 + [chunks] * 2 + [6 + pairs] * 2 + [20, 20, chunks + 1]
    return pl.pallas_call(
        backward_kernel,
        out_shape=[jax.ShapeDtypeStruct(shape, kind) for shape, kind in outs],
        in_specs=[smem, vmem, vmem] + [anywhere] * (6 + len(kept)),
        out_specs=[anywhere] * len(outs),
        scratch_shapes=[pltpu.VMEM(shape, kind) for shape, kind in scratch] + [dma(n) for n in sems],
        compiler_params=pltpu.CompilerParams(
            collective_id=2, has_side_effects=True, vmem_limit_bytes=60 * 1024 * 1024
        ),
        name="backward",
    )(starts, gain1, gain2, hidden, dy_all, q_all, o_all, u_all, d_all, *kept)


def finish_kernel(
    raw_output, raw_grad, units_lo, units_hi, pairs_in, small,
    output, grad_hidden, qkv, out, up, down, gain1, shift1, gain2, shift2, bias,
):
    f32 = jnp.float32
    step = pl.program_id(0)
    output[0] = raw_output[...]
    grad_hidden[0] = raw_grad[...]
    rows = out.shape[0]
    width = small.shape[2]
    units_in = (units_lo, units_hi)

    def mixed(first, second):
        each = first.shape[1] // 4
        blocks = []
        for j in range(4):
            at = slice(j * each, (j + 1) * each)
            blocks += [first[:, at].astype(f32), second[:, at].astype(f32)]
        return jnp.concatenate(blocks, axis=1)

    for now in range(2):

        @pl.when(step == now)
        def _():
            for i in range(4):
                h, column = divmod(i, 2)
                at = slice(column * UNIT, (column + 1) * UNIT)
                down[h * rows : (h + 1) * rows, at] = units_in[now][0, i].astype(f32)
            for i in range(2):
                chunk = 4 + 2 * now + i
                at = slice(i * 2 * UNIT, (i + 1) * 2 * UNIT)
                up[:, at] = mixed(units_lo[0, chunk], units_hi[0, chunk])
            out[...] = units_lo[0, 8 + now].astype(f32) + units_hi[0, 8 + now].astype(f32)
            pairs = pairs_in.shape[1]
            for block in range(3 * now, 3 * now + 3):
                part, piece = divmod(block, 2)
                for p in range(pairs):
                    at = (block - 3 * now) * pairs * PAIR + p * PAIR
                    chunk = pairs_in[piece, p, :, part * PAIR : (part + 1) * PAIR]
                    qkv[:, at : at + PAIR] = chunk.astype(f32)

    @pl.when(step == 0)
    def _():
        for i, ref in enumerate((gain1, shift1, gain2, shift2)):
            ref[...] = (small[0, i : i + 1, :] + small[1, i : i + 1, :]).reshape(width)
        for g in range(2):
            for j in range(2):
                at = slice(j * UNIT, (j + 1) * UNIT)
                lo, hi = small[0, 4 + g : 5 + g, at], small[1, 4 + g : 5 + g, at]
                begin = (2 * g + j) * 2 * UNIT
                bias[begin : begin + 2 * UNIT] = mixed(lo, hi).reshape(2 * UNIT)


def finish(raw_output, raw_grad, units_in, pairs_in, small):
    f32 = jnp.float32
    own_rows, width = raw_output.shape
    rows = units_in.shape[2]
    shapes = [
        (1, own_rows, width), (1, own_rows, width), (rows, 3 * width), (rows, width), (rows, 8 * UNIT),
        (4 * rows, width), (width,), (width,), (width,), (width,), (8 * UNIT,),
    ]
    token = pl.BlockSpec((own_rows // 2, width), lambda s: (s, 0))
    token_out = pl.BlockSpec((1, own_rows // 2, width), lambda s: (0, s, 0))
    columns = lambda n: pl.BlockSpec((rows, n // 2), lambda s: (0, s))
    fixed = lambda shape: pl.BlockSpec(shape, lambda s: (0,) * len(shape))
    half = lambda i: pl.BlockSpec((1,) + units_in.shape[1:], lambda s: (i, 0, 0, 0))
    return pl.pallas_call(
        finish_kernel,
        grid=(2,),
        out_shape=[jax.ShapeDtypeStruct(shape, f32) for shape in shapes],
        in_specs=[token, token, half(0), half(1), fixed(pairs_in.shape), fixed(small.shape)],
        out_specs=[
            token_out, token_out, columns(3 * width), columns(width), columns(8 * UNIT),
            pl.BlockSpec((2 * rows, width), lambda s: (s, 0)),
        ] + [fixed(shape) for shape in shapes[6:]],
        compiler_params=pltpu.CompilerParams(vmem_limit_bytes=60 * 1024 * 1024),
        name="finish",
    )(raw_output, raw_grad, units_in, units_in, pairs_in, small)


def split_layer(
    hidden, starts, first_gain, first_shift, qkv_weight, out_weight, second_gain, second_shift,
    up_weight, hidden_bias, down_weight, cotangent,
):
    shards = lax.axis_size("rows")
    (
        qkv_all, out_all, up_all, down_all, dy_all, down_sums, normed_t, packed, lse, att, att_t, residual, second_t,
        activated, slope,
    ) = forward(
        hidden[0], cotangent[0], starts, first_gain, first_shift, second_gain, second_shift, hidden_bias,
        qkv_weight, out_weight, up_weight, down_weight,
    )
    whole = lambda w: w.reshape(-1, w.shape[-1])
    blocks = lambda w: w.reshape(shards, -1, w.shape[-1])
    shares = backward(
        starts, first_gain, second_gain, hidden[0], dy_all, whole(qkv_all), whole(out_all),
        whole(up_all), whole(down_all), down_sums, normed_t, packed, lse, att, blocks(att_t), residual,
        blocks(second_t), activated, slope,
    )
    return tuple(finish(*shares))


def splits_evenly(mesh):
    pieces = mesh.shape["blk"]
    return pieces == 2 and mesh.shape["rows"] == 2 * ROWS_Z * ROWS_Y and HEADS % (2 * pieces) == 0


def solution(mesh):
    in_specs = (
        P("rows", "blk", None),
        P("rows", None),
        P(),
        P(),
        P("rows", None),
        P("rows", None),
        P(),
        P(),
        P("rows", None),
        P(),
        P("rows", None),
        P("rows", "blk", None),
    )
    out_specs = (
        P("rows", "blk", None),
        P("rows", "blk", None),
        P("rows", None),
        P("rows", None),
        P("rows", None),
        P("rows", None),
        P(),
        P(),
        P(),
        P(),
        P(),
    )
    layer = split_layer if splits_evenly(mesh) else on_device
    return jax.shard_map(
        layer, mesh=mesh, in_specs=in_specs, out_specs=out_specs, check_vma=False
    )
```

```python
import functools
import math

import jax
import jax.numpy as jnp
from jax import lax
from jax.experimental import pallas as pl
from jax.experimental.pallas import tpu as pltpu
from jax.sharding import PartitionSpec as P

HEADS = 20
HEAD_DIM = 64


masked_score = -1e30
block_limit = 512


def layer_norm(values, gain, shift):
    mean_value = jnp.mean(values, axis=-1, keepdims=True)
    centred = values - mean_value
    variance = jnp.mean(centred * centred, axis=-1, keepdims=True)
    return centred * lax.rsqrt(variance + 1e-05) * gain + shift


def segment_of(starts_row, positions):
    reached = starts_row[None, :] <= positions[:, None]
    return jnp.sum(reached.astype(jnp.int32), axis=1) - 1


def scores_with_mask(queries, key_block, query_seg, key_seg):
    products = jnp.einsum("qhe,khe->hqk", queries, key_block, preferred_element_type=jnp.float32)
    products = products * queries.shape[2] ** (-0.5)
    allowed = (query_seg[:, None] == key_seg[None, :])[None, :, :]
    return (jnp.where(allowed, products, masked_score), allowed)


def attend_rows(running, key_rows, value_rows, queries, query_seg, starts_row):
    piece_rows = key_rows.shape[0]
    step_rows = math.gcd(piece_rows, block_limit)
    head_count = queries.shape[1]
    head_width = queries.shape[2]

    def one_block(block_index, state):
        row_top, denominator, weighted = state
        block_start = block_index * step_rows
        key_block = lax.dynamic_slice_in_dim(key_rows, block_start, step_rows, 0).reshape(
            step_rows, head_count, head_width
        )
        value_block = lax.dynamic_slice_in_dim(value_rows, block_start, step_rows, 0).reshape(
            step_rows, head_count, head_width
        )
        key_seg = segment_of(starts_row, block_start + jnp.arange(step_rows, dtype=jnp.int32))
        scores, allowed = scores_with_mask(queries, key_block, query_seg, key_seg)
        new_top = jnp.maximum(row_top, jnp.max(scores, axis=-1))
        factor = jnp.exp(row_top - new_top)
        weights = jnp.where(allowed, jnp.exp(scores - new_top[:, :, None]), 0.0)
        denominator = denominator * factor + jnp.sum(weights, axis=-1)
        weighted = weighted * factor[:, :, None] + jnp.einsum(
            "hqk,khe->hqe",
            weights.astype(jnp.bfloat16),
            value_block,
            preferred_element_type=jnp.float32,
        )
        return (new_top, denominator, weighted)

    return lax.fori_loop(0, piece_rows // step_rows, one_block, running)


def on_device(
    hidden,
    starts,
    first_gain,
    first_shift,
    qkv_weight,
    out_weight,
    second_gain,
    second_shift,
    up_weight,
    hidden_bias,
    down_weight,
    cotangent,
):
    rows_here = hidden.shape[1]
    model_width = hidden.shape[2]
    head_count = HEADS
    head_width = HEAD_DIM
    score_scale = head_width ** (-0.5)
    inputs = hidden[0].astype(jnp.float32)
    starts_row = starts[0]
    offset = lax.axis_index("blk") * rows_here
    query_seg = segment_of(starts_row, offset + jnp.arange(rows_here, dtype=jnp.int32))
    qkv_full, out_full, up_full, down_full = (
        lax.all_gather(qkv_weight, "rows", axis=0, tiled=True),
        lax.all_gather(out_weight, "rows", axis=0, tiled=True),
        lax.all_gather(up_weight, "rows", axis=0, tiled=True),
        lax.all_gather(down_weight, "rows", axis=0, tiled=True),
    )
    normed_low = layer_norm(inputs, first_gain, first_shift).astype(jnp.bfloat16)
    packed = jnp.dot(normed_low, qkv_full, preferred_element_type=jnp.float32).astype(jnp.bfloat16)
    queries = packed[:, :model_width].reshape(rows_here, head_count, head_width)
    key_rows = packed[:, model_width : 2 * model_width]
    value_rows = packed[:, 2 * model_width :]
    initial = (
        jnp.full((head_count, rows_here), masked_score, jnp.float32),
        jnp.zeros((head_count, rows_here), jnp.float32),
        jnp.zeros((head_count, rows_here, head_width), jnp.float32),
    )
    row_top, denominator, weighted = attend_rows(
        initial,
        lax.all_gather(key_rows, "blk", axis=0, tiled=True),
        lax.all_gather(value_rows, "blk", axis=0, tiled=True),
        queries,
        query_seg,
        starts_row,
    )
    log_total = row_top + jnp.log(denominator)
    attended = jnp.transpose(weighted / denominator[:, :, None], (1, 0, 2))
    attended_low = attended.reshape(rows_here, model_width).astype(jnp.bfloat16)
    residual = inputs + jnp.dot(attended_low, out_full, preferred_element_type=jnp.float32)
    second_low = layer_norm(residual, second_gain, second_shift).astype(jnp.bfloat16)
    up_values = jnp.dot(second_low, up_full, preferred_element_type=jnp.float32) + hidden_bias
    activated_low = jax.nn.gelu(up_values, approximate=False).astype(jnp.bfloat16)
    output = residual + jnp.dot(activated_low, down_full, preferred_element_type=jnp.float32)
    cot_low = cotangent[0]
    d_activated = jnp.einsum("tc,fc->tf", cot_low, down_full, preferred_element_type=jnp.float32)
    unused_gelu, gelu_pull = jax.vjp(
        lambda values: jax.nn.gelu(values, approximate=False), up_values
    )
    d_up_low = gelu_pull(d_activated)[0].astype(jnp.bfloat16)
    d_second = jnp.einsum("tf,cf->tc", d_up_low, up_full, preferred_element_type=jnp.float32)
    unused_second, second_pull = jax.vjp(layer_norm, residual, second_gain, second_shift)
    d_norm_two, d_second_gain, d_second_shift = second_pull(d_second)
    d_residual = cot_low.astype(jnp.float32) + d_norm_two
    d_branch_low = d_residual.astype(jnp.bfloat16)
    d_attended_low = jnp.einsum(
        "tc,kc->tk", d_branch_low, out_full, preferred_element_type=jnp.float32
    ).astype(jnp.bfloat16)
    d_attended3 = d_attended_low.reshape(rows_here, head_count, head_width)
    row_dots = jnp.einsum("qhe,qhe->hq", d_attended3.astype(jnp.float32), attended)
    keys_all, values_all = (
        lax.all_gather(key_rows, "blk", axis=0, tiled=True),
        lax.all_gather(value_rows, "blk", axis=0, tiled=True),
    )
    length = keys_all.shape[0]
    step_rows = math.gcd(length, block_limit)

    def block_terms(block_index):
        block_start = block_index * step_rows
        key_block = lax.dynamic_slice_in_dim(keys_all, block_start, step_rows, 0).reshape(
            step_rows, head_count, head_width
        )
        value_block = lax.dynamic_slice_in_dim(values_all, block_start, step_rows, 0).reshape(
            step_rows, head_count, head_width
        )
        key_seg = segment_of(starts_row, block_start + jnp.arange(step_rows, dtype=jnp.int32))
        scores, allowed = scores_with_mask(queries, key_block, query_seg, key_seg)
        probability = jnp.where(allowed, jnp.exp(scores - log_total[:, :, None]), 0.0)
        d_probs = jnp.einsum(
            "qhe,khe->hqk", d_attended3, value_block, preferred_element_type=jnp.float32
        )
        d_scores = (probability * (d_probs - row_dots[:, :, None])).astype(jnp.bfloat16)
        return (key_block, probability, d_scores)

    dq_start = jnp.zeros((rows_here, head_count, head_width), jnp.float32)

    def back_block(dq_sum, block_index):
        key_block, probability, d_scores = block_terms(block_index)
        dq_sum = dq_sum + jnp.einsum(
            "hqk,khe->qhe", d_scores, key_block, preferred_element_type=jnp.float32
        )
        dk_block = (
            jnp.einsum("hqk,qhe->khe", d_scores, queries, preferred_element_type=jnp.float32)
            * score_scale
        )
        dv_block = jnp.einsum(
            "hqk,qhe->khe",
            probability.astype(jnp.bfloat16),
            d_attended3,
            preferred_element_type=jnp.float32,
        )
        return (
            dq_sum,
            (dk_block.reshape(step_rows, model_width), dv_block.reshape(step_rows, model_width)),
        )

    dq_sum, (dk_terms, dv_terms) = lax.scan(back_block, dq_start, jnp.arange(length // step_rows))
    dk_rows, dv_rows = (
        lax.psum_scatter(
            dk_terms.reshape(length, model_width).astype(jnp.bfloat16),
            "blk",
            scatter_dimension=0,
            tiled=True,
        ).astype(jnp.float32),
        lax.psum_scatter(
            dv_terms.reshape(length, model_width).astype(jnp.bfloat16),
            "blk",
            scatter_dimension=0,
            tiled=True,
        ).astype(jnp.float32),
    )
    d_packed = jnp.concatenate(
        [(dq_sum * score_scale).reshape(rows_here, model_width), dk_rows, dv_rows], axis=1
    ).astype(jnp.bfloat16)
    d_normed = jnp.einsum("tn,cn->tc", d_packed, qkv_full, preferred_element_type=jnp.float32)
    unused_first, first_pull = jax.vjp(layer_norm, inputs, first_gain, first_shift)
    d_norm_one, d_first_gain, d_first_shift = first_pull(d_normed)
    grad_hidden = d_residual + d_norm_one
    d_bias = jnp.sum(d_up_low, axis=0, dtype=jnp.float32)
    wide_share = lax.psum_scatter(
        jnp.concatenate(
            [
                jnp.einsum("tc,tn->cn", normed_low, d_packed, preferred_element_type=jnp.float32),
                jnp.einsum(
                    "tc,tn->cn", attended_low, d_branch_low, preferred_element_type=jnp.float32
                ),
                jnp.einsum("tc,tn->cn", second_low, d_up_low, preferred_element_type=jnp.float32),
            ],
            axis=1,
        ).astype(jnp.bfloat16),
        "rows",
        scatter_dimension=0,
        tiled=True,
    )
    down_share = lax.psum_scatter(
        jnp.einsum("tf,tn->fn", activated_low, cot_low, preferred_element_type=jnp.float32).astype(
            jnp.bfloat16
        ),
        "rows",
        scatter_dimension=0,
        tiled=True,
    )
    wide_grads, down_grads = (
        lax.psum(wide_share, "blk").astype(jnp.float32),
        lax.psum(down_share, "blk").astype(jnp.float32),
    )
    grad_qkv = wide_grads[:, : 3 * model_width]
    grad_out = wide_grads[:, 3 * model_width : 4 * model_width]
    grad_up = wide_grads[:, 4 * model_width :]
    small_grads = lax.psum(
        (d_first_gain, d_first_shift, d_second_gain, d_second_shift, d_bias), ("rows", "blk")
    )
    return (
        output[None],
        grad_hidden[None],
        grad_qkv,
        grad_out,
        grad_up,
        down_grads,
        small_grads[0],
        small_grads[1],
        small_grads[2],
        small_grads[3],
        small_grads[4],
    )


MESH = pl.DeviceIdType.MESH
FORWARD_MOVES = (
    ((0, 0), (1, 0), (2, 0), (0, 1), (1, 1), (2, 1),),
    (),
    (),
    (),
    (),
    (),
    ((2, 3),),
    (),
    (),
    (),
    ((3, 0, 1, 0), (4, 0, 0), (4, 1, 0), (3, 0, 0, 0), (3, 1, 1, 0), (4, 0, 2), (3, 1, 0, 0), (0, 2), (2, 2), (4, 0, 1), (3, 0, 2, 0), (4, 1, 2), (3, 1, 2, 0), (1, 2), (4, 1, 1), (2, 5),),
    (),
    (),
    ((4, 0, 3), (3, 2, 1, 0), (2, 4), (4, 1, 3), (3, 2, 0, 0),),
    (),
    (),
    ((4, 2, 0), (0, 3),),
    ((3, 2, 2, 0), (4, 2, 2), (1, 3),),
    (),
    (),
    (),
    (),
    (),
    (),
    ((4, 2, 1),),
    (),
    (),
    (),
    (),
    (),
    ((3, 3, 1, 0), (4, 2, 3),),
    (),
    (),
    ((3, 3, 0, 0), (4, 3, 0),),
    (),
    (),
    (),
    (),
    (),
    (),
    ((4, 3, 2), (3, 3, 2, 0), (0, 4), (1, 5), (3, 4, 1, 0), (4, 3, 1), (1, 4), (3, 4, 0, 0), (4, 3, 3), (0, 5), (3, 4, 2, 0),),
    (),
    (),
    ((4, 5, 0),),
    ((3, 5, 1, 0),),
    (),
    (),
    ((4, 4, 2),),
    (),
    (),
    ((3, 5, 0, 0),),
    (),
    ((4, 4, 0),),
    (),
    ((3, 5, 1, 1),),
    (),
    ((4, 4, 1),),
    (),
    ((3, 5, 0, 1),),
    ((4, 4, 3),),
    (),
    (),
    ((3, 5, 2, 0),),
    (),
    (),
    (),
    (),
    ((3, 5, 2, 1),),
    (),
    (),
    (),
    (),
    (),
)
ROWS_Z, ROWS_Y = 4, 2
PAIR = 128
UNIT = 640
SLOTS = 2
SPARE = 3


def place_of():
    index = lax.axis_index("rows")
    return index // 4, lax.rem(index // 2, 2), lax.rem(index, 2)


def row_of(z, y, core):
    return (lax.rem(z + ROWS_Z, ROWS_Z) * ROWS_Y + y) * 2 + core


def aligned(index, step):
    return pl.ds(pl.multiple_of(index * step, step), step)


def dot_nt(left, right):
    return lax.dot_general(left, right, (((1,), (1,)), ((), ())), preferred_element_type=jnp.float32)


def dot_nn(left, right):
    return jnp.dot(left, right, preferred_element_type=jnp.float32)


def head_lanes(width):
    lane = lax.broadcasted_iota(jnp.int32, (1, width), 1)
    return (lane < HEAD_DIM, lane >= HEAD_DIM)


def greet(peers):
    barrier = pltpu.get_barrier_semaphore()
    for peer in peers:
        pl.semaphore_signal(barrier, inc=1, device_id=peer, device_id_type=MESH)
    pl.semaphore_wait(barrier, len(peers))


def neighbours():
    z, y, core = place_of()
    return [
        {"rows": row_of(z + 1, y, core)},
        {"rows": row_of(z + 2, y, core)},
        {"rows": row_of(z + 3, y, core)},
        {"rows": row_of(z, 1 - y, core)},
        {"rows": row_of(z, y, 1 - core)},
        {"blk": 1 - lax.axis_index("blk")},
    ]


def write_marks(starts_ref, key_marks, query_marks):
    shape = key_marks.shape
    at = lax.broadcasted_iota(jnp.int32, shape, 0)
    lane = lax.broadcasted_iota(jnp.int32, shape, 1)
    lane = jnp.where(lane < HEAD_DIM, lane, lane - HEAD_DIM) - SPARE
    cell = jnp.zeros(shape, jnp.int32) - 1
    for i in range(starts_ref.shape[1]):
        cell += (at >= starts_ref[0, i]).astype(jnp.int32)
    key_marks[...] = jnp.where((lane == cell) | (lane < 0), 1.0, 0.0).astype(key_marks.dtype)
    blocked = (lane != cell) & (lane >= 0) & (lane < starts_ref.shape[1])
    query_marks[...] = jnp.where(blocked, masked_score, 0.0).astype(query_marks.dtype)


def z_place(z):
    return 2 * lax.rem(z, 2) + z // 2


def grad_chunk(target, left, right):
    def half(j, carry):
        value = dot_nn(left(j), right()).astype(jnp.bfloat16)
        n = value.shape[1]
        rows = value.shape[0] // 8
        for block in range(8):
            to_z, to_y, to_core = block // 4, block // 2 % 2, block % 2
            target[to_core, to_y, 2 * to_z + j, :, :n] = value[block * rows : (block + 1) * rows]
        return carry

    lax.fori_loop(0, 2, half, 0)


def forward_kernel(
    hidden, cot, starts, gain1, shift1, gain2, shift2, bias_in, q_in, o_in, u_in, d_in,
    q_all, o_all, u_all, d_all, dy_all, down_sums, normed_t_out, packed_out, lse_out, att_out, att_t_out, resid_out,
    second_t_out, act_out, slope_out,
    hid_other, normed, wq, wo, wu, packed, key_marks, query_marks, att_part, att_own, resid, second,
    act, act_t, slope, normed_t, att_t, second_t, lse, u_wide, q_own, o_own, u_own, d_own, dy, bias, parts, core_in,
    local_sem, send_sem, recv_sem, x_send, x_recv,
):
    bf16 = jnp.bfloat16
    z, y, core = place_of()
    me = row_of(z, y, core)
    piece = lax.axis_index("blk")
    other = 1 - piece
    own_rows, width = hidden.shape
    length = packed.shape[0]
    rows = o_own.shape[0]
    early = rows * 3 // 5
    d_half = lambda half: pl.ds(half * rows, rows)
    own = (
        q_own.at[pl.ds(0, early)], q_own.at[pl.ds(early, rows - early)], o_own, u_own,
        d_own.at[d_half(0)], d_own.at[d_half(1)],
    )
    last = len(own) - 1

    def slot_of(w, at_z, at_y, at_core):
        slot = row_of(at_z, at_y, at_core)
        if w < 2:
            return q_all.at[slot, pl.ds(w * early, own[w].shape[0])]
        if w < 4:
            return (o_all, u_all)[w - 2].at[slot]
        return d_all.at[slot, d_half(w - 4)]

    x_peer = {"blk": other}
    peers = neighbours()
    pairs = packed.shape[1] // (3 * PAIR)
    first_gain, first_shift, second_gain, second_shift = (
        ref[...].reshape(1, width) for ref in (gain1, shift1, gain2, shift2)
    )

    def local(src, dst, index):
        return pltpu.make_async_copy(src, dst, local_sem.at[index])

    near = z + 1 - 2 * lax.rem(z, 2)
    far = lax.rem(z + 2, ROWS_Z)
    spread = (z, far, near, ROWS_Z - 1 - z)

    def send(w, at_z, v, place, peer, first=False):
        block = slot_of(w, at_z, y if v == 0 else 1 - y, core)
        index = w * 18 + place
        return pltpu.make_async_remote_copy(
            src_ref=own[w] if first else block, dst_ref=block, send_sem=send_sem.at[index],
            recv_sem=recv_sem.at[index], device_id=peer, device_id_type=MESH,
        )

    def along(w, k, v):
        peer = {"rows": row_of(far if k == 0 else near, y, core)}
        return send(w, far if k == 2 else z, v, 2 * k + v, peer, k < 2 and v == 0)

    def to_y(w, at_z, first=False):
        return send(w, at_z, 0, 6 + at_z, peers[3], first)

    def to_core(w, at_z, v, first=False):
        return send(w, at_z, v, 10 + 2 * at_z + v, peers[4], first)

    def pass_on(w, v):
        inner = (z == 1) | (z == 2)

        @pl.when(inner)
        def _():
            along(w, 0, v).start()

        along(w, 1, v).start()

        @pl.when(jnp.logical_not(inner))
        def _():
            along(w, 0, v).start()

    def relay_z(w, k, v):
        along(w, k, v).wait_recv()
        if k == 0:
            along(w, 2, v).start()
        at_z = spread[k + 1]
        if w < last:
            to_y(w, at_z).start()
        to_core(w, at_z, v).start()

    def relay_y(w, k):
        to_y(w, spread[k]).wait_recv()
        to_core(w, spread[k], 1).start()
        if w == last:
            pass_on(w, 1)

    def all_here(ws):
        for w in ws:
            for at_z in range(ROWS_Z):
                for v in range(2):
                    to_core(w, at_z, v).wait_recv()

    def all_here_load(ws, source, target, first):
        for i, at_z in enumerate(spread):
            for v in range(2):
                for w in ws:
                    to_core(w, at_z, v).wait_recv()
                chip = pl.ds(row_of(at_z, y if v == 0 else 1 - y, 0), 2)
                local(source.at[chip], target.at[chip], first + 2 * i + v).start()

    def loaded(source, target, first):
        for i in range(2 * ROWS_Z):
            chip = pl.ds(0, 2)
            local(source.at[chip], target.at[chip], first + i).wait()

    def all_gone(w):
        for v in range(1 if w < last else 2):
            for k in range(3):
                along(w, k, v).wait_send()
        for at_z in range(ROWS_Z) if w < last else (z,):
            to_y(w, at_z).wait_send()
        for at_z in range(ROWS_Z):
            for v in range(2):
                to_core(w, at_z, v).wait_send()

    def to_x(src, dst, index):
        return pltpu.make_async_remote_copy(
            src_ref=src, dst_ref=dst, send_sem=x_send.at[index], recv_sem=x_recv.at[index],
            device_id=x_peer, device_id_type=MESH,
        )

    third = q_in.shape[1] // 3
    share = third // 2
    q_picks = []
    for part in range(3):
        picked = q_in.at[:, pl.ds(pl.multiple_of(part * third + piece * share, 128), share)]
        q_picks.append(local(picked, q_own.at[:, pl.ds(part * share, share)], 17 + part))
        q_picks[-1].start()
    d_mine = d_in.at[pl.ds(piece * 2 * rows, 2 * rows)]
    local(o_in, o_own, 1).start()
    local(u_in, u_wide, 2).start()
    local(d_mine, d_own, 3).start()
    local(cot, dy.at[piece], 4).start()
    greet(peers)
    for copy in q_picks:
        copy.wait()
    hidden_x = to_x(hidden, hid_other, 0)
    cot_x = to_x(cot, dy.at[piece], 1)
    local(o_in, o_own, 1).wait()
    local(d_mine, d_own, 3).wait()
    local(u_in, u_wide, 2).wait()
    half_rows = lambda half: pl.ds(pl.multiple_of(half * own_rows, 128), own_rows)

    def first_copies():
        local(q_own, q_all.at[me], 0).start()
        local(o_own, o_all.at[me], 1).start()
        local(d_own, d_all.at[me], 3).start()
        local(cot, dy.at[piece], 4).wait()

    units_each = 2 * rows
    group = 8 * units_each

    def mine(block):
        wide = block.astype(jnp.float32)
        halves = []
        for half in range(2):
            at = [slice((2 * j + half) * units_each, (2 * j + half + 1) * units_each) for j in range(4)]
            halves.append(jnp.concatenate([wide[:, cols] for cols in at], axis=1))
        return jnp.where(piece == 0, halves[0], halves[1])

    def pick_units(g):
        cols = slice(g * group // 2, (g + 1) * group // 2)
        u_own[:, cols] = mine(u_wide[:, g * group : (g + 1) * group]).astype(bf16)
        bias[:, cols] = mine(bias_in[g * group : (g + 1) * group].reshape(1, group))
        if g == u_own.shape[1] * 2 // group - 1:
            local(u_own, u_all.at[me], 2).start()

    def norm_rows(source, half, part):
        step = 64
        steps = own_rows // step

        def body(i, carry):
            value = source[aligned(i, step), :].astype(jnp.float32)
            low = layer_norm(value, first_gain, first_shift).astype(bf16)
            normed[pl.ds(pl.multiple_of(half * own_rows + i * step, step), step), :] = low
            return carry

        lax.fori_loop(steps * part // 2, steps * (part + 1) // 2, body, 0)

    def q_here():
        local(q_own, q_all.at[me], 0).wait()
        all_here_load((0, 1), q_all, wq, 20)

    def project(begin, end):
        def body(part, carry):
            cols = aligned(part, share)
            value = dot_nn(normed[...], wq[:, :, cols].reshape(width, share)).astype(bf16)
            packed[:, cols] = value * jnp.where(part == 0, HEAD_DIM ** (-0.5), 1.0).astype(bf16)
            return carry

        lax.fori_loop(begin, end, body, 0)
        if end == 3:
            local(packed, packed_out, 9).start()

    first_lanes = head_lanes(PAIR)

    def att_cols(half, p):
        return pl.ds(pl.multiple_of(half * pairs * PAIR + p * PAIR, PAIR), PAIR)

    def attend(p, half):
        at_q, at_k, at_v = (slice(t * share + PAIR * p, t * share + PAIR * (p + 1)) for t in range(3))
        value_t = packed[:, at_v].T
        at = half_rows(half)
        queries = packed[at, at_q]
        keys = packed[:, at_k]
        halves = []
        for h in range(2):
            one = jnp.where(first_lanes[h], queries, query_marks[at, :])
            scores = dot_nt(jnp.where(first_lanes[h], keys, key_marks[...]), one)
            top = jnp.max(scores, axis=0, keepdims=True)
            weights = jnp.exp(scores - top)
            total = jnp.sum(weights, axis=0, keepdims=True)
            lse[2 * p + h : 2 * p + h + 1, at] = top + jnp.log(total)
            summed = dot_nn(value_t[h * HEAD_DIM : (h + 1) * HEAD_DIM], weights.astype(bf16))
            halves.append(summed / total)
        return jnp.concatenate(halves, axis=0).T.astype(bf16)

    def attend_other(p):
        att_part[:, p * PAIR : (p + 1) * PAIR] = attend(p, other)

    def attend_own(p):
        att_own[:, att_cols(piece, p)] = attend(p, piece)
        if p == pairs - 1:
            for copy in att_outs:
                copy.start()

    att_x = [
        to_x(att_part.at[:, pl.ds(p * PAIR, PAIR)], att_own.at[:, att_cols(piece, p)], 2 + p) for p in range(pairs)
    ]

    att_outs = (
        local(att_part, att_out.at[half_rows(other)], 45),
        local(att_own.at[:, pl.ds(pl.multiple_of(piece * share, 128), share)], att_out.at[half_rows(piece)], 46),
    )

    def o_here():
        local(o_own, o_all.at[me], 1).wait()
        all_here_load((2,), o_all, wo, 28)

    def att_here():
        for copy in att_x:
            copy.wait_recv()
        loaded(o_all, wo, 28)

    part_rows = own_rows // 2
    second_x = [
        to_x(second.at[piece, pl.ds(i * part_rows, part_rows)], second.at[piece, pl.ds(i * part_rows, part_rows)], 2 + pairs + i)
        for i in range(2)
    ]

    def merge(part):
        for cols in (slice(0, 512), slice(512, width)) if part == 0 else ():
            weight = wo[:, :, cols].reshape(width, cols.stop - cols.start)
            resid[:, cols] = hidden[:, cols].astype(jnp.float32) + dot_nn(att_own[...], weight)

        def second_rows(i, carry):
            rows = aligned(i, 64)
            second[piece, rows, :] = layer_norm(resid[rows, :], second_gain, second_shift).astype(bf16)
            return carry

        lax.fori_loop(part * part_rows // 64, (part + 1) * part_rows // 64, second_rows, 0)
        if part == 1:
            local(resid, resid_out, 12).start()

    def flip_normed():
        def body(i, carry):
            normed_t[aligned(i, 128), :] = normed[:, aligned(i, 128)].T
            return carry

        lax.fori_loop(0, width // 128, body, 0)
        local(normed_t, normed_t_out, 8).start()
        local(lse, lse_out, 10).start()

    def flip_second(half):
        def body(i, carry):
            second_t[aligned(i, 128), half_rows(half)] = second[half, :, aligned(i, 128)].T
            return carry

        lax.fori_loop(0, width // 128, body, 0)

    def flip_att():
        def body(i, carry):
            att_t[aligned(i, 128), :] = att_own[:, aligned(i, 128)].T
            return carry

        lax.fori_loop(0, width // 128, body, 0)
        local(att_t, att_t_out, 11).start()
        flip_second(piece)

    def u_here():
        local(u_own, u_all.at[me], 2).wait()
        all_here_load((3,), u_all, wu, 36)

    unit = 512
    fifth = act.shape[1] // unit // 5

    def expand(half, begin):
        at = half_rows(half)

        def body(i, carry):
            cols = aligned(i, unit)
            weight = wu[:, :, cols].reshape(width, unit)
            up = dot_nn(second[half], weight) + bias[:, cols]
            cdf = 0.5 * (1.0 + lax.erf(up * (0.5 ** 0.5)))
            pdf = jnp.exp(up * up * -0.5) * ((2.0 * math.pi) ** -0.5)
            value = (up * cdf).astype(bf16)
            act[at, cols] = value
            act_t[cols, at] = value.T
            slope[at, cols] = (cdf + up * pdf).astype(bf16)
            return carry

        lax.fori_loop(begin * fifth, (begin + 1) * fifth, body, 0)
        if begin == 4:
            for copy in halves_out(half):
                copy.start()

    def halves_out(half):
        base = 54 if half is piece else 56
        at = half_rows(half)
        return (
            local(act.at[at], act_out.at[at], base),
            local(slope.at[at], slope_out.at[at], base + 1),
        )

    def second_here():
        for copy in second_x:
            copy.wait_recv()

    def flip_last():
        flip_second(other)
        local(second_t, second_t_out, 13).start()

    def dy_here():
        cot_x.wait_recv()
        local(dy.at[other], dy_all, 4).start()

    def grad_down(i):
        h, at = i // 2, slice(i % 2 * UNIT, (i % 2 + 1) * UNIT)

        def left(j):
            begin = lambda block: pl.multiple_of((8 * j + block) * 2 * rows + h * rows, 16)
            return jnp.concatenate([act_t[pl.ds(begin(block), rows), :] for block in range(8)], axis=0)

        grad_chunk(parts.at[i % SLOTS], left, lambda: dy[:, :, at].reshape(length, UNIT))

    sums_x = [
        pltpu.make_async_remote_copy(
            src_ref=parts.at[i % SLOTS, 1 - core], dst_ref=core_in.at[i], send_sem=x_send.at[4 + pairs + i],
            recv_sem=x_recv.at[4 + pairs + i], device_id=peers[4], device_id_type=MESH,
        )
        for i in range(4)
    ]

    def sum_down(i):
        core_in[i] += parts[i % SLOTS, core]
        sums_x[i].wait_send()
        local(core_in.at[i], down_sums.at[i], 50 + i).start()

    def outputs():
        for i in range(4):
            local(core_in.at[i], down_sums.at[i], 50 + i).wait()
        local(dy.at[other], dy_all, 4).wait()
        local(d_own, d_all.at[me], 3).wait()
        local(normed_t, normed_t_out, 8).wait()
        local(packed, packed_out, 9).wait()
        local(lse, lse_out, 10).wait()
        for copy in att_outs:
            copy.wait()
        local(att_t, att_t_out, 11).wait()
        local(resid, resid_out, 12).wait()
        local(second_t, second_t_out, 13).wait()
        for half in (piece, other):
            for copy in halves_out(half):
                copy.wait()

    act_now = functools.partial
    steps = [hidden_x.start, cot_x.start]
    steps += [act_now(pick_units, g) for g in range(4)]
    steps += [act_now(norm_rows, hidden, piece, part) for part in range(2)]
    steps += [act_now(write_marks, starts, key_marks, query_marks), lambda: None]
    steps += [hidden_x.wait_recv]
    steps += [act_now(norm_rows, hid_other, other, part) for part in range(2)]
    steps += [q_here, act_now(loaded, q_all, wq, 20), act_now(project, 0, 1), act_now(project, 1, 3)]
    for p in range(pairs):
        steps += [act_now(attend_other, p), att_x[p].start]
    steps += [act_now(attend_own, p) for p in range(pairs - 1)]
    steps += [o_here, act_now(attend_own, pairs - 1), att_here]
    steps += [act_now(merge, 0), second_x[0].start, act_now(merge, 1), second_x[1].start]
    steps += [flip_normed, flip_att, u_here, act_now(loaded, u_all, wu, 36)]
    steps += [act_now(expand, piece, i) for i in range(5)]
    steps += [second_here, flip_last]
    steps += [act_now(expand, other, i) for i in range(5)]
    steps += [dy_here]
    for i in range(4):
        steps += [act_now(grad_down, i), sums_x[i].start]
        if i:
            steps += [sums_x[i - 1].wait_recv, act_now(sum_down, i - 1)]
    steps += [sums_x[3].wait_recv, act_now(sum_down, 3), outputs, act_now(all_here, (4, 5))]
    moves = (
        lambda w: pass_on(w, 0),
        lambda w: to_y(w, z, True).start(),
        lambda w: to_core(w, z, 0, True).start(),
        relay_z,
        relay_y,
    )
    for i, step in enumerate(steps):
        for kind, *where in FORWARD_MOVES[i]:
            moves[kind](*where)
        step()
        if i == 1:
            first_copies()
    for w in range(len(own)):
        all_gone(w)
    for copy in [hidden_x, cot_x] + second_x + att_x:
        copy.wait_send()


def forward(hidden, cot, starts, gain1, shift1, gain2, shift2, bias, qkv, out, up, down):
    own_rows, width = hidden.shape
    length = 2 * own_rows
    cols = qkv.shape[1] // 2
    units = up.shape[1] // 2
    rows = up.shape[0]
    bf16, f32 = jnp.bfloat16, jnp.float32
    shards = lax.axis_size("rows")
    head_rows = 16
    outs = [
        ((shards, rows, cols), bf16),
        ((shards, rows, width), bf16),
        ((shards, rows, units), bf16),
        ((shards, down.shape[0] // 2, width), bf16),
        ((own_rows, width), bf16),
        ((4, 2, ROWS_Z, rows, UNIT), bf16),
        ((width, length), bf16),
        ((length, cols), bf16),
        ((head_rows, length), f32),
        ((length, cols // 3), bf16),
        ((width, own_rows), bf16),
        ((own_rows, width), f32),
        ((width, length), bf16),
        ((length, units), bf16),
        ((length, units), bf16),
    ]
    scratch = [
        ((own_rows, width), bf16),
        ((length, width), bf16),
        ((shards, rows, cols), bf16),
        ((shards, rows, width), bf16),
        ((shards, rows, units), bf16),
        ((length, cols), bf16),
        ((length, PAIR), bf16),
        ((length, PAIR), bf16),
        ((own_rows, cols // 3), bf16),
        ((own_rows, width), bf16),
        ((own_rows, width), f32),
        ((2, own_rows, width), bf16),
        ((length, units), bf16),
        ((units, length), bf16),
        ((length, units), bf16),
        ((width, length), bf16),
        ((width, own_rows), bf16),
        ((width, length), bf16),
        ((head_rows, length), f32),
        ((rows, 2 * units), bf16),
        ((rows, cols), bf16),
        ((rows, width), bf16),
        ((rows, units), bf16),
        ((2 * rows, width), bf16),
        ((2, own_rows, width), bf16),
        ((1, units), f32),
        ((SLOTS, 2, 2, ROWS_Z, rows, UNIT), bf16),
        ((4, 2, ROWS_Z, rows, UNIT), bf16),
    ]
    vmem = pl.BlockSpec(memory_space=pltpu.VMEM)
    anywhere = pl.BlockSpec(memory_space=pl.ANY)
    smem = pl.BlockSpec(memory_space=pltpu.SMEM)
    dma = pltpu.SemaphoreType.DMA
    x_copies = 8 + cols // (3 * PAIR)
    return pl.pallas_call(
        forward_kernel,
        out_shape=[jax.ShapeDtypeStruct(shape, kind) for shape, kind in outs],
        in_specs=[vmem, anywhere, smem] + [vmem] * 5 + [anywhere] * 4,
        out_specs=[anywhere] * len(outs),
        scratch_shapes=[pltpu.VMEM(shape, kind) for shape, kind in scratch]
        + [dma((58,)), dma((108,)), dma((108,)), dma((x_copies,)), dma((x_copies,))],
        compiler_params=pltpu.CompilerParams(
            collective_id=1, has_side_effects=True, vmem_limit_bytes=60 * 1024 * 1024
        ),
        name="forward",
    )(hidden, cot, starts, gain1, shift1, gain2, shift2, bias, qkv, out, up, down)


BACKWARD_MOVES = (
    ((1, 0), (2, 0), (3, 0), (0, 0),),
    (),
    (),
    (),
    (),
    (),
    (),
    ((2, 1), (1, 1),),
    (),
    (),
    (),
    (),
    (),
    ((4, 0), (3, 1), (0, 1),),
    ((5, 0),),
    ((2, 2),),
    (),
    ((6, 0), (1, 2),),
    ((7, 0), (4, 1), (3, 2),),
    (),
    (),
    ((0, 2),),
    (),
    (),
    (),
    (),
    (),
    (),
    (),
    (),
    ((2, 3), (5, 1),),
    (),
    (),
    ((8, 0), (4, 2), (9, 0), (3, 3),),
    (),
    (),
    ((5, 2), (10, 0), (6, 1), (1, 3),),
    (),
    (),
    (),
    ((11, 0),),
    (),
    (),
    ((7, 1), (0, 3), (8, 1), (4, 3), (12, 0), (5, 3),),
    (),
    (),
    ((6, 2),),
    (),
    (),
    (),
    ((9, 1),),
    (),
    (),
    (),
    ((7, 2), (13, 0), (14, 0), (10, 1), (8, 2), (11, 1), (6, 3), (9, 2), (12, 1), (7, 3), (10, 2), (13, 1), (11, 2), (9, 3), (14, 1),),
    ((8, 3), (12, 2), (10, 3),),
    (),
    (),
    ((13, 2),),
    ((11, 3), (14, 2), (12, 3), (13, 3),),
    ((14, 3),),
)


def thirds(value):
    high = value.astype(jnp.bfloat16)
    rest = value - high.astype(jnp.float32)
    middle = rest.astype(jnp.bfloat16)
    return high, middle, (rest - middle.astype(jnp.float32)).astype(jnp.bfloat16)


def norm_back(values, gain, grad):
    centred = values - jnp.mean(values, axis=-1, keepdims=True)
    scale = lax.rsqrt(jnp.mean(centred * centred, axis=-1, keepdims=True) + 1e-05)
    unit = centred * scale
    scaled = grad * gain
    mean_one = jnp.mean(scaled, axis=-1, keepdims=True)
    mean_two = jnp.mean(scaled * unit, axis=-1, keepdims=True)
    d_values = scale * (scaled - mean_one - unit * mean_two)
    d_gain = jnp.sum(grad * unit, axis=0, keepdims=True)
    d_shift = jnp.sum(grad, axis=0, keepdims=True)
    return d_values, d_gain, d_shift


def backward_kernel(
    starts, gain1, gain2, hidden, cot, dy_other, q_all, o_all, u_all, d_all, down_sums, normed_t, packed, lse_in, att_in, att_t_in,
    resid, second_t, act, slope,
    output, grad_hidden, units_out, pairs_out, small_out,
    lhs, att_t, att_own, half_act, wide, wd, wu, dy, first, second, d_att, x_in0, x_in1, x_out0, down_own,
    parts, core_in, core_in_q, y_in, y_in_q, z_in, z_in_q, down_early, lse_rows, lse, key_marks, query_marks, acc_k, acc_v, bias_sum, early, late,
    early_near, late_near, early_all, late_all, small,
    local_sem, a_send, a_recv, b_send, b_recv, c_send, c_recv, g_send, g_recv, x_send, x_recv,
    s_send, s_recv, keep_sem,
):
    bf16, f32 = jnp.bfloat16, jnp.float32
    z, y, core = place_of()
    piece = lax.axis_index("blk")
    other = 1 - piece
    own_rows, width = first.shape
    length = 2 * own_rows
    branch = half_act.at[:, pl.ds(0, width)]
    units = wide.shape[1]
    d_width = d_att.shape[1]
    cols = 3 * d_width
    pairs = d_width // PAIR
    near = z + 1 - 2 * lax.rem(z, 2)
    far = lax.rem(z + 2, ROWS_Z)
    peer_core, peer_y = {"rows": row_of(z, y, 1 - core)}, {"rows": row_of(z, 1 - y, core)}
    peer_near, peer_far = {"rows": row_of(near, y, core)}, {"rows": row_of(far, y, core)}
    peer_x = {"blk": other}
    group = [peer_core, peer_y, {"rows": row_of(z, 1 - y, 1 - core)}]
    line = [
        {"rows": row_of(z + k, y, core), "blk": lax.rem(piece + n, 2)} for n in range(2) for k in range(ROWS_Z) if n or k
    ]
    wide_chunks = core_in.shape[0]
    chunks = wide_chunks + pairs
    first_gain, second_gain = gain1[...].reshape(1, width), gain2[...].reshape(1, width)
    half_rows = lambda half: pl.ds(pl.multiple_of(half * own_rows, 128), own_rows)
    part_rows = own_rows // 2

    def remote(src, dst, sends, recvs, index, peer):
        return pltpu.make_async_remote_copy(
            src_ref=src, dst_ref=dst, send_sem=sends.at[index], recv_sem=recvs.at[index],
            device_id=peer, device_id_type=MESH,
        )

    loads = {
        "sums": (down_sums, core_in.at[pl.ds(0, 4)], 0),
        "dy": (cot, dy.at[piece], 1),
        "dy_other": (dy_other, dy.at[other], 2),
        "up": (u_all, wu, 4),
        "act_other": (act.at[half_rows(other)], half_act, 5),
        "act_own": (act.at[half_rows(piece)], half_act, 6),
        "resid": (resid, second, 7),
        "lse": (lse_in, lse_rows.at[pl.ds(0, 16)], 8),
        "second_t": (second_t, lhs, 9),
        "att_t": (att_t_in, att_t, 10),
        "out": (o_all, wd.at[pl.ds(0, width)], 11),
        "normed_t": (normed_t, wd.at[pl.ds(width, width), pl.ds(0, length)], 12),
        "qkv": (q_all, wu.at[:, pl.ds(0, cols)], 13),
        "packed": (packed, wide.at[:, pl.ds(0, cols)], 14),
        "hidden": (hidden, branch, 15),
        "output": (second, output, 16),
        "grad_hidden": (first, grad_hidden, 17),
        "att": (att_in, att_own, 18),
    }

    def local(name):
        src, dst, index = loads[name]
        return pltpu.make_async_copy(src, dst, local_sem.at[index])

    z_first = (0, 1, 8)
    mine, theirs = pl.ds(2 * lax.rem(z, 2), 2), pl.ds(2 - 2 * lax.rem(z, 2), 2)
    place, far_place = z_place(z), z_place(far)
    order = tuple(range(chunks))

    def buffers(i):
        if i < wide_chunks:
            return core_in.at[i], y_in.at[i], z_in.at[i], units_out.at[:, i], UNIT
        i -= wide_chunks
        return core_in_q.at[i], y_in_q.at[i], z_in_q.at[i], pairs_out.at[:, i], 3 * PAIR

    def copy_a(i):
        into, _, _, _, n = buffers(i)
        return remote(parts.at[i % SLOTS, 1 - core, :, :, :, pl.ds(0, n)], into, a_send, a_recv, i, peer_core)

    def copy_b(i):
        sums, by_y, by_z, _, _ = buffers(i)
        if i < 4 and i not in z_first:
            sums = down_sums.at[i]
        if i in z_first:
            return remote(sums.at[1 - y, place], by_z.at[2], b_send, b_recv, i, peer_y)
        return remote(sums.at[1 - y], by_y, b_send, b_recv, i, peer_y)

    def copies_c(i, step):
        sums, by_y, by_z, _, _ = buffers(i)
        index = 4 * i + 2 * step
        if i not in z_first:
            if step == 0:
                return [remote(by_y.at[theirs], by_z.at[pl.ds(0, 2)], c_send, c_recv, index, peer_near)]
            return [remote(by_y.at[far_place], by_z.at[2], c_send, c_recv, index, peer_far)]
        if step == 0:
            sums = down_sums.at[i] if i < 4 else sums
            return [
                remote(sums.at[v, theirs], by_y.at[pl.ds(2 * v, 2)], c_send, c_recv, index + v, peer_near)
                for v in range(2)
            ]
        return [remote(sums.at[v, far_place], by_z.at[v], c_send, c_recv, index + v, peer_far) for v in range(2)]

    def copy_g(i):
        _, _, by_z, out, _ = buffers(i)
        return remote(by_z.at[0], out.at[piece], g_send, g_recv, i, peer_x)

    def keep_g(i):
        _, _, by_z, out, _ = buffers(i)
        return pltpu.make_async_copy(by_z.at[0], out.at[piece], keep_sem.at[i])

    unread = ["sums"]

    def move(i, stage):
        sums, by_y, by_z, _, n = buffers(i)
        if i < 4 and stage and unread:
            local(unread.pop()).wait()
        if stage == 0:
            slot = i % SLOTS
            if i >= 4:
                copy_a(i).wait_recv()
                sums[1 - y] += parts[slot, core, 1 - y, :, :, :n]
                if i in z_first:
                    sums[y] += parts[slot, core, y, :, :, :n]
            if i in z_first:
                for copy in copies_c(i, 0):
                    copy.start()
            else:
                copy_b(i).start()
            if i >= 4:
                if i not in z_first:
                    sums[y] += parts[slot, core, y, :, :, :n]
                copy_a(i).wait_send()
        elif i in z_first and stage < 3:
            for v, copy in enumerate(copies_c(i, stage - 1)):
                copy.wait_recv()
                if stage == 1:
                    sums[v, mine] += by_y[2 * v : 2 * v + 2]
                else:
                    sums[v, place] += by_z[v]
            for copy in copies_c(i, 1) if stage == 1 else [copy_b(i)]:
                copy.start()
        elif stage == 1:
            copy_b(i).wait_recv()
            by_y[...] += sums[y]
            copies_c(i, 0)[0].start()
        elif stage == 2:
            copies_c(i, 0)[0].wait_recv()
            by_y[mine] += by_z[0:2]
            copies_c(i, 1)[0].start()
        else:
            if i in z_first:
                copy_b(i).wait_recv()
                total = sums[y, place].astype(f32) + by_z[2].astype(f32)
            else:
                copies_c(i, 1)[0].wait_recv()
                total = by_y[place].astype(f32) + by_z[2].astype(f32)
            by_z[0] = total.astype(bf16)
            copy_g(i).start()
            keep_g(i).start()

    tile = 512

    def tile_loads(i):
        at = aligned(i, tile)
        return (
            pltpu.make_async_copy(d_all.at[at], wd.at[at], local_sem.at[19 + 2 * i]),
            pltpu.make_async_copy(slope.at[:, at], wide.at[:, at], local_sem.at[20 + 2 * i]),
        )

    local("act_other").start()
    for i in range(units // tile):
        tile_loads(i)[0].start()
    local("dy").start()
    local("dy_other").start()
    for i in range(units // tile):
        tile_loads(i)[1].start()
    greet(group + line)

    def ready_units():
        local("act_other").wait()
        for i in range(units // tile):
            tile_loads(i)[0].wait()
        for name in ("sums", "up", "second_t", "resid", "lse", "att_t"):
            local(name).start()

    halves = (slice(0, 512), slice(512, width))

    def d_units(begin, end):
        if begin == 0:
            local("dy").wait()
            local("dy_other").wait()

        def body(i, carry):
            tile_loads(i)[1].wait()
            at = aligned(i, tile)
            value = dot_nt(dy[...].reshape(length, width), wd[at, :]) * wide[:, at].astype(f32)
            low = value.astype(bf16)
            wide[:, at] = low
            bias_sum[:, at] = jnp.sum(low.astype(f32), axis=0, keepdims=True)
            return carry

        lax.fori_loop(begin, end, body, 0)

    def d_second(half, part, target):
        if part == 0 and target is x_out0:
            local("up").wait()
        at = halves[part]
        target[:, at] = dot_nt(wide[half_rows(half), :], wu[at, :]).astype(target.dtype)

    def exchange(part, index):
        at = pl.ds(halves[part].start, halves[part].stop - halves[part].start)
        return remote(x_out0.at[:, at], x_in0.at[:, at], x_send, x_recv, index, peer_x)

    second_x = [exchange(part, part) for part in range(2)]
    normed_x = [exchange(part, 2 + part) for part in range(2)]
    first_cols, rest_cols = (pl.ds(at.start, at.stop - at.start) for at in halves)
    down_x = [
        remote(down_early, x_in1.at[:, first_cols], x_send, x_recv, 4, peer_x),
        remote(dy.at[other, :, rest_cols], x_in1.at[:, rest_cols], x_send, x_recv, 5 + pairs, peer_x),
    ]
    att_x = [
        remote(
            x_out0.at[:, pl.ds(p * PAIR, PAIR)], d_att.at[half_rows(piece), pl.ds(p * PAIR, PAIR)],
            x_send, x_recv, 5 + p, peer_x,
        )
        for p in range(pairs)
    ]

    def d_second_own():
        for part in range(2):
            d_second(piece, part, first)
        local("qkv").start()

    def down_first():
        down_early[...] = dot_nn(half_act[...], wd[:, halves[0]]).astype(bf16)

    def down_other():
        dy[other, :, halves[1]] = dot_nn(half_act[...], wd[:, halves[1]]).astype(bf16)
        local("act_own").start()

    def down_mine():
        local("act_own").wait()
        for at in halves:
            down_own[:, at] = dot_nn(half_act[...], wd[:, at]).astype(bf16)
        local("out").start()
        local("normed_t").start()

    def chunk(i, left, right):
        grad_chunk(parts.at[i % SLOTS], left, right)
        copy_a(i).start()

    def grad_up(i):
        if i == 0:
            local("second_t").wait()
        left = lambda j: lhs[pl.ds(8 * j, 8)].reshape(8 * lhs.shape[1], length)
        chunk(4 + i, left, lambda: wide[:, i * UNIT : (i + 1) * UNIT])
        if i == 3:
            local("packed").start()
            local("att").start()

    step = 64

    def back_two(part):
        if part == 0:
            local("resid").wait()
            for copy in second_x:
                copy.wait_recv()

        def body(i, carry):
            rows = aligned(i, step)
            grad = first[rows, :] + x_in0[rows, :].astype(f32)
            d_values, d_gain, d_shift = norm_back(second[rows, :], second_gain, grad)
            total = dy[piece, rows, :].astype(f32) + d_values
            first[rows, :] = total
            branch[rows, :] = total.astype(bf16)
            early[0:1, :] += d_gain
            early[1:2, :] += d_shift
            return carry

        steps_each = part_rows // step
        if part == 0:
            early[...] = jnp.zeros_like(early)
        lax.fori_loop(part * steps_each, (part + 1) * steps_each, body, 0)

    def d_attended(half):
        rows = pl.ds(pl.multiple_of(half * d_width, 128), d_width)
        return dot_nt(branch[...], wd[rows, :]).astype(bf16)

    def d_att_other():
        local("out").wait()
        for copy in second_x:
            copy.wait_send()
        x_out0[:, :d_width] = d_attended(other)

    def d_att_own():
        d_att[half_rows(piece), :] = d_attended(piece)

    def grad_out(i):
        if i == 0:
            local("att_t").wait()
        left = lambda j: att_t[pl.ds(8 * j, 8)].reshape(8 * att_t.shape[1], own_rows)
        chunk(8 + i, left, lambda: branch[:, i * UNIT : (i + 1) * UNIT])
        if i == 1:
            local("hidden").start()

    first_lanes = head_lanes(PAIR)
    query_chunk = 256

    def pair_cols(p):
        return tuple(slice(t * d_width + PAIR * p, t * d_width + PAIR * (p + 1)) for t in range(3))

    def att_here(p):
        if p == 0:
            for name in ("lse", "packed", "normed_t", "att"):
                local(name).wait()
            lse[...] = lse_rows[...].T
        att_x[p].wait_recv()
        acc_k[...] = jnp.zeros_like(acc_k)
        acc_v[...] = jnp.zeros_like(acc_v)

    lane = lax.broadcasted_iota(jnp.int32, (1, PAIR), 1)
    lane = jnp.where(lane < HEAD_DIM, lane, lane - HEAD_DIM)

    def marked(value, marks):
        for at, part in enumerate(thirds(value)):
            marks = jnp.where(lane == at, part, marks)
        return marks

    def attend_back(p):
        at_q, at_k, at_v = pair_cols(p)
        heads = slice(p * PAIR, (p + 1) * PAIR)
        keys_t = wide[:, at_k].T

        def one_chunk(i, carry):
            rows = aligned(i, query_chunk)
            keys, values, queries = wide[:, at_k], wide[:, at_v], wide[rows, at_q]
            grads = d_att[rows, heads]
            attended = att_own[rows, heads]
            products = grads.astype(f32) * attended.astype(f32)
            nothing = jnp.zeros_like(queries)
            parts_q = []
            for h in range(2):
                here = first_lanes[h]
                dots = jnp.sum(jnp.where(here, products, 0.0), axis=1, keepdims=True)
                top = lse[rows, 2 * p + h : 2 * p + h + 1]
                one_q = jnp.where(here, queries, marked(-top, query_marks[rows, :]))
                one_g = jnp.where(here, grads, marked(-dots, nothing))
                probs = jnp.exp(dot_nt(jnp.where(here, keys, key_marks[...]), one_q))
                d_scores = (probs * dot_nt(jnp.where(here, values, key_marks[...]), one_g)).astype(bf16)
                acc_v[...] += dot_nn(probs.astype(bf16), jnp.where(here, grads, nothing))
                acc_k[...] += dot_nn(d_scores, jnp.where(here, queries, nothing))
                parts_q.append(dot_nn(keys_t[h * HEAD_DIM : (h + 1) * HEAD_DIM], d_scores))
            d_queries = jnp.concatenate(parts_q, axis=0).T * HEAD_DIM ** (-0.5)
            wide[rows, at_q] = d_queries.astype(bf16)
            return carry

        lax.fori_loop(0, length // query_chunk, one_chunk, 0)
        wide[:, at_k] = acc_k[...].astype(bf16)
        wide[:, at_v] = acc_v[...].astype(bf16)

    def grad_pair(p):
        n = 8 * parts.shape[4]
        left = lambda j: wd[pl.ds(pl.multiple_of(width + j * n, 64), n), :length]
        chunk(10 + p, left, lambda: jnp.concatenate([wide[:, at] for at in pair_cols(p)], axis=1))

    def down_here():
        for copy in down_x:
            copy.wait_recv()

    def write_output():
        def body(i, carry):
            rows = aligned(i, step)
            second[rows, :] += down_own[rows, :].astype(f32) + x_in1[rows, :].astype(f32)
            return carry

        lax.fori_loop(0, own_rows // step, body, 0)
        local("output").start()

    def d_normed(half, part, target):
        if part == 0 and target is x_out0:
            local("qkv").wait()
            for copy in att_x:
                copy.wait_send()
        at = halves[part]
        target[:, at] = dot_nt(wide[half_rows(half), :cols], wu[at, :cols]).astype(target.dtype)

    def d_normed_own():
        local("output").wait()
        for part in range(2):
            d_normed(piece, part, second)

    def back_one(part):
        if part == 0:
            local("hidden").wait()
            late[...] = jnp.zeros_like(late)
            for copy in normed_x:
                copy.wait_recv()

        def body(i, carry):
            rows = aligned(i, step)
            grad = second[rows, :] + x_in0[rows, :].astype(f32)
            d_values, d_gain, d_shift = norm_back(branch[rows, :].astype(f32), first_gain, grad)
            first[rows, :] += d_values
            late[0:1, :] += d_gain
            late[1:2, :] += d_shift
            return carry

        steps_each = part_rows // step
        lax.fori_loop(part * steps_each, (part + 1) * steps_each, body, 0)
        if part == 1:
            local("grad_hidden").start()

    def small_near(value, near_slots, base):
        own_slot = 2 * y + core
        return [
            remote(value, near_slots.at[own_slot], s_send, s_recv, base + k, peer) for k, peer in enumerate(group)
        ]

    def small_line(all_slots, base):
        own_slot = z * 2 + piece
        return [
            remote(all_slots.at[own_slot], all_slots.at[own_slot], s_send, s_recv, base + 3 + k, peer)
            for k, peer in enumerate(line)
        ]

    def small_one(value, near_slots, base):
        near_slots[2 * y + core] = value[...]
        for copy in small_near(value, near_slots, base):
            copy.start()

    def small_two(value, near_slots, all_slots, base):
        for copy in small_near(value, near_slots, base):
            copy.wait()
        all_slots[z * 2 + piece] = ((near_slots[0] + near_slots[1]) + near_slots[2]) + near_slots[3]
        for copy in small_line(all_slots, base):
            copy.start()

    def small_three(all_slots, base, at):
        for copy in small_line(all_slots, base):
            copy.wait()
        n = all_slots.shape[1]
        for x in range(2):
            total = ((all_slots[x] + all_slots[2 + x]) + all_slots[4 + x]) + all_slots[6 + x]
            small[x, at : at + n, :] = total

    def early_one():
        early[2:3, :] = bias_sum[:, :width]
        early[3:4, :] = bias_sum[:, width:]
        small_one(early, early_near, 0)

    call = functools.partial
    steps = [ready_units, down_first, down_x[0].start, call(d_units, 0, 2), call(d_units, 2, 4), call(d_units, 4, 5)]
    for part in range(2):
        steps += [call(d_second, other, part, x_out0), second_x[part].start]
    steps += [call(grad_up, 0), call(grad_up, 1), d_second_own, down_other, call(grad_up, 2), call(grad_up, 3), down_mine]
    steps += [call(write_marks, starts, key_marks, query_marks), call(back_two, 0), call(back_two, 1), d_att_other]
    steps += [copy.start for copy in att_x]
    steps += [d_att_own, down_x[1].start, early_one, call(grad_out, 0), call(grad_out, 1)]
    for p in range(pairs):
        steps += [call(att_here, p)] + [call(attend_back, p)]
        if p < 3:
            steps += [call(grad_pair, p)]
        if p == 1:
            steps += [call(small_two, early, early_near, early_all, 0)]
    for part in range(2):
        steps += [call(d_normed, other, part, x_out0), normed_x[part].start]
    steps += [call(grad_pair, 3), call(grad_pair, 4), down_here, write_output, d_normed_own]
    steps += [call(back_one, 0), call(back_one, 1), call(small_one, late, late_near, 10)]
    steps += [call(small_three, early_all, 0, 2), call(small_two, late, late_near, late_all, 10)]
    steps += [call(small_three, late_all, 10, 0)]
    for i, one in enumerate(steps):
        for where in BACKWARD_MOVES[i]:
            move(*where)
        one()
    small_keep = pltpu.make_async_copy(small, small_out, keep_sem.at[chunks])
    small_keep.start()
    for where in BACKWARD_MOVES[len(steps)]:
        move(*where)
    for i in range(chunks):
        copy_b(i).wait_send()
        for copy in copies_c(i, 0) + copies_c(i, 1):
            copy.wait_send()
        copy_g(i).wait()
        keep_g(i).wait()
    small_keep.wait()
    for copy in down_x + normed_x:
        copy.wait_send()
    local("grad_hidden").wait()


def backward(starts, gain1, gain2, hidden, cot, dy_other, q_all, o_all, u_all, d_all, *kept):
    bf16, f32 = jnp.bfloat16, jnp.float32
    own_rows, width = hidden.shape
    length = 2 * own_rows
    cols, units = q_all.shape[1], u_all.shape[1]
    rows = width // 16
    wide_units, pairs = 10, cols // (3 * PAIR)
    pair_cols = 3 * PAIR
    outs = [
        ((own_rows, width), f32),
        ((own_rows, width), f32),
        ((2, wide_units, rows, UNIT), bf16),
        ((2, pairs, rows, pair_cols), bf16),
        ((2, 6, width), f32),
    ]
    token = ((own_rows, width), bf16)
    scratch = [
        ((16, rows, length), bf16),
        ((16, rows, own_rows), bf16),
        ((length, cols // 3), bf16),
        ((own_rows, units), bf16),
        ((length, units), bf16),
        ((units, width), bf16),
        ((width, units), bf16),
        ((2, own_rows, width), bf16),
        ((own_rows, width), f32),
        ((own_rows, width), f32),
        ((length, cols // 3), bf16),
        token, token, token, token,
        ((SLOTS, 2, 2, ROWS_Z, rows, UNIT), bf16),
        ((wide_units, 2, ROWS_Z, rows, UNIT), bf16),
        ((pairs, 2, ROWS_Z, rows, pair_cols), bf16),
        ((wide_units, ROWS_Z, rows, UNIT), bf16),
        ((pairs, ROWS_Z, rows, pair_cols), bf16),
        ((wide_units, 3, rows, UNIT), bf16),
        ((pairs, 3, rows, pair_cols), bf16),
        ((own_rows, 512), bf16),
        ((PAIR, length), f32),
        ((length, PAIR), f32),
        ((length, PAIR), bf16),
        ((length, PAIR), bf16),
        ((length, PAIR), f32),
        ((length, PAIR), f32),
        ((1, units), f32),
        ((4, width), f32),
        ((2, width), f32),
        ((4, 4, width), f32),
        ((4, 2, width), f32),
        ((8, 4, width), f32),
        ((8, 2, width), f32),
        ((2, 6, width), f32),
    ]
    vmem = pl.BlockSpec(memory_space=pltpu.VMEM)
    anywhere = pl.BlockSpec(memory_space=pl.ANY)
    smem = pl.BlockSpec(memory_space=pltpu.SMEM)
    chunks = wide_units + pairs
    dma = lambda n: pltpu.SemaphoreType.DMA((n,))
    sems = [29] + [chunks] * 4 + [4 * chunks] * 2 + [chunks] * 2 + [6 + pairs] * 2 + [20, 20, chunks + 1]
    return pl.pallas_call(
        backward_kernel,
        out_shape=[jax.ShapeDtypeStruct(shape, kind) for shape, kind in outs],
        in_specs=[smem, vmem, vmem] + [anywhere] * (7 + len(kept)),
        out_specs=[anywhere] * len(outs),
        scratch_shapes=[pltpu.VMEM(shape, kind) for shape, kind in scratch] + [dma(n) for n in sems],
        compiler_params=pltpu.CompilerParams(
            collective_id=2, has_side_effects=True, vmem_limit_bytes=60 * 1024 * 1024
        ),
        name="backward",
    )(starts, gain1, gain2, hidden, cot, dy_other, q_all, o_all, u_all, d_all, *kept)


def finish_kernel(
    raw_output, raw_grad, units_lo, units_hi, pairs_in, small,
    output, grad_hidden, qkv, out, up, down, gain1, shift1, gain2, shift2, bias,
):
    f32 = jnp.float32
    step = pl.program_id(0)
    output[0] = raw_output[...]
    grad_hidden[0] = raw_grad[...]
    rows = out.shape[0]
    width = small.shape[2]
    units_in = (units_lo, units_hi)

    def mixed(first, second):
        each = first.shape[1] // 4
        blocks = []
        for j in range(4):
            at = slice(j * each, (j + 1) * each)
            blocks += [first[:, at].astype(f32), second[:, at].astype(f32)]
        return jnp.concatenate(blocks, axis=1)

    for now in range(2):

        @pl.when(step == now)
        def _():
            for i in range(4):
                h, column = divmod(i, 2)
                at = slice(column * UNIT, (column + 1) * UNIT)
                down[h * rows : (h + 1) * rows, at] = units_in[now][0, i].astype(f32)
            for i in range(2):
                chunk = 4 + 2 * now + i
                at = slice(i * 2 * UNIT, (i + 1) * 2 * UNIT)
                up[:, at] = mixed(units_lo[0, chunk], units_hi[0, chunk])
            out[...] = units_lo[0, 8 + now].astype(f32) + units_hi[0, 8 + now].astype(f32)
            pairs = pairs_in.shape[1]
            for block in range(3 * now, 3 * now + 3):
                part, piece = divmod(block, 2)
                for p in range(pairs):
                    at = (block - 3 * now) * pairs * PAIR + p * PAIR
                    chunk = pairs_in[piece, p, :, part * PAIR : (part + 1) * PAIR]
                    qkv[:, at : at + PAIR] = chunk.astype(f32)

    @pl.when(step == 0)
    def _():
        for i, ref in enumerate((gain1, shift1, gain2, shift2)):
            ref[...] = (small[0, i : i + 1, :] + small[1, i : i + 1, :]).reshape(width)
        for g in range(2):
            for j in range(2):
                at = slice(j * UNIT, (j + 1) * UNIT)
                lo, hi = small[0, 4 + g : 5 + g, at], small[1, 4 + g : 5 + g, at]
                begin = (2 * g + j) * 2 * UNIT
                bias[begin : begin + 2 * UNIT] = mixed(lo, hi).reshape(2 * UNIT)


def finish(raw_output, raw_grad, units_in, pairs_in, small):
    f32 = jnp.float32
    own_rows, width = raw_output.shape
    rows = units_in.shape[2]
    shapes = [
        (1, own_rows, width), (1, own_rows, width), (rows, 3 * width), (rows, width), (rows, 8 * UNIT),
        (4 * rows, width), (width,), (width,), (width,), (width,), (8 * UNIT,),
    ]
    token = pl.BlockSpec((own_rows // 2, width), lambda s: (s, 0))
    token_out = pl.BlockSpec((1, own_rows // 2, width), lambda s: (0, s, 0))
    columns = lambda n: pl.BlockSpec((rows, n // 2), lambda s: (0, s))
    fixed = lambda shape: pl.BlockSpec(shape, lambda s: (0,) * len(shape))
    half = lambda i: pl.BlockSpec((1,) + units_in.shape[1:], lambda s: (i, 0, 0, 0))
    return pl.pallas_call(
        finish_kernel,
        grid=(2,),
        out_shape=[jax.ShapeDtypeStruct(shape, f32) for shape in shapes],
        in_specs=[token, token, half(0), half(1), fixed(pairs_in.shape), fixed(small.shape)],
        out_specs=[
            token_out, token_out, columns(3 * width), columns(width), columns(8 * UNIT),
            pl.BlockSpec((2 * rows, width), lambda s: (s, 0)),
        ] + [fixed(shape) for shape in shapes[6:]],
        compiler_params=pltpu.CompilerParams(vmem_limit_bytes=60 * 1024 * 1024),
        name="finish",
    )(raw_output, raw_grad, units_in, units_in, pairs_in, small)


def split_layer(
    hidden, starts, first_gain, first_shift, qkv_weight, out_weight, second_gain, second_shift,
    up_weight, hidden_bias, down_weight, cotangent,
):
    shards = lax.axis_size("rows")
    (
        qkv_all, out_all, up_all, down_all, dy_other, down_sums, normed_t, packed, lse, att, att_t, residual, second_t,
        activated, slope,
    ) = forward(
        hidden[0], cotangent[0], starts, first_gain, first_shift, second_gain, second_shift, hidden_bias,
        qkv_weight, out_weight, up_weight, down_weight,
    )
    whole = lambda w: w.reshape(-1, w.shape[-1])
    blocks = lambda w: w.reshape(shards, -1, w.shape[-1])
    shares = backward(
        starts, first_gain, second_gain, hidden[0], cotangent[0], dy_other, whole(qkv_all), whole(out_all),
        whole(up_all), whole(down_all), down_sums, normed_t, packed, lse, att, blocks(att_t), residual,
        blocks(second_t), activated, slope,
    )
    return tuple(finish(*shares))


def splits_evenly(mesh):
    pieces = mesh.shape["blk"]
    return pieces == 2 and mesh.shape["rows"] == 2 * ROWS_Z * ROWS_Y and HEADS % (2 * pieces) == 0


def solution(mesh):
    in_specs = (
        P("rows", "blk", None),
        P("rows", None),
        P(),
        P(),
        P("rows", None),
        P("rows", None),
        P(),
        P(),
        P("rows", None),
        P(),
        P("rows", None),
        P("rows", "blk", None),
    )
    out_specs = (
        P("rows", "blk", None),
        P("rows", "blk", None),
        P("rows", None),
        P("rows", None),
        P("rows", None),
        P("rows", None),
        P(),
        P(),
        P(),
        P(),
        P(),
    )
    layer = split_layer if splits_evenly(mesh) else on_device
    return jax.shard_map(
        layer, mesh=mesh, in_specs=in_specs, out_specs=out_specs, check_vma=False
    )
```

```python
import functools
import math

import jax
import jax.numpy as jnp
from jax import lax
from jax.experimental import pallas as pl
from jax.experimental.pallas import tpu as pltpu
from jax.sharding import PartitionSpec as P

HEADS = 20
HEAD_DIM = 64


masked_score = -1e30
block_limit = 512


def layer_norm(values, gain, shift):
    mean_value = jnp.mean(values, axis=-1, keepdims=True)
    centred = values - mean_value
    variance = jnp.mean(centred * centred, axis=-1, keepdims=True)
    return centred * lax.rsqrt(variance + 1e-05) * gain + shift


def segment_of(starts_row, positions):
    reached = starts_row[None, :] <= positions[:, None]
    return jnp.sum(reached.astype(jnp.int32), axis=1) - 1


def scores_with_mask(queries, key_block, query_seg, key_seg):
    products = jnp.einsum("qhe,khe->hqk", queries, key_block, preferred_element_type=jnp.float32)
    products = products * queries.shape[2] ** (-0.5)
    allowed = (query_seg[:, None] == key_seg[None, :])[None, :, :]
    return (jnp.where(allowed, products, masked_score), allowed)


def attend_rows(running, key_rows, value_rows, queries, query_seg, starts_row):
    piece_rows = key_rows.shape[0]
    step_rows = math.gcd(piece_rows, block_limit)
    head_count = queries.shape[1]
    head_width = queries.shape[2]

    def one_block(block_index, state):
        row_top, denominator, weighted = state
        block_start = block_index * step_rows
        key_block = lax.dynamic_slice_in_dim(key_rows, block_start, step_rows, 0).reshape(
            step_rows, head_count, head_width
        )
        value_block = lax.dynamic_slice_in_dim(value_rows, block_start, step_rows, 0).reshape(
            step_rows, head_count, head_width
        )
        key_seg = segment_of(starts_row, block_start + jnp.arange(step_rows, dtype=jnp.int32))
        scores, allowed = scores_with_mask(queries, key_block, query_seg, key_seg)
        new_top = jnp.maximum(row_top, jnp.max(scores, axis=-1))
        factor = jnp.exp(row_top - new_top)
        weights = jnp.where(allowed, jnp.exp(scores - new_top[:, :, None]), 0.0)
        denominator = denominator * factor + jnp.sum(weights, axis=-1)
        weighted = weighted * factor[:, :, None] + jnp.einsum(
            "hqk,khe->hqe",
            weights.astype(jnp.bfloat16),
            value_block,
            preferred_element_type=jnp.float32,
        )
        return (new_top, denominator, weighted)

    return lax.fori_loop(0, piece_rows // step_rows, one_block, running)


def on_device(
    hidden,
    starts,
    first_gain,
    first_shift,
    qkv_weight,
    out_weight,
    second_gain,
    second_shift,
    up_weight,
    hidden_bias,
    down_weight,
    cotangent,
):
    rows_here = hidden.shape[1]
    model_width = hidden.shape[2]
    head_count = HEADS
    head_width = HEAD_DIM
    score_scale = head_width ** (-0.5)
    inputs = hidden[0].astype(jnp.float32)
    starts_row = starts[0]
    offset = lax.axis_index("blk") * rows_here
    query_seg = segment_of(starts_row, offset + jnp.arange(rows_here, dtype=jnp.int32))
    qkv_full, out_full, up_full, down_full = (
        lax.all_gather(qkv_weight, "rows", axis=0, tiled=True),
        lax.all_gather(out_weight, "rows", axis=0, tiled=True),
        lax.all_gather(up_weight, "rows", axis=0, tiled=True),
        lax.all_gather(down_weight, "rows", axis=0, tiled=True),
    )
    normed_low = layer_norm(inputs, first_gain, first_shift).astype(jnp.bfloat16)
    packed = jnp.dot(normed_low, qkv_full, preferred_element_type=jnp.float32).astype(jnp.bfloat16)
    queries = packed[:, :model_width].reshape(rows_here, head_count, head_width)
    key_rows = packed[:, model_width : 2 * model_width]
    value_rows = packed[:, 2 * model_width :]
    initial = (
        jnp.full((head_count, rows_here), masked_score, jnp.float32),
        jnp.zeros((head_count, rows_here), jnp.float32),
        jnp.zeros((head_count, rows_here, head_width), jnp.float32),
    )
    row_top, denominator, weighted = attend_rows(
        initial,
        lax.all_gather(key_rows, "blk", axis=0, tiled=True),
        lax.all_gather(value_rows, "blk", axis=0, tiled=True),
        queries,
        query_seg,
        starts_row,
    )
    log_total = row_top + jnp.log(denominator)
    attended = jnp.transpose(weighted / denominator[:, :, None], (1, 0, 2))
    attended_low = attended.reshape(rows_here, model_width).astype(jnp.bfloat16)
    residual = inputs + jnp.dot(attended_low, out_full, preferred_element_type=jnp.float32)
    second_low = layer_norm(residual, second_gain, second_shift).astype(jnp.bfloat16)
    up_values = jnp.dot(second_low, up_full, preferred_element_type=jnp.float32) + hidden_bias
    activated_low = jax.nn.gelu(up_values, approximate=False).astype(jnp.bfloat16)
    output = residual + jnp.dot(activated_low, down_full, preferred_element_type=jnp.float32)
    cot_low = cotangent[0]
    d_activated = jnp.einsum("tc,fc->tf", cot_low, down_full, preferred_element_type=jnp.float32)
    unused_gelu, gelu_pull = jax.vjp(
        lambda values: jax.nn.gelu(values, approximate=False), up_values
    )
    d_up_low = gelu_pull(d_activated)[0].astype(jnp.bfloat16)
    d_second = jnp.einsum("tf,cf->tc", d_up_low, up_full, preferred_element_type=jnp.float32)
    unused_second, second_pull = jax.vjp(layer_norm, residual, second_gain, second_shift)
    d_norm_two, d_second_gain, d_second_shift = second_pull(d_second)
    d_residual = cot_low.astype(jnp.float32) + d_norm_two
    d_branch_low = d_residual.astype(jnp.bfloat16)
    d_attended_low = jnp.einsum(
        "tc,kc->tk", d_branch_low, out_full, preferred_element_type=jnp.float32
    ).astype(jnp.bfloat16)
    d_attended3 = d_attended_low.reshape(rows_here, head_count, head_width)
    row_dots = jnp.einsum("qhe,qhe->hq", d_attended3.astype(jnp.float32), attended)
    keys_all, values_all = (
        lax.all_gather(key_rows, "blk", axis=0, tiled=True),
        lax.all_gather(value_rows, "blk", axis=0, tiled=True),
    )
    length = keys_all.shape[0]
    step_rows = math.gcd(length, block_limit)

    def block_terms(block_index):
        block_start = block_index * step_rows
        key_block = lax.dynamic_slice_in_dim(keys_all, block_start, step_rows, 0).reshape(
            step_rows, head_count, head_width
        )
        value_block = lax.dynamic_slice_in_dim(values_all, block_start, step_rows, 0).reshape(
            step_rows, head_count, head_width
        )
        key_seg = segment_of(starts_row, block_start + jnp.arange(step_rows, dtype=jnp.int32))
        scores, allowed = scores_with_mask(queries, key_block, query_seg, key_seg)
        probability = jnp.where(allowed, jnp.exp(scores - log_total[:, :, None]), 0.0)
        d_probs = jnp.einsum(
            "qhe,khe->hqk", d_attended3, value_block, preferred_element_type=jnp.float32
        )
        d_scores = (probability * (d_probs - row_dots[:, :, None])).astype(jnp.bfloat16)
        return (key_block, probability, d_scores)

    dq_start = jnp.zeros((rows_here, head_count, head_width), jnp.float32)

    def back_block(dq_sum, block_index):
        key_block, probability, d_scores = block_terms(block_index)
        dq_sum = dq_sum + jnp.einsum(
            "hqk,khe->qhe", d_scores, key_block, preferred_element_type=jnp.float32
        )
        dk_block = (
            jnp.einsum("hqk,qhe->khe", d_scores, queries, preferred_element_type=jnp.float32)
            * score_scale
        )
        dv_block = jnp.einsum(
            "hqk,qhe->khe",
            probability.astype(jnp.bfloat16),
            d_attended3,
            preferred_element_type=jnp.float32,
        )
        return (
            dq_sum,
            (dk_block.reshape(step_rows, model_width), dv_block.reshape(step_rows, model_width)),
        )

    dq_sum, (dk_terms, dv_terms) = lax.scan(back_block, dq_start, jnp.arange(length // step_rows))
    dk_rows, dv_rows = (
        lax.psum_scatter(
            dk_terms.reshape(length, model_width).astype(jnp.bfloat16),
            "blk",
            scatter_dimension=0,
            tiled=True,
        ).astype(jnp.float32),
        lax.psum_scatter(
            dv_terms.reshape(length, model_width).astype(jnp.bfloat16),
            "blk",
            scatter_dimension=0,
            tiled=True,
        ).astype(jnp.float32),
    )
    d_packed = jnp.concatenate(
        [(dq_sum * score_scale).reshape(rows_here, model_width), dk_rows, dv_rows], axis=1
    ).astype(jnp.bfloat16)
    d_normed = jnp.einsum("tn,cn->tc", d_packed, qkv_full, preferred_element_type=jnp.float32)
    unused_first, first_pull = jax.vjp(layer_norm, inputs, first_gain, first_shift)
    d_norm_one, d_first_gain, d_first_shift = first_pull(d_normed)
    grad_hidden = d_residual + d_norm_one
    d_bias = jnp.sum(d_up_low, axis=0, dtype=jnp.float32)
    wide_share = lax.psum_scatter(
        jnp.concatenate(
            [
                jnp.einsum("tc,tn->cn", normed_low, d_packed, preferred_element_type=jnp.float32),
                jnp.einsum(
                    "tc,tn->cn", attended_low, d_branch_low, preferred_element_type=jnp.float32
                ),
                jnp.einsum("tc,tn->cn", second_low, d_up_low, preferred_element_type=jnp.float32),
            ],
            axis=1,
        ).astype(jnp.bfloat16),
        "rows",
        scatter_dimension=0,
        tiled=True,
    )
    down_share = lax.psum_scatter(
        jnp.einsum("tf,tn->fn", activated_low, cot_low, preferred_element_type=jnp.float32).astype(
            jnp.bfloat16
        ),
        "rows",
        scatter_dimension=0,
        tiled=True,
    )
    wide_grads, down_grads = (
        lax.psum(wide_share, "blk").astype(jnp.float32),
        lax.psum(down_share, "blk").astype(jnp.float32),
    )
    grad_qkv = wide_grads[:, : 3 * model_width]
    grad_out = wide_grads[:, 3 * model_width : 4 * model_width]
    grad_up = wide_grads[:, 4 * model_width :]
    small_grads = lax.psum(
        (d_first_gain, d_first_shift, d_second_gain, d_second_shift, d_bias), ("rows", "blk")
    )
    return (
        output[None],
        grad_hidden[None],
        grad_qkv,
        grad_out,
        grad_up,
        down_grads,
        small_grads[0],
        small_grads[1],
        small_grads[2],
        small_grads[3],
        small_grads[4],
    )


MESH = pl.DeviceIdType.MESH
FORWARD_MOVES = (
    ((0, 0), (1, 0), (2, 0), (0, 1), (1, 1), (2, 1),),
    (),
    (),
    (),
    (),
    (),
    ((2, 3),),
    (),
    (),
    (),
    ((3, 0, 1, 0), (4, 0, 0), (4, 1, 0), (3, 0, 0, 0), (3, 1, 1, 0), (4, 0, 2), (3, 1, 0, 0), (0, 2), (2, 2), (4, 0, 1), (3, 0, 2, 0), (4, 1, 2), (3, 1, 2, 0), (1, 2), (4, 1, 1), (2, 5),),
    (),
    (),
    ((4, 0, 3), (3, 2, 1, 0), (2, 4), (4, 1, 3), (3, 2, 0, 0),),
    (),
    (),
    ((4, 2, 0), (0, 3),),
    ((3, 2, 2, 0), (4, 2, 2), (1, 3),),
    (),
    (),
    (),
    (),
    (),
    (),
    ((4, 2, 1),),
    (),
    (),
    (),
    (),
    (),
    ((3, 3, 1, 0), (4, 2, 3),),
    (),
    (),
    ((3, 3, 0, 0), (4, 3, 0),),
    (),
    (),
    (),
    (),
    (),
    (),
    ((4, 3, 2), (3, 3, 2, 0), (0, 4), (1, 5), (3, 4, 1, 0), (4, 3, 1), (1, 4), (3, 4, 0, 0), (4, 3, 3), (0, 5), (3, 4, 2, 0),),
    (),
    (),
    ((4, 5, 0),),
    ((3, 5, 1, 0),),
    (),
    (),
    ((4, 4, 2),),
    (),
    (),
    ((3, 5, 0, 0),),
    (),
    ((4, 4, 0),),
    (),
    ((3, 5, 1, 1),),
    (),
    ((4, 4, 1),),
    (),
    ((3, 5, 0, 1),),
    ((4, 4, 3),),
    (),
    (),
    ((3, 5, 2, 0),),
    (),
    (),
    (),
    (),
    ((3, 5, 2, 1),),
    (),
    (),
    (),
    (),
    (),
)
ROWS_Z, ROWS_Y = 4, 2
PAIR = 128
UNIT = 640
SLOTS = 2
SPARE = 3


def place_of():
    index = lax.axis_index("rows")
    return index // 4, lax.rem(index // 2, 2), lax.rem(index, 2)


def row_of(z, y, core):
    return (lax.rem(z + ROWS_Z, ROWS_Z) * ROWS_Y + y) * 2 + core


def aligned(index, step):
    return pl.ds(pl.multiple_of(index * step, step), step)


def dot_nt(left, right):
    return lax.dot_general(left, right, (((1,), (1,)), ((), ())), preferred_element_type=jnp.float32)


def dot_nn(left, right):
    return jnp.dot(left, right, preferred_element_type=jnp.float32)


def head_lanes(width):
    lane = lax.broadcasted_iota(jnp.int32, (1, width), 1)
    return (lane < HEAD_DIM, lane >= HEAD_DIM)


def greet(peers):
    barrier = pltpu.get_barrier_semaphore()
    for peer in peers:
        pl.semaphore_signal(barrier, inc=1, device_id=peer, device_id_type=MESH)
    pl.semaphore_wait(barrier, len(peers))


def neighbours():
    z, y, core = place_of()
    return [
        {"rows": row_of(z + 1, y, core)},
        {"rows": row_of(z + 2, y, core)},
        {"rows": row_of(z + 3, y, core)},
        {"rows": row_of(z, 1 - y, core)},
        {"rows": row_of(z, y, 1 - core)},
        {"blk": 1 - lax.axis_index("blk")},
    ]


def write_marks(starts_ref, key_marks, query_marks):
    shape = key_marks.shape
    at = lax.broadcasted_iota(jnp.int32, shape, 0)
    lane = lax.broadcasted_iota(jnp.int32, shape, 1)
    lane = jnp.where(lane < HEAD_DIM, lane, lane - HEAD_DIM) - SPARE
    cell = jnp.zeros(shape, jnp.int32) - 1
    for i in range(starts_ref.shape[1]):
        cell += (at >= starts_ref[0, i]).astype(jnp.int32)
    key_marks[...] = jnp.where((lane == cell) | (lane < 0), 1.0, 0.0).astype(key_marks.dtype)
    blocked = (lane != cell) & (lane >= 0) & (lane < starts_ref.shape[1])
    query_marks[...] = jnp.where(blocked, masked_score, 0.0).astype(query_marks.dtype)


def z_place(z):
    return 2 * lax.rem(z, 2) + z // 2


def grad_chunk(target, left, right):
    def half(j, carry):
        value = dot_nn(left(j), right()).astype(jnp.bfloat16)
        n = value.shape[1]
        rows = value.shape[0] // 8
        for block in range(8):
            to_z, to_y, to_core = block // 4, block // 2 % 2, block % 2
            target[to_core, to_y, 2 * to_z + j, :, :n] = value[block * rows : (block + 1) * rows]
        return carry

    lax.fori_loop(0, 2, half, 0)


def forward_kernel(
    hidden, cot, starts, gain1, shift1, gain2, shift2, bias_in, q_in, o_in, u_in, d_in,
    q_all, o_all, u_all, d_all, dy_all, down_sums, normed_t_out, packed_out, lse_out, att_out, att_t_out, resid_out,
    second_t_out, act_out, slope_out,
    hid_other, normed, wq, wo, wu, packed, key_marks, query_marks, att_part, att_own, resid, second,
    act, act_t, slope, normed_t, att_t, second_t, lse, u_wide, q_own, o_own, u_own, d_own, dy, bias, parts, core_in,
    local_sem, send_sem, recv_sem, x_send, x_recv,
):
    bf16 = jnp.bfloat16
    z, y, core = place_of()
    me = row_of(z, y, core)
    piece = lax.axis_index("blk")
    other = 1 - piece
    own_rows, width = hidden.shape
    length = packed.shape[0]
    rows = o_own.shape[0]
    early = rows * 3 // 5
    d_half = lambda half: pl.ds(half * rows, rows)
    own = (
        q_own.at[pl.ds(0, early)], q_own.at[pl.ds(early, rows - early)], o_own, u_own,
        d_own.at[d_half(0)], d_own.at[d_half(1)],
    )
    last = len(own) - 1

    def slot_of(w, at_z, at_y, at_core):
        slot = row_of(at_z, at_y, at_core)
        if w < 2:
            return q_all.at[slot, pl.ds(w * early, own[w].shape[0])]
        if w < 4:
            return (o_all, u_all)[w - 2].at[slot]
        return d_all.at[slot, d_half(w - 4)]

    x_peer = {"blk": other}
    peers = neighbours()
    pairs = packed.shape[1] // (3 * PAIR)
    first_gain, first_shift, second_gain, second_shift = (
        ref[...].reshape(1, width) for ref in (gain1, shift1, gain2, shift2)
    )

    def local(src, dst, index):
        return pltpu.make_async_copy(src, dst, local_sem.at[index])

    near = z + 1 - 2 * lax.rem(z, 2)
    far = lax.rem(z + 2, ROWS_Z)
    spread = (z, far, near, ROWS_Z - 1 - z)

    def send(w, at_z, v, place, peer, first=False):
        block = slot_of(w, at_z, y if v == 0 else 1 - y, core)
        index = w * 18 + place
        return pltpu.make_async_remote_copy(
            src_ref=own[w] if first else block, dst_ref=block, send_sem=send_sem.at[index],
            recv_sem=recv_sem.at[index], device_id=peer, device_id_type=MESH,
        )

    def along(w, k, v):
        peer = {"rows": row_of(far if k == 0 else near, y, core)}
        return send(w, far if k == 2 else z, v, 2 * k + v, peer, k < 2 and v == 0)

    def to_y(w, at_z, first=False):
        return send(w, at_z, 0, 6 + at_z, peers[3], first)

    def to_core(w, at_z, v, first=False):
        return send(w, at_z, v, 10 + 2 * at_z + v, peers[4], first)

    def pass_on(w, v):
        inner = (z == 1) | (z == 2)

        @pl.when(inner)
        def _():
            along(w, 0, v).start()

        along(w, 1, v).start()

        @pl.when(jnp.logical_not(inner))
        def _():
            along(w, 0, v).start()

    def relay_z(w, k, v):
        along(w, k, v).wait_recv()
        if k == 0:
            along(w, 2, v).start()
        at_z = spread[k + 1]
        if w < last:
            to_y(w, at_z).start()
        to_core(w, at_z, v).start()

    def relay_y(w, k):
        to_y(w, spread[k]).wait_recv()
        to_core(w, spread[k], 1).start()
        if w == last:
            pass_on(w, 1)

    def all_here(ws):
        for w in ws:
            for at_z in range(ROWS_Z):
                for v in range(2):
                    to_core(w, at_z, v).wait_recv()

    def all_here_load(ws, source, target, first):
        for i, at_z in enumerate(spread):
            for v in range(2):
                for w in ws:
                    to_core(w, at_z, v).wait_recv()
                chip = pl.ds(row_of(at_z, y if v == 0 else 1 - y, 0), 2)
                local(source.at[chip], target.at[chip], first + 2 * i + v).start()

    def loaded(source, target, first):
        for i in range(2 * ROWS_Z):
            chip = pl.ds(0, 2)
            local(source.at[chip], target.at[chip], first + i).wait()

    def all_gone(w):
        for v in range(1 if w < last else 2):
            for k in range(3):
                along(w, k, v).wait_send()
        for at_z in range(ROWS_Z) if w < last else (z,):
            to_y(w, at_z).wait_send()
        for at_z in range(ROWS_Z):
            for v in range(2):
                to_core(w, at_z, v).wait_send()

    def to_x(src, dst, index):
        return pltpu.make_async_remote_copy(
            src_ref=src, dst_ref=dst, send_sem=x_send.at[index], recv_sem=x_recv.at[index],
            device_id=x_peer, device_id_type=MESH,
        )

    third = q_in.shape[1] // 3
    share = third // 2
    q_picks = []
    for part in range(3):
        picked = q_in.at[:, pl.ds(pl.multiple_of(part * third + piece * share, 128), share)]
        q_picks.append(local(picked, q_own.at[:, pl.ds(part * share, share)], 17 + part))
        q_picks[-1].start()
    d_mine = d_in.at[pl.ds(piece * 2 * rows, 2 * rows)]
    local(o_in, o_own, 1).start()
    local(u_in, u_wide, 2).start()
    local(d_mine, d_own, 3).start()
    local(cot, dy.at[piece], 4).start()
    greet(peers)
    for copy in q_picks:
        copy.wait()
    hidden_x = to_x(hidden, hid_other, 0)
    cot_x = to_x(cot, dy.at[piece], 1)
    half_rows = lambda half: pl.ds(pl.multiple_of(half * own_rows, 128), own_rows)

    def first_copies():
        local(o_in, o_own, 1).wait()
        local(d_mine, d_own, 3).wait()
        local(u_in, u_wide, 2).wait()
        local(q_own, q_all.at[me], 0).start()
        local(o_own, o_all.at[me], 1).start()
        local(d_own, d_all.at[me], 3).start()
        local(cot, dy.at[piece], 4).wait()

    units_each = 2 * rows
    group = 8 * units_each

    def mine(block):
        wide = block.astype(jnp.float32)
        halves = []
        for half in range(2):
            at = [slice((2 * j + half) * units_each, (2 * j + half + 1) * units_each) for j in range(4)]
            halves.append(jnp.concatenate([wide[:, cols] for cols in at], axis=1))
        return jnp.where(piece == 0, halves[0], halves[1])

    def pick_units(g):
        cols = slice(g * group // 2, (g + 1) * group // 2)
        u_own[:, cols] = mine(u_wide[:, g * group : (g + 1) * group]).astype(bf16)
        bias[:, cols] = mine(bias_in[g * group : (g + 1) * group].reshape(1, group))
        if g == u_own.shape[1] * 2 // group - 1:
            local(u_own, u_all.at[me], 2).start()

    def norm_rows(source, half, part):
        step = 64
        steps = own_rows // step

        def body(i, carry):
            value = source[aligned(i, step), :].astype(jnp.float32)
            low = layer_norm(value, first_gain, first_shift).astype(bf16)
            normed[pl.ds(pl.multiple_of(half * own_rows + i * step, step), step), :] = low
            return carry

        lax.fori_loop(steps * part // 2, steps * (part + 1) // 2, body, 0)

    def q_here():
        local(q_own, q_all.at[me], 0).wait()
        all_here_load((0, 1), q_all, wq, 20)

    def project(begin, end):
        def body(part, carry):
            cols = aligned(part, share)
            value = dot_nn(normed[...], wq[:, :, cols].reshape(width, share)).astype(bf16)
            packed[:, cols] = value * jnp.where(part == 0, HEAD_DIM ** (-0.5), 1.0).astype(bf16)
            return carry

        lax.fori_loop(begin, end, body, 0)
        if end == 3:
            local(packed, packed_out, 9).start()

    first_lanes = head_lanes(PAIR)

    def att_cols(half, p):
        return pl.ds(pl.multiple_of(half * pairs * PAIR + p * PAIR, PAIR), PAIR)

    def attend(p, half):
        at_q, at_k, at_v = (slice(t * share + PAIR * p, t * share + PAIR * (p + 1)) for t in range(3))
        value_t = packed[:, at_v].T
        at = half_rows(half)
        queries = packed[at, at_q]
        keys = packed[:, at_k]
        halves = []
        for h in range(2):
            one = jnp.where(first_lanes[h], queries, query_marks[at, :])
            scores = dot_nt(jnp.where(first_lanes[h], keys, key_marks[...]), one)
            top = jnp.max(scores, axis=0, keepdims=True)
            weights = jnp.exp(scores - top)
            total = jnp.sum(weights, axis=0, keepdims=True)
            lse[2 * p + h : 2 * p + h + 1, at] = top + jnp.log(total)
            summed = dot_nn(value_t[h * HEAD_DIM : (h + 1) * HEAD_DIM], weights.astype(bf16))
            halves.append(summed / total)
        return jnp.concatenate(halves, axis=0).T.astype(bf16)

    def attend_other(p):
        att_part[:, p * PAIR : (p + 1) * PAIR] = attend(p, other)

    def attend_own(p):
        att_own[:, att_cols(piece, p)] = attend(p, piece)
        if p == pairs - 1:
            for copy in att_outs:
                copy.start()

    att_x = [
        to_x(att_part.at[:, pl.ds(p * PAIR, PAIR)], att_own.at[:, att_cols(piece, p)], 2 + p) for p in range(pairs)
    ]

    att_outs = (
        local(att_part, att_out.at[half_rows(other)], 45),
        local(att_own.at[:, pl.ds(pl.multiple_of(piece * share, 128), share)], att_out.at[half_rows(piece)], 46),
    )

    def o_here():
        local(o_own, o_all.at[me], 1).wait()
        all_here_load((2,), o_all, wo, 28)

    def att_here():
        for copy in att_x:
            copy.wait_recv()
        loaded(o_all, wo, 28)

    part_rows = own_rows // 2
    second_x = [
        to_x(second.at[piece, pl.ds(i * part_rows, part_rows)], second.at[piece, pl.ds(i * part_rows, part_rows)], 2 + pairs + i)
        for i in range(2)
    ]

    def merge(part):
        for cols in (slice(0, 512), slice(512, width)) if part == 0 else ():
            weight = wo[:, :, cols].reshape(width, cols.stop - cols.start)
            resid[:, cols] = hidden[:, cols].astype(jnp.float32) + dot_nn(att_own[...], weight)

        def second_rows(i, carry):
            rows = aligned(i, 64)
            second[piece, rows, :] = layer_norm(resid[rows, :], second_gain, second_shift).astype(bf16)
            return carry

        lax.fori_loop(part * part_rows // 64, (part + 1) * part_rows // 64, second_rows, 0)
        if part == 1:
            local(resid, resid_out, 12).start()

    def flip_normed():
        def body(i, carry):
            normed_t[aligned(i, 128), :] = normed[:, aligned(i, 128)].T
            return carry

        lax.fori_loop(0, width // 128, body, 0)
        local(normed_t, normed_t_out, 8).start()
        local(lse, lse_out, 10).start()

    def flip_second(half):
        def body(i, carry):
            second_t[aligned(i, 128), half_rows(half)] = second[half, :, aligned(i, 128)].T
            return carry

        lax.fori_loop(0, width // 128, body, 0)

    def flip_att():
        def body(i, carry):
            att_t[aligned(i, 128), :] = att_own[:, aligned(i, 128)].T
            return carry

        lax.fori_loop(0, width // 128, body, 0)
        local(att_t, att_t_out, 11).start()
        flip_second(piece)

    def u_here():
        local(u_own, u_all.at[me], 2).wait()
        all_here_load((3,), u_all, wu, 36)

    unit = 512
    fifth = act.shape[1] // unit // 5

    def expand(half, begin):
        at = half_rows(half)

        def body(i, carry):
            cols = aligned(i, unit)
            weight = wu[:, :, cols].reshape(width, unit)
            up = dot_nn(second[half], weight) + bias[:, cols]
            cdf = 0.5 * (1.0 + lax.erf(up * (0.5 ** 0.5)))
            pdf = jnp.exp(up * up * -0.5) * ((2.0 * math.pi) ** -0.5)
            value = (up * cdf).astype(bf16)
            act[at, cols] = value
            act_t[cols, at] = value.T
            slope[at, cols] = (cdf + up * pdf).astype(bf16)
            return carry

        lax.fori_loop(begin * fifth, (begin + 1) * fifth, body, 0)
        if begin == 4:
            for copy in halves_out(half):
                copy.start()

    def halves_out(half):
        base = 54 if half is piece else 56
        at = half_rows(half)
        return (
            local(act.at[at], act_out.at[at], base),
            local(slope.at[at], slope_out.at[at], base + 1),
        )

    def second_here():
        for copy in second_x:
            copy.wait_recv()

    def flip_last():
        flip_second(other)
        local(second_t, second_t_out, 13).start()

    def dy_here():
        cot_x.wait_recv()
        local(dy.at[other], dy_all, 4).start()

    def grad_down(i):
        h, at = i // 2, slice(i % 2 * UNIT, (i % 2 + 1) * UNIT)

        def left(j):
            begin = lambda block: pl.multiple_of((8 * j + block) * 2 * rows + h * rows, 16)
            return jnp.concatenate([act_t[pl.ds(begin(block), rows), :] for block in range(8)], axis=0)

        grad_chunk(parts.at[i % SLOTS], left, lambda: dy[:, :, at].reshape(length, UNIT))

    sums_x = [
        pltpu.make_async_remote_copy(
            src_ref=parts.at[i % SLOTS, 1 - core], dst_ref=core_in.at[i], send_sem=x_send.at[4 + pairs + i],
            recv_sem=x_recv.at[4 + pairs + i], device_id=peers[4], device_id_type=MESH,
        )
        for i in range(4)
    ]

    def sum_down(i):
        core_in[i] += parts[i % SLOTS, core]
        sums_x[i].wait_send()
        local(core_in.at[i], down_sums.at[i], 50 + i).start()

    def outputs():
        for i in range(4):
            local(core_in.at[i], down_sums.at[i], 50 + i).wait()
        local(dy.at[other], dy_all, 4).wait()
        local(d_own, d_all.at[me], 3).wait()
        local(normed_t, normed_t_out, 8).wait()
        local(packed, packed_out, 9).wait()
        local(lse, lse_out, 10).wait()
        for copy in att_outs:
            copy.wait()
        local(att_t, att_t_out, 11).wait()
        local(resid, resid_out, 12).wait()
        local(second_t, second_t_out, 13).wait()
        for half in (piece, other):
            for copy in halves_out(half):
                copy.wait()

    act_now = functools.partial
    steps = [hidden_x.start, cot_x.start]
    steps += [act_now(pick_units, g) for g in range(4)]
    steps += [act_now(norm_rows, hidden, piece, part) for part in range(2)]
    steps += [act_now(write_marks, starts, key_marks, query_marks), lambda: None]
    steps += [hidden_x.wait_recv]
    steps += [act_now(norm_rows, hid_other, other, part) for part in range(2)]
    steps += [q_here, act_now(loaded, q_all, wq, 20), act_now(project, 0, 1), act_now(project, 1, 3)]
    for p in range(pairs):
        steps += [act_now(attend_other, p), att_x[p].start]
    steps += [act_now(attend_own, p) for p in range(pairs - 1)]
    steps += [o_here, act_now(attend_own, pairs - 1), att_here]
    steps += [act_now(merge, 0), second_x[0].start, act_now(merge, 1), second_x[1].start]
    steps += [flip_normed, flip_att, u_here, act_now(loaded, u_all, wu, 36)]
    steps += [act_now(expand, piece, i) for i in range(5)]
    steps += [second_here, flip_last]
    steps += [act_now(expand, other, i) for i in range(5)]
    steps += [dy_here]
    for i in range(4):
        steps += [act_now(grad_down, i), sums_x[i].start]
        if i:
            steps += [sums_x[i - 1].wait_recv, act_now(sum_down, i - 1)]
    steps += [sums_x[3].wait_recv, act_now(sum_down, 3), outputs, act_now(all_here, (4, 5))]
    moves = (
        lambda w: pass_on(w, 0),
        lambda w: to_y(w, z, True).start(),
        lambda w: to_core(w, z, 0, True).start(),
        relay_z,
        relay_y,
    )
    for i, step in enumerate(steps):
        for kind, *where in FORWARD_MOVES[i]:
            moves[kind](*where)
        step()
        if i == 1:
            first_copies()
    for w in range(len(own)):
        all_gone(w)
    for copy in [hidden_x, cot_x] + second_x + att_x:
        copy.wait_send()


def forward(hidden, cot, starts, gain1, shift1, gain2, shift2, bias, qkv, out, up, down):
    own_rows, width = hidden.shape
    length = 2 * own_rows
    cols = qkv.shape[1] // 2
    units = up.shape[1] // 2
    rows = up.shape[0]
    bf16, f32 = jnp.bfloat16, jnp.float32
    shards = lax.axis_size("rows")
    head_rows = 16
    outs = [
        ((shards, rows, cols), bf16),
        ((shards, rows, width), bf16),
        ((shards, rows, units), bf16),
        ((shards, down.shape[0] // 2, width), bf16),
        ((own_rows, width), bf16),
        ((4, 2, ROWS_Z, rows, UNIT), bf16),
        ((width, length), bf16),
        ((length, cols), bf16),
        ((head_rows, length), f32),
        ((length, cols // 3), bf16),
        ((width, own_rows), bf16),
        ((own_rows, width), f32),
        ((width, length), bf16),
        ((length, units), bf16),
        ((length, units), bf16),
    ]
    scratch = [
        ((own_rows, width), bf16),
        ((length, width), bf16),
        ((shards, rows, cols), bf16),
        ((shards, rows, width), bf16),
        ((shards, rows, units), bf16),
        ((length, cols), bf16),
        ((length, PAIR), bf16),
        ((length, PAIR), bf16),
        ((own_rows, cols // 3), bf16),
        ((own_rows, width), bf16),
        ((own_rows, width), f32),
        ((2, own_rows, width), bf16),
        ((length, units), bf16),
        ((units, length), bf16),
        ((length, units), bf16),
        ((width, length), bf16),
        ((width, own_rows), bf16),
        ((width, length), bf16),
        ((head_rows, length), f32),
        ((rows, 2 * units), bf16),
        ((rows, cols), bf16),
        ((rows, width), bf16),
        ((rows, units), bf16),
        ((2 * rows, width), bf16),
        ((2, own_rows, width), bf16),
        ((1, units), f32),
        ((SLOTS, 2, 2, ROWS_Z, rows, UNIT), bf16),
        ((4, 2, ROWS_Z, rows, UNIT), bf16),
    ]
    vmem = pl.BlockSpec(memory_space=pltpu.VMEM)
    anywhere = pl.BlockSpec(memory_space=pl.ANY)
    smem = pl.BlockSpec(memory_space=pltpu.SMEM)
    dma = pltpu.SemaphoreType.DMA
    x_copies = 8 + cols // (3 * PAIR)
    return pl.pallas_call(
        forward_kernel,
        out_shape=[jax.ShapeDtypeStruct(shape, kind) for shape, kind in outs],
        in_specs=[vmem, anywhere, smem] + [vmem] * 5 + [anywhere] * 4,
        out_specs=[anywhere] * len(outs),
        scratch_shapes=[pltpu.VMEM(shape, kind) for shape, kind in scratch]
        + [dma((58,)), dma((108,)), dma((108,)), dma((x_copies,)), dma((x_copies,))],
        compiler_params=pltpu.CompilerParams(
            collective_id=1, has_side_effects=True, vmem_limit_bytes=60 * 1024 * 1024
        ),
        name="forward",
    )(hidden, cot, starts, gain1, shift1, gain2, shift2, bias, qkv, out, up, down)


BACKWARD_MOVES = (
    ((1, 0), (2, 0), (3, 0), (0, 0),),
    (),
    (),
    (),
    (),
    (),
    (),
    ((2, 1), (1, 1),),
    (),
    (),
    (),
    (),
    (),
    ((4, 0), (3, 1), (0, 1),),
    ((5, 0),),
    ((2, 2),),
    (),
    ((6, 0), (1, 2),),
    ((7, 0), (4, 1), (3, 2),),
    (),
    (),
    ((0, 2),),
    (),
    (),
    (),
    (),
    (),
    (),
    (),
    (),
    ((2, 3), (5, 1),),
    (),
    (),
    ((8, 0), (4, 2), (9, 0), (3, 3),),
    (),
    (),
    ((5, 2), (10, 0), (6, 1), (1, 3),),
    (),
    (),
    (),
    ((11, 0),),
    (),
    (),
    ((7, 1), (0, 3), (8, 1), (4, 3), (12, 0), (5, 3),),
    (),
    (),
    ((6, 2),),
    (),
    (),
    (),
    ((9, 1),),
    (),
    (),
    (),
    ((7, 2), (13, 0), (14, 0), (10, 1), (8, 2), (11, 1), (6, 3), (9, 2), (12, 1), (7, 3), (10, 2), (13, 1), (11, 2), (9, 3), (14, 1),),
    ((8, 3), (12, 2), (10, 3),),
    (),
    (),
    ((13, 2),),
    ((11, 3), (14, 2), (12, 3), (13, 3),),
    ((14, 3),),
)


def thirds(value):
    high = value.astype(jnp.bfloat16)
    rest = value - high.astype(jnp.float32)
    middle = rest.astype(jnp.bfloat16)
    return high, middle, (rest - middle.astype(jnp.float32)).astype(jnp.bfloat16)


def norm_back(values, gain, grad):
    centred = values - jnp.mean(values, axis=-1, keepdims=True)
    scale = lax.rsqrt(jnp.mean(centred * centred, axis=-1, keepdims=True) + 1e-05)
    unit = centred * scale
    scaled = grad * gain
    mean_one = jnp.mean(scaled, axis=-1, keepdims=True)
    mean_two = jnp.mean(scaled * unit, axis=-1, keepdims=True)
    d_values = scale * (scaled - mean_one - unit * mean_two)
    d_gain = jnp.sum(grad * unit, axis=0, keepdims=True)
    d_shift = jnp.sum(grad, axis=0, keepdims=True)
    return d_values, d_gain, d_shift


def backward_kernel(
    starts, gain1, gain2, hidden, cot, dy_other, q_all, o_all, u_all, d_all, down_sums, normed_t, packed, lse_in, att_in, att_t_in,
    resid, second_t, act, slope,
    output, grad_hidden, units_out, pairs_out, small_out,
    lhs, att_t, att_own, half_act, wide, wd, wu, dy, first, second, d_att, x_in0, x_in1, x_out0, down_own,
    parts, core_in, core_in_q, y_in, y_in_q, z_in, z_in_q, down_early, lse_rows, lse, key_marks, query_marks, acc_k, acc_v, bias_sum, early, late,
    early_near, late_near, early_all, late_all, small,
    local_sem, a_send, a_recv, b_send, b_recv, c_send, c_recv, g_send, g_recv, x_send, x_recv,
    s_send, s_recv, keep_sem,
):
    bf16, f32 = jnp.bfloat16, jnp.float32
    z, y, core = place_of()
    piece = lax.axis_index("blk")
    other = 1 - piece
    own_rows, width = first.shape
    length = 2 * own_rows
    branch = half_act.at[:, pl.ds(0, width)]
    units = wide.shape[1]
    d_width = d_att.shape[1]
    cols = 3 * d_width
    pairs = d_width // PAIR
    near = z + 1 - 2 * lax.rem(z, 2)
    far = lax.rem(z + 2, ROWS_Z)
    peer_core, peer_y = {"rows": row_of(z, y, 1 - core)}, {"rows": row_of(z, 1 - y, core)}
    peer_near, peer_far = {"rows": row_of(near, y, core)}, {"rows": row_of(far, y, core)}
    peer_x = {"blk": other}
    group = [peer_core, peer_y, {"rows": row_of(z, 1 - y, 1 - core)}]
    line = [
        {"rows": row_of(z + k, y, core), "blk": lax.rem(piece + n, 2)} for n in range(2) for k in range(ROWS_Z) if n or k
    ]
    wide_chunks = core_in.shape[0]
    chunks = wide_chunks + pairs
    first_gain, second_gain = gain1[...].reshape(1, width), gain2[...].reshape(1, width)
    half_rows = lambda half: pl.ds(pl.multiple_of(half * own_rows, 128), own_rows)
    part_rows = own_rows // 2

    def remote(src, dst, sends, recvs, index, peer):
        return pltpu.make_async_remote_copy(
            src_ref=src, dst_ref=dst, send_sem=sends.at[index], recv_sem=recvs.at[index],
            device_id=peer, device_id_type=MESH,
        )

    loads = {
        "sums": (down_sums, core_in.at[pl.ds(0, 4)], 0),
        "dy": (cot, dy.at[piece], 1),
        "dy_other": (dy_other, dy.at[other], 2),
        "up": (u_all, wu, 4),
        "act_other": (act.at[half_rows(other)], half_act, 5),
        "act_own": (act.at[half_rows(piece)], half_act, 6),
        "resid": (resid, second, 7),
        "lse": (lse_in, lse_rows.at[pl.ds(0, 16)], 8),
        "second_t": (second_t, lhs, 9),
        "att_t": (att_t_in, att_t, 10),
        "out": (o_all, wd.at[pl.ds(0, width)], 11),
        "normed_t": (normed_t, wd.at[pl.ds(width, width), pl.ds(0, length)], 12),
        "qkv": (q_all, wu.at[:, pl.ds(0, cols)], 13),
        "packed": (packed, wide.at[:, pl.ds(0, cols)], 14),
        "hidden": (hidden, branch, 15),
        "output": (second, output, 16),
        "grad_hidden": (first, grad_hidden, 17),
        "att": (att_in, att_own, 18),
    }

    def local(name):
        src, dst, index = loads[name]
        return pltpu.make_async_copy(src, dst, local_sem.at[index])

    z_first = (0, 1, 8)
    mine, theirs = pl.ds(2 * lax.rem(z, 2), 2), pl.ds(2 - 2 * lax.rem(z, 2), 2)
    place, far_place = z_place(z), z_place(far)
    order = tuple(range(chunks))

    def buffers(i):
        if i < wide_chunks:
            return core_in.at[i], y_in.at[i], z_in.at[i], units_out.at[:, i], UNIT
        i -= wide_chunks
        return core_in_q.at[i], y_in_q.at[i], z_in_q.at[i], pairs_out.at[:, i], 3 * PAIR

    def copy_a(i):
        into, _, _, _, n = buffers(i)
        return remote(parts.at[i % SLOTS, 1 - core, :, :, :, pl.ds(0, n)], into, a_send, a_recv, i, peer_core)

    def copy_b(i):
        sums, by_y, by_z, _, _ = buffers(i)
        if i < 4 and i not in z_first:
            sums = down_sums.at[i]
        if i in z_first:
            return remote(sums.at[1 - y, place], by_z.at[2], b_send, b_recv, i, peer_y)
        return remote(sums.at[1 - y], by_y, b_send, b_recv, i, peer_y)

    def copies_c(i, step):
        sums, by_y, by_z, _, _ = buffers(i)
        index = 4 * i + 2 * step
        if i not in z_first:
            if step == 0:
                return [remote(by_y.at[theirs], by_z.at[pl.ds(0, 2)], c_send, c_recv, index, peer_near)]
            return [remote(by_y.at[far_place], by_z.at[2], c_send, c_recv, index, peer_far)]
        if step == 0:
            sums = down_sums.at[i] if i < 4 else sums
            return [
                remote(sums.at[v, theirs], by_y.at[pl.ds(2 * v, 2)], c_send, c_recv, index + v, peer_near)
                for v in range(2)
            ]
        return [remote(sums.at[v, far_place], by_z.at[v], c_send, c_recv, index + v, peer_far) for v in range(2)]

    def copy_g(i):
        _, _, by_z, out, _ = buffers(i)
        return remote(by_z.at[0], out.at[piece], g_send, g_recv, i, peer_x)

    def keep_g(i):
        _, _, by_z, out, _ = buffers(i)
        return pltpu.make_async_copy(by_z.at[0], out.at[piece], keep_sem.at[i])

    unread = ["sums"]

    def move(i, stage):
        sums, by_y, by_z, _, n = buffers(i)
        if i < 4 and stage and unread:
            local(unread.pop()).wait()
        if stage == 0:
            slot = i % SLOTS
            if i >= 4:
                copy_a(i).wait_recv()
                sums[1 - y] += parts[slot, core, 1 - y, :, :, :n]
                if i in z_first:
                    sums[y] += parts[slot, core, y, :, :, :n]
            if i in z_first:
                for copy in copies_c(i, 0):
                    copy.start()
            else:
                copy_b(i).start()
            if i >= 4:
                if i not in z_first:
                    sums[y] += parts[slot, core, y, :, :, :n]
                copy_a(i).wait_send()
        elif i in z_first and stage < 3:
            for v, copy in enumerate(copies_c(i, stage - 1)):
                copy.wait_recv()
                if stage == 1:
                    sums[v, mine] += by_y[2 * v : 2 * v + 2]
                else:
                    sums[v, place] += by_z[v]
            for copy in copies_c(i, 1) if stage == 1 else [copy_b(i)]:
                copy.start()
        elif stage == 1:
            copy_b(i).wait_recv()
            by_y[...] += sums[y]
            copies_c(i, 0)[0].start()
        elif stage == 2:
            copies_c(i, 0)[0].wait_recv()
            by_y[mine] += by_z[0:2]
            copies_c(i, 1)[0].start()
        else:
            if i in z_first:
                copy_b(i).wait_recv()
                total = sums[y, place].astype(f32) + by_z[2].astype(f32)
            else:
                copies_c(i, 1)[0].wait_recv()
                total = by_y[place].astype(f32) + by_z[2].astype(f32)
            by_z[0] = total.astype(bf16)
            copy_g(i).start()
            keep_g(i).start()

    tile = 512

    def tile_loads(i):
        at = aligned(i, tile)
        return (
            pltpu.make_async_copy(d_all.at[at], wd.at[at], local_sem.at[19 + 2 * i]),
            pltpu.make_async_copy(slope.at[:, at], wide.at[:, at], local_sem.at[20 + 2 * i]),
        )

    local("act_other").start()
    for i in range(units // tile):
        tile_loads(i)[0].start()
    local("dy").start()
    local("dy_other").start()
    for i in range(units // tile):
        tile_loads(i)[1].start()
    greet(group + line)

    def ready_units():
        local("act_other").wait()
        for i in range(units // tile):
            tile_loads(i)[0].wait()
        for name in ("sums", "up", "second_t", "resid", "lse", "att_t"):
            local(name).start()

    halves = (slice(0, 512), slice(512, width))

    def d_units(begin, end):
        if begin == 0:
            local("dy").wait()
            local("dy_other").wait()

        def body(i, carry):
            tile_loads(i)[1].wait()
            at = aligned(i, tile)
            value = dot_nt(dy[...].reshape(length, width), wd[at, :]) * wide[:, at].astype(f32)
            low = value.astype(bf16)
            wide[:, at] = low
            bias_sum[:, at] = jnp.sum(low.astype(f32), axis=0, keepdims=True)
            return carry

        lax.fori_loop(begin, end, body, 0)

    def d_second(half, part, target):
        if part == 0 and target is x_out0:
            local("up").wait()
        at = halves[part]
        target[:, at] = dot_nt(wide[half_rows(half), :], wu[at, :]).astype(target.dtype)

    def exchange(part, index):
        at = pl.ds(halves[part].start, halves[part].stop - halves[part].start)
        return remote(x_out0.at[:, at], x_in0.at[:, at], x_send, x_recv, index, peer_x)

    second_x = [exchange(part, part) for part in range(2)]
    normed_x = [exchange(part, 2 + part) for part in range(2)]
    first_cols, rest_cols = (pl.ds(at.start, at.stop - at.start) for at in halves)
    down_x = [
        remote(down_early, x_in1.at[:, first_cols], x_send, x_recv, 4, peer_x),
        remote(dy.at[other, :, rest_cols], x_in1.at[:, rest_cols], x_send, x_recv, 5 + pairs, peer_x),
    ]
    att_x = [
        remote(
            x_out0.at[:, pl.ds(p * PAIR, PAIR)], d_att.at[half_rows(piece), pl.ds(p * PAIR, PAIR)],
            x_send, x_recv, 5 + p, peer_x,
        )
        for p in range(pairs)
    ]

    def d_second_own():
        for part in range(2):
            d_second(piece, part, first)
        local("qkv").start()

    def down_first():
        down_early[...] = dot_nn(half_act[...], wd[:, halves[0]]).astype(bf16)

    def down_other():
        dy[other, :, halves[1]] = dot_nn(half_act[...], wd[:, halves[1]]).astype(bf16)
        local("act_own").start()

    def down_mine():
        local("act_own").wait()
        for at in halves:
            down_own[:, at] = dot_nn(half_act[...], wd[:, at]).astype(bf16)
        local("out").start()
        local("normed_t").start()

    def chunk(i, left, right):
        grad_chunk(parts.at[i % SLOTS], left, right)
        copy_a(i).start()

    def grad_up(i):
        if i == 0:
            local("second_t").wait()
        left = lambda j: lhs[pl.ds(8 * j, 8)].reshape(8 * lhs.shape[1], length)
        chunk(4 + i, left, lambda: wide[:, i * UNIT : (i + 1) * UNIT])
        if i == 3:
            local("packed").start()
            local("att").start()

    step = 64

    def back_two(part):
        if part == 0:
            local("resid").wait()
            for copy in second_x:
                copy.wait_recv()

        def body(i, carry):
            rows = aligned(i, step)
            grad = first[rows, :] + x_in0[rows, :].astype(f32)
            d_values, d_gain, d_shift = norm_back(second[rows, :], second_gain, grad)
            total = dy[piece, rows, :].astype(f32) + d_values
            first[rows, :] = total
            branch[rows, :] = total.astype(bf16)
            early[0:1, :] += d_gain
            early[1:2, :] += d_shift
            return carry

        steps_each = part_rows // step
        if part == 0:
            early[...] = jnp.zeros_like(early)
        lax.fori_loop(part * steps_each, (part + 1) * steps_each, body, 0)

    def d_attended(half):
        rows = pl.ds(pl.multiple_of(half * d_width, 128), d_width)
        return dot_nt(branch[...], wd[rows, :]).astype(bf16)

    def d_att_other():
        local("out").wait()
        for copy in second_x:
            copy.wait_send()
        x_out0[:, :d_width] = d_attended(other)

    def d_att_own():
        d_att[half_rows(piece), :] = d_attended(piece)

    def grad_out(i):
        if i == 0:
            local("att_t").wait()
        left = lambda j: att_t[pl.ds(8 * j, 8)].reshape(8 * att_t.shape[1], own_rows)
        chunk(8 + i, left, lambda: branch[:, i * UNIT : (i + 1) * UNIT])
        if i == 1:
            local("hidden").start()

    first_lanes = head_lanes(PAIR)
    query_chunk = 256

    def pair_cols(p):
        return tuple(slice(t * d_width + PAIR * p, t * d_width + PAIR * (p + 1)) for t in range(3))

    def att_here(p):
        if p == 0:
            for name in ("lse", "packed", "normed_t", "att"):
                local(name).wait()
            lse[...] = lse_rows[...].T
        att_x[p].wait_recv()
        acc_k[...] = jnp.zeros_like(acc_k)
        acc_v[...] = jnp.zeros_like(acc_v)

    lane = lax.broadcasted_iota(jnp.int32, (1, PAIR), 1)
    lane = jnp.where(lane < HEAD_DIM, lane, lane - HEAD_DIM)

    def marked(value, marks):
        for at, part in enumerate(thirds(value)):
            marks = jnp.where(lane == at, part, marks)
        return marks

    def attend_back(p):
        at_q, at_k, at_v = pair_cols(p)
        heads = slice(p * PAIR, (p + 1) * PAIR)
        keys_t = wide[:, at_k].T

        def one_chunk(i, carry):
            rows = aligned(i, query_chunk)
            keys, values, queries = wide[:, at_k], wide[:, at_v], wide[rows, at_q]
            grads = d_att[rows, heads]
            attended = att_own[rows, heads]
            products = grads.astype(f32) * attended.astype(f32)
            nothing = jnp.zeros_like(queries)
            parts_q = []
            for h in range(2):
                here = first_lanes[h]
                dots = jnp.sum(jnp.where(here, products, 0.0), axis=1, keepdims=True)
                top = lse[rows, 2 * p + h : 2 * p + h + 1]
                one_q = jnp.where(here, queries, marked(-top, query_marks[rows, :]))
                one_g = jnp.where(here, grads, marked(-dots, nothing))
                probs = jnp.exp(dot_nt(jnp.where(here, keys, key_marks[...]), one_q))
                d_scores = (probs * dot_nt(jnp.where(here, values, key_marks[...]), one_g)).astype(bf16)
                acc_v[...] += dot_nn(probs.astype(bf16), jnp.where(here, grads, nothing))
                acc_k[...] += dot_nn(d_scores, jnp.where(here, queries, nothing))
                parts_q.append(dot_nn(keys_t[h * HEAD_DIM : (h + 1) * HEAD_DIM], d_scores))
            d_queries = jnp.concatenate(parts_q, axis=0).T * HEAD_DIM ** (-0.5)
            wide[rows, at_q] = d_queries.astype(bf16)
            return carry

        lax.fori_loop(0, length // query_chunk, one_chunk, 0)
        wide[:, at_k] = acc_k[...].astype(bf16)
        wide[:, at_v] = acc_v[...].astype(bf16)

    def grad_pair(p):
        n = 8 * parts.shape[4]
        left = lambda j: wd[pl.ds(pl.multiple_of(width + j * n, 64), n), :length]
        chunk(10 + p, left, lambda: jnp.concatenate([wide[:, at] for at in pair_cols(p)], axis=1))

    def down_here():
        for copy in down_x:
            copy.wait_recv()

    def write_output():
        def body(i, carry):
            rows = aligned(i, step)
            second[rows, :] += down_own[rows, :].astype(f32) + x_in1[rows, :].astype(f32)
            return carry

        lax.fori_loop(0, own_rows // step, body, 0)
        local("output").start()

    def d_normed(half, part, target):
        if part == 0 and target is x_out0:
            local("qkv").wait()
            for copy in att_x:
                copy.wait_send()
        at = halves[part]
        target[:, at] = dot_nt(wide[half_rows(half), :cols], wu[at, :cols]).astype(target.dtype)

    def d_normed_own():
        local("output").wait()
        for part in range(2):
            d_normed(piece, part, second)

    def back_one(part):
        if part == 0:
            local("hidden").wait()
            late[...] = jnp.zeros_like(late)
            for copy in normed_x:
                copy.wait_recv()

        def body(i, carry):
            rows = aligned(i, step)
            grad = second[rows, :] + x_in0[rows, :].astype(f32)
            d_values, d_gain, d_shift = norm_back(branch[rows, :].astype(f32), first_gain, grad)
            first[rows, :] += d_values
            late[0:1, :] += d_gain
            late[1:2, :] += d_shift
            return carry

        steps_each = part_rows // step
        lax.fori_loop(part * steps_each, (part + 1) * steps_each, body, 0)
        if part == 1:
            local("grad_hidden").start()

    def small_near(value, near_slots, base):
        own_slot = 2 * y + core
        return [
            remote(value, near_slots.at[own_slot], s_send, s_recv, base + k, peer) for k, peer in enumerate(group)
        ]

    def small_line(all_slots, base):
        own_slot = z * 2 + piece
        return [
            remote(all_slots.at[own_slot], all_slots.at[own_slot], s_send, s_recv, base + 3 + k, peer)
            for k, peer in enumerate(line)
        ]

    def small_one(value, near_slots, base):
        near_slots[2 * y + core] = value[...]
        for copy in small_near(value, near_slots, base):
            copy.start()

    def small_two(value, near_slots, all_slots, base):
        for copy in small_near(value, near_slots, base):
            copy.wait()
        all_slots[z * 2 + piece] = ((near_slots[0] + near_slots[1]) + near_slots[2]) + near_slots[3]
        for copy in small_line(all_slots, base):
            copy.start()

    def small_three(all_slots, base, at):
        for copy in small_line(all_slots, base):
            copy.wait()
        n = all_slots.shape[1]
        for x in range(2):
            total = ((all_slots[x] + all_slots[2 + x]) + all_slots[4 + x]) + all_slots[6 + x]
            small[x, at : at + n, :] = total

    def early_one():
        early[2:3, :] = bias_sum[:, :width]
        early[3:4, :] = bias_sum[:, width:]
        small_one(early, early_near, 0)

    call = functools.partial
    steps = [ready_units, down_first, down_x[0].start, call(d_units, 0, 2), call(d_units, 2, 4), call(d_units, 4, 5)]
    for part in range(2):
        steps += [call(d_second, other, part, x_out0), second_x[part].start]
    steps += [call(grad_up, 0), call(grad_up, 1), d_second_own, down_other, call(grad_up, 2), call(grad_up, 3), down_mine]
    steps += [call(write_marks, starts, key_marks, query_marks), call(back_two, 0), call(back_two, 1), d_att_other]
    steps += [copy.start for copy in att_x]
    steps += [d_att_own, down_x[1].start, early_one, call(grad_out, 0), call(grad_out, 1)]
    for p in range(pairs):
        steps += [call(att_here, p)] + [call(attend_back, p)]
        if p < 3:
            steps += [call(grad_pair, p)]
        if p == 1:
            steps += [call(small_two, early, early_near, early_all, 0)]
    for part in range(2):
        steps += [call(d_normed, other, part, x_out0), normed_x[part].start]
    steps += [call(grad_pair, 3), call(grad_pair, 4), down_here, write_output, d_normed_own]
    steps += [call(back_one, 0), call(back_one, 1), call(small_one, late, late_near, 10)]
    steps += [call(small_three, early_all, 0, 2), call(small_two, late, late_near, late_all, 10)]
    steps += [call(small_three, late_all, 10, 0)]
    for i, one in enumerate(steps):
        for where in BACKWARD_MOVES[i]:
            move(*where)
        one()
    small_keep = pltpu.make_async_copy(small, small_out, keep_sem.at[chunks])
    small_keep.start()
    for where in BACKWARD_MOVES[len(steps)]:
        move(*where)
    for i in range(chunks):
        copy_b(i).wait_send()
        for copy in copies_c(i, 0) + copies_c(i, 1):
            copy.wait_send()
        copy_g(i).wait()
        keep_g(i).wait()
    small_keep.wait()
    for copy in down_x + normed_x:
        copy.wait_send()
    local("grad_hidden").wait()


def backward(starts, gain1, gain2, hidden, cot, dy_other, q_all, o_all, u_all, d_all, *kept):
    bf16, f32 = jnp.bfloat16, jnp.float32
    own_rows, width = hidden.shape
    length = 2 * own_rows
    cols, units = q_all.shape[1], u_all.shape[1]
    rows = width // 16
    wide_units, pairs = 10, cols // (3 * PAIR)
    pair_cols = 3 * PAIR
    outs = [
        ((own_rows, width), f32),
        ((own_rows, width), f32),
        ((2, wide_units, rows, UNIT), bf16),
        ((2, pairs, rows, pair_cols), bf16),
        ((2, 6, width), f32),
    ]
    token = ((own_rows, width), bf16)
    scratch = [
        ((16, rows, length), bf16),
        ((16, rows, own_rows), bf16),
        ((length, cols // 3), bf16),
        ((own_rows, units), bf16),
        ((length, units), bf16),
        ((units, width), bf16),
        ((width, units), bf16),
        ((2, own_rows, width), bf16),
        ((own_rows, width), f32),
        ((own_rows, width), f32),
        ((length, cols // 3), bf16),
        token, token, token, token,
        ((SLOTS, 2, 2, ROWS_Z, rows, UNIT), bf16),
        ((wide_units, 2, ROWS_Z, rows, UNIT), bf16),
        ((pairs, 2, ROWS_Z, rows, pair_cols), bf16),
        ((wide_units, ROWS_Z, rows, UNIT), bf16),
        ((pairs, ROWS_Z, rows, pair_cols), bf16),
        ((wide_units, 3, rows, UNIT), bf16),
        ((pairs, 3, rows, pair_cols), bf16),
        ((own_rows, 512), bf16),
        ((PAIR, length), f32),
        ((length, PAIR), f32),
        ((length, PAIR), bf16),
        ((length, PAIR), bf16),
        ((length, PAIR), f32),
        ((length, PAIR), f32),
        ((1, units), f32),
        ((4, width), f32),
        ((2, width), f32),
        ((4, 4, width), f32),
        ((4, 2, width), f32),
        ((8, 4, width), f32),
        ((8, 2, width), f32),
        ((2, 6, width), f32),
    ]
    vmem = pl.BlockSpec(memory_space=pltpu.VMEM)
    anywhere = pl.BlockSpec(memory_space=pl.ANY)
    smem = pl.BlockSpec(memory_space=pltpu.SMEM)
    chunks = wide_units + pairs
    dma = lambda n: pltpu.SemaphoreType.DMA((n,))
    sems = [29] + [chunks] * 4 + [4 * chunks] * 2 + [chunks] * 2 + [6 + pairs] * 2 + [20, 20, chunks + 1]
    return pl.pallas_call(
        backward_kernel,
        out_shape=[jax.ShapeDtypeStruct(shape, kind) for shape, kind in outs],
        in_specs=[smem, vmem, vmem] + [anywhere] * (7 + len(kept)),
        out_specs=[anywhere] * len(outs),
        scratch_shapes=[pltpu.VMEM(shape, kind) for shape, kind in scratch] + [dma(n) for n in sems],
        compiler_params=pltpu.CompilerParams(
            collective_id=2, has_side_effects=True, vmem_limit_bytes=60 * 1024 * 1024
        ),
        name="backward",
    )(starts, gain1, gain2, hidden, cot, dy_other, q_all, o_all, u_all, d_all, *kept)


def finish_kernel(
    raw_output, raw_grad, units_lo, units_hi, pairs_in, small,
    output, grad_hidden, qkv, out, up, down, gain1, shift1, gain2, shift2, bias,
):
    f32 = jnp.float32
    step = pl.program_id(0)
    output[0] = raw_output[...]
    grad_hidden[0] = raw_grad[...]
    rows = out.shape[0]
    width = small.shape[2]
    units_in = (units_lo, units_hi)

    def mixed(first, second):
        each = first.shape[1] // 4
        blocks = []
        for j in range(4):
            at = slice(j * each, (j + 1) * each)
            blocks += [first[:, at].astype(f32), second[:, at].astype(f32)]
        return jnp.concatenate(blocks, axis=1)

    for now in range(2):

        @pl.when(step == now)
        def _():
            for i in range(4):
                h, column = divmod(i, 2)
                at = slice(column * UNIT, (column + 1) * UNIT)
                down[h * rows : (h + 1) * rows, at] = units_in[now][0, i].astype(f32)
            for i in range(2):
                chunk = 4 + 2 * now + i
                at = slice(i * 2 * UNIT, (i + 1) * 2 * UNIT)
                up[:, at] = mixed(units_lo[0, chunk], units_hi[0, chunk])
            out[...] = units_lo[0, 8 + now].astype(f32) + units_hi[0, 8 + now].astype(f32)
            pairs = pairs_in.shape[1]
            for block in range(3 * now, 3 * now + 3):
                part, piece = divmod(block, 2)
                for p in range(pairs):
                    at = (block - 3 * now) * pairs * PAIR + p * PAIR
                    chunk = pairs_in[piece, p, :, part * PAIR : (part + 1) * PAIR]
                    qkv[:, at : at + PAIR] = chunk.astype(f32)

    @pl.when(step == 0)
    def _():
        for i, ref in enumerate((gain1, shift1, gain2, shift2)):
            ref[...] = (small[0, i : i + 1, :] + small[1, i : i + 1, :]).reshape(width)
        for g in range(2):
            for j in range(2):
                at = slice(j * UNIT, (j + 1) * UNIT)
                lo, hi = small[0, 4 + g : 5 + g, at], small[1, 4 + g : 5 + g, at]
                begin = (2 * g + j) * 2 * UNIT
                bias[begin : begin + 2 * UNIT] = mixed(lo, hi).reshape(2 * UNIT)


def finish(raw_output, raw_grad, units_in, pairs_in, small):
    f32 = jnp.float32
    own_rows, width = raw_output.shape
    rows = units_in.shape[2]
    shapes = [
        (1, own_rows, width), (1, own_rows, width), (rows, 3 * width), (rows, width), (rows, 8 * UNIT),
        (4 * rows, width), (width,), (width,), (width,), (width,), (8 * UNIT,),
    ]
    token = pl.BlockSpec((own_rows // 2, width), lambda s: (s, 0))
    token_out = pl.BlockSpec((1, own_rows // 2, width), lambda s: (0, s, 0))
    columns = lambda n: pl.BlockSpec((rows, n // 2), lambda s: (0, s))
    fixed = lambda shape: pl.BlockSpec(shape, lambda s: (0,) * len(shape))
    half = lambda i: pl.BlockSpec((1,) + units_in.shape[1:], lambda s: (i, 0, 0, 0))
    return pl.pallas_call(
        finish_kernel,
        grid=(2,),
        out_shape=[jax.ShapeDtypeStruct(shape, f32) for shape in shapes],
        in_specs=[token, token, half(0), half(1), fixed(pairs_in.shape), fixed(small.shape)],
        out_specs=[
            token_out, token_out, columns(3 * width), columns(width), columns(8 * UNIT),
            pl.BlockSpec((2 * rows, width), lambda s: (s, 0)),
        ] + [fixed(shape) for shape in shapes[6:]],
        compiler_params=pltpu.CompilerParams(vmem_limit_bytes=60 * 1024 * 1024),
        name="finish",
    )(raw_output, raw_grad, units_in, units_in, pairs_in, small)


def split_layer(
    hidden, starts, first_gain, first_shift, qkv_weight, out_weight, second_gain, second_shift,
    up_weight, hidden_bias, down_weight, cotangent,
):
    shards = lax.axis_size("rows")
    (
        qkv_all, out_all, up_all, down_all, dy_other, down_sums, normed_t, packed, lse, att, att_t, residual, second_t,
        activated, slope,
    ) = forward(
        hidden[0], cotangent[0], starts, first_gain, first_shift, second_gain, second_shift, hidden_bias,
        qkv_weight, out_weight, up_weight, down_weight,
    )
    whole = lambda w: w.reshape(-1, w.shape[-1])
    blocks = lambda w: w.reshape(shards, -1, w.shape[-1])
    shares = backward(
        starts, first_gain, second_gain, hidden[0], cotangent[0], dy_other, whole(qkv_all), whole(out_all),
        whole(up_all), whole(down_all), down_sums, normed_t, packed, lse, att, blocks(att_t), residual,
        blocks(second_t), activated, slope,
    )
    return tuple(finish(*shares))


def splits_evenly(mesh):
    pieces = mesh.shape["blk"]
    return pieces == 2 and mesh.shape["rows"] == 2 * ROWS_Z * ROWS_Y and HEADS % (2 * pieces) == 0


def solution(mesh):
    in_specs = (
        P("rows", "blk", None),
        P("rows", None),
        P(),
        P(),
        P("rows", None),
        P("rows", None),
        P(),
        P(),
        P("rows", None),
        P(),
        P("rows", None),
        P("rows", "blk", None),
    )
    out_specs = (
        P("rows", "blk", None),
        P("rows", "blk", None),
        P("rows", None),
        P("rows", None),
        P("rows", None),
        P("rows", None),
        P(),
        P(),
        P(),
        P(),
        P(),
    )
    layer = split_layer if splits_evenly(mesh) else on_device
    return jax.shard_map(
        layer, mesh=mesh, in_specs=in_specs, out_specs=out_specs, check_vma=False
    )
```
